32 devices in a mesh: dp: 8 (over z, core), tensor: 4 (over y, x).
Axes of the slice: x: 2, y: 2, z: 4, core: 2. Of those that a mesh axis runs over, the one named last changes fastest.
Arguments:
- train_states: bfloat16 [2048, 8192], P('dp'), may hold values from -6 to 6
- qkv_cotangent: bfloat16 [2048, 3072], P('dp', 'tensor'), may hold values from -0.13183594 to 0.13183594
- w_master: float32 [8192, 3072], P('dp', 'tensor'), may hold values from -1.1048543 to 1.1048543
- moment_one: float32 [8192, 3072], P('dp', 'tensor'), may hold values from -1.8 to 1.8
- moment_two: float32 [8192, 3072], P('dp', 'tensor'), may hold values from 0.02 to 2
- prompt_states: bfloat16 [4096, 8192], P('dp'), may hold values from -45 to 45
- norm_gain: float32 [8192], replicated, may hold values from 0.1 to 1.9
- w_out: bfloat16 [2048, 8192], P('tensor'), may hold values from -0.125 to 0.125
Outputs:
- update_dir: float32 [8192, 3072], P('dp', 'tensor')
- prefill_out: bfloat16 [4096, 8192], P(('dp', 'tensor'))
The draws below stay inside these ranges and needn't reach their ends.
All inputs are finite; a program needn't handle non-finite values.
Results may differ from the reference program's by a relative error of at most 0.02.
Values may be sent and summed in bfloat16 or wider, within the bound.
No kernel may reach another device: no remote copies, remote signals or barrier semaphores. Data moves between devices by JAX's collectives and lax.ppermute only.
A program may use at most 128 MiB of HBM per device.

```python
import math
import jax
import jax.numpy as jnp
from jax import lax

D = 8192
HD = 128
QH_DEV = 4
KV_DEV = 1
TRG = 256
LEN = 512
HEADS = 16
QKV_COLS = 3072
TRAIN = 2048
N_DP = 8
N_TENSOR = 4


def draw_prompt_states(key, part):
    row_total = LEN * N_DP
    key_values, key_scales, key_columns = jax.random.split(key, 3)
    spread = 0.5 * math.log(10.0)
    values_draw = jax.random.truncated_normal(key_values, -4.0, 4.0, (row_total, D), jnp.float32)
    row_scale = jnp.exp(jax.random.uniform(key_scales, (row_total, 1), jnp.float32, -spread, spread))
    column_scale = jnp.exp(jax.random.uniform(key_columns, (1, D), jnp.float32, -spread, spread))
    return (values_draw * row_scale * column_scale).astype(jnp.bfloat16)


def draw_w_master(key, part):
    slice_width = (QH_DEV + 2 * KV_DEV) * HD
    key_base = jax.random.fold_in(key, 0)
    base_draw = jax.random.truncated_normal(key_base, -4.0, 4.0, (D, N_TENSOR, slice_width), jnp.float32) / math.sqrt(D)
    return base_draw.reshape(D, N_TENSOR * slice_width)


def spiked(entries, key, source, target, parts, factor):
    def block_of(axis_at):
        return (jnp.arange(entries.shape[axis_at]) // (entries.shape[axis_at] // parts)).reshape((-1,) + (1,) * (entries.ndim - 1 - axis_at))

    first = jax.random.permutation(key, parts)[block_of(target)]
    other_side = (block_of(target) + parts // 2) % parts
    return jnp.where((block_of(source) == first) | (block_of(source) == other_side), factor * entries, entries)


def shard_levels(stream_key, shape, cuts, low, largest):
    gain = 1.0
    for dim, parts in cuts:
        steps = jax.random.uniform(jax.random.fold_in(jax.random.fold_in(stream_key, 6), dim), (parts,), jnp.float32, low / len(cuts), largest / len(cuts))
        gain = gain * jnp.repeat(jnp.exp(steps), shape[dim] // parts).reshape((-1,) + (1,) * (len(shape) - 1 - dim))
    return gain


def scatter_about(rng, extent, width, reach, cuts=(), held_as=jnp.bfloat16):
    drawn = width * jax.random.normal(rng, extent, jnp.float32)
    if cuts:
        drawn = drawn * shard_levels(rng, extent, cuts, -0.22, 0.18)
    return jnp.clip(drawn, -reach, reach).astype(held_as)


def gaussian_with(own_key, extent, deviation, reach, shards, heavy, held_as=jnp.bfloat16):
    drawn = deviation * jax.random.normal(own_key, extent, jnp.float32)
    if shards:
        drawn = drawn * shard_levels(own_key, extent, shards, -0.22, 0.18)
    return jnp.clip(spiked(drawn, jax.random.fold_in(own_key, 3), *heavy), -reach, reach).astype(held_as)


def setup_inputs(seed: int = 0) -> dict:
    arg_keys = jax.random.split(jax.random.key(seed), 9)
    return {
        "train_states": gaussian_with(arg_keys[0], (TRAIN, D), 1.0, 6.0, ((0, 8),), (0, 1, 8, 2.0)),
        "qkv_cotangent": scatter_about(arg_keys[1], (TRAIN, QKV_COLS), (1.0 / (TRG * N_DP) ** 0.5), 0.13183594, ((0, 8), (1, 4))),
        "w_master": draw_w_master(jax.random.fold_in(arg_keys[8], 71), 0),
        "moment_one": scatter_about(arg_keys[3], (D, QKV_COLS), 0.3, 1.8, ((0, 8), (1, 4)), jnp.float32),
        "moment_two": jnp.clip(jnp.exp(math.log(2.0) - 4.6051702 * jax.random.uniform(arg_keys[4], (D, QKV_COLS), jnp.float32) ** shard_levels(arg_keys[4], (D, QKV_COLS), ((0, 8), (1, 4)), -0.2, 0.2)), 0.02, 2.0),
        "prompt_states": draw_prompt_states(jax.random.fold_in(arg_keys[8], 71), 0),
        "norm_gain": jnp.clip(1.0 + 0.18 * jax.random.normal(arg_keys[6], (D,), jnp.float32), 0.1, 1.9),
        "w_out": scatter_about(arg_keys[7], (HEADS * HD, D), (HEADS * HD) ** -0.5, 0.125, ((0, 4),)),
    }


beta_one = 0.9
beta_two = 0.95
bias_one = 1.0 - 0.9 ** 8
bias_two = 1.0 - 0.95 ** 8
learn_rate = 0.002
adam_eps = 1e-08
norm_eps = 1e-05
rope_base = 500000.0

def rope_tables(length, head_size):
    half_width = head_size // 2
    exponent = jnp.arange(half_width, dtype=jnp.float32) * (2.0 / head_size)
    inverse = jnp.power(jnp.float32(rope_base), -exponent)
    position = jnp.arange(length, dtype=jnp.float32)
    angles = position[:, None] * inverse[None, :]
    cosine_table = jnp.concatenate([jnp.cos(angles), jnp.cos(angles)], axis=1)
    sine_table = jnp.concatenate([jnp.sin(angles), jnp.sin(angles)], axis=1)
    return (cosine_table, sine_table)

def rotate(head_block, cosine_table, sine_table):
    half_width = head_block.shape[-1] // 2
    turned = jnp.concatenate([-head_block[..., half_width:], head_block[..., :half_width]], axis=-1)
    return head_block * cosine_table + turned * sine_table

def reference(train_states, qkv_cotangent, w_master, moment_one, moment_two, prompt_states, norm_gain, w_out):
    gradient = jnp.dot(train_states.T, qkv_cotangent, preferred_element_type=jnp.float32)
    moment_new = beta_one * moment_one + (1.0 - beta_one) * gradient
    second_new = beta_two * moment_two + (1.0 - beta_two) * gradient * gradient
    update_dir = moment_new / bias_one / (jnp.sqrt(second_new / bias_two) + adam_eps)
    qkv_weight = (w_master - learn_rate * update_dir).astype(jnp.bfloat16)
    slice_width = (QH_DEV + 2 * KV_DEV) * HD
    query_width = QH_DEV * HD
    score_scale = HD ** (-0.5)
    cosine_table, sine_table = rope_tables(LEN, HD)
    causal = jnp.arange(LEN)[:, None] >= jnp.arange(LEN)[None, :]
    out_blocks = w_out.reshape(N_TENSOR, query_width, D).astype(jnp.float32)

    def prefill_group(states):
        widened = states.astype(jnp.float32)
        mean_square = lax.optimization_barrier(jnp.mean(widened * widened, axis=1, keepdims=True))
        normed = (widened * lax.rsqrt(mean_square + norm_eps) * norm_gain).astype(jnp.bfloat16)
        projected = jnp.dot(normed, qkv_weight, preferred_element_type=jnp.float32)
        projected = projected.reshape(LEN, N_TENSOR, slice_width)
        queries = projected[:, :, :query_width].reshape(LEN, N_TENSOR, QH_DEV, HD)
        queries = (rotate(queries, cosine_table[:, None, None, :], sine_table[:, None, None, :]) * score_scale).astype(jnp.bfloat16)
        key_rows = rotate(projected[:, :, query_width:query_width + HD], cosine_table[:, None, :], sine_table[:, None, :]).astype(jnp.bfloat16)
        value_rows = projected[:, :, query_width + HD:].astype(jnp.bfloat16)
        scores = jnp.einsum('qjhd,kjd->jhqk', queries.astype(jnp.float32), key_rows.astype(jnp.float32))
        scores = jnp.where(causal[None, None], scores, -jnp.inf)
        attend_weights = jax.nn.softmax(scores, axis=-1).astype(jnp.bfloat16)
        attended = jnp.einsum('jhqk,kjd->qjhd', attend_weights.astype(jnp.float32), value_rows.astype(jnp.float32)).astype(jnp.bfloat16)
        attended = attended.reshape(LEN, N_TENSOR, query_width)
        head_part = jnp.einsum('qja,jad->jqd', attended.astype(jnp.float32), out_blocks).astype(jnp.bfloat16)
        head_part = lax.optimization_barrier(head_part)
        return lax.optimization_barrier(jnp.sum(head_part.astype(jnp.float32), axis=0)).astype(jnp.bfloat16)
    outputs = lax.map(prefill_group, prompt_states.reshape(N_DP, LEN, D))
    return (update_dir, outputs.reshape(N_DP * LEN, D))
```

```python
import jax
import jax.numpy as jnp
from jax import lax
from jax.sharding import PartitionSpec as P

HD = 128


beta_one = 0.9
beta_two = 0.95
bias_one = 1.0 - 0.9**8
bias_two = 1.0 - 0.95**8
learn_rate = 0.002
adam_eps = 1e-08
norm_eps = 1e-05
rope_base = 500000.0

WEIGHT_CHUNKS = 2


def rope_tables(length, head_size):
    half_width = head_size // 2
    exponent = jnp.arange(half_width, dtype=jnp.float32) * (2.0 / head_size)
    inverse = jnp.power(jnp.float32(rope_base), -exponent)
    position = jnp.arange(length, dtype=jnp.float32)
    angles = position[:, None] * inverse[None, :]
    cosine_table = jnp.concatenate([jnp.cos(angles), jnp.cos(angles)], axis=1)
    sine_table = jnp.concatenate([jnp.sin(angles), jnp.sin(angles)], axis=1)
    return (cosine_table, sine_table)


def rotate(head_block, cosine_table, sine_table):
    half_width = head_block.shape[-1] // 2
    turned = jnp.concatenate([-head_block[..., half_width:], head_block[..., :half_width]], axis=-1)
    return head_block * cosine_table + turned * sine_table


def ring_order(count):
    return list(range(0, count, 2)) + list(range(count - 1, 0, -2))


def ring_shift(count, step):
    order = ring_order(count)
    return [(order[place], order[(place + step) % count]) for place in range(count)]


def ring_place(index, count):
    half = index // 2
    return jnp.where(index % 2 == 0, half, count - 1 - half)


def ring_index(place, count):
    return jnp.where(place < (count + 1) // 2, 2 * place, 2 * (count - place) - 1)


def gather_ring(piece, count):
    half = piece.shape[0] // 2
    forward, backward = [piece[:half]], [piece[half:]]
    for _ in range(count - 1):
        forward.append(lax.ppermute(forward[-1], "tensor", ring_shift(count, 1)))
        backward.append(lax.ppermute(backward[-1], "tensor", ring_shift(count, -1)))
    return forward, backward


def body(
    train_states, qkv_cotangent, w_master, moment_one, moment_two, prompt_states, norm_gain, w_out
):
    n_dp = lax.axis_size("dp")
    n_tensor = lax.axis_size("tensor")
    dp_index = lax.axis_index("dp")
    tensor_index = lax.axis_index("tensor")
    core = dp_index % 2
    pairs = [(i, i ^ 1) for i in range(n_dp)]
    rows, slice_width = w_master.shape
    tokens, width = train_states.shape
    length = prompt_states.shape[0]

    share = rows // n_tensor
    outgoing = jnp.stack(
        [
            lax.dynamic_slice(
                train_states, (0, owner * rows + tensor_index * share), (tokens, share)
            )
            for owner in range(n_dp)
        ]
    )
    cotangents = lax.all_gather(qkv_cotangent, "dp", axis=0, tiled=True)
    incoming = lax.all_to_all(outgoing, "dp", 0, 0, tiled=True).reshape(n_dp * tokens, share)
    columns = lax.all_gather(incoming, "tensor", axis=0)
    gradient = lax.dot_general(
        columns, cotangents, (((1,), (0,)), ((), ())), preferred_element_type=jnp.float32
    ).reshape(rows, slice_width)

    moment_new = beta_one * moment_one + (1.0 - beta_one) * gradient
    second_new = beta_two * moment_two + (1.0 - beta_two) * gradient * gradient
    update_dir = moment_new / bias_one / (jnp.sqrt(second_new / bias_two) + adam_eps)
    owned_weight = (w_master - learn_rate * update_dir).astype(jnp.bfloat16)

    half_width = width // 2
    w_half = lax.dynamic_slice(w_out, (0, core * half_width), (w_out.shape[0], half_width))
    out_forward, out_backward = gather_ring(w_half, n_tensor)
    out_weight = jnp.concatenate(out_forward + out_backward, axis=0)

    widened = prompt_states.astype(jnp.float32)
    mean_square = jnp.mean(widened * widened, axis=1, keepdims=True)
    normed = (widened * lax.rsqrt(mean_square + norm_eps) * norm_gain).astype(jnp.bfloat16)
    chunk = rows // WEIGHT_CHUNKS
    normed_chunks = [
        jnp.concatenate(
            [
                normed[:, owner * rows + part * chunk : owner * rows + (part + 1) * chunk]
                for owner in range(n_dp)
            ],
            axis=1,
        )
        for part in range(WEIGHT_CHUNKS)
    ]
    normed_chunks = lax.optimization_barrier(normed_chunks)
    projected = 0.0
    for part in range(WEIGHT_CHUNKS):
        weight = lax.all_gather(
            owned_weight[part * chunk : (part + 1) * chunk], "dp", axis=0, tiled=True
        )
        projected = projected + jnp.dot(
            normed_chunks[part], weight, preferred_element_type=jnp.float32
        )

    query_width = slice_width - 2 * HD
    head_count = query_width // HD
    score_scale = HD ** (-0.5)
    cosine_table, sine_table = rope_tables(length, HD)
    queries = projected[:, :query_width].reshape(length, head_count, HD)
    queries = (
        rotate(queries, cosine_table[:, None, :], sine_table[:, None, :]) * score_scale
    ).astype(jnp.bfloat16)
    key_rows = rotate(
        projected[:, query_width : query_width + HD], cosine_table, sine_table
    ).astype(jnp.bfloat16)
    value_rows = projected[:, query_width + HD :].astype(jnp.bfloat16)
    scores = jnp.einsum("qhd,kd->hqk", queries, key_rows, preferred_element_type=jnp.float32)
    causal = jnp.arange(length)[:, None] >= jnp.arange(length)[None, :]
    scores = jnp.where(causal[None], scores, -jnp.inf)
    attend_weights = jax.nn.softmax(scores, axis=-1).astype(jnp.bfloat16)
    attended = jnp.einsum(
        "hqk,kd->qhd", attend_weights, value_rows, preferred_element_type=jnp.float32
    ).astype(jnp.bfloat16)
    attended = attended.reshape(length, query_width)

    kept = length // n_tensor
    place = ring_place(tensor_index, n_tensor)
    heads = []
    for step in range(n_tensor):
        target = ring_index((place + step) % n_tensor, n_tensor)
        block = lax.dynamic_slice(attended, (target * kept, 0), (kept, query_width))
        if step:
            block = lax.ppermute(block, "tensor", ring_shift(n_tensor, step))
        heads.append(block)
    half = query_width // 2
    mine = jnp.concatenate(
        [heads[step][:, :half] for step in range(n_tensor)]
        + [heads[-step][:, half:] for step in range(n_tensor)],
        axis=1,
    )
    other = lax.ppermute(mine, "dp", pairs)
    both = jnp.concatenate([mine, other], axis=0)
    made = jnp.dot(both, out_weight, preferred_element_type=jnp.float32).astype(jnp.bfloat16)
    swapped = lax.ppermute(made[kept:], "dp", pairs)
    first = core == 0
    summed = jnp.concatenate(
        [jnp.where(first, made[:kept], swapped), jnp.where(first, swapped, made[:kept])], axis=1
    )
    return (update_dir, summed)


def solution(mesh):
    placed = (
        P("dp", None),
        P("dp", "tensor"),
        P("dp", "tensor"),
        P("dp", "tensor"),
        P("dp", "tensor"),
        P("dp", None),
        P(),
        P("tensor", None),
    )
    return jax.shard_map(
        body,
        mesh=mesh,
        in_specs=placed,
        out_specs=(P("dp", "tensor"), P(("dp", "tensor"), None)),
        check_vma=False,
    )
```

```python
import jax
import jax.numpy as jnp
from jax import lax
from jax.sharding import PartitionSpec as P

HD = 128


beta_one = 0.9
beta_two = 0.95
bias_one = 1.0 - 0.9**8
bias_two = 1.0 - 0.95**8
learn_rate = 0.002
adam_eps = 1e-08
norm_eps = 1e-05
rope_base = 500000.0

def rope_tables(length, head_size):
    half_width = head_size // 2
    exponent = jnp.arange(half_width, dtype=jnp.float32) * (2.0 / head_size)
    inverse = jnp.power(jnp.float32(rope_base), -exponent)
    position = jnp.arange(length, dtype=jnp.float32)
    angles = position[:, None] * inverse[None, :]
    cosine_table = jnp.concatenate([jnp.cos(angles), jnp.cos(angles)], axis=1)
    sine_table = jnp.concatenate([jnp.sin(angles), jnp.sin(angles)], axis=1)
    return (cosine_table, sine_table)


def rotate(head_block, cosine_table, sine_table):
    half_width = head_block.shape[-1] // 2
    turned = jnp.concatenate([-head_block[..., half_width:], head_block[..., :half_width]], axis=-1)
    return head_block * cosine_table + turned * sine_table


WEIGHT_CHUNKS = 2


def line_pairs(places):
    return [(2 * a + core, 2 * b + core) for a, b in places for core in range(2)]


def line_gather(block, place, count):
    from_low, from_high = [block], [block]
    for step in range(1, count - 1):
        from_low.append(
            lax.ppermute(
                from_low[-1], "dp", line_pairs([(i, i + 1) for i in range(step - 1, count - 1)])
            )
        )
        from_high.append(
            lax.ppermute(
                from_high[-1], "dp", line_pairs([(i, i - 1) for i in range(1, count - step + 1)])
            )
        )
    last = lax.ppermute(
        jnp.where(place == count - 2, from_low[-1], from_high[-1]),
        "dp",
        line_pairs([(count - 2, count - 1), (1, 0)]),
    )
    slots = [(place, block)]
    for step in range(1, count):
        if step < count - 1:
            low, high = from_low[step], from_high[step]
        else:
            low, high = last, last
        spare = count - step
        is_low = place >= step
        is_high = place <= count - 1 - step
        if step <= count - step - 1 or 2 * step <= count:
            chosen = jnp.where(is_low, low, high)
            owner = jnp.where(is_low, place - step, place + step)
        else:
            chosen = jnp.where(is_low, low, jnp.where(is_high, high, from_high[spare]))
            owner = jnp.where(
                is_low, place - step, jnp.where(is_high, place + step, place + spare)
            )
        slots.append((owner, chosen))
    return slots


def plane_gather(block, count):
    if count != 4:
        gathered = lax.all_gather(block, "tensor", axis=0)
        own = lax.axis_index("tensor")
        return [
            lax.dynamic_index_in_dim(gathered, own ^ b, 0, keepdims=False) for b in range(count)
        ]
    half = block.shape[0] // 2
    by_one = [(j, j ^ 1) for j in range(count)]
    by_two = [(j, j ^ 2) for j in range(count)]
    one = lax.ppermute(block, "tensor", by_one)
    two = lax.ppermute(block, "tensor", by_two)
    upper = lax.ppermute(one[:half], "tensor", by_two)
    lower = lax.ppermute(two[half:], "tensor", by_one)
    return [block, one, two, jnp.concatenate([upper, lower], axis=0)]


def place_blocks(blocks, owners):
    stacked = jnp.zeros((len(blocks),) + blocks[0].shape, blocks[0].dtype)
    for block, owner in zip(blocks, owners):
        stacked = lax.dynamic_update_index_in_dim(stacked, block, owner, 0)
    return stacked


def body(
    train_states, qkv_cotangent, w_master, moment_one, moment_two, prompt_states, norm_gain, w_out
):
    n_dp = lax.axis_size("dp")
    n_tensor = lax.axis_size("tensor")
    line = n_dp // 2
    dp_index = lax.axis_index("dp")
    tensor_index = lax.axis_index("tensor")
    core = dp_index % 2
    place = dp_index // 2
    siblings = [(i, i ^ 1) for i in range(n_dp)]
    rows, slice_width = w_master.shape
    tokens, width = train_states.shape
    length = prompt_states.shape[0]
    chunk = rows // WEIGHT_CHUNKS
    share = chunk // n_tensor

    half_width = width // 2
    w_half = lax.dynamic_slice(w_out, (0, core * half_width), (w_out.shape[0], half_width))
    out_weight = lax.all_gather(w_half, "tensor", axis=0, tiled=True)

    own_cotangents = line_gather(qkv_cotangent, place, line)
    own_cotangents = place_blocks(
        [block for _, block in own_cotangents], [owner for owner, _ in own_cotangents]
    ).reshape(line * tokens, slice_width)
    other_cotangents = lax.ppermute(own_cotangents, "dp", siblings)
    cotangents = jnp.concatenate([own_cotangents, other_cotangents], axis=0)

    widened = prompt_states.astype(jnp.float32)
    mean_square = jnp.mean(widened * widened, axis=1, keepdims=True)
    normed = (widened * lax.rsqrt(mean_square + norm_eps) * norm_gain).astype(jnp.bfloat16)

    def owner_columns(which):
        picked = []
        for part in range(WEIGHT_CHUNKS):
            picked.append(
                jnp.stack(
                    [
                        lax.dynamic_slice(
                            normed,
                            (0, (2 * i + which) * rows + part * chunk),
                            (length, chunk),
                        )
                        for i in range(line)
                    ]
                )
            )
        return jnp.stack(picked)

    kept_columns = owner_columns(core)
    sent_columns = owner_columns(1 - core)
    got_columns = lax.ppermute(sent_columns, "dp", siblings)
    both_columns = jnp.concatenate([kept_columns, got_columns], axis=2)

    updates, partial = [], 0.0
    ready = train_states
    for part in range(WEIGHT_CHUNKS):
        pieces, owners = [], []
        for distance in range(n_dp):
            target = dp_index ^ distance
            piece = lax.dynamic_slice(
                ready,
                (0, target * rows + part * chunk + tensor_index * share),
                (tokens, share),
            )
            if distance:
                piece = lax.ppermute(piece, "dp", [(i, i ^ distance) for i in range(n_dp)])
            pieces.append(piece)
            owners.append((distance % 2) * line + target // 2)
        pieces, ready = lax.optimization_barrier((pieces, ready))
        columns = place_blocks(pieces, owners).reshape(n_dp * tokens, share)
        spread = plane_gather(columns, n_tensor)
        columns = place_blocks(spread, [tensor_index ^ b for b in range(n_tensor)])
        gradient = lax.dot_general(
            columns, cotangents, (((1,), (0,)), ((), ())), preferred_element_type=jnp.float32
        ).reshape(chunk, slice_width)

        here = slice(part * chunk, (part + 1) * chunk)
        moment_new = beta_one * moment_one[here] + (1.0 - beta_one) * gradient
        second_new = beta_two * moment_two[here] + (1.0 - beta_two) * gradient * gradient
        update = moment_new / bias_one / (jnp.sqrt(second_new / bias_two) + adam_eps)
        updates.append(update)
        owned_weight = (w_master[here] - learn_rate * update).astype(jnp.bfloat16)

        for owner, weight in line_gather(owned_weight, place, line):
            states = lax.dynamic_index_in_dim(both_columns[part], owner, 0, keepdims=False)
            partial = partial + jnp.dot(states, weight, preferred_element_type=jnp.float32)
    update_dir = jnp.concatenate(updates, axis=0)
    projected = partial[:length] + lax.ppermute(partial[length:], "dp", siblings)

    query_width = slice_width - 2 * HD
    head_count = query_width // HD
    score_scale = HD ** (-0.5)
    cosine_table, sine_table = rope_tables(length, HD)
    queries = projected[:, :query_width].reshape(length, head_count, HD)
    queries = (
        rotate(queries, cosine_table[:, None, :], sine_table[:, None, :]) * score_scale
    ).astype(jnp.bfloat16)
    key_rows = rotate(
        projected[:, query_width : query_width + HD], cosine_table, sine_table
    ).astype(jnp.bfloat16)
    value_rows = projected[:, query_width + HD :].astype(jnp.bfloat16)
    scores = jnp.einsum("qhd,kd->hqk", queries, key_rows, preferred_element_type=jnp.float32)
    causal = jnp.arange(length)[:, None] >= jnp.arange(length)[None, :]
    scores = jnp.where(causal[None], scores, -jnp.inf)
    attend_weights = jax.nn.softmax(scores, axis=-1).astype(jnp.bfloat16)
    attended = jnp.einsum(
        "hqk,kd->qhd", attend_weights, value_rows, preferred_element_type=jnp.float32
    ).astype(jnp.bfloat16)
    attended = attended.reshape(length, query_width)

    kept = length // n_tensor
    heads = []
    for distance in range(n_tensor):
        target = tensor_index ^ distance
        block = lax.dynamic_slice(attended, (target * kept, 0), (kept, query_width))
        if distance:
            block = lax.ppermute(block, "tensor", [(j, j ^ distance) for j in range(n_tensor)])
        heads.append(block)
    mine = jnp.zeros((kept, n_tensor * query_width), jnp.bfloat16)
    for distance in range(n_tensor):
        mine = lax.dynamic_update_slice(
            mine, heads[distance], (0, (tensor_index ^ distance) * query_width)
        )
    other = lax.ppermute(mine, "dp", siblings)
    both = jnp.concatenate([mine, other], axis=0)
    made = jnp.dot(both, out_weight, preferred_element_type=jnp.float32).astype(jnp.bfloat16)
    swapped = lax.ppermute(made[kept:], "dp", siblings)
    first = core == 0
    summed = jnp.concatenate(
        [jnp.where(first, made[:kept], swapped), jnp.where(first, swapped, made[:kept])], axis=1
    )
    return (update_dir, summed)


def solution(mesh):
    placed = (
        P("dp", None),
        P("dp", "tensor"),
        P("dp", "tensor"),
        P("dp", "tensor"),
        P("dp", "tensor"),
        P("dp", None),
        P(),
        P("tensor", None),
    )
    return jax.shard_map(
        body,
        mesh=mesh,
        in_specs=placed,
        out_specs=(P("dp", "tensor"), P(("dp", "tensor"), None)),
        check_vma=False,
    )
```

```python
import functools

import jax
import jax.numpy as jnp
from jax import lax
from jax.experimental import pallas as pl
from jax.experimental.pallas import tpu as pltpu
from jax.sharding import PartitionSpec as P

HD = 128


beta_one = 0.9
beta_two = 0.95
bias_one = 1.0 - 0.9**8
bias_two = 1.0 - 0.95**8
learn_rate = 0.002
adam_eps = 1e-08
norm_eps = 1e-05
rope_base = 500000.0

CHUNK_QUARTERS = (1, 2, 1)
VMEM_BYTES = 32 * 1024 * 1024


def rope_tables(length, head_size):
    half_width = head_size // 2
    exponent = jnp.arange(half_width, dtype=jnp.float32) * (2.0 / head_size)
    inverse = jnp.power(jnp.float32(rope_base), -exponent)
    position = jnp.arange(length, dtype=jnp.float32)
    angles = position[:, None] * inverse[None, :]
    cosine_table = jnp.concatenate([jnp.cos(angles), jnp.cos(angles)], axis=1)
    sine_table = jnp.concatenate([-jnp.sin(angles), jnp.sin(angles)], axis=1)
    return (cosine_table, sine_table)


def chunk_ranges(rows):
    quarter, start, ranges = rows // 4, 0, []
    for quarters in CHUNK_QUARTERS:
        ranges.append((start, quarters * quarter))
        start += quarters * quarter
    return ranges


def params():
    return pltpu.CompilerParams(vmem_limit_bytes=VMEM_BYTES)


def whole_vmem(count):
    return [pl.BlockSpec(memory_space=pltpu.VMEM)] * count


def anywhere(count):
    return [pl.BlockSpec(memory_space=pl.ANY)] * count


def own_core():
    return lax.rem(lax.axis_index("dp"), 2)


def own_place():
    return lax.div(lax.axis_index("dp"), 2)


def run_copies(copies):
    for copy in copies:
        copy.start()
    for copy in copies:
        copy.wait()


def pack_columns(train_states, rows, line, quarter):
    ranges = chunk_ranges(rows)

    def kernel(train_ref, *refs):
        outs, sems = refs[:-1], refs[-1]
        place, index = own_place(), lax.axis_index("tensor")
        tokens = pl.ds(pl.multiple_of(index * quarter, quarter), quarter)
        copies = []
        for part, (start, size) in enumerate(ranges):
            for distance in range(line):
                for owner in range(2):
                    column = ((place ^ distance) * 2 + owner) * rows + start
                    copies.append(
                        pltpu.make_async_copy(
                            train_ref.at[tokens, pl.ds(pl.multiple_of(column, 128), size)],
                            outs[part * line + distance].at[owner],
                            sems.at[len(copies)],
                        )
                    )
        run_copies(copies)

    shapes = [
        jax.ShapeDtypeStruct((2, quarter, size), train_states.dtype)
        for _, size in ranges
        for _ in range(line)
    ]
    flat = pl.pallas_call(
        kernel,
        out_shape=shapes,
        in_specs=anywhere(1),
        out_specs=anywhere(len(shapes)),
        scratch_shapes=[pltpu.SemaphoreType.DMA((2 * len(shapes),))],
        name="pack_columns",
    )(train_states)
    return [flat[part * line : (part + 1) * line] for part in range(len(ranges))]


def stack_pieces(pieces):
    outer, height, width = pieces[0].shape
    count = len(pieces)

    def kernel(*refs):
        out_ref, sems = refs[count], refs[count + 1]
        run_copies(
            [
                pltpu.make_async_copy(
                    refs[i], out_ref.at[:, pl.ds(i * height, height)], sems.at[i]
                )
                for i in range(count)
            ]
        )

    return pl.pallas_call(
        kernel,
        out_shape=jax.ShapeDtypeStruct((outer, count * height, width), pieces[0].dtype),
        in_specs=anywhere(count),
        out_specs=pl.BlockSpec(memory_space=pl.ANY),
        scratch_shapes=[pltpu.SemaphoreType.DMA((count,))],
        name="stack_pieces",
    )(*pieces)


def line_pairs(places):
    return [(2 * a + core, 2 * b + core) for a, b in places for core in range(2)]


def line_steps(block, place, count):
    low, high = [block], [block]
    for step in range(1, count - 1):
        low.append(
            lax.ppermute(low[-1], "dp", line_pairs([(i, i + 1) for i in range(step - 1, count - 1)]))
        )
        high.append(
            lax.ppermute(high[-1], "dp", line_pairs([(i, i - 1) for i in range(1, count - step + 1)]))
        )
    last = lax.ppermute(
        jnp.where(place == count - 2, low[-1], high[-1]),
        "dp",
        line_pairs([(count - 2, count - 1), (1, 0)]),
    )
    return low + [last], high + [last]


def line_choice(step, place, count):
    is_low, is_high = place >= step, place <= count - 1 - step
    spare = count - step
    return [
        (is_low, 0, step, place - step),
        (jnp.logical_and(jnp.logical_not(is_low), is_high), 1, step, place + step),
        (
            jnp.logical_and(jnp.logical_not(is_low), jnp.logical_not(is_high)),
            1,
            spare,
            place + spare,
        ),
    ][: 2 if 2 * step <= count else 3]


def line_slots(arrivals, place, count):
    slots = [(place, arrivals[0][0])]
    for step in range(1, count):
        choices = line_choice(step, place, count)
        _, side, entry, owner = choices[-1]
        block = arrivals[side][entry]
        for holds, side, entry, other in reversed(choices[:-1]):
            if arrivals[side][entry] is not block:
                block = jnp.where(holds, arrivals[side][entry], block)
            owner = jnp.where(holds, other, owner)
        slots.append((owner, block))
    return slots


def place_cotangents(arrivals, line, n_tensor):
    tokens, width = arrivals[0][0].shape
    quarter = tokens // n_tensor
    low = [a.reshape(n_tensor, quarter, width) for a in arrivals[0]]
    high = [a.reshape(n_tensor, quarter, width) for a in arrivals[1][1:-1]]

    def kernel(*refs):
        low_refs = refs[: len(low)]
        high_refs = [low_refs[0]] + list(refs[len(low) : len(low) + len(high)]) + [low_refs[-1]]
        out_ref, sems = refs[-2], refs[-1]
        place = own_place()

        def to(owner):
            begin = pl.multiple_of((owner ^ place) * quarter, quarter)
            return out_ref.at[:, pl.ds(begin, quarter)]

        pltpu.make_async_copy(low_refs[0], to(place), sems.at[0]).start()
        for step in range(1, line):
            for holds, side, entry, owner in line_choice(step, place, line):
                source = (low_refs, high_refs)[side][entry]

                @pl.when(holds)
                def _():
                    pltpu.make_async_copy(source, to(owner), sems.at[step]).start()

        for step in range(line):
            pltpu.make_async_copy(low_refs[0], to(place ^ step), sems.at[step]).wait()

    return pl.pallas_call(
        kernel,
        out_shape=jax.ShapeDtypeStruct((n_tensor, line * quarter, width), low[0].dtype),
        in_specs=anywhere(len(low) + len(high)),
        out_specs=pl.BlockSpec(memory_space=pl.ANY),
        scratch_shapes=[pltpu.SemaphoreType.DMA((line,))],
        name="place_cotangents",
    )(*low, *high)


def plane_gather(block, count):
    if count != 4:
        gathered = lax.all_gather(block, "tensor", axis=0)
        own = lax.axis_index("tensor")
        return [
            lax.dynamic_index_in_dim(gathered, own ^ b, 0, keepdims=False) for b in range(count)
        ]
    by_one = [(j, j ^ 1) for j in range(count)]
    by_two = [(j, j ^ 2) for j in range(count)]
    one = lax.ppermute(block, "tensor", by_one)
    two = lax.ppermute(block, "tensor", by_two)
    upper = lax.ppermute(one[:1], "tensor", by_two)
    lower = lax.ppermute(two[1:], "tensor", by_one)
    return [block, one, two, upper, lower]


def gradient_terms(blocks, cotangents, n_tensor):
    size = blocks[0].shape[2]
    width = cotangents.shape[2]
    split = len(blocks) > n_tensor

    def kernel(*refs):
        block_refs, cotangent_ref = refs[: len(blocks)], refs[len(blocks)]
        kept_ref, sent_ref = refs[len(blocks) + 1 :]
        index, core = lax.axis_index("tensor"), own_core()

        def term(owner):
            total = None
            for distance in range(n_tensor):
                if split and distance == n_tensor - 1:
                    upper, lower = block_refs[-2], block_refs[-1]
                    left = jnp.where(owner == 0, upper[0], lower[0])
                else:
                    left = block_refs[distance][owner]
                product = lax.dot_general(
                    left,
                    cotangent_ref[index ^ distance],
                    (((0,), (0,)), ((), ())),
                    preferred_element_type=jnp.float32,
                )
                total = product if total is None else total + product
            return total

        sent_ref[...] = term(1 - core).astype(sent_ref.dtype)
        kept_ref[...] = term(core)

    depth = n_tensor * blocks[0].shape[1]
    return pl.pallas_call(
        kernel,
        out_shape=(
            jax.ShapeDtypeStruct((size, width), jnp.float32),
            jax.ShapeDtypeStruct((size, width), jnp.bfloat16),
        ),
        in_specs=whole_vmem(len(blocks) + 1),
        out_specs=whole_vmem(2),
        compiler_params=params(),
        cost_estimate=pl.CostEstimate(
            flops=4 * depth * size * width,
            bytes_accessed=4 * depth * size + 2 * depth * width + 6 * size * width,
            transcendentals=0,
        ),
        name="gradient_terms",
    )(*blocks, cotangents)


def norm_columns(states, gain, rows, line):
    length, width = states.shape
    ranges = chunk_ranges(rows)
    tile = 64

    def kernel(states_ref, gain_ref, *outs):
        kept, sent = outs[: len(ranges)], outs[len(ranges) :]
        core = own_core()
        total = jnp.zeros((tile, 1), jnp.float32)
        for block in range(2 * line):
            piece = states_ref[:, block * rows : (block + 1) * rows].astype(jnp.float32)
            total = total + jnp.sum(piece * piece, axis=1, keepdims=True)
        scale = lax.rsqrt(total / width + norm_eps)
        for flag in range(2):

            @pl.when(core == flag)
            def _():
                for block in range(2 * line):
                    group = kept if block % 2 == flag else sent
                    for (start, size), out in zip(ranges, group):
                        columns = slice(block * rows + start, block * rows + start + size)
                        piece = states_ref[:, columns].astype(jnp.float32)
                        out[block // 2] = (piece * scale * gain_ref[:, columns]).astype(out.dtype)

    shapes = [
        jax.ShapeDtypeStruct((line, length, size), jnp.bfloat16) for _, size in ranges
    ] * 2
    outs = pl.pallas_call(
        kernel,
        grid=(length // tile,),
        out_shape=shapes,
        in_specs=[
            pl.BlockSpec((tile, width), lambda i: (i, 0)),
            pl.BlockSpec((1, width), lambda i: (0, 0)),
        ],
        out_specs=[pl.BlockSpec((line, tile, size), lambda i: (0, i, 0)) for _, size in ranges] * 2,
        compiler_params=params(),
        cost_estimate=pl.CostEstimate(
            flops=6 * length * width, bytes_accessed=4 * length * width, transcendentals=0
        ),
        name="norm_columns",
    )(states, gain.reshape(1, width))
    return outs[: len(ranges)], outs[len(ranges) :]


def accumulate(total, states, slots):
    _, length, depth = states.shape
    width = slots[0][1].shape[1]
    count = len(slots)
    tile = min(256, length)
    owners = jnp.stack([jnp.asarray(owner, jnp.int32) for owner, _ in slots])
    weights = [weight for _, weight in slots]

    def kernel(owners_ref, *refs):
        state_refs, weight_refs = refs[:count], refs[count : 2 * count]
        out_ref = refs[-1]
        result = None if total is None else refs[2 * count][...]
        for state_ref, weight_ref in zip(state_refs, weight_refs):
            product = jnp.dot(state_ref[0], weight_ref[...], preferred_element_type=jnp.float32)
            result = product if result is None else result + product
        out_ref[...] = result

    def state_spec(slot):
        return pl.BlockSpec((1, tile, depth), lambda i, chosen: (chosen[slot], i, 0))

    totals = [] if total is None else [total]
    row_spec = pl.BlockSpec((tile, width), lambda i, chosen: (i, 0))
    return pl.pallas_call(
        kernel,
        grid_spec=pltpu.PrefetchScalarGridSpec(
            num_scalar_prefetch=1,
            grid=(length // tile,),
            in_specs=[state_spec(slot) for slot in range(count)]
            + [pl.BlockSpec((depth, width), lambda i, chosen: (0, 0))] * count
            + [row_spec] * len(totals),
            out_specs=row_spec,
        ),
        out_shape=jax.ShapeDtypeStruct((length, width), jnp.float32),
        input_output_aliases={1 + 2 * count: 0} if totals else {},
        compiler_params=params(),
        cost_estimate=pl.CostEstimate(
            flops=2 * count * length * depth * width,
            bytes_accessed=2 * count * depth * (length + width) + 8 * length * width,
            transcendentals=0,
        ),
        name="accumulate",
    )(owners, *([states] * count), *weights, *totals)


def attention(kept, got, cosine_table, sine_table):
    length, width = kept.shape
    heads = width // HD - 2
    tile = min(128, length)

    def rope(u, cosine, sine):
        return u * cosine + pltpu.roll(u, HD // 2, 1) * sine

    def kernel(q_ref, q2_ref, k_ref, k2_ref, v_ref, v2_ref, cos_ref, sin_ref, out_ref, keys, values):
        @pl.when(pl.program_id(0) == 0)
        def _():
            key_rows = rope(k_ref[...] + k2_ref[...], cos_ref[...], sin_ref[...])
            keys[...] = key_rows.astype(jnp.bfloat16)
            values[...] = (v_ref[...] + v2_ref[...]).astype(jnp.bfloat16)

        for begin in range(0, length, tile):
            here, upto = slice(begin, begin + tile), begin + tile
            query = rope(q_ref[here] + q2_ref[here], cos_ref[here], sin_ref[here])
            query = (query * HD**-0.5).astype(jnp.bfloat16)
            scores = lax.dot_general(
                query,
                keys[:upto],
                (((1,), (1,)), ((), ())),
                preferred_element_type=jnp.float32,
            )
            row = lax.broadcasted_iota(jnp.int32, scores.shape, 0) + begin
            column = lax.broadcasted_iota(jnp.int32, scores.shape, 1)
            scores = jnp.where(row >= column, scores, -jnp.inf)
            raised = jnp.exp(scores - jnp.max(scores, axis=1, keepdims=True))
            weights = raised / jnp.sum(raised, axis=1, keepdims=True)
            out_ref[here] = jnp.dot(
                weights.astype(jnp.bfloat16), values[:upto], preferred_element_type=jnp.float32
            ).astype(jnp.bfloat16)

    def column(index):
        return pl.BlockSpec((length, HD), lambda h: (0, index))

    head = pl.BlockSpec((length, HD), lambda h: (0, h))
    return pl.pallas_call(
        kernel,
        grid=(heads,),
        out_shape=jax.ShapeDtypeStruct((length, heads * HD), jnp.bfloat16),
        in_specs=[head, head]
        + [column(heads)] * 2
        + [column(heads + 1)] * 2
        + [column(0)] * 2,
        out_specs=head,
        scratch_shapes=[pltpu.VMEM((length, HD), jnp.bfloat16)] * 2,
        compiler_params=params(),
        cost_estimate=pl.CostEstimate(
            flops=4 * heads * length * length * HD,
            bytes_accessed=9 * length * width,
            transcendentals=heads * length * length,
        ),
        name="attention",
    )(kept, got, kept, got, kept, got, cosine_table, sine_table)


def output_rows(mine, other, out_weight, n_tensor):
    kept, depth = mine.shape[1], mine.shape[2]
    width = out_weight.shape[1]
    tile = 512
    index = jnp.reshape(lax.axis_index("tensor"), (1,)).astype(jnp.int32)

    def kernel(index_ref, mine_ref, other_ref, *refs):
        weight_refs, (made_ref, sent_ref) = refs[:n_tensor], refs[n_tensor:]
        for left_ref, out_ref in ((other_ref, sent_ref), (mine_ref, made_ref)):
            total = None
            for distance in range(n_tensor):
                product = jnp.dot(
                    left_ref[distance],
                    weight_refs[distance][...],
                    preferred_element_type=jnp.float32,
                )
                total = product if total is None else total + product
            out_ref[...] = total.astype(out_ref.dtype)

    def weight_spec(distance):
        return pl.BlockSpec((depth, tile), lambda i, chosen: (chosen[0] ^ distance, i))

    whole = pl.BlockSpec((n_tensor, kept, depth), lambda i, chosen: (0, 0, 0))
    out_spec = pl.BlockSpec((kept, tile), lambda i, chosen: (0, i))
    return pl.pallas_call(
        kernel,
        grid_spec=pltpu.PrefetchScalarGridSpec(
            num_scalar_prefetch=1,
            grid=(width // tile,),
            in_specs=[whole, whole] + [weight_spec(distance) for distance in range(n_tensor)],
            out_specs=[out_spec, out_spec],
        ),
        out_shape=[jax.ShapeDtypeStruct((kept, width), jnp.bfloat16)] * 2,
        compiler_params=params(),
        cost_estimate=pl.CostEstimate(
            flops=4 * kept * n_tensor * depth * width,
            bytes_accessed=2 * n_tensor * depth * width + 4 * kept * width,
            transcendentals=0,
        ),
        name="output_rows",
    )(index, mine, other, *([out_weight] * n_tensor))


def body(
    train_states, qkv_cotangent, w_master, moment_one, moment_two, prompt_states, norm_gain, w_out
):
    n_dp = lax.axis_size("dp")
    n_tensor = lax.axis_size("tensor")
    line = n_dp // 2
    tensor_index = lax.axis_index("tensor")
    core, place = own_core(), own_place()
    siblings = [(i, i ^ 1) for i in range(n_dp)]
    rows, slice_width = w_master.shape
    tokens, width = train_states.shape
    length = prompt_states.shape[0]
    query_width = slice_width - 2 * HD
    ranges = chunk_ranges(rows)

    arrivals = line_steps(qkv_cotangent, place, line)
    cotangents = place_cotangents(arrivals, line, n_tensor)

    half_width = width // 2
    w_half = lax.dynamic_slice(w_out, (0, core * half_width), (w_out.shape[0], half_width))
    out_weight = lax.all_gather(w_half, "tensor", axis=0, tiled=True)

    packed = pack_columns(train_states, rows, line, tokens // n_tensor)
    updates, gathers = [], []
    for part, (start, size) in enumerate(ranges):
        pieces = [packed[part][0]] + [
            lax.ppermute(
                packed[part][distance],
                "dp",
                line_pairs([(i, i ^ distance) for i in range(line)]),
            )
            for distance in range(1, line)
        ]
        spread = plane_gather(stack_pieces(pieces), n_tensor)
        kept, sent = gradient_terms(spread, cotangents, n_tensor)
        gradient = kept + lax.ppermute(sent, "dp", siblings).astype(jnp.float32)

        here = slice(start, start + size)
        moment_new = beta_one * moment_one[here] + (1.0 - beta_one) * gradient
        second_new = beta_two * moment_two[here] + (1.0 - beta_two) * gradient * gradient
        update = moment_new / bias_one / (jnp.sqrt(second_new / bias_two) + adam_eps)
        updates.append(update)
        owned_weight = (w_master[here] - learn_rate * update).astype(jnp.bfloat16)
        if part == 0:
            owned_weight, prompt_states = lax.optimization_barrier((owned_weight, prompt_states))
        gathers.append(line_slots(line_steps(owned_weight, place, line), place, line))
    update_dir = jnp.concatenate(updates, axis=0)

    kept_states, sent_states = norm_columns(prompt_states, norm_gain, rows, line)
    got_states = [lax.ppermute(states, "dp", siblings) for states in sent_states]
    own_total, other_total = None, None
    for part, slots in enumerate(gathers):
        for group in (slots[:-1], slots[-1:]):
            other_total = accumulate(other_total, got_states[part], group)
            own_total = accumulate(own_total, kept_states[part], group)
    cosine_table, sine_table = rope_tables(length, HD)
    update_dir, cosine_table, sine_table, own_total = lax.optimization_barrier(
        (update_dir, cosine_table, sine_table, own_total)
    )
    attended = attention(
        own_total, lax.ppermute(other_total, "dp", siblings), cosine_table, sine_table
    )

    kept_rows = length // n_tensor
    heads = []
    for distance in range(n_tensor):
        target = tensor_index ^ distance
        block = lax.dynamic_slice(attended, (target * kept_rows, 0), (kept_rows, query_width))
        if distance:
            block = lax.ppermute(block, "tensor", [(j, j ^ distance) for j in range(n_tensor)])
        heads.append(block)
    mine = stack_pieces([head[None] for head in heads]).reshape(n_tensor, kept_rows, query_width)
    other = lax.ppermute(mine, "dp", siblings)
    made, sent_rows = output_rows(mine, other, out_weight, n_tensor)
    swapped = lax.ppermute(sent_rows, "dp", siblings)
    first = core == 0
    summed = jnp.concatenate(
        [jnp.where(first, made, swapped), jnp.where(first, swapped, made)], axis=1
    )
    return (update_dir, summed)


def solution(mesh):
    placed = (
        P("dp", None),
        P("dp", "tensor"),
        P("dp", "tensor"),
        P("dp", "tensor"),
        P("dp", "tensor"),
        P("dp", None),
        P(),
        P("tensor", None),
    )
    return jax.shard_map(
        body,
        mesh=mesh,
        in_specs=placed,
        out_specs=(P("dp", "tensor"), P(("dp", "tensor"), None)),
        check_vma=False,
    )
```

```python
import functools

import jax
import jax.numpy as jnp
from jax import lax
from jax.experimental import pallas as pl
from jax.experimental.pallas import tpu as pltpu
from jax.sharding import PartitionSpec as P

HD = 128


beta_one = 0.9
beta_two = 0.95
bias_one = 1.0 - 0.9**8
bias_two = 1.0 - 0.95**8
learn_rate = 0.002
adam_eps = 1e-08
norm_eps = 1e-05
rope_base = 500000.0

CHUNK_QUARTERS = (1, 2, 1)
VMEM_BYTES = 32 * 1024 * 1024


def rope_tables(length, head_size):
    half_width = head_size // 2
    exponent = jnp.arange(half_width, dtype=jnp.float32) * (2.0 / head_size)
    inverse = jnp.power(jnp.float32(rope_base), -exponent)
    position = jnp.arange(length, dtype=jnp.float32)
    angles = position[:, None] * inverse[None, :]
    cosine_table = jnp.concatenate([jnp.cos(angles), jnp.cos(angles)], axis=1)
    sine_table = jnp.concatenate([-jnp.sin(angles), jnp.sin(angles)], axis=1)
    return (cosine_table, sine_table)


def chunk_ranges(rows):
    quarter, start, ranges = rows // 4, 0, []
    for quarters in CHUNK_QUARTERS:
        ranges.append((start, quarters * quarter))
        start += quarters * quarter
    return ranges


def params():
    return pltpu.CompilerParams(vmem_limit_bytes=VMEM_BYTES)


def whole_vmem(count):
    return [pl.BlockSpec(memory_space=pltpu.VMEM)] * count


def own_core():
    return lax.rem(lax.axis_index("dp"), 2)


def own_place():
    return lax.div(lax.axis_index("dp"), 2)


def pack_columns(train_states, rows, line, quarter):
    ranges = chunk_ranges(rows)

    def kernel(index_ref, train_ref, *outs):
        place = own_place()
        for part, (start, size) in enumerate(ranges):
            for distance in range(line):
                for owner in range(2):
                    column = pl.multiple_of(((place ^ distance) * 2 + owner) * rows + start, 128)
                    outs[part * line + distance][owner] = train_ref[:, pl.ds(column, size)]

    shapes = [
        jax.ShapeDtypeStruct((2, quarter, size), train_states.dtype)
        for _, size in ranges
        for _ in range(line)
    ]
    index = jnp.reshape(lax.axis_index("tensor"), (1,)).astype(jnp.int32)
    flat = pl.pallas_call(
        kernel,
        grid_spec=pltpu.PrefetchScalarGridSpec(
            num_scalar_prefetch=1,
            grid=(1,),
            in_specs=[
                pl.BlockSpec((quarter, train_states.shape[1]), lambda i, chosen: (chosen[0], 0))
            ],
            out_specs=[pl.BlockSpec(s.shape, lambda i, chosen: (0, 0, 0)) for s in shapes],
        ),
        out_shape=shapes,
        compiler_params=params(),
        name="pack_columns",
    )(index, train_states)
    return [flat[part * line : (part + 1) * line] for part in range(len(ranges))]


def stack_pieces(pieces):
    outer, height, width = pieces[0].shape
    count = len(pieces)

    def kernel(*refs):
        for i in range(count):
            refs[count][:, i * height : (i + 1) * height] = refs[i][...]

    return pl.pallas_call(
        kernel,
        out_shape=jax.ShapeDtypeStruct((outer, count * height, width), pieces[0].dtype),
        in_specs=whole_vmem(count),
        out_specs=pl.BlockSpec(memory_space=pltpu.VMEM),
        compiler_params=params(),
        name="stack_pieces",
    )(*pieces)


def line_pairs(places):
    return [(2 * a + core, 2 * b + core) for a, b in places for core in range(2)]


def line_steps(block, place, count):
    low, high = [block], [block]
    for step in range(1, count - 1):
        low.append(
            lax.ppermute(low[-1], "dp", line_pairs([(i, i + 1) for i in range(step - 1, count - 1)]))
        )
        high.append(
            lax.ppermute(high[-1], "dp", line_pairs([(i, i - 1) for i in range(1, count - step + 1)]))
        )
    last = lax.ppermute(
        jnp.where(place == count - 2, low[-1], high[-1]),
        "dp",
        line_pairs([(count - 2, count - 1), (1, 0)]),
    )
    return low + [last], high + [last]


def line_choice(step, place, count):
    is_low, is_high = place >= step, place <= count - 1 - step
    spare = count - step
    return [
        (is_low, 0, step, place - step),
        (jnp.logical_and(jnp.logical_not(is_low), is_high), 1, step, place + step),
        (
            jnp.logical_and(jnp.logical_not(is_low), jnp.logical_not(is_high)),
            1,
            spare,
            place + spare,
        ),
    ][: 2 if 2 * step <= count else 3]


def line_slots(arrivals, place, count):
    slots = [(place, arrivals[0][0])]
    for step in range(1, count):
        choices = line_choice(step, place, count)
        _, side, entry, owner = choices[-1]
        block = arrivals[side][entry]
        for holds, side, entry, other in reversed(choices[:-1]):
            if arrivals[side][entry] is not block:
                block = jnp.where(holds, arrivals[side][entry], block)
            owner = jnp.where(holds, other, owner)
        slots.append((owner, block))
    return slots


def place_cotangents(arrivals, line, n_tensor):
    tokens, width = arrivals[0][0].shape
    quarter = tokens // n_tensor
    low = [a.reshape(n_tensor, quarter, width) for a in arrivals[0]]
    high = [a.reshape(n_tensor, quarter, width) for a in arrivals[1][1:-1]]

    def kernel(*refs):
        low_refs = refs[: len(low)]
        high_refs = [low_refs[0]] + list(refs[len(low) : len(low) + len(high)]) + [low_refs[-1]]
        out_ref = refs[-1]
        place = own_place()

        def put(owner, source):
            begin = pl.multiple_of((owner ^ place) * quarter, quarter)
            out_ref[:, pl.ds(begin, quarter)] = source[...]

        put(place, low_refs[0])
        for step in range(1, line):
            for holds, side, entry, owner in line_choice(step, place, line):
                pl.when(holds)(functools.partial(put, owner, (low_refs, high_refs)[side][entry]))

    return pl.pallas_call(
        kernel,
        out_shape=jax.ShapeDtypeStruct((n_tensor, line * quarter, width), low[0].dtype),
        in_specs=whole_vmem(len(low) + len(high)),
        out_specs=pl.BlockSpec(memory_space=pltpu.VMEM),
        compiler_params=params(),
        name="place_cotangents",
    )(*low, *high)


def plane_gather(block, count):
    if count != 4:
        gathered = lax.all_gather(block, "tensor", axis=0)
        own = lax.axis_index("tensor")
        return [
            lax.dynamic_index_in_dim(gathered, own ^ b, 0, keepdims=False) for b in range(count)
        ]
    by_one = [(j, j ^ 1) for j in range(count)]
    by_two = [(j, j ^ 2) for j in range(count)]
    one = lax.ppermute(block, "tensor", by_one)
    two = lax.ppermute(block, "tensor", by_two)
    upper = lax.ppermute(one[:1], "tensor", by_two)
    lower = lax.ppermute(two[1:], "tensor", by_one)
    return [block, one, two, upper, lower]


def gradient_terms(blocks, cotangents, n_tensor):
    size = blocks[0].shape[2]
    width = cotangents.shape[2]
    split = len(blocks) > n_tensor

    def kernel(*refs):
        block_refs, cotangent_ref = refs[: len(blocks)], refs[len(blocks)]
        kept_ref, sent_ref = refs[len(blocks) + 1 :]
        index, core = lax.axis_index("tensor"), own_core()

        def term(owner):
            total = None
            for distance in range(n_tensor):
                if split and distance == n_tensor - 1:
                    upper, lower = block_refs[-2], block_refs[-1]
                    left = jnp.where(owner == 0, upper[0], lower[0])
                else:
                    left = block_refs[distance][owner]
                product = lax.dot_general(
                    left,
                    cotangent_ref[index ^ distance],
                    (((0,), (0,)), ((), ())),
                    preferred_element_type=jnp.float32,
                )
                total = product if total is None else total + product
            return total

        sent_ref[...] = term(1 - core).astype(sent_ref.dtype)
        kept_ref[...] = term(core)

    depth = n_tensor * blocks[0].shape[1]
    return pl.pallas_call(
        kernel,
        out_shape=(
            jax.ShapeDtypeStruct((size, width), jnp.float32),
            jax.ShapeDtypeStruct((size, width), jnp.bfloat16),
        ),
        in_specs=whole_vmem(len(blocks) + 1),
        out_specs=whole_vmem(2),
        compiler_params=params(),
        cost_estimate=pl.CostEstimate(
            flops=4 * depth * size * width,
            bytes_accessed=4 * depth * size + 2 * depth * width + 6 * size * width,
            transcendentals=0,
        ),
        name="gradient_terms",
    )(*blocks, cotangents)


def norm_columns(states, gain, rows, line):
    length, width = states.shape
    ranges = chunk_ranges(rows)
    tile = 64

    def kernel(states_ref, gain_ref, *outs):
        kept, sent = outs[: len(ranges)], outs[len(ranges) :]
        core = own_core()
        total = jnp.zeros((tile, 1), jnp.float32)
        for block in range(2 * line):
            piece = states_ref[:, block * rows : (block + 1) * rows].astype(jnp.float32)
            total = total + jnp.sum(piece * piece, axis=1, keepdims=True)
        scale = lax.rsqrt(total / width + norm_eps)
        for flag in range(2):

            @pl.when(core == flag)
            def _():
                for block in range(2 * line):
                    group = kept if block % 2 == flag else sent
                    for (start, size), out in zip(ranges, group):
                        columns = slice(block * rows + start, block * rows + start + size)
                        piece = states_ref[:, columns].astype(jnp.float32)
                        out[block // 2] = (piece * scale * gain_ref[:, columns]).astype(out.dtype)

    shapes = [
        jax.ShapeDtypeStruct((line, length, size), jnp.bfloat16) for _, size in ranges
    ] * 2
    outs = pl.pallas_call(
        kernel,
        grid=(length // tile,),
        out_shape=shapes,
        in_specs=[
            pl.BlockSpec((tile, width), lambda i: (i, 0)),
            pl.BlockSpec((1, width), lambda i: (0, 0)),
        ],
        out_specs=[pl.BlockSpec((line, tile, size), lambda i: (0, i, 0)) for _, size in ranges] * 2,
        compiler_params=params(),
        cost_estimate=pl.CostEstimate(
            flops=6 * length * width, bytes_accessed=4 * length * width, transcendentals=0
        ),
        name="norm_columns",
    )(states, gain.reshape(1, width))
    return outs[: len(ranges)], outs[len(ranges) :]


def accumulate(total, states, slots):
    _, length, depth = states.shape
    width = slots[0][1].shape[1]
    count = len(slots)
    tile = min(256, length)
    owners = jnp.stack([jnp.asarray(owner, jnp.int32) for owner, _ in slots])
    weights = [weight for _, weight in slots]

    def kernel(owners_ref, *refs):
        state_refs, weight_refs = refs[:count], refs[count : 2 * count]
        out_ref = refs[-1]
        result = None if total is None else refs[2 * count][...]
        for state_ref, weight_ref in zip(state_refs, weight_refs):
            product = jnp.dot(state_ref[0], weight_ref[...], preferred_element_type=jnp.float32)
            result = product if result is None else result + product
        out_ref[...] = result

    def state_spec(slot):
        return pl.BlockSpec((1, tile, depth), lambda i, chosen: (chosen[slot], i, 0))

    totals = [] if total is None else [total]
    row_spec = pl.BlockSpec((tile, width), lambda i, chosen: (i, 0))
    return pl.pallas_call(
        kernel,
        grid_spec=pltpu.PrefetchScalarGridSpec(
            num_scalar_prefetch=1,
            grid=(length // tile,),
            in_specs=[state_spec(slot) for slot in range(count)]
            + [pl.BlockSpec((depth, width), lambda i, chosen: (0, 0))] * count
            + [row_spec] * len(totals),
            out_specs=row_spec,
        ),
        out_shape=jax.ShapeDtypeStruct((length, width), jnp.float32),
        input_output_aliases={1 + 2 * count: 0} if totals else {},
        compiler_params=params(),
        cost_estimate=pl.CostEstimate(
            flops=2 * count * length * depth * width,
            bytes_accessed=2 * count * depth * (length + width) + 8 * length * width,
            transcendentals=0,
        ),
        name="accumulate",
    )(owners, *([states] * count), *weights, *totals)


def attention(kept, got, cosine_table, sine_table):
    length, width = kept.shape
    heads = width // HD - 2
    tile = min(128, length)

    def rope(u, cosine, sine):
        return u * cosine + pltpu.roll(u, HD // 2, 1) * sine

    def kernel(q_ref, q2_ref, k_ref, k2_ref, v_ref, v2_ref, cos_ref, sin_ref, out_ref, keys, values):
        @pl.when(pl.program_id(0) == 0)
        def _():
            key_rows = rope(k_ref[...] + k2_ref[...], cos_ref[...], sin_ref[...])
            keys[...] = key_rows.astype(jnp.bfloat16)
            values[...] = (v_ref[...] + v2_ref[...]).astype(jnp.bfloat16)

        for begin in range(0, length, tile):
            here, upto = slice(begin, begin + tile), begin + tile
            query = rope(q_ref[here] + q2_ref[here], cos_ref[here], sin_ref[here])
            query = (query * HD**-0.5).astype(jnp.bfloat16)
            scores = lax.dot_general(
                query,
                keys[:upto],
                (((1,), (1,)), ((), ())),
                preferred_element_type=jnp.float32,
            )
            row = lax.broadcasted_iota(jnp.int32, scores.shape, 0) + begin
            column = lax.broadcasted_iota(jnp.int32, scores.shape, 1)
            scores = jnp.where(row >= column, scores, -jnp.inf)
            raised = jnp.exp(scores - jnp.max(scores, axis=1, keepdims=True))
            weights = raised / jnp.sum(raised, axis=1, keepdims=True)
            out_ref[here] = jnp.dot(
                weights.astype(jnp.bfloat16), values[:upto], preferred_element_type=jnp.float32
            ).astype(jnp.bfloat16)

    def column(index):
        return pl.BlockSpec((length, HD), lambda h: (0, index))

    head = pl.BlockSpec((length, HD), lambda h: (0, h))
    return pl.pallas_call(
        kernel,
        grid=(heads,),
        out_shape=jax.ShapeDtypeStruct((length, heads * HD), jnp.bfloat16),
        in_specs=[head, head]
        + [column(heads)] * 2
        + [column(heads + 1)] * 2
        + [column(0)] * 2,
        out_specs=head,
        scratch_shapes=[pltpu.VMEM((length, HD), jnp.bfloat16)] * 2,
        compiler_params=params(),
        cost_estimate=pl.CostEstimate(
            flops=4 * heads * length * length * HD,
            bytes_accessed=9 * length * width,
            transcendentals=heads * length * length,
        ),
        name="attention",
    )(kept, got, kept, got, kept, got, cosine_table, sine_table)


def output_rows(mine, other, out_weight, n_tensor):
    kept, depth = mine.shape[1], mine.shape[2]
    width = out_weight.shape[1]
    tile = 512
    index = jnp.reshape(lax.axis_index("tensor"), (1,)).astype(jnp.int32)

    def kernel(index_ref, mine_ref, other_ref, *refs):
        weight_refs, (made_ref, sent_ref) = refs[:n_tensor], refs[n_tensor:]
        for left_ref, out_ref in ((other_ref, sent_ref), (mine_ref, made_ref)):
            total = None
            for distance in range(n_tensor):
                product = jnp.dot(
                    left_ref[distance],
                    weight_refs[distance][...],
                    preferred_element_type=jnp.float32,
                )
                total = product if total is None else total + product
            out_ref[...] = total.astype(out_ref.dtype)

    def weight_spec(distance):
        return pl.BlockSpec((depth, tile), lambda i, chosen: (chosen[0] ^ distance, i))

    whole = pl.BlockSpec((n_tensor, kept, depth), lambda i, chosen: (0, 0, 0))
    out_spec = pl.BlockSpec((kept, tile), lambda i, chosen: (0, i))
    return pl.pallas_call(
        kernel,
        grid_spec=pltpu.PrefetchScalarGridSpec(
            num_scalar_prefetch=1,
            grid=(width // tile,),
            in_specs=[whole, whole] + [weight_spec(distance) for distance in range(n_tensor)],
            out_specs=[out_spec, out_spec],
        ),
        out_shape=[jax.ShapeDtypeStruct((kept, width), jnp.bfloat16)] * 2,
        compiler_params=params(),
        cost_estimate=pl.CostEstimate(
            flops=4 * kept * n_tensor * depth * width,
            bytes_accessed=2 * n_tensor * depth * width + 4 * kept * width,
            transcendentals=0,
        ),
        name="output_rows",
    )(index, mine, other, *([out_weight] * n_tensor))


def body(
    train_states, qkv_cotangent, w_master, moment_one, moment_two, prompt_states, norm_gain, w_out
):
    n_dp = lax.axis_size("dp")
    n_tensor = lax.axis_size("tensor")
    line = n_dp // 2
    tensor_index = lax.axis_index("tensor")
    core, place = own_core(), own_place()
    siblings = [(i, i ^ 1) for i in range(n_dp)]
    rows, slice_width = w_master.shape
    tokens, width = train_states.shape
    length = prompt_states.shape[0]
    query_width = slice_width - 2 * HD
    ranges = chunk_ranges(rows)

    arrivals = line_steps(qkv_cotangent, place, line)
    cotangents = place_cotangents(arrivals, line, n_tensor)

    half_width = width // 2
    w_half = lax.dynamic_slice(w_out, (0, core * half_width), (w_out.shape[0], half_width))
    out_weight = lax.all_gather(w_half, "tensor", axis=0, tiled=True)

    packed = pack_columns(train_states, rows, line, tokens // n_tensor)
    updates, gathers = [], []
    for part, (start, size) in enumerate(ranges):
        pieces = [packed[part][0]] + [
            lax.ppermute(
                packed[part][distance],
                "dp",
                line_pairs([(i, i ^ distance) for i in range(line)]),
            )
            for distance in range(1, line)
        ]
        spread = plane_gather(stack_pieces(pieces), n_tensor)
        kept, sent = gradient_terms(spread, cotangents, n_tensor)
        gradient = kept + lax.ppermute(sent, "dp", siblings).astype(jnp.float32)

        here = slice(start, start + size)
        moment_new = beta_one * moment_one[here] + (1.0 - beta_one) * gradient
        second_new = beta_two * moment_two[here] + (1.0 - beta_two) * gradient * gradient
        update = moment_new / bias_one / (jnp.sqrt(second_new / bias_two) + adam_eps)
        updates.append(update)
        owned_weight = (w_master[here] - learn_rate * update).astype(jnp.bfloat16)
        if part == 0:
            owned_weight, prompt_states = lax.optimization_barrier((owned_weight, prompt_states))
        gathers.append(line_slots(line_steps(owned_weight, place, line), place, line))
    update_dir = jnp.concatenate(updates, axis=0)

    kept_states, sent_states = norm_columns(prompt_states, norm_gain, rows, line)
    got_states = [lax.ppermute(states, "dp", siblings) for states in sent_states]
    own_total, other_total = None, None
    for part, slots in enumerate(gathers):
        for group in (slots[:-1], slots[-1:]):
            other_total = accumulate(other_total, got_states[part], group)
            own_total = accumulate(own_total, kept_states[part], group)
    cosine_table, sine_table = rope_tables(length, HD)
    update_dir, cosine_table, sine_table, own_total = lax.optimization_barrier(
        (update_dir, cosine_table, sine_table, own_total)
    )
    attended = attention(
        own_total, lax.ppermute(other_total, "dp", siblings), cosine_table, sine_table
    )

    kept_rows = length // n_tensor
    heads = []
    for distance in range(n_tensor):
        target = tensor_index ^ distance
        block = lax.dynamic_slice(attended, (target * kept_rows, 0), (kept_rows, query_width))
        if distance:
            block = lax.ppermute(block, "tensor", [(j, j ^ distance) for j in range(n_tensor)])
        heads.append(block)
    mine = stack_pieces([head[None] for head in heads]).reshape(n_tensor, kept_rows, query_width)
    other = lax.ppermute(mine, "dp", siblings)
    made, sent_rows = output_rows(mine, other, out_weight, n_tensor)
    swapped = lax.ppermute(sent_rows, "dp", siblings)
    first = core == 0
    summed = jnp.concatenate(
        [jnp.where(first, made, swapped), jnp.where(first, swapped, made)], axis=1
    )
    return (update_dir, summed)


def solution(mesh):
    placed = (
        P("dp", None),
        P("dp", "tensor"),
        P("dp", "tensor"),
        P("dp", "tensor"),
        P("dp", "tensor"),
        P("dp", None),
        P(),
        P("tensor", None),
    )
    return jax.shard_map(
        body,
        mesh=mesh,
        in_specs=placed,
        out_specs=(P("dp", "tensor"), P(("dp", "tensor"), None)),
        check_vma=False,
    )
```

```python
import functools

import jax
import jax.numpy as jnp
from jax import lax
from jax.experimental import pallas as pl
from jax.experimental.pallas import tpu as pltpu
from jax.sharding import PartitionSpec as P

HD = 128


beta_one = 0.9
beta_two = 0.95
bias_one = 1.0 - 0.9**8
bias_two = 1.0 - 0.95**8
learn_rate = 0.002
adam_eps = 1e-08
norm_eps = 1e-05
rope_base = 500000.0

CHUNK_QUARTERS = (1, 2, 1)
GROUPS = ((0, 1), (1, 3))
VMEM_BYTES = 32 * 1024 * 1024


def rope_tables(length, head_size):
    half_width = head_size // 2
    exponent = jnp.arange(half_width, dtype=jnp.float32) * (2.0 / head_size)
    inverse = jnp.power(jnp.float32(rope_base), -exponent)
    position = jnp.arange(length, dtype=jnp.float32)
    angles = position[:, None] * inverse[None, :]
    cosine_table = jnp.concatenate([jnp.cos(angles), jnp.cos(angles)], axis=1)
    sine_table = jnp.concatenate([-jnp.sin(angles), jnp.sin(angles)], axis=1)
    return (cosine_table, sine_table)


def chunk_ranges(rows):
    quarter, start, ranges = rows // 4, 0, []
    for quarters in CHUNK_QUARTERS:
        ranges.append((start, quarters * quarter))
        start += quarters * quarter
    return ranges


def params():
    return pltpu.CompilerParams(vmem_limit_bytes=VMEM_BYTES)


def whole_vmem(count):
    return [pl.BlockSpec(memory_space=pltpu.VMEM)] * count


def own_core():
    return lax.rem(lax.axis_index("dp"), 2)


def own_place():
    return lax.div(lax.axis_index("dp"), 2)


def pack_columns(train_states, rows, line, quarter):
    def kernel(index_ref, train_ref, *outs):
        place = own_place()
        for distance in range(line):
            for owner in range(2):
                column = pl.multiple_of(((place ^ distance) * 2 + owner) * rows, 128)
                outs[distance][owner] = train_ref[:, pl.ds(column, rows)]

    shapes = [jax.ShapeDtypeStruct((2, quarter, rows), train_states.dtype)] * line
    index = jnp.reshape(lax.axis_index("tensor"), (1,)).astype(jnp.int32)
    return pl.pallas_call(
        kernel,
        grid_spec=pltpu.PrefetchScalarGridSpec(
            num_scalar_prefetch=1,
            grid=(1,),
            in_specs=[
                pl.BlockSpec((quarter, train_states.shape[1]), lambda i, chosen: (chosen[0], 0))
            ],
            out_specs=[pl.BlockSpec(s.shape, lambda i, chosen: (0, 0, 0)) for s in shapes],
        ),
        out_shape=shapes,
        compiler_params=params(),
        name="pack_columns",
    )(index, train_states)


def stack_pieces(pieces, cuts):
    outer, height, _ = pieces[0].shape
    count = len(pieces)

    def kernel(*refs):
        for (start, stop), out_ref in zip(cuts, refs[count:]):
            for i in range(count):
                out_ref[:, i * height : (i + 1) * height] = refs[i][:, :, start:stop]

    return pl.pallas_call(
        kernel,
        out_shape=[
            jax.ShapeDtypeStruct((outer, count * height, stop - start), pieces[0].dtype)
            for start, stop in cuts
        ],
        in_specs=whole_vmem(count),
        out_specs=whole_vmem(len(cuts)),
        compiler_params=params(),
        name="stack_pieces",
    )(*pieces)


def line_pairs(places):
    return [(2 * a + core, 2 * b + core) for a, b in places for core in range(2)]


def line_steps(block, place, count, ahead_of_last=None):
    low, high = [block], [block]
    for step in range(1, count - 1):
        low.append(
            lax.ppermute(low[-1], "dp", line_pairs([(i, i + 1) for i in range(step - 1, count - 1)]))
        )
        high.append(
            lax.ppermute(high[-1], "dp", line_pairs([(i, i - 1) for i in range(1, count - step + 1)]))
        )
    onward = jnp.where(place == count - 2, low[-1], high[-1])
    if ahead_of_last is not None:
        onward = ahead_of_last(onward, low, high)
    last = lax.ppermute(
        onward,
        "dp",
        line_pairs([(count - 2, count - 1), (1, 0)]),
    )
    return low + [last], high + [last]


def line_choice(step, place, count):
    is_low, is_high = place >= step, place <= count - 1 - step
    spare = count - step
    return [
        (is_low, 0, step, place - step),
        (jnp.logical_and(jnp.logical_not(is_low), is_high), 1, step, place + step),
        (
            jnp.logical_and(jnp.logical_not(is_low), jnp.logical_not(is_high)),
            1,
            spare,
            place + spare,
        ),
    ][: 2 if 2 * step <= count else 3]


def line_slots(arrivals, place, count):
    slots = [(place, arrivals[0][0])]
    for step in range(1, count):
        choices = line_choice(step, place, count)
        _, side, entry, owner = choices[-1]
        block = arrivals[side][entry]
        for holds, side, entry, other in reversed(choices[:-1]):
            if arrivals[side][entry] is not block:
                block = jnp.where(holds, arrivals[side][entry], block)
            owner = jnp.where(holds, other, owner)
        slots.append((owner, block))
    return slots


def place_cotangents(arrivals, line, n_tensor):
    tokens, width = arrivals[0][0].shape
    quarter = tokens // n_tensor
    low = [a.reshape(n_tensor, quarter, width) for a in arrivals[0]]
    high = [a.reshape(n_tensor, quarter, width) for a in arrivals[1][1:-1]]

    def kernel(*refs):
        low_refs = refs[: len(low)]
        high_refs = [low_refs[0]] + list(refs[len(low) : len(low) + len(high)]) + [low_refs[-1]]
        out_ref = refs[-1]
        place = own_place()

        def put(owner, source):
            begin = pl.multiple_of((owner ^ place) * quarter, quarter)
            out_ref[:, pl.ds(begin, quarter)] = source[...]

        put(place, low_refs[0])
        for step in range(1, line):
            for holds, side, entry, owner in line_choice(step, place, line):
                pl.when(holds)(functools.partial(put, owner, (low_refs, high_refs)[side][entry]))

    return pl.pallas_call(
        kernel,
        out_shape=jax.ShapeDtypeStruct((n_tensor, line * quarter, width), low[0].dtype),
        in_specs=whole_vmem(len(low) + len(high)),
        out_specs=pl.BlockSpec(memory_space=pltpu.VMEM),
        compiler_params=params(),
        name="place_cotangents",
    )(*low, *high)


def plane_gather(block, count):
    if count != 4:
        gathered = lax.all_gather(block, "tensor", axis=0)
        own = lax.axis_index("tensor")
        return [
            lax.dynamic_index_in_dim(gathered, own ^ b, 0, keepdims=False) for b in range(count)
        ]
    by_one = [(j, j ^ 1) for j in range(count)]
    by_two = [(j, j ^ 2) for j in range(count)]
    one = lax.ppermute(block, "tensor", by_one)
    two = lax.ppermute(block, "tensor", by_two)
    upper = lax.ppermute(one[:1], "tensor", by_two)
    lower = lax.ppermute(two[1:], "tensor", by_one)
    return [block, one, two, upper, lower]


def gradient_terms(blocks, cotangents, n_tensor):
    size = blocks[0].shape[2]
    width = cotangents.shape[2]
    split = len(blocks) > n_tensor

    def kernel(*refs):
        block_refs, cotangent_ref = refs[: len(blocks)], refs[len(blocks)]
        kept_ref, sent_ref = refs[len(blocks) + 1 :]
        index, core = lax.axis_index("tensor"), own_core()

        def term(owner):
            total = None
            for distance in range(n_tensor):
                if split and distance == n_tensor - 1:
                    upper, lower = block_refs[-2], block_refs[-1]
                    left = jnp.where(owner == 0, upper[0], lower[0])
                else:
                    left = block_refs[distance][owner]
                product = lax.dot_general(
                    left,
                    cotangent_ref[index ^ distance],
                    (((0,), (0,)), ((), ())),
                    preferred_element_type=jnp.float32,
                )
                total = product if total is None else total + product
            return total

        sent_ref[...] = term(1 - core).astype(sent_ref.dtype)
        kept_ref[...] = term(core)

    depth = n_tensor * blocks[0].shape[1]
    return pl.pallas_call(
        kernel,
        out_shape=(
            jax.ShapeDtypeStruct((size, width), jnp.float32),
            jax.ShapeDtypeStruct((size, width), jnp.bfloat16),
        ),
        in_specs=whole_vmem(len(blocks) + 1),
        out_specs=whole_vmem(2),
        compiler_params=params(),
        cost_estimate=pl.CostEstimate(
            flops=4 * depth * size * width,
            bytes_accessed=4 * depth * size + 2 * depth * width + 6 * size * width,
            transcendentals=0,
        ),
        name="gradient_terms",
    )(*blocks, cotangents)


def norm_columns(states, gain, rows, line):
    length, width = states.shape
    ranges = chunk_ranges(rows)
    tile = 64

    def kernel(states_ref, gain_ref, *outs):
        kept, sent = outs[: len(ranges)], outs[len(ranges) :]
        core = own_core()
        total = jnp.zeros((tile, 1), jnp.float32)
        for block in range(2 * line):
            piece = states_ref[:, block * rows : (block + 1) * rows].astype(jnp.float32)
            total = total + jnp.sum(piece * piece, axis=1, keepdims=True)
        scale = lax.rsqrt(total / width + norm_eps)
        for flag in range(2):

            @pl.when(core == flag)
            def _():
                for block in range(2 * line):
                    group = kept if block % 2 == flag else sent
                    for (start, size), out in zip(ranges, group):
                        columns = slice(block * rows + start, block * rows + start + size)
                        piece = states_ref[:, columns].astype(jnp.float32)
                        out[block // 2] = (piece * scale * gain_ref[:, columns]).astype(out.dtype)

    shapes = [
        jax.ShapeDtypeStruct((line, length, size), jnp.bfloat16) for _, size in ranges
    ] * 2
    outs = pl.pallas_call(
        kernel,
        grid=(length // tile,),
        out_shape=shapes,
        in_specs=[
            pl.BlockSpec((tile, width), lambda i: (i, 0)),
            pl.BlockSpec((1, width), lambda i: (0, 0)),
        ],
        out_specs=[pl.BlockSpec((line, tile, size), lambda i: (0, i, 0)) for _, size in ranges] * 2,
        compiler_params=params(),
        cost_estimate=pl.CostEstimate(
            flops=6 * length * width, bytes_accessed=4 * length * width, transcendentals=0
        ),
        name="norm_columns",
    )(states, gain.reshape(1, width))
    return outs[: len(ranges)], outs[len(ranges) :]


def accumulate(total, states, slots):
    _, length, depth = states.shape
    width = slots[0][1].shape[1]
    count = len(slots)
    tile = min(256, length)
    owners = jnp.stack([jnp.asarray(owner, jnp.int32) for owner, _ in slots])
    weights = [weight for _, weight in slots]

    def kernel(owners_ref, *refs):
        state_refs, weight_refs = refs[:count], refs[count : 2 * count]
        out_ref = refs[-1]
        result = None if total is None else refs[2 * count][...]
        for state_ref, weight_ref in zip(state_refs, weight_refs):
            product = jnp.dot(state_ref[0], weight_ref[...], preferred_element_type=jnp.float32)
            result = product if result is None else result + product
        out_ref[...] = result

    def state_spec(slot):
        return pl.BlockSpec((1, tile, depth), lambda i, chosen: (chosen[slot], i, 0))

    totals = [] if total is None else [total]
    row_spec = pl.BlockSpec((tile, width), lambda i, chosen: (i, 0))
    return pl.pallas_call(
        kernel,
        grid_spec=pltpu.PrefetchScalarGridSpec(
            num_scalar_prefetch=1,
            grid=(length // tile,),
            in_specs=[state_spec(slot) for slot in range(count)]
            + [pl.BlockSpec((depth, width), lambda i, chosen: (0, 0))] * count
            + [row_spec] * len(totals),
            out_specs=row_spec,
        ),
        out_shape=jax.ShapeDtypeStruct((length, width), jnp.float32),
        input_output_aliases={1 + 2 * count: 0} if totals else {},
        compiler_params=params(),
        cost_estimate=pl.CostEstimate(
            flops=2 * count * length * depth * width,
            bytes_accessed=2 * count * depth * (length + width) + 8 * length * width,
            transcendentals=0,
        ),
        name="accumulate",
    )(owners, *([states] * count), *weights, *totals)


def attention(kept, got, cosine_table, sine_table):
    length, width = kept.shape
    heads = width // HD - 2
    tile = min(128, length)

    def rope(u, cosine, sine):
        return u * cosine + pltpu.roll(u, HD // 2, 1) * sine

    def kernel(q_ref, q2_ref, k_ref, k2_ref, v_ref, v2_ref, cos_ref, sin_ref, out_ref, keys, values):
        @pl.when(pl.program_id(0) == 0)
        def _():
            key_rows = rope(k_ref[...] + k2_ref[...], cos_ref[...], sin_ref[...])
            keys[...] = key_rows.astype(jnp.bfloat16)
            values[...] = (v_ref[...] + v2_ref[...]).astype(jnp.bfloat16)

        for begin in range(0, length, tile):
            here, upto = slice(begin, begin + tile), begin + tile
            query = rope(q_ref[here] + q2_ref[here], cos_ref[here], sin_ref[here])
            query = (query * HD**-0.5).astype(jnp.bfloat16)
            scores = lax.dot_general(
                query,
                keys[:upto],
                (((1,), (1,)), ((), ())),
                preferred_element_type=jnp.float32,
            )
            row = lax.broadcasted_iota(jnp.int32, scores.shape, 0) + begin
            column = lax.broadcasted_iota(jnp.int32, scores.shape, 1)
            scores = jnp.where(row >= column, scores, -jnp.inf)
            raised = jnp.exp(scores - jnp.max(scores, axis=1, keepdims=True))
            weights = raised * (1.0 / jnp.sum(raised, axis=1, keepdims=True))
            out_ref[here] = jnp.dot(
                weights.astype(jnp.bfloat16), values[:upto], preferred_element_type=jnp.float32
            ).astype(jnp.bfloat16)

    def column(index):
        return pl.BlockSpec((length, HD), lambda h: (0, index))

    head = pl.BlockSpec((length, HD), lambda h: (0, h))
    return pl.pallas_call(
        kernel,
        grid=(heads,),
        out_shape=jax.ShapeDtypeStruct((length, heads * HD), jnp.bfloat16),
        in_specs=[head, head]
        + [column(heads)] * 2
        + [column(heads + 1)] * 2
        + [column(0)] * 2,
        out_specs=head,
        scratch_shapes=[pltpu.VMEM((length, HD), jnp.bfloat16)] * 2,
        compiler_params=params(),
        cost_estimate=pl.CostEstimate(
            flops=4 * heads * length * length * HD,
            bytes_accessed=9 * length * width,
            transcendentals=heads * length * length,
        ),
        name="attention",
    )(kept, got, kept, got, kept, got, cosine_table, sine_table)


def output_rows(mine, other, out_weight, n_tensor):
    kept, depth = mine.shape[1], mine.shape[2]
    width = out_weight.shape[1]
    tile = 512
    tiles = width // tile
    chosen = jnp.stack([lax.axis_index("tensor"), own_core()]).astype(jnp.int32)

    def kernel(chosen_ref, mine_ref, other_ref, *refs):
        weight_refs, (made_ref, sent_ref) = refs[:n_tensor], refs[n_tensor:]
        total = None
        for distance in range(n_tensor):
            left = jnp.concatenate([mine_ref[distance], other_ref[distance]], axis=0)
            product = jnp.dot(
                left, weight_refs[distance][...], preferred_element_type=jnp.float32
            )
            total = product if total is None else total + product
        made_ref[...] = total[:kept].astype(made_ref.dtype)
        sent_ref[...] = total[kept:].astype(sent_ref.dtype)

    def weight_spec(distance):
        return pl.BlockSpec((depth, tile), lambda i, chosen: (chosen[0] ^ distance, i))

    whole = pl.BlockSpec((n_tensor, kept, depth), lambda i, chosen: (0, 0, 0))
    return pl.pallas_call(
        kernel,
        grid_spec=pltpu.PrefetchScalarGridSpec(
            num_scalar_prefetch=1,
            grid=(tiles,),
            in_specs=[whole, whole] + [weight_spec(distance) for distance in range(n_tensor)],
            out_specs=[
                pl.BlockSpec((kept, tile), lambda i, chosen: (0, chosen[1] * tiles + i)),
                pl.BlockSpec((kept, tile), lambda i, chosen: (0, i)),
            ],
        ),
        out_shape=[
            jax.ShapeDtypeStruct((kept, 2 * width), jnp.bfloat16),
            jax.ShapeDtypeStruct((kept, width), jnp.bfloat16),
        ],
        compiler_params=params(),
        cost_estimate=pl.CostEstimate(
            flops=4 * kept * n_tensor * depth * width,
            bytes_accessed=2 * n_tensor * depth * width + 4 * kept * width,
            transcendentals=0,
        ),
        name="output_rows",
    )(chosen, mine, other, *([out_weight] * n_tensor))


def fill_columns(made, swapped):
    kept, width = swapped.shape
    chosen = jnp.reshape(1 - own_core(), (1,)).astype(jnp.int32)

    def kernel(chosen_ref, made_ref, swapped_ref, out_ref):
        out_ref[...] = swapped_ref[...]

    return pl.pallas_call(
        kernel,
        grid_spec=pltpu.PrefetchScalarGridSpec(
            num_scalar_prefetch=1,
            grid=(1,),
            in_specs=[
                pl.BlockSpec(memory_space=pl.ANY),
                pl.BlockSpec((kept, width), lambda i, chosen: (0, 0)),
            ],
            out_specs=pl.BlockSpec((kept, width), lambda i, chosen: (0, chosen[0])),
        ),
        out_shape=jax.ShapeDtypeStruct(made.shape, made.dtype),
        input_output_aliases={1: 0},
        compiler_params=params(),
        name="fill_columns",
    )(chosen, made, swapped)


def body(
    train_states, qkv_cotangent, w_master, moment_one, moment_two, prompt_states, norm_gain, w_out
):
    n_dp = lax.axis_size("dp")
    n_tensor = lax.axis_size("tensor")
    line = n_dp // 2
    tensor_index = lax.axis_index("tensor")
    core, place = own_core(), own_place()
    siblings = [(i, i ^ 1) for i in range(n_dp)]
    rows, slice_width = w_master.shape
    tokens, width = train_states.shape
    length = prompt_states.shape[0]
    query_width = slice_width - 2 * HD
    ranges = chunk_ranges(rows)

    arrivals = line_steps(qkv_cotangent, place, line)
    cotangents = place_cotangents(arrivals, line, n_tensor)

    half_width = width // 2
    w_half = lax.dynamic_slice(w_out, (0, core * half_width), (w_out.shape[0], half_width))
    out_weight = lax.all_gather(w_half, "tensor", axis=0, tiled=True)

    packed = pack_columns(train_states, rows, line, tokens // n_tensor)
    pieces = [packed[0]] + [
        lax.ppermute(
            packed[distance], "dp", line_pairs([(i, i ^ distance) for i in range(line)])
        )
        for distance in range(1, line)
    ]
    cuts = [(ranges[a][0], sum(ranges[b - 1])) for a, b in GROUPS]
    spread = [plane_gather(block, n_tensor) for block in stack_pieces(pieces, cuts)]

    cosine_table, sine_table = rope_tables(length, HD)
    updates, gathers = [], []
    own_total, other_total = None, None
    for group, (first_part, last_part) in enumerate(GROUPS):
        if group:
            low, high = gathers[0]
            low[1], high[1], spread[group] = lax.optimization_barrier(
                (low[1], high[1], spread[group])
            )
        kept, sent = gradient_terms(spread[group], cotangents, n_tensor)
        gradient = kept + lax.ppermute(sent, "dp", siblings).astype(jnp.float32)

        here = slice(*cuts[group])
        moment_new = beta_one * moment_one[here] + (1.0 - beta_one) * gradient
        second_new = beta_two * moment_two[here] + (1.0 - beta_two) * gradient * gradient
        update = moment_new / bias_one / (jnp.sqrt(second_new / bias_two) + adam_eps)
        updates.append(update)
        owned_weight = (w_master[here] - learn_rate * update).astype(jnp.bfloat16)
        if group == len(GROUPS) - 1:
            owned_weight, prompt_states = lax.optimization_barrier((owned_weight, prompt_states))
            update_dir = jnp.concatenate(updates, axis=0)
            kept_states, sent_states = norm_columns(prompt_states, norm_gain, rows, line)
            got_states = [lax.ppermute(states, "dp", siblings) for states in sent_states]
        for part in range(first_part, last_part):
            start, size = ranges[part]
            weight = owned_weight[start - cuts[group][0] : start - cuts[group][0] + size]
            if part < len(ranges) - 1:
                gathers.append(line_steps(weight, place, line))
                continue

            def accumulate_earlier(onward, low, high):
                nonlocal own_total, other_total, update_dir, cosine_table, sine_table
                for before, arrivals in enumerate(gathers):
                    slots = line_slots(arrivals, place, line)
                    other_total = accumulate(other_total, got_states[before], slots)
                    own_total = accumulate(own_total, kept_states[before], slots)
                onward, own_total, other_total, update_dir, cosine_table, sine_table = (
                    lax.optimization_barrier(
                        (onward, own_total, other_total, update_dir, cosine_table, sine_table)
                    )
                )
                return onward

            arrivals = line_steps(weight, place, line, accumulate_earlier)
            slots = line_slots(arrivals, place, line)
            for some in (slots[:-1], slots[-1:]):
                other_total = accumulate(other_total, got_states[part], some)
                own_total = accumulate(own_total, kept_states[part], some)
    attended = attention(
        own_total, lax.ppermute(other_total, "dp", siblings), cosine_table, sine_table
    )

    kept_rows = length // n_tensor
    heads = []
    for distance in range(n_tensor):
        target = tensor_index ^ distance
        block = lax.dynamic_slice(attended, (target * kept_rows, 0), (kept_rows, query_width))
        if distance:
            block = lax.ppermute(block, "tensor", [(j, j ^ distance) for j in range(n_tensor)])
        heads.append(block)
    (mine,) = stack_pieces([head[None] for head in heads], [(0, query_width)])
    mine = mine.reshape(n_tensor, kept_rows, query_width)
    other = lax.ppermute(mine, "dp", siblings)
    made, sent_rows = output_rows(mine, other, out_weight, n_tensor)
    swapped = lax.ppermute(sent_rows, "dp", siblings)
    summed = fill_columns(made, swapped)
    return (update_dir, summed)


def solution(mesh):
    placed = (
        P("dp", None),
        P("dp", "tensor"),
        P("dp", "tensor"),
        P("dp", "tensor"),
        P("dp", "tensor"),
        P("dp", None),
        P(),
        P("tensor", None),
    )
    return jax.shard_map(
        body,
        mesh=mesh,
        in_specs=placed,
        out_specs=(P("dp", "tensor"), P(("dp", "tensor"), None)),
        check_vma=False,
    )
```

```python
import functools

import jax
import jax.numpy as jnp
from jax import lax
from jax.experimental import pallas as pl
from jax.experimental.pallas import tpu as pltpu
from jax.sharding import PartitionSpec as P

HD = 128


beta_one = 0.9
beta_two = 0.95
bias_one = 1.0 - 0.9**8
bias_two = 1.0 - 0.95**8
learn_rate = 0.002
adam_eps = 1e-08
norm_eps = 1e-05
rope_base = 500000.0

CHUNK_QUARTERS = (1, 2, 1)
GROUPS = ((0, 1), (1, 3))
MIB = 1024 * 1024
SUMMED_SHARE = 4


def rope_tables(length, head_size):
    half_width = head_size // 2
    exponent = jnp.arange(half_width, dtype=jnp.float32) * (2.0 / head_size)
    inverse = jnp.power(jnp.float32(rope_base), -exponent)
    position = jnp.arange(length, dtype=jnp.float32)
    angles = position[:, None] * inverse[None, :]
    cosine_table = jnp.concatenate([jnp.cos(angles), jnp.cos(angles)], axis=1)
    sine_table = jnp.concatenate([-jnp.sin(angles), jnp.sin(angles)], axis=1)
    return (cosine_table, sine_table)


def chunk_ranges(rows):
    quarter, start, ranges = rows // 4, 0, []
    for quarters in CHUNK_QUARTERS:
        ranges.append((start, quarters * quarter))
        start += quarters * quarter
    return ranges


def params(mib=16):
    return pltpu.CompilerParams(vmem_limit_bytes=mib * MIB)


def whole_vmem(count):
    return [pl.BlockSpec(memory_space=pltpu.VMEM)] * count


def own_core():
    return lax.rem(lax.axis_index("dp"), 2)


def own_place():
    return lax.div(lax.axis_index("dp"), 2)


def pack_columns(train_states, rows, line, quarter):
    def kernel(index_ref, train_ref, *outs):
        place = own_place()
        for distance in range(line):
            for owner in range(2):
                column = pl.multiple_of(((place ^ distance) * 2 + owner) * rows, 128)
                outs[distance][owner] = train_ref[:, pl.ds(column, rows)]

    shapes = [jax.ShapeDtypeStruct((2, quarter, rows), train_states.dtype)] * line
    index = jnp.reshape(lax.axis_index("tensor"), (1,)).astype(jnp.int32)
    return pl.pallas_call(
        kernel,
        grid_spec=pltpu.PrefetchScalarGridSpec(
            num_scalar_prefetch=1,
            grid=(1,),
            in_specs=[
                pl.BlockSpec((quarter, train_states.shape[1]), lambda i, chosen: (chosen[0], 0))
            ],
            out_specs=[pl.BlockSpec(s.shape, lambda i, chosen: (0, 0, 0)) for s in shapes],
        ),
        out_shape=shapes,
        compiler_params=params(),
        name="pack_columns",
    )(index, train_states)


def stack_pieces(pieces, cuts):
    outer, height, _ = pieces[0].shape
    count = len(pieces)

    def kernel(*refs):
        for (start, stop), out_ref in zip(cuts, refs[count:]):
            for i in range(count):
                out_ref[:, i * height : (i + 1) * height] = refs[i][:, :, start:stop]

    return pl.pallas_call(
        kernel,
        out_shape=[
            jax.ShapeDtypeStruct((outer, count * height, stop - start), pieces[0].dtype)
            for start, stop in cuts
        ],
        in_specs=whole_vmem(count),
        out_specs=whole_vmem(len(cuts)),
        compiler_params=params(),
        name="stack_pieces",
    )(*pieces)


def line_pairs(places):
    return [(2 * a + core, 2 * b + core) for a, b in places for core in range(2)]


def line_steps(block, place, count, ahead=None):
    ahead = ahead or {}
    low, high = [block], [block]
    for step in range(1, count - 1):
        up, down = low[-1], high[-1]
        if step in ahead:
            up, down = ahead[step](up, down)
        low.append(
            lax.ppermute(up, "dp", line_pairs([(i, i + 1) for i in range(step - 1, count - 1)]))
        )
        high.append(
            lax.ppermute(down, "dp", line_pairs([(i, i - 1) for i in range(1, count - step + 1)]))
        )
    up, down = low[-1], high[-1]
    if count - 1 in ahead:
        up, down = ahead[count - 1](up, down)
    last = lax.ppermute(
        jnp.where(place == count - 2, up, down),
        "dp",
        line_pairs([(count - 2, count - 1), (1, 0)]),
    )
    return low + [last], high + [last]


def line_choice(step, place, count):
    is_low, is_high = place >= step, place <= count - 1 - step
    spare = count - step
    return [
        (is_low, 0, step, place - step),
        (jnp.logical_and(jnp.logical_not(is_low), is_high), 1, step, place + step),
        (
            jnp.logical_and(jnp.logical_not(is_low), jnp.logical_not(is_high)),
            1,
            spare,
            place + spare,
        ),
    ][: 2 if 2 * step <= count else 3]


def line_slots(arrivals, place, count):
    slots = [(place, arrivals[0][0])]
    for step in range(1, count):
        choices = line_choice(step, place, count)
        _, side, entry, owner = choices[-1]
        block = arrivals[side][entry]
        for holds, side, entry, other in reversed(choices[:-1]):
            if arrivals[side][entry] is not block:
                block = jnp.where(holds, arrivals[side][entry], block)
            owner = jnp.where(holds, other, owner)
        slots.append((owner, block))
    return slots


def place_cotangents(arrivals, line, n_tensor):
    tokens, width = arrivals[0][0].shape
    quarter = tokens // n_tensor
    low = [a.reshape(n_tensor, quarter, width) for a in arrivals[0]]
    high = [a.reshape(n_tensor, quarter, width) for a in arrivals[1][1:-1]]

    def kernel(*refs):
        low_refs = refs[: len(low)]
        high_refs = [low_refs[0]] + list(refs[len(low) : len(low) + len(high)]) + [low_refs[-1]]
        out_ref = refs[-1]
        place = own_place()

        def put(owner, source):
            begin = pl.multiple_of((owner ^ place) * quarter, quarter)
            out_ref[:, pl.ds(begin, quarter)] = source[...]

        put(place, low_refs[0])
        for step in range(1, line):
            for holds, side, entry, owner in line_choice(step, place, line):
                pl.when(holds)(functools.partial(put, owner, (low_refs, high_refs)[side][entry]))

    return pl.pallas_call(
        kernel,
        out_shape=jax.ShapeDtypeStruct((n_tensor, line * quarter, width), low[0].dtype),
        in_specs=whole_vmem(len(low) + len(high)),
        out_specs=pl.BlockSpec(memory_space=pltpu.VMEM),
        compiler_params=params(),
        name="place_cotangents",
    )(*low, *high)


def plane_gather(block, count):
    if count != 4:
        gathered = lax.all_gather(block, "tensor", axis=0)
        own = lax.axis_index("tensor")
        return [
            lax.dynamic_index_in_dim(gathered, own ^ b, 0, keepdims=False) for b in range(count)
        ]
    by_one = [(j, j ^ 1) for j in range(count)]
    by_two = [(j, j ^ 2) for j in range(count)]
    one = lax.ppermute(block, "tensor", by_one)
    two = lax.ppermute(block, "tensor", by_two)
    upper = lax.ppermute(one[:1], "tensor", by_two)
    lower = lax.ppermute(two[1:], "tensor", by_one)
    return [block, one, two, upper, lower]


def gradient_terms(blocks, cotangents, n_tensor):
    size = blocks[0].shape[2]
    width = cotangents.shape[2]
    split = len(blocks) > n_tensor

    def kernel(*refs):
        block_refs, cotangent_ref = refs[: len(blocks)], refs[len(blocks)]
        kept_ref, sent_ref = refs[len(blocks) + 1 :]
        index, core = lax.axis_index("tensor"), own_core()

        def term(owner):
            total = None
            for distance in range(n_tensor):
                if split and distance == n_tensor - 1:
                    upper, lower = block_refs[-2], block_refs[-1]
                    left = jnp.where(owner == 0, upper[0], lower[0])
                else:
                    left = block_refs[distance][owner]
                product = lax.dot_general(
                    left,
                    cotangent_ref[index ^ distance],
                    (((0,), (0,)), ((), ())),
                    preferred_element_type=jnp.float32,
                )
                total = product if total is None else total + product
            return total

        sent_ref[...] = term(1 - core).astype(sent_ref.dtype)
        kept_ref[...] = term(core)

    depth = n_tensor * blocks[0].shape[1]
    return pl.pallas_call(
        kernel,
        out_shape=(
            jax.ShapeDtypeStruct((size, width), jnp.float32),
            jax.ShapeDtypeStruct((size, width), jnp.bfloat16),
        ),
        in_specs=whole_vmem(len(blocks) + 1),
        out_specs=whole_vmem(2),
        compiler_params=params(),
        cost_estimate=pl.CostEstimate(
            flops=4 * depth * size * width,
            bytes_accessed=4 * depth * size + 2 * depth * width + 6 * size * width,
            transcendentals=0,
        ),
        name="gradient_terms",
    )(*blocks, cotangents)


def norm_columns(states, gain, rows, line):
    length, width = states.shape
    ranges = chunk_ranges(rows)
    tile = 64

    def kernel(states_ref, gain_ref, *outs):
        kept, sent = outs[: len(ranges)], outs[len(ranges) :]
        core = own_core()
        total = jnp.zeros((tile, 1), jnp.float32)
        for block in range(2 * line):
            piece = states_ref[:, block * rows : (block + 1) * rows].astype(jnp.float32)
            total = total + jnp.sum(piece * piece, axis=1, keepdims=True)
        scale = lax.rsqrt(total / width + norm_eps)
        for flag in range(2):

            @pl.when(core == flag)
            def _():
                for block in range(2 * line):
                    group = kept if block % 2 == flag else sent
                    for (start, size), out in zip(ranges, group):
                        columns = slice(block * rows + start, block * rows + start + size)
                        piece = states_ref[:, columns].astype(jnp.float32)
                        out[block // 2] = (piece * scale * gain_ref[:, columns]).astype(out.dtype)

    shapes = [
        jax.ShapeDtypeStruct((line, length, size), jnp.bfloat16) for _, size in ranges
    ] * 2
    outs = pl.pallas_call(
        kernel,
        grid=(length // tile,),
        out_shape=shapes,
        in_specs=[
            pl.BlockSpec((tile, width), lambda i: (i, 0)),
            pl.BlockSpec((1, width), lambda i: (0, 0)),
        ],
        out_specs=[pl.BlockSpec((line, tile, size), lambda i: (0, i, 0)) for _, size in ranges] * 2,
        compiler_params=params(),
        cost_estimate=pl.CostEstimate(
            flops=6 * length * width, bytes_accessed=4 * length * width, transcendentals=0
        ),
        name="norm_columns",
    )(states, gain.reshape(1, width))
    return outs[: len(ranges)], outs[len(ranges) :]


def accumulate(totals, kept, got, slots, last=False):
    _, length, depth = kept.shape
    width = slots[0][1].shape[1]
    count = len(slots)
    tile = min(256, length)
    owners = jnp.stack([jnp.asarray(owner, jnp.int32) for owner, _ in slots])
    weights = [weight for _, weight in slots]

    def kernel(owners_ref, *refs):
        weight_refs = refs[2 * count : 3 * count]
        for side, out_ref in zip((1, 0), reversed(refs[-2:])):
            result = None if totals is None else refs[3 * count + side][...]
            for slot in range(count):
                product = jnp.dot(
                    refs[side * count + slot][0],
                    weight_refs[slot][...],
                    preferred_element_type=jnp.float32,
                )
                result = product if result is None else result + product
            out_ref[...] = result.astype(out_ref.dtype)

    def state_spec(slot):
        return pl.BlockSpec((1, tile, depth), lambda i, chosen: (chosen[slot], i, 0))

    before = list(totals or [])
    row_spec = pl.BlockSpec((tile, width), lambda i, chosen: (i, 0))
    return pl.pallas_call(
        kernel,
        grid_spec=pltpu.PrefetchScalarGridSpec(
            num_scalar_prefetch=1,
            grid=(length // tile,),
            in_specs=[state_spec(slot) for slot in range(count)] * 2
            + [pl.BlockSpec((depth, width), lambda i, chosen: (0, 0))] * count
            + [row_spec] * len(before),
            out_specs=[row_spec] * 2,
        ),
        out_shape=[
            jax.ShapeDtypeStruct((length, width), jnp.float32),
            jax.ShapeDtypeStruct((length, width), jnp.bfloat16 if last else jnp.float32),
        ],
        compiler_params=params(24),
        cost_estimate=pl.CostEstimate(
            flops=4 * count * length * depth * width,
            bytes_accessed=2 * count * depth * (2 * length + width) + 16 * length * width,
            transcendentals=0,
        ),
        name="accumulate",
    )(owners, *([kept] * count), *([got] * count), *weights, *before)


def attention(kept, got, cosine_table, sine_table):
    length, width = kept.shape
    heads = width // HD - 2
    tile = min(128, length)

    def rope(u, cosine, sine):
        return u * cosine + pltpu.roll(u, HD // 2, 1) * sine

    def kernel(q_ref, q2_ref, k_ref, k2_ref, v_ref, v2_ref, cos_ref, sin_ref, out_ref, keys, values):
        @pl.when(pl.program_id(0) == 0)
        def _():
            key_rows = rope(k_ref[...] + k2_ref[...], cos_ref[...], sin_ref[...])
            keys[...] = key_rows.astype(jnp.bfloat16)
            values[...] = (v_ref[...] + v2_ref[...]).astype(jnp.bfloat16)

        for begin in range(0, length, tile):
            here, upto = slice(begin, begin + tile), begin + tile
            query = rope(q_ref[here] + q2_ref[here], cos_ref[here], sin_ref[here])
            query = (query * HD**-0.5).astype(jnp.bfloat16)
            scores = lax.dot_general(
                query,
                keys[:upto],
                (((1,), (1,)), ((), ())),
                preferred_element_type=jnp.float32,
            )
            row = lax.broadcasted_iota(jnp.int32, scores.shape, 0) + begin
            column = lax.broadcasted_iota(jnp.int32, scores.shape, 1)
            scores = jnp.where(row >= column, scores, -jnp.inf)
            raised = jnp.exp(scores - jnp.max(scores, axis=1, keepdims=True))
            weights = raised * (1.0 / jnp.sum(raised, axis=1, keepdims=True))
            out_ref[here] = jnp.dot(
                weights.astype(jnp.bfloat16), values[:upto], preferred_element_type=jnp.float32
            ).astype(jnp.bfloat16)

    def column(index):
        return pl.BlockSpec((length, HD), lambda h: (0, index))

    head = pl.BlockSpec((length, HD), lambda h: (0, h))
    return pl.pallas_call(
        kernel,
        grid=(heads,),
        out_shape=jax.ShapeDtypeStruct((length, heads * HD), jnp.bfloat16),
        in_specs=[head, head]
        + [column(heads)] * 2
        + [column(heads + 1)] * 2
        + [column(0)] * 2,
        out_specs=head,
        scratch_shapes=[pltpu.VMEM((length, HD), jnp.bfloat16)] * 2,
        compiler_params=params(),
        cost_estimate=pl.CostEstimate(
            flops=4 * heads * length * length * HD,
            bytes_accessed=9 * length * width,
            transcendentals=heads * length * length,
        ),
        name="attention",
    )(kept, got, kept, got, kept, got, cosine_table, sine_table)


def output_rows(mine, other, first_weight, rest_weight, n_tensor, full_width):
    kept, depth = mine.shape[1], mine.shape[2]
    tile = first_weight.shape[1]
    width = tile + rest_weight.shape[1]
    tiles = width // tile
    chosen = jnp.stack([lax.axis_index("tensor"), own_core()]).astype(jnp.int32)

    def kernel(chosen_ref, mine_ref, other_ref, *refs):
        first_refs, rest_refs = refs[:n_tensor], refs[n_tensor : 2 * n_tensor]
        made_ref, sent_ref, left_ref = refs[2 * n_tensor :]

        def product(weight_refs):
            total = None
            for distance in range(n_tensor):
                term = jnp.dot(
                    left_ref[distance],
                    weight_refs[distance][...],
                    preferred_element_type=jnp.float32,
                )
                total = term if total is None else total + term
            made_ref[...] = total[:kept].astype(made_ref.dtype)
            sent_ref[...] = total[kept:].astype(sent_ref.dtype)

        @pl.when(pl.program_id(0) == 0)
        def _():
            left_ref[:, :kept] = mine_ref[...]
            left_ref[:, kept:] = other_ref[...]
            product(first_refs)

        @pl.when(pl.program_id(0) > 0)
        def _():
            product(rest_refs)

    def first_spec(distance):
        return pl.BlockSpec((depth, tile), lambda i, chosen: (chosen[0] ^ distance, 0))

    def rest_spec(distance):
        return pl.BlockSpec(
            (depth, tile), lambda i, chosen: (chosen[0] ^ distance, jnp.maximum(i - 1, 0))
        )

    whole = pl.BlockSpec((n_tensor, kept, depth), lambda i, chosen: (0, 0, 0))
    return pl.pallas_call(
        kernel,
        grid_spec=pltpu.PrefetchScalarGridSpec(
            num_scalar_prefetch=1,
            grid=(tiles,),
            in_specs=[whole, whole]
            + [first_spec(distance) for distance in range(n_tensor)]
            + [rest_spec(distance) for distance in range(n_tensor)],
            out_specs=[
                pl.BlockSpec((kept, tile), lambda i, chosen: (0, chosen[1] * tiles + i)),
                pl.BlockSpec((kept, tile), lambda i, chosen: (0, i)),
            ],
            scratch_shapes=[pltpu.VMEM((n_tensor, 2 * kept, depth), jnp.bfloat16)],
        ),
        out_shape=[
            jax.ShapeDtypeStruct((kept, full_width), jnp.bfloat16),
            jax.ShapeDtypeStruct((kept, width), jnp.bfloat16),
        ],
        compiler_params=params(52),
        cost_estimate=pl.CostEstimate(
            flops=4 * kept * n_tensor * depth * width,
            bytes_accessed=2 * n_tensor * depth * width + 4 * kept * width,
            transcendentals=0,
        ),
        name="output_rows",
    )(
        chosen,
        mine,
        other,
        *([first_weight] * n_tensor),
        *([rest_weight] * n_tensor),
    )


def head_parts(attended, weight, n_tensor):
    length, depth = attended.shape
    kept, width = length // n_tensor, weight.shape[1]
    index = jnp.reshape(lax.axis_index("tensor"), (1,)).astype(jnp.int32)

    def kernel(index_ref, attended_ref, weight_ref, *outs):
        for distance in reversed(range(n_tensor)):
            begin = pl.multiple_of((index_ref[0] ^ distance) * kept, kept)
            outs[distance][...] = jnp.dot(
                attended_ref[pl.ds(begin, kept)],
                weight_ref[...],
                preferred_element_type=jnp.float32,
            ).astype(outs[distance].dtype)

    return pl.pallas_call(
        kernel,
        in_specs=[pl.BlockSpec(memory_space=pltpu.SMEM)] + whole_vmem(2),
        out_specs=whole_vmem(n_tensor),
        out_shape=[jax.ShapeDtypeStruct((kept, width), jnp.bfloat16)] * n_tensor,
        compiler_params=params(),
        cost_estimate=pl.CostEstimate(
            flops=2 * length * depth * width,
            bytes_accessed=2 * depth * width + 2 * length * width,
            transcendentals=0,
        ),
        name="head_parts",
    )(index, attended, weight)


def add_columns(made, parts):
    kept, width = parts[0].shape

    def kernel(made_ref, *refs):
        total = refs[0][...].astype(jnp.float32)
        for ref in refs[1:-1]:
            total = total + ref[...].astype(jnp.float32)
        refs[-1][...] = total.astype(refs[-1].dtype)

    last = made.shape[1] // width - 1
    return pl.pallas_call(
        kernel,
        grid=(1,),
        in_specs=[pl.BlockSpec(memory_space=pl.ANY)]
        + [pl.BlockSpec((kept, width), lambda i: (0, 0))] * len(parts),
        out_specs=pl.BlockSpec((kept, width), lambda i: (0, last)),
        out_shape=jax.ShapeDtypeStruct(made.shape, made.dtype),
        input_output_aliases={0: 0},
        compiler_params=params(),
        name="add_columns",
    )(made, *parts)


def fill_columns(made, swapped):
    kept, width = swapped.shape
    chosen = jnp.reshape(1 - own_core(), (1,)).astype(jnp.int32)

    def kernel(chosen_ref, made_ref, swapped_ref, out_ref):
        out_ref[...] = swapped_ref[...]

    return pl.pallas_call(
        kernel,
        grid_spec=pltpu.PrefetchScalarGridSpec(
            num_scalar_prefetch=1,
            grid=(1,),
            in_specs=[
                pl.BlockSpec(memory_space=pl.ANY),
                pl.BlockSpec((kept, width), lambda i, chosen: (0, 0)),
            ],
            out_specs=pl.BlockSpec((kept, width), lambda i, chosen: (0, chosen[0])),
        ),
        out_shape=jax.ShapeDtypeStruct(made.shape, made.dtype),
        input_output_aliases={1: 0},
        compiler_params=params(),
        name="fill_columns",
    )(chosen, made, swapped)


def body(
    train_states, qkv_cotangent, w_master, moment_one, moment_two, prompt_states, norm_gain, w_out
):
    n_dp = lax.axis_size("dp")
    n_tensor = lax.axis_size("tensor")
    line = n_dp // 2
    tensor_index = lax.axis_index("tensor")
    core, place = own_core(), own_place()
    siblings = [(i, i ^ 1) for i in range(n_dp)]
    rows, slice_width = w_master.shape
    tokens, width = train_states.shape
    length = prompt_states.shape[0]
    query_width = slice_width - 2 * HD
    ranges = chunk_ranges(rows)

    packed = pack_columns(train_states, rows, line, tokens // n_tensor)
    packed, qkv_cotangent = lax.optimization_barrier((packed, qkv_cotangent))
    pieces = [packed[0]] + [
        lax.ppermute(
            packed[distance], "dp", line_pairs([(i, i ^ distance) for i in range(line)])
        )
        for distance in range(1, line)
    ]

    def behind_columns(up, down):
        nonlocal pieces
        up, down, pieces = lax.optimization_barrier((up, down, pieces))
        return up, down

    arrivals = line_steps(qkv_cotangent, place, line, {2: behind_columns})
    cotangents = place_cotangents(arrivals, line, n_tensor)
    cuts = [(ranges[a][0], sum(ranges[b - 1])) for a, b in GROUPS]
    stacked = list(stack_pieces(pieces, cuts))
    spread = [plane_gather(stacked[0], n_tensor)]

    summed_width = width // SUMMED_SHARE
    core_width = (width - summed_width) // 2
    early_width = core_width // 6
    begin = core * core_width
    early_weight = lax.all_gather(
        lax.dynamic_slice(w_out, (0, begin), (w_out.shape[0], early_width)),
        "tensor",
        axis=0,
        tiled=True,
    )
    w_out, stacked[1], spread[0] = lax.optimization_barrier((w_out, stacked[1], spread[0]))
    rest_weight = lax.all_gather(
        lax.dynamic_slice(
            w_out, (0, begin + early_width), (w_out.shape[0], core_width - early_width)
        ),
        "tensor",
        axis=0,
        tiled=True,
    )
    spread.append(plane_gather(stacked[1], n_tensor))

    cosine_table, sine_table = rope_tables(length, HD)
    updates, gathers = [], []
    totals = None
    for group, (first_part, last_part) in enumerate(GROUPS):
        if group:
            low, high = gathers[0]
            low[1], high[1], spread[group] = lax.optimization_barrier(
                (low[1], high[1], spread[group])
            )
        kept, sent = gradient_terms(spread[group], cotangents, n_tensor)
        gradient = kept + lax.ppermute(sent, "dp", siblings).astype(jnp.float32)

        here = slice(*cuts[group])
        moment_new = beta_one * moment_one[here] + (1.0 - beta_one) * gradient
        second_new = beta_two * moment_two[here] + (1.0 - beta_two) * gradient * gradient
        update = moment_new / bias_one / (jnp.sqrt(second_new / bias_two) + adam_eps)
        updates.append(update)
        owned_weight = (w_master[here] - learn_rate * update).astype(jnp.bfloat16)
        if group == len(GROUPS) - 1:
            owned_weight, prompt_states = lax.optimization_barrier((owned_weight, prompt_states))
            update_dir = jnp.concatenate(updates, axis=0)
            kept_states, sent_states = norm_columns(prompt_states, norm_gain, rows, line)
            got_states = [lax.ppermute(states, "dp", siblings) for states in sent_states]
        for part in range(first_part, last_part):
            start, size = ranges[part]
            weight = owned_weight[start - cuts[group][0] : start - cuts[group][0] + size]
            if part < len(ranges) - 1:
                gathers.append(line_steps(weight, place, line))
                continue

            def accumulate_earlier(up, down):
                nonlocal totals, update_dir, cosine_table, sine_table
                for before, arrivals in enumerate(gathers):
                    slots = line_slots(arrivals, place, line)
                    if before == len(gathers) - 1:
                        slots = slots[:-1]
                    totals = accumulate(totals, kept_states[before], got_states[before], slots)
                up, down, totals, update_dir, cosine_table, sine_table = (
                    lax.optimization_barrier(
                        (up, down, totals, update_dir, cosine_table, sine_table)
                    )
                )
                return up, down

            arrivals = line_steps(weight, place, line, {line - 1: accumulate_earlier})
            slots = line_slots(gathers[-1], place, line)
            totals = accumulate(
                totals, kept_states[part - 1], got_states[part - 1], slots[-1:]
            )
            slots = line_slots(arrivals, place, line)
            totals = accumulate(totals, kept_states[part], got_states[part], slots[:-1])
            totals = accumulate(totals, kept_states[part], got_states[part], slots[-1:], True)
    attended = attention(
        totals[0], lax.ppermute(totals[1], "dp", siblings), cosine_table, sine_table
    )

    kept_rows = length // n_tensor
    heads = []
    for distance in range(n_tensor):
        target = tensor_index ^ distance
        block = lax.dynamic_slice(attended, (target * kept_rows, 0), (kept_rows, query_width))
        if distance:
            block = lax.ppermute(block, "tensor", [(j, j ^ distance) for j in range(n_tensor)])
        heads.append(block)
    parts = head_parts(attended, w_out[:, width - summed_width :], n_tensor)
    parts, heads = lax.optimization_barrier((parts, heads))
    (mine,) = stack_pieces([head[None] for head in heads], [(0, query_width)])
    mine = mine.reshape(n_tensor, kept_rows, query_width)
    other = lax.ppermute(mine, "dp", siblings)

    parts = [parts[0]] + [
        lax.ppermute(parts[distance], "tensor", [(j, j ^ distance) for j in range(n_tensor)])
        for distance in range(1, n_tensor)
    ]
    made, sent_rows = output_rows(mine, other, early_weight, rest_weight, n_tensor, width)
    swapped = lax.ppermute(sent_rows, "dp", siblings)
    summed = add_columns(fill_columns(made, swapped), parts)
    return (update_dir, summed)


def solution(mesh):
    placed = (
        P("dp", None),
        P("dp", "tensor"),
        P("dp", "tensor"),
        P("dp", "tensor"),
        P("dp", "tensor"),
        P("dp", None),
        P(),
        P("tensor", None),
    )
    return jax.shard_map(
        body,
        mesh=mesh,
        in_specs=placed,
        out_specs=(P("dp", "tensor"), P(("dp", "tensor"), None)),
        check_vma=False,
    )
```

```python
import functools

import jax
import jax.numpy as jnp
from jax import lax
from jax.experimental import pallas as pl
from jax.experimental.pallas import tpu as pltpu
from jax.sharding import PartitionSpec as P

HD = 128


beta_one = 0.9
beta_two = 0.95
bias_one = 1.0 - 0.9**8
bias_two = 1.0 - 0.95**8
learn_rate = 0.002
adam_eps = 1e-08
norm_eps = 1e-05
rope_base = 500000.0

CHUNK_QUARTERS = (1, 3)
MIB = 1024 * 1024
SUMMED_SHARE = 4


def rope_tables(length, head_size):
    half_width = head_size // 2
    exponent = jnp.arange(half_width, dtype=jnp.float32) * (2.0 / head_size)
    inverse = jnp.power(jnp.float32(rope_base), -exponent)
    position = jnp.arange(length, dtype=jnp.float32)
    angles = position[:, None] * inverse[None, :]
    cosine_table = jnp.concatenate([jnp.cos(angles), jnp.cos(angles)], axis=1)
    sine_table = jnp.concatenate([-jnp.sin(angles), jnp.sin(angles)], axis=1)
    return (cosine_table, sine_table)


def chunk_ranges(rows):
    quarter, start, ranges = rows // 4, 0, []
    for quarters in CHUNK_QUARTERS:
        ranges.append((start, quarters * quarter))
        start += quarters * quarter
    return ranges


def params(mib=16):
    return pltpu.CompilerParams(vmem_limit_bytes=mib * MIB)


def whole_vmem(count):
    return [pl.BlockSpec(memory_space=pltpu.VMEM)] * count


def own_core():
    return lax.rem(lax.axis_index("dp"), 2)


def own_place():
    return lax.div(lax.axis_index("dp"), 2)


def pack_columns(train_states, rows, line, quarter):
    def kernel(index_ref, train_ref, *outs):
        place = own_place()
        for distance in range(line):
            for owner in range(2):
                column = pl.multiple_of(((place ^ distance) * 2 + owner) * rows, 128)
                outs[distance][owner] = train_ref[:, pl.ds(column, rows)]

    shapes = [jax.ShapeDtypeStruct((2, quarter, rows), train_states.dtype)] * line
    index = jnp.reshape(lax.axis_index("tensor"), (1,)).astype(jnp.int32)
    return pl.pallas_call(
        kernel,
        grid_spec=pltpu.PrefetchScalarGridSpec(
            num_scalar_prefetch=1,
            grid=(1,),
            in_specs=[
                pl.BlockSpec((quarter, train_states.shape[1]), lambda i, chosen: (chosen[0], 0))
            ],
            out_specs=[pl.BlockSpec(s.shape, lambda i, chosen: (0, 0, 0)) for s in shapes],
        ),
        out_shape=shapes,
        compiler_params=params(56),
        name="pack_columns",
    )(index, train_states)


def stack_pieces(pieces, cuts):
    outer, height, _ = pieces[0].shape
    count = len(pieces)

    def kernel(*refs):
        for (start, stop), out_ref in zip(cuts, refs[count:]):
            for i in range(count):
                out_ref[:, i * height : (i + 1) * height] = refs[i][:, :, start:stop]

    return pl.pallas_call(
        kernel,
        out_shape=[
            jax.ShapeDtypeStruct((outer, count * height, stop - start), pieces[0].dtype)
            for start, stop in cuts
        ],
        in_specs=whole_vmem(count),
        out_specs=whole_vmem(len(cuts)),
        compiler_params=params(),
        name="stack_pieces",
    )(*pieces)


def line_pairs(places):
    return [(2 * a + core, 2 * b + core) for a, b in places for core in range(2)]


def line_steps(block, place, count, ahead=None):
    ahead = ahead or {}
    low, high = [block], [block]
    for step in range(1, count - 1):
        up, down = low[-1], high[-1]
        if step in ahead:
            up, down = ahead[step](up, down)
        low.append(
            lax.ppermute(up, "dp", line_pairs([(i, i + 1) for i in range(step - 1, count - 1)]))
        )
        high.append(
            lax.ppermute(down, "dp", line_pairs([(i, i - 1) for i in range(1, count - step + 1)]))
        )
    up, down = low[-1], high[-1]
    if count - 1 in ahead:
        up, down = ahead[count - 1](up, down)
    last = lax.ppermute(
        jnp.where(place == count - 2, up, down),
        "dp",
        line_pairs([(count - 2, count - 1), (1, 0)]),
    )
    return low + [last], high + [last]


def line_choice(step, place, count):
    is_low, is_high = place >= step, place <= count - 1 - step
    spare = count - step
    return [
        (is_low, 0, step, place - step),
        (jnp.logical_and(jnp.logical_not(is_low), is_high), 1, step, place + step),
        (
            jnp.logical_and(jnp.logical_not(is_low), jnp.logical_not(is_high)),
            1,
            spare,
            place + spare,
        ),
    ][: 2 if 2 * step <= count else 3]


def line_slots(arrivals, place, count):
    slots = [(place, arrivals[0][0])]
    for step in range(1, count):
        choices = line_choice(step, place, count)
        _, side, entry, owner = choices[-1]
        block = arrivals[side][entry]
        for holds, side, entry, other in reversed(choices[:-1]):
            if arrivals[side][entry] is not block:
                block = jnp.where(holds, arrivals[side][entry], block)
            owner = jnp.where(holds, other, owner)
        slots.append((owner, block))
    return slots


def place_cotangents(arrivals, line, n_tensor):
    tokens, width = arrivals[0][0].shape
    quarter = tokens // n_tensor
    low = [a.reshape(n_tensor, quarter, width) for a in arrivals[0]]
    high = [a.reshape(n_tensor, quarter, width) for a in arrivals[1][1:-1]]

    def kernel(*refs):
        low_refs = refs[: len(low)]
        high_refs = [low_refs[0]] + list(refs[len(low) : len(low) + len(high)]) + [low_refs[-1]]
        out_ref = refs[-1]
        place = own_place()

        def put(owner, source):
            begin = pl.multiple_of((owner ^ place) * quarter, quarter)
            out_ref[:, pl.ds(begin, quarter)] = source[...]

        put(place, low_refs[0])
        for step in range(1, line):
            for holds, side, entry, owner in line_choice(step, place, line):
                pl.when(holds)(functools.partial(put, owner, (low_refs, high_refs)[side][entry]))

    return pl.pallas_call(
        kernel,
        out_shape=jax.ShapeDtypeStruct((n_tensor, line * quarter, width), low[0].dtype),
        in_specs=whole_vmem(len(low) + len(high)),
        out_specs=pl.BlockSpec(memory_space=pltpu.VMEM),
        compiler_params=params(),
        name="place_cotangents",
    )(*low, *high)


def plane_gather(block, count, ahead=None):
    if count != 4:
        gathered = lax.all_gather(block, "tensor", axis=0)
        own = lax.axis_index("tensor")
        return [
            lax.dynamic_index_in_dim(gathered, own ^ b, 0, keepdims=False) for b in range(count)
        ]
    by_one = [(j, j ^ 1) for j in range(count)]
    by_two = [(j, j ^ 2) for j in range(count)]
    one = lax.ppermute(block, "tensor", by_one)
    two = lax.ppermute(block, "tensor", by_two)
    up, down = one[:1], two[1:]
    if ahead is not None:
        up, down = ahead(up, down)
    upper = lax.ppermute(up, "tensor", by_two)
    lower = lax.ppermute(down, "tensor", by_one)
    return [block, one, two, upper, lower]


def gradient_terms(blocks, cotangents, n_tensor):
    size = blocks[0].shape[2]
    width = cotangents.shape[2]
    split = len(blocks) > n_tensor

    def kernel(*refs):
        block_refs, cotangent_ref = refs[: len(blocks)], refs[len(blocks)]
        kept_ref, sent_ref = refs[len(blocks) + 1 :]
        index, core = lax.axis_index("tensor"), own_core()

        def term(owner):
            total = None
            for distance in range(n_tensor):
                if split and distance == n_tensor - 1:
                    upper, lower = block_refs[-2], block_refs[-1]
                    left = jnp.where(owner == 0, upper[0], lower[0])
                else:
                    left = block_refs[distance][owner]
                product = lax.dot_general(
                    left,
                    cotangent_ref[index ^ distance],
                    (((0,), (0,)), ((), ())),
                    preferred_element_type=jnp.float32,
                )
                total = product if total is None else total + product
            return total

        sent_ref[...] = term(1 - core).astype(sent_ref.dtype)
        kept_ref[...] = term(core)

    depth = n_tensor * blocks[0].shape[1]
    return pl.pallas_call(
        kernel,
        out_shape=(
            jax.ShapeDtypeStruct((size, width), jnp.float32),
            jax.ShapeDtypeStruct((size, width), jnp.bfloat16),
        ),
        in_specs=whole_vmem(len(blocks) + 1),
        out_specs=whole_vmem(2),
        compiler_params=params(),
        cost_estimate=pl.CostEstimate(
            flops=4 * depth * size * width,
            bytes_accessed=4 * depth * size + 2 * depth * width + 6 * size * width,
            transcendentals=0,
        ),
        name="gradient_terms",
    )(*blocks, cotangents)


def norm_columns(states, gain, rows, line):
    length, width = states.shape
    ranges = chunk_ranges(rows)
    tile = 64

    def kernel(states_ref, gain_ref, *outs):
        kept, sent = outs[: len(ranges)], outs[len(ranges) :]
        core = own_core()
        total = jnp.zeros((tile, 1), jnp.float32)
        for block in range(2 * line):
            piece = states_ref[:, block * rows : (block + 1) * rows].astype(jnp.float32)
            total = total + jnp.sum(piece * piece, axis=1, keepdims=True)
        scale = lax.rsqrt(total / width + norm_eps)
        for flag in range(2):

            @pl.when(core == flag)
            def _():
                for block in range(2 * line):
                    group = kept if block % 2 == flag else sent
                    for (start, size), out in zip(ranges, group):
                        columns = slice(block * rows + start, block * rows + start + size)
                        piece = states_ref[:, columns].astype(jnp.float32)
                        out[block // 2] = (piece * scale * gain_ref[:, columns]).astype(out.dtype)

    shapes = [
        jax.ShapeDtypeStruct((line, length, size), jnp.bfloat16) for _, size in ranges
    ] * 2
    outs = pl.pallas_call(
        kernel,
        grid=(length // tile,),
        out_shape=shapes,
        in_specs=[
            pl.BlockSpec((tile, width), lambda i: (i, 0)),
            pl.BlockSpec((1, width), lambda i: (0, 0)),
        ],
        out_specs=[pl.BlockSpec((line, tile, size), lambda i: (0, i, 0)) for _, size in ranges] * 2,
        compiler_params=params(48),
        cost_estimate=pl.CostEstimate(
            flops=6 * length * width, bytes_accessed=4 * length * width, transcendentals=0
        ),
        name="norm_columns",
    )(states, gain.reshape(1, width))
    return outs[: len(ranges)], outs[len(ranges) :]


def accumulate(totals, kept, got, slots, last=False):
    _, length, depth = kept.shape
    width = slots[0][1].shape[1]
    count = len(slots)
    tile = min(256, length)
    owners = jnp.stack([jnp.asarray(owner, jnp.int32) for owner, _ in slots])
    weights = [weight for _, weight in slots]

    def kernel(owners_ref, *refs):
        weight_refs = refs[2 * count : 3 * count]
        for side, out_ref in zip((1, 0), reversed(refs[-2:])):
            result = None if totals is None else refs[3 * count + side][...]
            for slot in range(count):
                product = jnp.dot(
                    refs[side * count + slot][0],
                    weight_refs[slot][...],
                    preferred_element_type=jnp.float32,
                )
                result = product if result is None else result + product
            out_ref[...] = result.astype(out_ref.dtype)

    def state_spec(slot):
        return pl.BlockSpec((1, tile, depth), lambda i, chosen: (chosen[slot], i, 0))

    before = list(totals or [])
    row_spec = pl.BlockSpec((tile, width), lambda i, chosen: (i, 0))
    return pl.pallas_call(
        kernel,
        grid_spec=pltpu.PrefetchScalarGridSpec(
            num_scalar_prefetch=1,
            grid=(length // tile,),
            in_specs=[state_spec(slot) for slot in range(count)] * 2
            + [pl.BlockSpec((depth, width), lambda i, chosen: (0, 0))] * count
            + [row_spec] * len(before),
            out_specs=[row_spec] * 2,
        ),
        out_shape=[
            jax.ShapeDtypeStruct((length, width), jnp.float32),
            jax.ShapeDtypeStruct((length, width), jnp.bfloat16 if last else jnp.float32),
        ],
        compiler_params=params(24),
        cost_estimate=pl.CostEstimate(
            flops=4 * count * length * depth * width,
            bytes_accessed=2 * count * depth * (2 * length + width) + 16 * length * width,
            transcendentals=0,
        ),
        name="accumulate",
    )(owners, *([kept] * count), *([got] * count), *weights, *before)


def attention(kept, got, cosine_table, sine_table):
    length, width = kept.shape
    heads = width // HD - 2
    tile = min(128, length)

    def rope(u, cosine, sine):
        return u * cosine + pltpu.roll(u, HD // 2, 1) * sine

    def kernel(q_ref, q2_ref, k_ref, k2_ref, v_ref, v2_ref, cos_ref, sin_ref, out_ref, keys, values):
        @pl.when(pl.program_id(0) == 0)
        def _():
            key_rows = rope(k_ref[...] + k2_ref[...], cos_ref[...], sin_ref[...])
            keys[...] = key_rows.astype(jnp.bfloat16)
            values[...] = (v_ref[...] + v2_ref[...]).astype(jnp.bfloat16)

        for begin in range(0, length, tile):
            here, upto = slice(begin, begin + tile), begin + tile
            query = rope(q_ref[here] + q2_ref[here], cos_ref[here], sin_ref[here])
            query = (query * HD**-0.5).astype(jnp.bfloat16)
            scores = lax.dot_general(
                query,
                keys[:upto],
                (((1,), (1,)), ((), ())),
                preferred_element_type=jnp.float32,
            )
            row = lax.broadcasted_iota(jnp.int32, scores.shape, 0) + begin
            column = lax.broadcasted_iota(jnp.int32, scores.shape, 1)
            scores = jnp.where(row >= column, scores, -jnp.inf)
            raised = jnp.exp(scores - jnp.max(scores, axis=1, keepdims=True))
            weights = raised * (1.0 / jnp.sum(raised, axis=1, keepdims=True))
            out_ref[here] = jnp.dot(
                weights.astype(jnp.bfloat16), values[:upto], preferred_element_type=jnp.float32
            ).astype(jnp.bfloat16)

    def column(index):
        return pl.BlockSpec((length, HD), lambda h: (0, index))

    head = pl.BlockSpec((length, HD), lambda h: (0, h))
    return pl.pallas_call(
        kernel,
        grid=(heads,),
        out_shape=jax.ShapeDtypeStruct((length, heads * HD), jnp.bfloat16),
        in_specs=[head, head]
        + [column(heads)] * 2
        + [column(heads + 1)] * 2
        + [column(0)] * 2,
        out_specs=head,
        scratch_shapes=[pltpu.VMEM((length, HD), jnp.bfloat16)] * 2,
        compiler_params=params(),
        cost_estimate=pl.CostEstimate(
            flops=4 * heads * length * length * HD,
            bytes_accessed=9 * length * width,
            transcendentals=heads * length * length,
        ),
        name="attention",
    )(kept, got, kept, got, kept, got, cosine_table, sine_table)


def output_rows(mine, other, first_weight, rest_weight, n_tensor, full_width):
    kept, depth = mine.shape[1], mine.shape[2]
    tile = first_weight.shape[1]
    width = tile + rest_weight.shape[1]
    tiles = width // tile
    chosen = jnp.stack([lax.axis_index("tensor"), own_core()]).astype(jnp.int32)

    def kernel(chosen_ref, mine_ref, other_ref, first_ref, rest_ref, made_ref, sent_ref, left_ref):
        def product(weight_ref):
            total = jnp.dot(left_ref[...], weight_ref[...], preferred_element_type=jnp.float32)
            made_ref[...] = total[:kept].astype(made_ref.dtype)
            sent_ref[...] = total[kept:].astype(sent_ref.dtype)

        @pl.when(pl.program_id(0) == 0)
        def _():
            for distance in range(n_tensor):
                begin = pl.multiple_of((chosen_ref[0] ^ distance) * depth, depth)
                left_ref[:kept, pl.ds(begin, depth)] = mine_ref[distance]
                left_ref[kept:, pl.ds(begin, depth)] = other_ref[distance]
            product(first_ref)

        @pl.when(pl.program_id(0) > 0)
        def _():
            product(rest_ref)

    whole = pl.BlockSpec((n_tensor, kept, depth), lambda i, chosen: (0, 0, 0))
    return pl.pallas_call(
        kernel,
        grid_spec=pltpu.PrefetchScalarGridSpec(
            num_scalar_prefetch=1,
            grid=(tiles,),
            in_specs=[
                whole,
                whole,
                pl.BlockSpec((n_tensor * depth, tile), lambda i, chosen: (0, 0)),
                pl.BlockSpec(
                    (n_tensor * depth, tile), lambda i, chosen: (0, jnp.maximum(i - 1, 0))
                ),
            ],
            out_specs=[
                pl.BlockSpec((kept, tile), lambda i, chosen: (0, chosen[1] * tiles + i)),
                pl.BlockSpec((kept, tile), lambda i, chosen: (0, i)),
            ],
            scratch_shapes=[pltpu.VMEM((2 * kept, n_tensor * depth), jnp.bfloat16)],
        ),
        out_shape=[
            jax.ShapeDtypeStruct((kept, full_width), jnp.bfloat16),
            jax.ShapeDtypeStruct((kept, width), jnp.bfloat16),
        ],
        compiler_params=params(52),
        cost_estimate=pl.CostEstimate(
            flops=4 * kept * n_tensor * depth * width,
            bytes_accessed=2 * n_tensor * depth * width + 4 * kept * width,
            transcendentals=0,
        ),
        name="output_rows",
    )(chosen, mine, other, first_weight, rest_weight)


def fill_columns(made, block, index):
    kept, width = block.shape
    chosen = jnp.reshape(index, (1,)).astype(jnp.int32)

    def kernel(chosen_ref, made_ref, block_ref, out_ref):
        out_ref[...] = block_ref[...]

    return pl.pallas_call(
        kernel,
        grid_spec=pltpu.PrefetchScalarGridSpec(
            num_scalar_prefetch=1,
            grid=(1,),
            in_specs=[
                pl.BlockSpec(memory_space=pl.ANY),
                pl.BlockSpec((kept, width), lambda i, chosen: (0, 0)),
            ],
            out_specs=pl.BlockSpec((kept, width), lambda i, chosen: (0, chosen[0])),
        ),
        out_shape=jax.ShapeDtypeStruct(made.shape, made.dtype),
        input_output_aliases={1: 0},
        compiler_params=params(),
        name="fill_columns",
    )(chosen, made, block)


def body(
    train_states, qkv_cotangent, w_master, moment_one, moment_two, prompt_states, norm_gain, w_out
):
    n_dp = lax.axis_size("dp")
    n_tensor = lax.axis_size("tensor")
    line = n_dp // 2
    tensor_index = lax.axis_index("tensor")
    core, place = own_core(), own_place()
    siblings = [(i, i ^ 1) for i in range(n_dp)]
    rows, slice_width = w_master.shape
    tokens, width = train_states.shape
    length = prompt_states.shape[0]
    query_width = slice_width - 2 * HD
    ranges = chunk_ranges(rows)

    packed = pack_columns(train_states, rows, line, tokens // n_tensor)
    packed, qkv_cotangent = lax.optimization_barrier((packed, qkv_cotangent))
    pieces = [packed[0]] + [
        lax.ppermute(
            packed[distance], "dp", line_pairs([(i, i ^ distance) for i in range(line)])
        )
        for distance in range(1, line)
    ]

    def behind_columns(up, down):
        nonlocal pieces
        up, down, pieces = lax.optimization_barrier((up, down, pieces))
        return up, down

    arrivals = line_steps(qkv_cotangent, place, line, {2: behind_columns})
    cotangents = place_cotangents(arrivals, line, n_tensor)
    stacked = list(stack_pieces(pieces, [(start, start + size) for start, size in ranges]))

    def behind_cotangents(up, down):
        return lax.optimization_barrier((up, down, arrivals[0][2], arrivals[1][2]))[:2]

    spread = [plane_gather(stacked[0], n_tensor, behind_cotangents)]
    stacked[1], spread[0] = lax.optimization_barrier((stacked[1], spread[0]))
    spread.append(plane_gather(stacked[1], n_tensor))

    summed_width = width // SUMMED_SHARE
    core_width = (width - summed_width) // 2
    early_width = core_width // 4
    begin = core * core_width
    w_early = lax.dynamic_slice(w_out, (0, begin), (w_out.shape[0], early_width))
    w_rest = lax.dynamic_slice(
        w_out, (0, begin + early_width), (w_out.shape[0], core_width - early_width)
    )
    early_weight = lax.all_gather(w_early, "tensor", axis=0, tiled=True)
    w_rest, spread[1] = lax.optimization_barrier((w_rest, spread[1]))
    rest_weight = lax.all_gather(w_rest, "tensor", axis=0, tiled=True)

    cosine_table, sine_table = rope_tables(length, HD)
    updates, gathers = [], []
    for part, (start, size) in enumerate(ranges):
        if part:
            low, high = gathers[0]
            low[1], high[1], spread[part] = lax.optimization_barrier(
                (low[1], high[1], spread[part])
            )
        kept, sent = gradient_terms(spread[part], cotangents, n_tensor)
        gradient = kept + lax.ppermute(sent, "dp", siblings).astype(jnp.float32)

        here = slice(start, start + size)
        moment_new = beta_one * moment_one[here] + (1.0 - beta_one) * gradient
        second_new = beta_two * moment_two[here] + (1.0 - beta_two) * gradient * gradient
        update = moment_new / bias_one / (jnp.sqrt(second_new / bias_two) + adam_eps)
        updates.append(update)
        owned_weight = (w_master[here] - learn_rate * update).astype(jnp.bfloat16)
        if part:
            owned_weight, prompt_states = lax.optimization_barrier((owned_weight, prompt_states))
            update_dir = jnp.concatenate(updates, axis=0)
            kept_states, sent_states = norm_columns(prompt_states, norm_gain, rows, line)
            got_states = [lax.ppermute(states, "dp", siblings) for states in sent_states]

        def accumulate_earlier(up, down):
            nonlocal totals, update_dir, cosine_table, sine_table
            totals = accumulate(
                None, kept_states[0], got_states[0], line_slots(gathers[0], place, line)
            )
            up, down, totals, update_dir, cosine_table, sine_table = lax.optimization_barrier(
                (up, down, totals, update_dir, cosine_table, sine_table)
            )
            return up, down

        ahead = {line - 1: accumulate_earlier} if part else {}
        gathers.append(line_steps(owned_weight, place, line, ahead))
    slots = line_slots(gathers[1], place, line)
    totals = accumulate(totals, kept_states[1], got_states[1], slots[:-1])
    totals = accumulate(totals, kept_states[1], got_states[1], slots[-1:], True)
    attended = attention(
        totals[0], lax.ppermute(totals[1], "dp", siblings), cosine_table, sine_table
    )

    kept_rows = length // n_tensor
    heads = []
    for distance in range(n_tensor):
        target = tensor_index ^ distance
        block = lax.dynamic_slice(attended, (target * kept_rows, 0), (kept_rows, query_width))
        if distance:
            block = lax.ppermute(block, "tensor", [(j, j ^ distance) for j in range(n_tensor)])
        heads.append(block)
    (mine,) = stack_pieces([head[None] for head in heads], [(0, query_width)])
    mine = mine.reshape(n_tensor, kept_rows, query_width)
    other = lax.ppermute(mine, "dp", siblings)

    part = jnp.dot(
        attended, w_out[:, width - summed_width :], preferred_element_type=jnp.float32
    ).astype(jnp.bfloat16)
    part_sum = lax.psum_scatter(part, "tensor", scatter_dimension=0, tiled=True)
    made, sent_rows = output_rows(mine, other, early_weight, rest_weight, n_tensor, width)
    swapped = lax.ppermute(sent_rows, "dp", siblings)
    summed = fill_columns(made, swapped, 1 - core)
    summed = fill_columns(summed, part_sum, jnp.int32(SUMMED_SHARE - 1))
    return (update_dir, summed)


def solution(mesh):
    placed = (
        P("dp", None),
        P("dp", "tensor"),
        P("dp", "tensor"),
        P("dp", "tensor"),
        P("dp", "tensor"),
        P("dp", None),
        P(),
        P("tensor", None),
    )
    return jax.shard_map(
        body,
        mesh=mesh,
        in_specs=placed,
        out_specs=(P("dp", "tensor"), P(("dp", "tensor"), None)),
        check_vma=False,
    )
```

```python
import functools

import jax
import jax.numpy as jnp
from jax import lax
from jax.experimental import pallas as pl
from jax.experimental.pallas import tpu as pltpu
from jax.sharding import PartitionSpec as P

HD = 128


beta_one = 0.9
beta_two = 0.95
bias_one = 1.0 - 0.9**8
bias_two = 1.0 - 0.95**8
learn_rate = 0.002
adam_eps = 1e-08
norm_eps = 1e-05
rope_base = 500000.0

CHUNK_QUARTERS = (1, 3)
MIB = 1024 * 1024
SUMMED_SHARE = 8


def rope_tables(length, head_size):
    half_width = head_size // 2
    exponent = jnp.arange(half_width, dtype=jnp.float32) * (2.0 / head_size)
    inverse = jnp.power(jnp.float32(rope_base), -exponent)
    position = jnp.arange(length, dtype=jnp.float32)
    angles = position[:, None] * inverse[None, :]
    cosine_table = jnp.concatenate([jnp.cos(angles), jnp.cos(angles)], axis=1)
    sine_table = jnp.concatenate([-jnp.sin(angles), jnp.sin(angles)], axis=1)
    return (cosine_table, sine_table)


def chunk_ranges(rows):
    quarter, start, ranges = rows // 4, 0, []
    for quarters in CHUNK_QUARTERS:
        ranges.append((start, quarters * quarter))
        start += quarters * quarter
    return ranges


def params(mib=16):
    return pltpu.CompilerParams(vmem_limit_bytes=mib * MIB)


def whole_vmem(count):
    return [pl.BlockSpec(memory_space=pltpu.VMEM)] * count


def own_core():
    return lax.rem(lax.axis_index("dp"), 2)


def own_place():
    return lax.div(lax.axis_index("dp"), 2)


def pack_columns(train_states, rows, line, quarter):
    def kernel(index_ref, train_ref, *outs):
        place = own_place()
        for distance in range(line):
            for owner in range(2):
                column = pl.multiple_of(((place ^ distance) * 2 + owner) * rows, 128)
                outs[distance][owner] = train_ref[:, pl.ds(column, rows)]

    shapes = [jax.ShapeDtypeStruct((2, quarter, rows), train_states.dtype)] * line
    index = jnp.reshape(lax.axis_index("tensor"), (1,)).astype(jnp.int32)
    return pl.pallas_call(
        kernel,
        grid_spec=pltpu.PrefetchScalarGridSpec(
            num_scalar_prefetch=1,
            grid=(1,),
            in_specs=[
                pl.BlockSpec((quarter, train_states.shape[1]), lambda i, chosen: (chosen[0], 0))
            ],
            out_specs=[pl.BlockSpec(s.shape, lambda i, chosen: (0, 0, 0)) for s in shapes],
        ),
        out_shape=shapes,
        compiler_params=params(56),
        name="pack_columns",
    )(index, train_states)


def stack_pieces(pieces, cuts):
    outer, height, _ = pieces[0].shape
    count = len(pieces)

    def kernel(*refs):
        for (start, stop), out_ref in zip(cuts, refs[count:]):
            for i in range(count):
                out_ref[:, i * height : (i + 1) * height] = refs[i][:, :, start:stop]

    return pl.pallas_call(
        kernel,
        out_shape=[
            jax.ShapeDtypeStruct((outer, count * height, stop - start), pieces[0].dtype)
            for start, stop in cuts
        ],
        in_specs=whole_vmem(count),
        out_specs=whole_vmem(len(cuts)),
        compiler_params=params(),
        name="stack_pieces",
    )(*pieces)


def line_pairs(places):
    return [(2 * a + core, 2 * b + core) for a, b in places for core in range(2)]


def line_steps(block, place, count, ahead=None):
    ahead = ahead or {}
    low, high = [block], [block]
    for step in range(1, count - 1):
        up, down = low[-1], high[-1]
        if step in ahead:
            up, down = ahead[step](up, down)
        low.append(
            lax.ppermute(up, "dp", line_pairs([(i, i + 1) for i in range(step - 1, count - 1)]))
        )
        high.append(
            lax.ppermute(down, "dp", line_pairs([(i, i - 1) for i in range(1, count - step + 1)]))
        )
    up, down = low[-1], high[-1]
    if count - 1 in ahead:
        up, down = ahead[count - 1](up, down)
    last = lax.ppermute(
        jnp.where(place == count - 2, up, down),
        "dp",
        line_pairs([(count - 2, count - 1), (1, 0)]),
    )
    return low + [last], high + [last]


def line_choice(step, place, count):
    is_low, is_high = place >= step, place <= count - 1 - step
    spare = count - step
    return [
        (is_low, 0, step, place - step),
        (jnp.logical_and(jnp.logical_not(is_low), is_high), 1, step, place + step),
        (
            jnp.logical_and(jnp.logical_not(is_low), jnp.logical_not(is_high)),
            1,
            spare,
            place + spare,
        ),
    ][: 2 if 2 * step <= count else 3]


def line_slots(arrivals, place, count):
    slots = [(place, arrivals[0][0])]
    for step in range(1, count):
        choices = line_choice(step, place, count)
        _, side, entry, owner = choices[-1]
        block = arrivals[side][entry]
        for holds, side, entry, other in reversed(choices[:-1]):
            if arrivals[side][entry] is not block:
                block = jnp.where(holds, arrivals[side][entry], block)
            owner = jnp.where(holds, other, owner)
        slots.append((owner, block))
    return slots


def place_cotangents(arrivals, line, n_tensor):
    tokens, width = arrivals[0][0].shape
    quarter = tokens // n_tensor
    low = [a.reshape(n_tensor, quarter, width) for a in arrivals[0]]
    high = [a.reshape(n_tensor, quarter, width) for a in arrivals[1][1:-1]]

    def kernel(*refs):
        low_refs = refs[: len(low)]
        high_refs = [low_refs[0]] + list(refs[len(low) : len(low) + len(high)]) + [low_refs[-1]]
        out_ref = refs[-1]
        place = own_place()

        def put(owner, source):
            begin = pl.multiple_of((owner ^ place) * quarter, quarter)
            out_ref[:, pl.ds(begin, quarter)] = source[...]

        put(place, low_refs[0])
        for step in range(1, line):
            for holds, side, entry, owner in line_choice(step, place, line):
                pl.when(holds)(functools.partial(put, owner, (low_refs, high_refs)[side][entry]))

    return pl.pallas_call(
        kernel,
        out_shape=jax.ShapeDtypeStruct((n_tensor, line * quarter, width), low[0].dtype),
        in_specs=whole_vmem(len(low) + len(high)),
        out_specs=pl.BlockSpec(memory_space=pltpu.VMEM),
        compiler_params=params(),
        name="place_cotangents",
    )(*low, *high)


def plane_gather(block, count, ahead=None):
    if count != 4:
        gathered = lax.all_gather(block, "tensor", axis=0)
        own = lax.axis_index("tensor")
        return [
            lax.dynamic_index_in_dim(gathered, own ^ b, 0, keepdims=False) for b in range(count)
        ]
    by_one = [(j, j ^ 1) for j in range(count)]
    by_two = [(j, j ^ 2) for j in range(count)]
    one = lax.ppermute(block, "tensor", by_one)
    two = lax.ppermute(block, "tensor", by_two)
    up, down = one[:1], two[1:]
    if ahead is not None:
        up, down = ahead(up, down)
    upper = lax.ppermute(up, "tensor", by_two)
    lower = lax.ppermute(down, "tensor", by_one)
    return [block, one, two, upper, lower]


def gradient_terms(blocks, cotangents, n_tensor):
    size = blocks[0].shape[2]
    width = cotangents.shape[2]
    split = len(blocks) > n_tensor

    def kernel(*refs):
        block_refs, cotangent_ref = refs[: len(blocks)], refs[len(blocks)]
        kept_ref, sent_ref = refs[len(blocks) + 1 :]
        index, core = lax.axis_index("tensor"), own_core()

        def term(owner):
            total = None
            for distance in range(n_tensor):
                if split and distance == n_tensor - 1:
                    upper, lower = block_refs[-2], block_refs[-1]
                    left = jnp.where(owner == 0, upper[0], lower[0])
                else:
                    left = block_refs[distance][owner]
                product = lax.dot_general(
                    left,
                    cotangent_ref[index ^ distance],
                    (((0,), (0,)), ((), ())),
                    preferred_element_type=jnp.float32,
                )
                total = product if total is None else total + product
            return total

        sent_ref[...] = term(1 - core).astype(sent_ref.dtype)
        kept_ref[...] = term(core)

    depth = n_tensor * blocks[0].shape[1]
    return pl.pallas_call(
        kernel,
        out_shape=(
            jax.ShapeDtypeStruct((size, width), jnp.float32),
            jax.ShapeDtypeStruct((size, width), jnp.bfloat16),
        ),
        in_specs=whole_vmem(len(blocks) + 1),
        out_specs=whole_vmem(2),
        compiler_params=params(),
        cost_estimate=pl.CostEstimate(
            flops=4 * depth * size * width,
            bytes_accessed=4 * depth * size + 2 * depth * width + 6 * size * width,
            transcendentals=0,
        ),
        name="gradient_terms",
    )(*blocks, cotangents)


def norm_columns(states, gain, rows, line):
    length, width = states.shape
    ranges = chunk_ranges(rows)
    tile = 64

    def kernel(states_ref, gain_ref, *outs):
        kept, sent = outs[: len(ranges)], outs[len(ranges) :]
        core = own_core()
        total = jnp.zeros((tile, 1), jnp.float32)
        for block in range(2 * line):
            piece = states_ref[:, block * rows : (block + 1) * rows].astype(jnp.float32)
            total = total + jnp.sum(piece * piece, axis=1, keepdims=True)
        scale = lax.rsqrt(total / width + norm_eps)
        for flag in range(2):

            @pl.when(core == flag)
            def _():
                for block in range(2 * line):
                    group = kept if block % 2 == flag else sent
                    for (start, size), out in zip(ranges, group):
                        columns = slice(block * rows + start, block * rows + start + size)
                        piece = states_ref[:, columns].astype(jnp.float32)
                        out[block // 2] = (piece * scale * gain_ref[:, columns]).astype(out.dtype)

    shapes = [
        jax.ShapeDtypeStruct((line, length, size), jnp.bfloat16) for _, size in ranges
    ] * 2
    outs = pl.pallas_call(
        kernel,
        grid=(length // tile,),
        out_shape=shapes,
        in_specs=[
            pl.BlockSpec((tile, width), lambda i: (i, 0)),
            pl.BlockSpec((1, width), lambda i: (0, 0)),
        ],
        out_specs=[pl.BlockSpec((line, tile, size), lambda i: (0, i, 0)) for _, size in ranges] * 2,
        compiler_params=params(),
        cost_estimate=pl.CostEstimate(
            flops=6 * length * width, bytes_accessed=4 * length * width, transcendentals=0
        ),
        name="norm_columns",
    )(states, gain.reshape(1, width))
    return outs[: len(ranges)], outs[len(ranges) :]


def accumulate(totals, kept, got, slots, last=False):
    _, length, depth = kept.shape
    width = slots[0][1].shape[1]
    count = len(slots)
    tile = min(256, length)
    owners = jnp.stack([jnp.asarray(owner, jnp.int32) for owner, _ in slots])
    weights = [weight for _, weight in slots]

    def kernel(owners_ref, *refs):
        weight_refs = refs[2 * count : 3 * count]
        for side, out_ref in zip((1, 0), reversed(refs[-2:])):
            result = None if totals is None else refs[3 * count + side][...]
            for slot in range(count):
                product = jnp.dot(
                    refs[side * count + slot][0],
                    weight_refs[slot][...],
                    preferred_element_type=jnp.float32,
                )
                result = product if result is None else result + product
            out_ref[...] = result.astype(out_ref.dtype)

    def state_spec(slot):
        return pl.BlockSpec((1, tile, depth), lambda i, chosen: (chosen[slot], i, 0))

    before = list(totals or [])
    row_spec = pl.BlockSpec((tile, width), lambda i, chosen: (i, 0))
    return pl.pallas_call(
        kernel,
        grid_spec=pltpu.PrefetchScalarGridSpec(
            num_scalar_prefetch=1,
            grid=(length // tile,),
            in_specs=[state_spec(slot) for slot in range(count)] * 2
            + [pl.BlockSpec((depth, width), lambda i, chosen: (0, 0))] * count
            + [row_spec] * len(before),
            out_specs=[row_spec] * 2,
        ),
        out_shape=[
            jax.ShapeDtypeStruct((length, width), jnp.float32),
            jax.ShapeDtypeStruct((length, width), jnp.bfloat16 if last else jnp.float32),
        ],
        compiler_params=params(24),
        cost_estimate=pl.CostEstimate(
            flops=4 * count * length * depth * width,
            bytes_accessed=2 * count * depth * (2 * length + width) + 16 * length * width,
            transcendentals=0,
        ),
        name="accumulate",
    )(owners, *([kept] * count), *([got] * count), *weights, *before)


def attention(kept, got, cosine_table, sine_table):
    length, width = kept.shape
    heads = width // HD - 2
    tile = min(128, length)

    def rope(u, cosine, sine):
        return u * cosine + pltpu.roll(u, HD // 2, 1) * sine

    def kernel(q_ref, q2_ref, k_ref, k2_ref, v_ref, v2_ref, cos_ref, sin_ref, out_ref, keys, values):
        @pl.when(pl.program_id(0) == 0)
        def _():
            key_rows = rope(k_ref[...] + k2_ref[...], cos_ref[...], sin_ref[...])
            keys[...] = key_rows.astype(jnp.bfloat16)
            values[...] = (v_ref[...] + v2_ref[...]).astype(jnp.bfloat16)

        for begin in range(0, length, tile):
            here, upto = slice(begin, begin + tile), begin + tile
            query = rope(q_ref[here] + q2_ref[here], cos_ref[here], sin_ref[here])
            query = (query * HD**-0.5).astype(jnp.bfloat16)
            scores = lax.dot_general(
                query,
                keys[:upto],
                (((1,), (1,)), ((), ())),
                preferred_element_type=jnp.float32,
            )
            row = lax.broadcasted_iota(jnp.int32, scores.shape, 0) + begin
            column = lax.broadcasted_iota(jnp.int32, scores.shape, 1)
            scores = jnp.where(row >= column, scores, -jnp.inf)
            raised = jnp.exp(scores - jnp.max(scores, axis=1, keepdims=True))
            weights = raised * (1.0 / jnp.sum(raised, axis=1, keepdims=True))
            out_ref[here] = jnp.dot(
                weights.astype(jnp.bfloat16), values[:upto], preferred_element_type=jnp.float32
            ).astype(jnp.bfloat16)

    def column(index):
        return pl.BlockSpec((length, HD), lambda h: (0, index))

    head = pl.BlockSpec((length, HD), lambda h: (0, h))
    return pl.pallas_call(
        kernel,
        grid=(heads,),
        out_shape=jax.ShapeDtypeStruct((length, heads * HD), jnp.bfloat16),
        in_specs=[head, head]
        + [column(heads)] * 2
        + [column(heads + 1)] * 2
        + [column(0)] * 2,
        out_specs=head,
        scratch_shapes=[pltpu.VMEM((length, HD), jnp.bfloat16)] * 2,
        compiler_params=params(),
        cost_estimate=pl.CostEstimate(
            flops=4 * heads * length * length * HD,
            bytes_accessed=9 * length * width,
            transcendentals=heads * length * length,
        ),
        name="attention",
    )(kept, got, kept, got, kept, got, cosine_table, sine_table)


def output_rows(mine, other, first_weight, rest_weight, n_tensor, full_width):
    kept, depth = mine.shape[1], mine.shape[2]
    tile = first_weight.shape[1]
    width = tile + rest_weight.shape[1]
    tiles = width // tile
    chosen = jnp.stack([lax.axis_index("tensor"), own_core()]).astype(jnp.int32)

    def kernel(chosen_ref, mine_ref, other_ref, first_ref, rest_ref, made_ref, sent_ref, left_ref):
        def product(weight_ref):
            total = jnp.dot(left_ref[...], weight_ref[...], preferred_element_type=jnp.float32)
            made_ref[...] = total[:kept].astype(made_ref.dtype)
            sent_ref[...] = total[kept:].astype(sent_ref.dtype)

        @pl.when(pl.program_id(0) == 0)
        def _():
            for distance in range(n_tensor):
                begin = pl.multiple_of((chosen_ref[0] ^ distance) * depth, depth)
                left_ref[:kept, pl.ds(begin, depth)] = mine_ref[distance]
                left_ref[kept:, pl.ds(begin, depth)] = other_ref[distance]
            product(first_ref)

        @pl.when(pl.program_id(0) > 0)
        def _():
            product(rest_ref)

    whole = pl.BlockSpec((n_tensor, kept, depth), lambda i, chosen: (0, 0, 0))
    return pl.pallas_call(
        kernel,
        grid_spec=pltpu.PrefetchScalarGridSpec(
            num_scalar_prefetch=1,
            grid=(tiles,),
            in_specs=[
                whole,
                whole,
                pl.BlockSpec((n_tensor * depth, tile), lambda i, chosen: (0, 0)),
                pl.BlockSpec(
                    (n_tensor * depth, tile), lambda i, chosen: (0, jnp.maximum(i - 1, 0))
                ),
            ],
            out_specs=[
                pl.BlockSpec((kept, tile), lambda i, chosen: (0, chosen[1] * tiles + i)),
                pl.BlockSpec((kept, tile), lambda i, chosen: (0, i)),
            ],
            scratch_shapes=[pltpu.VMEM((2 * kept, n_tensor * depth), jnp.bfloat16)],
        ),
        out_shape=[
            jax.ShapeDtypeStruct((kept, full_width), jnp.bfloat16),
            jax.ShapeDtypeStruct((kept, width), jnp.bfloat16),
        ],
        compiler_params=params(52),
        cost_estimate=pl.CostEstimate(
            flops=4 * kept * n_tensor * depth * width,
            bytes_accessed=2 * n_tensor * depth * width + 4 * kept * width,
            transcendentals=0,
        ),
        name="output_rows",
    )(chosen, mine, other, first_weight, rest_weight)


def fill_columns(made, block, index):
    kept, width = block.shape
    chosen = jnp.reshape(index, (1,)).astype(jnp.int32)

    def kernel(chosen_ref, made_ref, block_ref, out_ref):
        out_ref[...] = block_ref[...]

    return pl.pallas_call(
        kernel,
        grid_spec=pltpu.PrefetchScalarGridSpec(
            num_scalar_prefetch=1,
            grid=(1,),
            in_specs=[
                pl.BlockSpec(memory_space=pl.ANY),
                pl.BlockSpec((kept, width), lambda i, chosen: (0, 0)),
            ],
            out_specs=pl.BlockSpec((kept, width), lambda i, chosen: (0, chosen[0])),
        ),
        out_shape=jax.ShapeDtypeStruct(made.shape, made.dtype),
        input_output_aliases={1: 0},
        compiler_params=params(),
        name="fill_columns",
    )(chosen, made, block)


def body(
    train_states, qkv_cotangent, w_master, moment_one, moment_two, prompt_states, norm_gain, w_out
):
    n_dp = lax.axis_size("dp")
    n_tensor = lax.axis_size("tensor")
    line = n_dp // 2
    tensor_index = lax.axis_index("tensor")
    core, place = own_core(), own_place()
    siblings = [(i, i ^ 1) for i in range(n_dp)]
    rows, slice_width = w_master.shape
    tokens, width = train_states.shape
    length = prompt_states.shape[0]
    query_width = slice_width - 2 * HD
    ranges = chunk_ranges(rows)

    packed = pack_columns(train_states, rows, line, tokens // n_tensor)
    packed, qkv_cotangent = lax.optimization_barrier((packed, qkv_cotangent))
    pieces = [packed[0]] + [
        lax.ppermute(
            packed[distance], "dp", line_pairs([(i, i ^ distance) for i in range(line)])
        )
        for distance in range(1, line)
    ]

    def behind_columns(up, down):
        nonlocal pieces
        up, down, pieces = lax.optimization_barrier((up, down, pieces))
        return up, down

    arrivals = line_steps(qkv_cotangent, place, line, {2: behind_columns})
    cotangents = place_cotangents(arrivals, line, n_tensor)
    stacked = list(stack_pieces(pieces, [(start, start + size) for start, size in ranges]))

    def behind_cotangents(up, down):
        return lax.optimization_barrier((up, down, arrivals[0][2], arrivals[1][2]))[:2]

    summed_width = width // SUMMED_SHARE
    core_width = (width - summed_width) // 2
    early_width = core_width // (SUMMED_SHARE - 1)
    begin = core * core_width
    w_early = lax.dynamic_slice(w_out, (0, begin), (w_out.shape[0], early_width))
    w_rest = lax.dynamic_slice(
        w_out, (0, begin + early_width), (w_out.shape[0], core_width - early_width)
    )
    early_weight = lax.all_gather(w_early, "tensor", axis=0, tiled=True)

    cosine_table, sine_table = rope_tables(length, HD)
    updates, gathers = [], []
    owned_weight, totals = None, None
    for part, (start, size) in enumerate(ranges):
        if part == 0:
            spread = plane_gather(stacked[0], n_tensor, behind_cotangents)
        else:
            block = lax.optimization_barrier((stacked[part], spread, arrivals[0][-1]))[0]
            low, high = gathers[0]

            def behind_weight(up, down):
                return lax.optimization_barrier((up, down, low[1], high[1]))[:2]

            spread = plane_gather(block, n_tensor, behind_weight)
            w_rest, spread, low[2], high[2] = lax.optimization_barrier(
                (w_rest, spread, low[2], high[2])
            )
            rest_weight = lax.all_gather(w_rest, "tensor", axis=0, tiled=True)
        kept, sent = gradient_terms(spread, cotangents, n_tensor)
        gradient = kept + lax.ppermute(sent, "dp", siblings).astype(jnp.float32)

        here = slice(start, start + size)
        moment_new = beta_one * moment_one[here] + (1.0 - beta_one) * gradient
        second_new = beta_two * moment_two[here] + (1.0 - beta_two) * gradient * gradient
        update = moment_new / bias_one / (jnp.sqrt(second_new / bias_two) + adam_eps)
        updates.append(update)
        owned_weight = (w_master[here] - learn_rate * update).astype(jnp.bfloat16)
        if part == 0:
            gathers.append(line_steps(owned_weight, place, line))
            continue

        low, high = gathers[0]
        owned_weight, prompt_states, low[-1] = lax.optimization_barrier(
            (owned_weight, prompt_states, low[-1])
        )
        high[-1] = low[-1]
        kept_states, sent_states = norm_columns(prompt_states, norm_gain, rows, line)
        got_states = [lax.ppermute(states, "dp", siblings) for states in sent_states]
        update_dir = jnp.concatenate(updates, axis=0)
        first_slots = line_slots(gathers[0], place, line)

        def accumulate_earlier(up, down):
            nonlocal totals, update_dir, cosine_table, sine_table
            totals = accumulate(None, kept_states[0], got_states[0], first_slots)
            own_slot = [(place, owned_weight)]
            totals = accumulate(totals, kept_states[1], got_states[1], own_slot)
            up, down, totals, update_dir, cosine_table, sine_table = lax.optimization_barrier(
                (up, down, totals, update_dir, cosine_table, sine_table)
            )
            return up, down

        gathers.append(line_steps(owned_weight, place, line, {line - 1: accumulate_earlier}))
    slots = line_slots(gathers[1], place, line)[1:]
    totals = accumulate(totals, kept_states[1], got_states[1], slots, True)
    attended = attention(
        totals[0], lax.ppermute(totals[1], "dp", siblings), cosine_table, sine_table
    )

    kept_rows = length // n_tensor
    heads = []
    for distance in range(n_tensor):
        target = tensor_index ^ distance
        block = lax.dynamic_slice(attended, (target * kept_rows, 0), (kept_rows, query_width))
        if distance:
            block = lax.ppermute(block, "tensor", [(j, j ^ distance) for j in range(n_tensor)])
        heads.append(block)
    (mine,) = stack_pieces([head[None] for head in heads], [(0, query_width)])
    mine = mine.reshape(n_tensor, kept_rows, query_width)
    other = lax.ppermute(mine, "dp", siblings)

    part = jnp.dot(
        attended, w_out[:, width - summed_width :], preferred_element_type=jnp.float32
    ).astype(jnp.bfloat16)
    part_sum = lax.psum_scatter(part, "tensor", scatter_dimension=0, tiled=True)
    made, sent_rows = output_rows(mine, other, early_weight, rest_weight, n_tensor, width)
    swapped = lax.ppermute(sent_rows, "dp", siblings)
    summed = fill_columns(made, swapped, 1 - core)
    summed = fill_columns(summed, part_sum, jnp.int32(SUMMED_SHARE - 1))
    return (update_dir, summed)


def solution(mesh):
    placed = (
        P("dp", None),
        P("dp", "tensor"),
        P("dp", "tensor"),
        P("dp", "tensor"),
        P("dp", "tensor"),
        P("dp", None),
        P(),
        P("tensor", None),
    )
    return jax.shard_map(
        body,
        mesh=mesh,
        in_specs=placed,
        out_specs=(P("dp", "tensor"), P(("dp", "tensor"), None)),
        check_vma=False,
    )
```

```python
import functools

import jax
import jax.numpy as jnp
from jax import lax
from jax.experimental import pallas as pl
from jax.experimental.pallas import tpu as pltpu
from jax.sharding import PartitionSpec as P

HD = 128


beta_one = 0.9
beta_two = 0.95
bias_one = 1.0 - 0.9**8
bias_two = 1.0 - 0.95**8
learn_rate = 0.002
adam_eps = 1e-08
norm_eps = 1e-05
rope_base = 500000.0

CHUNK_QUARTERS = (2, 2)
MIB = 1024 * 1024
EARLY_SHARE = 8


def rope_tables(length, head_size):
    half_width = head_size // 2
    exponent = jnp.arange(half_width, dtype=jnp.float32) * (2.0 / head_size)
    inverse = jnp.power(jnp.float32(rope_base), -exponent)
    position = jnp.arange(length, dtype=jnp.float32)
    angles = position[:, None] * inverse[None, :]
    cosine_table = jnp.concatenate([jnp.cos(angles), jnp.cos(angles)], axis=1)
    sine_table = jnp.concatenate([-jnp.sin(angles), jnp.sin(angles)], axis=1)
    return (cosine_table, sine_table)


def chunk_ranges(rows):
    quarter, start, ranges = rows // 4, 0, []
    for quarters in CHUNK_QUARTERS:
        ranges.append((start, quarters * quarter))
        start += quarters * quarter
    return ranges


def params(mib=16):
    return pltpu.CompilerParams(vmem_limit_bytes=mib * MIB)


def whole_vmem(count):
    return [pl.BlockSpec(memory_space=pltpu.VMEM)] * count


def own_core():
    return lax.rem(lax.axis_index("dp"), 2)


def own_place():
    return lax.div(lax.axis_index("dp"), 2)


def pack_columns(train_states, rows, line, quarter):
    def kernel(index_ref, train_ref, *outs):
        place = own_place()
        for distance in range(line):
            for owner in range(2):
                column = pl.multiple_of(((place ^ distance) * 2 + owner) * rows, 128)
                outs[distance][owner] = train_ref[:, pl.ds(column, rows)]

    shapes = [jax.ShapeDtypeStruct((2, quarter, rows), train_states.dtype)] * line
    index = jnp.reshape(lax.axis_index("tensor"), (1,)).astype(jnp.int32)
    return pl.pallas_call(
        kernel,
        grid_spec=pltpu.PrefetchScalarGridSpec(
            num_scalar_prefetch=1,
            grid=(1,),
            in_specs=[
                pl.BlockSpec((quarter, train_states.shape[1]), lambda i, chosen: (chosen[0], 0))
            ],
            out_specs=[pl.BlockSpec(s.shape, lambda i, chosen: (0, 0, 0)) for s in shapes],
        ),
        out_shape=shapes,
        compiler_params=params(56),
        name="pack_columns",
    )(index, train_states)


def stack_pieces(pieces, cuts):
    outer, height, _ = pieces[0].shape
    count = len(pieces)

    def kernel(*refs):
        for (start, stop), out_ref in zip(cuts, refs[count:]):
            for i in range(count):
                out_ref[:, i * height : (i + 1) * height] = refs[i][:, :, start:stop]

    return pl.pallas_call(
        kernel,
        out_shape=[
            jax.ShapeDtypeStruct((outer, count * height, stop - start), pieces[0].dtype)
            for start, stop in cuts
        ],
        in_specs=whole_vmem(count),
        out_specs=whole_vmem(len(cuts)),
        compiler_params=params(),
        name="stack_pieces",
    )(*pieces)


def line_pairs(places):
    return [(2 * a + core, 2 * b + core) for a, b in places for core in range(2)]


def tie(arrays, *others):
    return lax.optimization_barrier((tuple(arrays), others))[0]


class LineGather:
    def __init__(self, block, place, count):
        self.place, self.count = place, count
        self.low, self.high = [block], [block]

    def hop(self, *behind):
        step, count = len(self.low), self.count
        up, down = self.low[-1], self.high[-1]
        if behind:
            up, down = tie((up, down), *behind)
        if step < count - 1:
            right = line_pairs([(i, i + 1) for i in range(step - 1, count - 1)])
            left = line_pairs([(i, i - 1) for i in range(1, count - step + 1)])
            self.low.append(lax.ppermute(up, "dp", right))
            self.high.append(lax.ppermute(down, "dp", left))
            return
        last = lax.ppermute(
            jnp.where(self.place == count - 2, up, down),
            "dp",
            line_pairs([(count - 2, count - 1), (1, 0)]),
        )
        self.low.append(last)
        self.high.append(last)

    def arrived(self):
        return self.low[-1], self.high[-1]

    def slot(self, step):
        if step == 0:
            return self.place, self.low[0]
        sides = (self.low, self.high)
        choices = line_choice(step, self.place, self.count)
        _, side, entry, owner = choices[-1]
        block = sides[side][entry]
        for holds, side, entry, other in reversed(choices[:-1]):
            if sides[side][entry] is not block:
                block = jnp.where(holds, sides[side][entry], block)
            owner = jnp.where(holds, other, owner)
        return owner, block


def line_choice(step, place, count):
    is_low, is_high = place >= step, place <= count - 1 - step
    spare = count - step
    return [
        (is_low, 0, step, place - step),
        (jnp.logical_and(jnp.logical_not(is_low), is_high), 1, step, place + step),
        (
            jnp.logical_and(jnp.logical_not(is_low), jnp.logical_not(is_high)),
            1,
            spare,
            place + spare,
        ),
    ][: 2 if 2 * step <= count else 3]


def place_cotangents(arrivals, line, n_tensor):
    tokens, width = arrivals[0][0].shape
    quarter = tokens // n_tensor
    low = [a.reshape(n_tensor, quarter, width) for a in arrivals[0]]
    high = [a.reshape(n_tensor, quarter, width) for a in arrivals[1][1:-1]]

    def kernel(*refs):
        low_refs = refs[: len(low)]
        high_refs = [low_refs[0]] + list(refs[len(low) : len(low) + len(high)]) + [low_refs[-1]]
        out_ref = refs[-1]
        place = own_place()

        def put(owner, source):
            begin = pl.multiple_of((owner ^ place) * quarter, quarter)
            out_ref[:, pl.ds(begin, quarter)] = source[...]

        put(place, low_refs[0])
        for step in range(1, line):
            for holds, side, entry, owner in line_choice(step, place, line):
                pl.when(holds)(functools.partial(put, owner, (low_refs, high_refs)[side][entry]))

    return pl.pallas_call(
        kernel,
        out_shape=jax.ShapeDtypeStruct((n_tensor, line * quarter, width), low[0].dtype),
        in_specs=whole_vmem(len(low) + len(high)),
        out_specs=pl.BlockSpec(memory_space=pltpu.VMEM),
        compiler_params=params(),
        name="place_cotangents",
    )(*low, *high)


def plane_first(block, count):
    if count != 4:
        gathered = lax.all_gather(block, "tensor", axis=0)
        own = lax.axis_index("tensor")
        return [
            lax.dynamic_index_in_dim(gathered, own ^ b, 0, keepdims=False) for b in range(count)
        ]
    one = lax.ppermute(block, "tensor", [(j, j ^ 1) for j in range(count)])
    two = lax.ppermute(block, "tensor", [(j, j ^ 2) for j in range(count)])
    return [block, one, two]


def plane_second(blocks, count, *behind):
    if count != 4:
        return blocks
    up, down = tie((blocks[1][:1], blocks[2][1:]), *behind)
    upper = lax.ppermute(up, "tensor", [(j, j ^ 2) for j in range(count)])
    lower = lax.ppermute(down, "tensor", [(j, j ^ 1) for j in range(count)])
    return blocks + [upper, lower]


def gradient_terms(blocks, cotangents, n_tensor):
    size = blocks[0].shape[2]
    width = cotangents.shape[2]
    split = len(blocks) > n_tensor

    def kernel(*refs):
        block_refs, cotangent_ref = refs[: len(blocks)], refs[len(blocks)]
        kept_ref, sent_ref = refs[len(blocks) + 1 :]
        index, core = lax.axis_index("tensor"), own_core()

        def term(owner):
            total = None
            for distance in range(n_tensor):
                if split and distance == n_tensor - 1:
                    upper, lower = block_refs[-2], block_refs[-1]
                    left = jnp.where(owner == 0, upper[0], lower[0])
                else:
                    left = block_refs[distance][owner]
                product = lax.dot_general(
                    left,
                    cotangent_ref[index ^ distance],
                    (((0,), (0,)), ((), ())),
                    preferred_element_type=jnp.float32,
                )
                total = product if total is None else total + product
            return total

        sent_ref[...] = term(1 - core).astype(sent_ref.dtype)
        kept_ref[...] = term(core)

    depth = n_tensor * blocks[0].shape[1]
    return pl.pallas_call(
        kernel,
        out_shape=(
            jax.ShapeDtypeStruct((size, width), jnp.float32),
            jax.ShapeDtypeStruct((size, width), jnp.bfloat16),
        ),
        in_specs=whole_vmem(len(blocks) + 1),
        out_specs=whole_vmem(2),
        compiler_params=params(),
        cost_estimate=pl.CostEstimate(
            flops=4 * depth * size * width,
            bytes_accessed=4 * depth * size + 2 * depth * width + 6 * size * width,
            transcendentals=0,
        ),
        name="gradient_terms",
    )(*blocks, cotangents)


def norm_columns(states, gain, rows, line):
    length, width = states.shape
    ranges = chunk_ranges(rows)
    tile = 64

    def kernel(states_ref, gain_ref, *outs):
        kept, sent = outs[: len(ranges)], outs[len(ranges) :]
        core = own_core()
        total = jnp.zeros((tile, 1), jnp.float32)
        for block in range(2 * line):
            piece = states_ref[:, block * rows : (block + 1) * rows].astype(jnp.float32)
            total = total + jnp.sum(piece * piece, axis=1, keepdims=True)
        scale = lax.rsqrt(total / width + norm_eps)
        for flag in range(2):

            @pl.when(core == flag)
            def _():
                for block in range(2 * line):
                    group = kept if block % 2 == flag else sent
                    for (start, size), out in zip(ranges, group):
                        columns = slice(block * rows + start, block * rows + start + size)
                        piece = states_ref[:, columns].astype(jnp.float32)
                        out[block // 2] = (piece * scale * gain_ref[:, columns]).astype(out.dtype)

    shapes = [
        jax.ShapeDtypeStruct((line, length, size), jnp.bfloat16) for _, size in ranges
    ] * 2
    outs = pl.pallas_call(
        kernel,
        grid=(length // tile,),
        out_shape=shapes,
        in_specs=[
            pl.BlockSpec((tile, width), lambda i: (i, 0)),
            pl.BlockSpec((1, width), lambda i: (0, 0)),
        ],
        out_specs=[pl.BlockSpec((line, tile, size), lambda i: (0, i, 0)) for _, size in ranges] * 2,
        compiler_params=params(),
        cost_estimate=pl.CostEstimate(
            flops=6 * length * width, bytes_accessed=4 * length * width, transcendentals=0
        ),
        name="norm_columns",
    )(states, gain.reshape(1, width))
    return outs[: len(ranges)], outs[len(ranges) :]


def accumulate(totals, kept, got, slots, last=False):
    _, length, depth = kept.shape
    width = slots[0][1].shape[1]
    count = len(slots)
    tile = min(256, length)
    owners = jnp.stack([jnp.asarray(owner, jnp.int32) for owner, _ in slots])
    weights = [weight for _, weight in slots]

    def kernel(owners_ref, *refs):
        weight_refs = refs[2 * count : 3 * count]
        for side, out_ref in zip((1, 0), reversed(refs[-2:])):
            result = None if totals is None else refs[3 * count + side][...]
            for slot in range(count):
                product = jnp.dot(
                    refs[side * count + slot][0],
                    weight_refs[slot][...],
                    preferred_element_type=jnp.float32,
                )
                result = product if result is None else result + product
            out_ref[...] = result.astype(out_ref.dtype)

    def state_spec(slot):
        return pl.BlockSpec((1, tile, depth), lambda i, chosen: (chosen[slot], i, 0))

    before = list(totals or [])
    row_spec = pl.BlockSpec((tile, width), lambda i, chosen: (i, 0))
    return pl.pallas_call(
        kernel,
        grid_spec=pltpu.PrefetchScalarGridSpec(
            num_scalar_prefetch=1,
            grid=(length // tile,),
            in_specs=[state_spec(slot) for slot in range(count)] * 2
            + [pl.BlockSpec((depth, width), lambda i, chosen: (0, 0))] * count
            + [row_spec] * len(before),
            out_specs=[row_spec] * 2,
        ),
        out_shape=[
            jax.ShapeDtypeStruct((length, width), jnp.float32),
            jax.ShapeDtypeStruct((length, width), jnp.bfloat16 if last else jnp.float32),
        ],
        compiler_params=params(24),
        cost_estimate=pl.CostEstimate(
            flops=4 * count * length * depth * width,
            bytes_accessed=2 * count * depth * (2 * length + width) + 16 * length * width,
            transcendentals=0,
        ),
        name="accumulate",
    )(owners, *([kept] * count), *([got] * count), *weights, *before)


def attention(kept, got, cosine_table, sine_table):
    length, width = kept.shape
    heads = width // HD - 2
    tile = min(128, length)

    def rope(u, cosine, sine):
        return u * cosine + pltpu.roll(u, HD // 2, 1) * sine

    def kernel(q_ref, q2_ref, k_ref, k2_ref, v_ref, v2_ref, cos_ref, sin_ref, out_ref, keys, values):
        @pl.when(pl.program_id(0) == 0)
        def _():
            key_rows = rope(k_ref[...] + k2_ref[...], cos_ref[...], sin_ref[...])
            keys[...] = key_rows.astype(jnp.bfloat16)
            values[...] = (v_ref[...] + v2_ref[...]).astype(jnp.bfloat16)

        for begin in range(0, length, tile):
            here, upto = slice(begin, begin + tile), begin + tile
            query = rope(q_ref[here] + q2_ref[here], cos_ref[here], sin_ref[here])
            query = (query * HD**-0.5).astype(jnp.bfloat16)
            scores = lax.dot_general(
                query,
                keys[:upto],
                (((1,), (1,)), ((), ())),
                preferred_element_type=jnp.float32,
            )
            row = lax.broadcasted_iota(jnp.int32, scores.shape, 0) + begin
            column = lax.broadcasted_iota(jnp.int32, scores.shape, 1)
            scores = jnp.where(row >= column, scores, -jnp.inf)
            raised = jnp.exp(scores - jnp.max(scores, axis=1, keepdims=True))
            weights = raised * (1.0 / jnp.sum(raised, axis=1, keepdims=True))
            out_ref[here] = jnp.dot(
                weights.astype(jnp.bfloat16), values[:upto], preferred_element_type=jnp.float32
            ).astype(jnp.bfloat16)

    def column(index):
        return pl.BlockSpec((length, HD), lambda h: (0, index))

    head = pl.BlockSpec((length, HD), lambda h: (0, h))
    return pl.pallas_call(
        kernel,
        grid=(heads,),
        out_shape=jax.ShapeDtypeStruct((length, heads * HD), jnp.bfloat16),
        in_specs=[head, head]
        + [column(heads)] * 2
        + [column(heads + 1)] * 2
        + [column(0)] * 2,
        out_specs=head,
        scratch_shapes=[pltpu.VMEM((length, HD), jnp.bfloat16)] * 2,
        compiler_params=params(),
        cost_estimate=pl.CostEstimate(
            flops=4 * heads * length * length * HD,
            bytes_accessed=9 * length * width,
            transcendentals=heads * length * length,
        ),
        name="attention",
    )(kept, got, kept, got, kept, got, cosine_table, sine_table)


def output_rows(mine, other, first_weight, rest_weight, n_tensor, full_width):
    kept, depth = mine.shape[1], mine.shape[2]
    tile = first_weight.shape[1]
    width = tile + rest_weight.shape[1]
    tiles = width // tile
    chosen = jnp.stack([lax.axis_index("tensor"), own_core()]).astype(jnp.int32)

    def kernel(chosen_ref, mine_ref, other_ref, first_ref, rest_ref, made_ref, sent_ref, left_ref):
        def product(weight_ref):
            total = jnp.dot(left_ref[...], weight_ref[...], preferred_element_type=jnp.float32)
            made_ref[...] = total[:kept].astype(made_ref.dtype)
            sent_ref[...] = total[kept:].astype(sent_ref.dtype)

        @pl.when(pl.program_id(0) == 0)
        def _():
            for distance in range(n_tensor):
                begin = pl.multiple_of((chosen_ref[0] ^ distance) * depth, depth)
                left_ref[:kept, pl.ds(begin, depth)] = mine_ref[distance]
                left_ref[kept:, pl.ds(begin, depth)] = other_ref[distance]
            product(first_ref)

        @pl.when(pl.program_id(0) > 0)
        def _():
            product(rest_ref)

    whole = pl.BlockSpec((n_tensor, kept, depth), lambda i, chosen: (0, 0, 0))
    return pl.pallas_call(
        kernel,
        grid_spec=pltpu.PrefetchScalarGridSpec(
            num_scalar_prefetch=1,
            grid=(tiles,),
            in_specs=[
                whole,
                whole,
                pl.BlockSpec((n_tensor * depth, tile), lambda i, chosen: (0, 0)),
                pl.BlockSpec(
                    (n_tensor * depth, tile), lambda i, chosen: (0, jnp.maximum(i - 1, 0))
                ),
            ],
            out_specs=[
                pl.BlockSpec((kept, tile), lambda i, chosen: (0, chosen[1] * tiles + i)),
                pl.BlockSpec((kept, tile), lambda i, chosen: (0, i)),
            ],
            scratch_shapes=[pltpu.VMEM((2 * kept, n_tensor * depth), jnp.bfloat16)],
        ),
        out_shape=[
            jax.ShapeDtypeStruct((kept, full_width), jnp.bfloat16),
            jax.ShapeDtypeStruct((kept, width), jnp.bfloat16),
        ],
        compiler_params=params(52),
        cost_estimate=pl.CostEstimate(
            flops=4 * kept * n_tensor * depth * width,
            bytes_accessed=2 * n_tensor * depth * width + 4 * kept * width,
            transcendentals=0,
        ),
        name="output_rows",
    )(chosen, mine, other, first_weight, rest_weight)


def fill_columns(made, block, index):
    kept, width = block.shape
    chosen = jnp.reshape(index, (1,)).astype(jnp.int32)

    def kernel(chosen_ref, made_ref, block_ref, out_ref):
        out_ref[...] = block_ref[...]

    return pl.pallas_call(
        kernel,
        grid_spec=pltpu.PrefetchScalarGridSpec(
            num_scalar_prefetch=1,
            grid=(1,),
            in_specs=[
                pl.BlockSpec(memory_space=pl.ANY),
                pl.BlockSpec((kept, width), lambda i, chosen: (0, 0)),
            ],
            out_specs=pl.BlockSpec((kept, width), lambda i, chosen: (0, chosen[0])),
        ),
        out_shape=jax.ShapeDtypeStruct(made.shape, made.dtype),
        input_output_aliases={1: 0},
        compiler_params=params(),
        name="fill_columns",
    )(chosen, made, block)


def body(
    train_states, qkv_cotangent, w_master, moment_one, moment_two, prompt_states, norm_gain, w_out
):
    n_dp = lax.axis_size("dp")
    n_tensor = lax.axis_size("tensor")
    line = n_dp // 2
    tensor_index = lax.axis_index("tensor")
    core, place = own_core(), own_place()
    siblings = [(i, i ^ 1) for i in range(n_dp)]
    rows, slice_width = w_master.shape
    tokens, width = train_states.shape
    length = prompt_states.shape[0]
    query_width = slice_width - 2 * HD
    ranges = chunk_ranges(rows)

    kept_states, sent_states = norm_columns(prompt_states, norm_gain, rows, line)
    got_states = [lax.ppermute(states, "dp", siblings) for states in sent_states]

    packed = pack_columns(train_states, rows, line, tokens // n_tensor)
    pieces = [packed[0]] + [
        lax.ppermute(
            packed[distance], "dp", line_pairs([(i, i ^ distance) for i in range(line)])
        )
        for distance in range(1, line)
    ]
    pieces = tie(pieces, kept_states[0])

    cotangents = LineGather(tie((qkv_cotangent,), *pieces)[0], place, line)
    cotangents.hop()
    stacked = stack_pieces(pieces, [(start, start + size) for start, size in ranges])
    spread = [plane_first(block, n_tensor) for block in stacked]
    for _ in range(2, line):
        cotangents.hop()
    behind = (cotangents.low[2], cotangents.high[2], spread[0], spread[1])
    spread = [plane_second(blocks, n_tensor, *behind) for blocks in spread]
    all_cotangents = place_cotangents((cotangents.low, cotangents.high), line, n_tensor)

    core_width = width // 2
    early_width = core_width // EARLY_SHARE
    begin = core * core_width
    w_early = lax.dynamic_slice(w_out, (0, begin), (w_out.shape[0], early_width))
    w_rest = lax.dynamic_slice(
        w_out, (0, begin + early_width), (w_out.shape[0], core_width - early_width)
    )
    early_weight = lax.all_gather(w_early, "tensor", axis=0, tiled=True)
    (w_rest,) = tie((w_rest,), spread, cotangents.low[-1])
    rest_weight = lax.all_gather(w_rest, "tensor", axis=0, tiled=True)

    def gradient_of(part):
        kept, sent = gradient_terms(spread[part], all_cotangents, n_tensor)
        return kept, lax.ppermute(sent, "dp", siblings)

    def adam(part, gradient):
        start, size = ranges[part]
        here = slice(start, start + size)
        moment_new = beta_one * moment_one[here] + (1.0 - beta_one) * gradient
        second_new = beta_two * moment_two[here] + (1.0 - beta_two) * gradient * gradient
        update = moment_new / bias_one / (jnp.sqrt(second_new / bias_two) + adam_eps)
        return update, (w_master[here] - learn_rate * update).astype(jnp.bfloat16)

    kept, got = gradient_of(0)
    first_update, first_weight = adam(0, kept + got.astype(jnp.float32))
    first = LineGather(first_weight, place, line)
    first.hop()
    kept, got = tie(gradient_of(1), *first.arrived())
    second_update, second_weight = adam(1, kept + got.astype(jnp.float32))
    second = LineGather(second_weight, place, line)
    first.hop()
    second.hop()
    for _ in range(3, line):
        before = first.arrived()
        first.hop(*second.arrived())
        second.hop(*before)

    def add(totals, gather, part, steps, last=False):
        slots = [gather.slot(step) for step in steps]
        return accumulate(totals, kept_states[part], got_states[part], slots, last)

    totals = add(None, first, 0, range(line - 1))
    totals = add(totals, second, 1, range(line - 2))
    update_dir = jnp.concatenate([first_update, second_update], axis=0)
    cosine_table, sine_table = rope_tables(length, HD)
    update_dir, cosine_table, sine_table, *totals = lax.optimization_barrier(
        (update_dir, cosine_table, sine_table, *totals)
    )
    second.hop(*totals, update_dir, cosine_table, sine_table, *first.arrived())
    totals = add(totals, first, 0, [line - 1])
    totals = add(totals, second, 1, [line - 2])
    totals = add(totals, second, 1, [line - 1], True)
    attended = attention(
        totals[0], lax.ppermute(totals[1], "dp", siblings), cosine_table, sine_table
    )

    kept_rows = length // n_tensor
    heads = []
    for distance in range(n_tensor):
        target = tensor_index ^ distance
        block = lax.dynamic_slice(attended, (target * kept_rows, 0), (kept_rows, query_width))
        if distance:
            block = lax.ppermute(block, "tensor", [(j, j ^ distance) for j in range(n_tensor)])
        heads.append(block)
    (mine,) = stack_pieces([head[None] for head in heads], [(0, query_width)])
    mine = mine.reshape(n_tensor, kept_rows, query_width)
    other = lax.ppermute(mine, "dp", siblings)

    made, sent_rows = output_rows(mine, other, early_weight, rest_weight, n_tensor, width)
    swapped = lax.ppermute(sent_rows, "dp", siblings)
    summed = fill_columns(made, swapped, 1 - core)
    return (update_dir, summed)


def solution(mesh):
    placed = (
        P("dp", None),
        P("dp", "tensor"),
        P("dp", "tensor"),
        P("dp", "tensor"),
        P("dp", "tensor"),
        P("dp", None),
        P(),
        P("tensor", None),
    )
    return jax.shard_map(
        body,
        mesh=mesh,
        in_specs=placed,
        out_specs=(P("dp", "tensor"), P(("dp", "tensor"), None)),
        check_vma=False,
    )
```

```python
import functools

import jax
import jax.numpy as jnp
from jax import lax
from jax.experimental import pallas as pl
from jax.experimental.pallas import tpu as pltpu
from jax.sharding import PartitionSpec as P

HD = 128


beta_one = 0.9
beta_two = 0.95
bias_one = 1.0 - 0.9**8
bias_two = 1.0 - 0.95**8
learn_rate = 0.002
adam_eps = 1e-08
norm_eps = 1e-05
rope_base = 500000.0

MIB = 1024 * 1024
EARLY_SHARE = 8


def rope_tables(length, head_size):
    half_width = head_size // 2
    exponent = jnp.arange(half_width, dtype=jnp.float32) * (2.0 / head_size)
    inverse = jnp.power(jnp.float32(rope_base), -exponent)
    position = jnp.arange(length, dtype=jnp.float32)
    angles = position[:, None] * inverse[None, :]
    cosine_table = jnp.concatenate([jnp.cos(angles), jnp.cos(angles)], axis=1)
    sine_table = jnp.concatenate([-jnp.sin(angles), jnp.sin(angles)], axis=1)
    return (cosine_table, sine_table)


def params(mib=16):
    return pltpu.CompilerParams(vmem_limit_bytes=mib * MIB)


def whole_vmem(count):
    return [pl.BlockSpec(memory_space=pltpu.VMEM)] * count


def own_core():
    return lax.rem(lax.axis_index("dp"), 2)


def own_place():
    return lax.div(lax.axis_index("dp"), 2)


def pack_columns(train_states, rows, line, quarter):
    def kernel(index_ref, train_ref, *outs):
        place = own_place()
        for distance in range(line):
            for owner in range(2):
                column = pl.multiple_of(((place ^ distance) * 2 + owner) * rows, 128)
                outs[distance][owner] = train_ref[:, pl.ds(column, rows)]

    shapes = [jax.ShapeDtypeStruct((2, quarter, rows), train_states.dtype)] * line
    index = jnp.reshape(lax.axis_index("tensor"), (1,)).astype(jnp.int32)
    return pl.pallas_call(
        kernel,
        grid_spec=pltpu.PrefetchScalarGridSpec(
            num_scalar_prefetch=1,
            grid=(1,),
            in_specs=[
                pl.BlockSpec((quarter, train_states.shape[1]), lambda i, chosen: (chosen[0], 0))
            ],
            out_specs=[pl.BlockSpec(s.shape, lambda i, chosen: (0, 0, 0)) for s in shapes],
        ),
        out_shape=shapes,
        compiler_params=params(56),
        name="pack_columns",
    )(index, train_states)


def stack_pieces(pieces):
    outer, height, width = pieces[0].shape
    count = len(pieces)

    def kernel(*refs):
        for which in range(outer):
            for i in range(count):
                refs[count + which][i * height : (i + 1) * height] = refs[i][which]

    return pl.pallas_call(
        kernel,
        out_shape=[jax.ShapeDtypeStruct((count * height, width), pieces[0].dtype)] * outer,
        in_specs=whole_vmem(count),
        out_specs=whole_vmem(outer),
        compiler_params=params(),
        name="stack_pieces",
    )(*pieces)


def line_pairs(places):
    return [(2 * a + core, 2 * b + core) for a, b in places for core in range(2)]


def tie(arrays, *others):
    return lax.optimization_barrier((tuple(arrays), others))[0]


class LineGather:
    def __init__(self, block, place, count):
        self.place, self.count = place, count
        self.low, self.high = [block], [block]

    def hop(self, *behind):
        step, count = len(self.low), self.count
        up, down = self.low[-1], self.high[-1]
        if behind:
            up, down = tie((up, down), *behind)
        if step < count - 1:
            right = line_pairs([(i, i + 1) for i in range(step - 1, count - 1)])
            left = line_pairs([(i, i - 1) for i in range(1, count - step + 1)])
            self.low.append(lax.ppermute(up, "dp", right))
            self.high.append(lax.ppermute(down, "dp", left))
            return
        last = lax.ppermute(
            jnp.where(self.place == count - 2, up, down),
            "dp",
            line_pairs([(count - 2, count - 1), (1, 0)]),
        )
        self.low.append(last)
        self.high.append(last)

    def arrived(self):
        return self.low[-1], self.high[-1]

    def slot(self, step):
        if step == 0:
            return self.place, self.low[0]
        sides = (self.low, self.high)
        choices = line_choice(step, self.place, self.count)
        _, side, entry, owner = choices[-1]
        block = sides[side][entry]
        for holds, side, entry, other in reversed(choices[:-1]):
            if sides[side][entry] is not block:
                block = jnp.where(holds, sides[side][entry], block)
            owner = jnp.where(holds, other, owner)
        return owner, block


def line_choice(step, place, count):
    is_low, is_high = place >= step, place <= count - 1 - step
    spare = count - step
    return [
        (is_low, 0, step, place - step),
        (jnp.logical_and(jnp.logical_not(is_low), is_high), 1, step, place + step),
        (
            jnp.logical_and(jnp.logical_not(is_low), jnp.logical_not(is_high)),
            1,
            spare,
            place + spare,
        ),
    ][: 2 if 2 * step <= count else 3]


def place_cotangents(arrivals, line, n_tensor):
    tokens, width = arrivals[0][0].shape
    quarter = tokens // n_tensor
    low = [a.reshape(n_tensor, quarter, width) for a in arrivals[0]]
    high = [a.reshape(n_tensor, quarter, width) for a in arrivals[1][1:-1]]

    def kernel(*refs):
        low_refs = refs[: len(low)]
        high_refs = [low_refs[0]] + list(refs[len(low) : len(low) + len(high)]) + [low_refs[-1]]
        out_ref = refs[-1]
        place = own_place()

        def put(owner, source):
            begin = pl.multiple_of((owner ^ place) * quarter, quarter)
            out_ref[:, pl.ds(begin, quarter)] = source[...]

        put(place, low_refs[0])
        for step in range(1, line):
            for holds, side, entry, owner in line_choice(step, place, line):
                pl.when(holds)(functools.partial(put, owner, (low_refs, high_refs)[side][entry]))

    return pl.pallas_call(
        kernel,
        out_shape=jax.ShapeDtypeStruct((n_tensor, line * quarter, width), low[0].dtype),
        in_specs=whole_vmem(len(low) + len(high)),
        out_specs=pl.BlockSpec(memory_space=pltpu.VMEM),
        compiler_params=params(),
        name="place_cotangents",
    )(*low, *high)


def plane_permute(block, count, distance):
    return lax.ppermute(block, "tensor", [(j, j ^ distance) for j in range(count)])


class PlaneGather:
    def __init__(self, pair, count):
        self.count = count
        if count != 4:
            own = lax.axis_index("tensor")
            gathered = [lax.all_gather(block, "tensor", axis=0) for block in pair]
            self.blocks = [
                [lax.dynamic_index_in_dim(g, own ^ b, 0, keepdims=False) for g in gathered]
                for b in range(count)
            ]
            return
        one, two = [None, None], [None, None]
        for owner in range(2):
            one[owner] = plane_permute(pair[owner], count, 1)
            two[1 - owner] = plane_permute(pair[1 - owner], count, 2)
        self.blocks = [list(pair), one, two]

    def passed(self):
        return [self.blocks[1][0], self.blocks[2][1]]

    def second(self, *behind):
        if self.count == 4:
            up, down = tie(self.passed(), *behind)
            self.blocks.append(
                [plane_permute(up, self.count, 2), plane_permute(down, self.count, 1)]
            )


def gradient_terms(blocks, cotangents):
    n_tensor, depth, width = cotangents.shape
    size = blocks[0][0].shape[1]
    flat = [block for pair in blocks for block in pair]

    def kernel(*refs):
        cotangent_ref, kept_ref, sent_ref = refs[len(flat) :]
        index, core = lax.axis_index("tensor"), own_core()

        def term(owner):
            total = None
            for distance in range(n_tensor):
                lower, upper = refs[2 * distance : 2 * distance + 2]
                left = jnp.where(owner == 0, lower[...], upper[...])
                product = lax.dot_general(
                    left,
                    cotangent_ref[index ^ distance],
                    (((0,), (0,)), ((), ())),
                    preferred_element_type=jnp.float32,
                )
                total = product if total is None else total + product
            return total

        sent_ref[...] = term(1 - core).astype(sent_ref.dtype)
        kept_ref[...] = term(core)

    return pl.pallas_call(
        kernel,
        out_shape=(
            jax.ShapeDtypeStruct((size, width), jnp.float32),
            jax.ShapeDtypeStruct((size, width), jnp.bfloat16),
        ),
        in_specs=whole_vmem(len(flat) + 1),
        out_specs=whole_vmem(2),
        compiler_params=params(32),
        cost_estimate=pl.CostEstimate(
            flops=4 * n_tensor * depth * size * width,
            bytes_accessed=n_tensor * depth * (4 * size + 2 * width) + 6 * size * width,
            transcendentals=0,
        ),
        name="gradient_terms",
    )(*flat, cotangents)


def adam_rows(kept, got, w_master, moment_one, moment_two):
    rows, width = kept.shape
    tile = min(128, rows)

    def kernel(kept_ref, got_ref, master_ref, one_ref, two_ref, update_ref, weight_ref):
        gradient = kept_ref[...] + got_ref[...].astype(jnp.float32)
        moment_new = beta_one * one_ref[...] + (1.0 - beta_one) * gradient
        second_new = beta_two * two_ref[...] + (1.0 - beta_two) * gradient * gradient
        update = moment_new / bias_one / (jnp.sqrt(second_new / bias_two) + adam_eps)
        update_ref[...] = update
        weight_ref[...] = (master_ref[...] - learn_rate * update).astype(weight_ref.dtype)

    here = pl.BlockSpec((tile, width), lambda i: (i, 0))
    return pl.pallas_call(
        kernel,
        grid=(rows // tile,),
        out_shape=[
            jax.ShapeDtypeStruct((rows, width), jnp.float32),
            jax.ShapeDtypeStruct((rows, width), jnp.bfloat16),
        ],
        in_specs=[here] * 5,
        out_specs=[here] * 2,
        compiler_params=params(),
        cost_estimate=pl.CostEstimate(
            flops=16 * rows * width, bytes_accessed=24 * rows * width, transcendentals=rows * width
        ),
        name="adam_rows",
    )(kept, got, w_master, moment_one, moment_two)


def norm_columns(states, gain, rows, line):
    length, width = states.shape
    tile = 64

    def kernel(states_ref, gain_ref, kept, sent):
        core = own_core()
        total = jnp.zeros((tile, 1), jnp.float32)
        for block in range(2 * line):
            piece = states_ref[:, block * rows : (block + 1) * rows].astype(jnp.float32)
            total = total + jnp.sum(piece * piece, axis=1, keepdims=True)
        scale = lax.rsqrt(total / width + norm_eps)
        for flag in range(2):

            @pl.when(core == flag)
            def _():
                for block in range(2 * line):
                    out = kept if block % 2 == flag else sent
                    columns = slice(block * rows, (block + 1) * rows)
                    piece = states_ref[:, columns].astype(jnp.float32)
                    out[block // 2] = (piece * scale * gain_ref[:, columns]).astype(out.dtype)

    return pl.pallas_call(
        kernel,
        grid=(length // tile,),
        out_shape=[jax.ShapeDtypeStruct((line, length, rows), jnp.bfloat16)] * 2,
        in_specs=[
            pl.BlockSpec((tile, width), lambda i: (i, 0)),
            pl.BlockSpec((1, width), lambda i: (0, 0)),
        ],
        out_specs=[pl.BlockSpec((line, tile, rows), lambda i: (0, i, 0))] * 2,
        compiler_params=params(),
        cost_estimate=pl.CostEstimate(
            flops=6 * length * width, bytes_accessed=4 * length * width, transcendentals=0
        ),
        name="norm_columns",
    )(states, gain.reshape(1, width))


def accumulate(totals, kept, got, slots, last=False):
    _, length, depth = kept.shape
    width = slots[0][1].shape[1]
    count = len(slots)
    tile = min(256, length)
    owners = jnp.stack([jnp.asarray(owner, jnp.int32) for owner, _ in slots])
    weights = [weight for _, weight in slots]

    def kernel(owners_ref, *refs):
        weight_refs = refs[2 * count : 3 * count]
        for side, out_ref in zip((1, 0), reversed(refs[-2:])):
            result = None if totals is None else refs[3 * count + side][...]
            for slot in range(count):
                product = jnp.dot(
                    refs[side * count + slot][0],
                    weight_refs[slot][...],
                    preferred_element_type=jnp.float32,
                )
                result = product if result is None else result + product
            out_ref[...] = result.astype(out_ref.dtype)

    def state_spec(slot):
        return pl.BlockSpec((1, tile, depth), lambda i, chosen: (chosen[slot], i, 0))

    before = list(totals or [])
    row_spec = pl.BlockSpec((tile, width), lambda i, chosen: (i, 0))
    return pl.pallas_call(
        kernel,
        grid_spec=pltpu.PrefetchScalarGridSpec(
            num_scalar_prefetch=1,
            grid=(length // tile,),
            in_specs=[state_spec(slot) for slot in range(count)] * 2
            + [pl.BlockSpec((depth, width), lambda i, chosen: (0, 0))] * count
            + [row_spec] * len(before),
            out_specs=[row_spec] * 2,
        ),
        out_shape=[
            jax.ShapeDtypeStruct((length, width), jnp.float32),
            jax.ShapeDtypeStruct((length, width), jnp.bfloat16 if last else jnp.float32),
        ],
        compiler_params=params(28),
        cost_estimate=pl.CostEstimate(
            flops=4 * count * length * depth * width,
            bytes_accessed=2 * count * depth * (2 * length + width) + 16 * length * width,
            transcendentals=0,
        ),
        name="accumulate",
    )(owners, *([kept] * count), *([got] * count), *weights, *before)


def attention(kept, got, cosine_table, sine_table):
    length, width = kept.shape
    heads = width // HD - 2
    tile = min(128, length)

    def rope(u, cosine, sine):
        return u * cosine + pltpu.roll(u, HD // 2, 1) * sine

    def kernel(kept_ref, got_ref, cos_ref, sin_ref, out_ref):
        def columns(index, here=slice(None)):
            there = slice(index * HD, (index + 1) * HD)
            return kept_ref[here, there] + got_ref[here, there].astype(jnp.float32)

        keys = rope(columns(heads), cos_ref[...], sin_ref[...]).astype(jnp.bfloat16)
        values = columns(heads + 1).astype(jnp.bfloat16)
        for begin in range(0, length, tile):
            here, upto = slice(begin, begin + tile), begin + tile
            row = lax.broadcasted_iota(jnp.int32, (tile, upto), 0) + begin
            seen = row >= lax.broadcasted_iota(jnp.int32, (tile, upto), 1)
            for head in range(heads):
                query = rope(columns(head, here), cos_ref[here], sin_ref[here])
                query = (query * HD**-0.5).astype(jnp.bfloat16)
                scores = lax.dot_general(
                    query,
                    keys[:upto],
                    (((1,), (1,)), ((), ())),
                    preferred_element_type=jnp.float32,
                )
                scores = jnp.where(seen, scores, -jnp.inf)
                raised = jnp.exp(scores - jnp.max(scores, axis=1, keepdims=True))
                weights = raised * (1.0 / jnp.sum(raised, axis=1, keepdims=True))
                out_ref[here, head * HD : (head + 1) * HD] = jnp.dot(
                    weights.astype(jnp.bfloat16), values[:upto], preferred_element_type=jnp.float32
                ).astype(jnp.bfloat16)

    return pl.pallas_call(
        kernel,
        out_shape=jax.ShapeDtypeStruct((length, heads * HD), jnp.bfloat16),
        in_specs=whole_vmem(4),
        out_specs=pl.BlockSpec(memory_space=pltpu.VMEM),
        compiler_params=params(),
        cost_estimate=pl.CostEstimate(
            flops=4 * heads * length * length * HD,
            bytes_accessed=9 * length * width,
            transcendentals=heads * length * length,
        ),
        name="attention",
    )(kept, got, cosine_table, sine_table)


def by_source(mine, other, n_tensor):
    kept, depth = mine.shape[0] // n_tensor, mine.shape[1]

    def kernel(mine_ref, other_ref, out_ref):
        index = lax.axis_index("tensor")
        for distance in range(n_tensor):
            columns = pl.ds(pl.multiple_of((index ^ distance) * depth, depth), depth)
            rows = slice(distance * kept, (distance + 1) * kept)
            out_ref[:kept, columns] = mine_ref[rows]
            out_ref[kept:, columns] = other_ref[rows]

    return pl.pallas_call(
        kernel,
        out_shape=jax.ShapeDtypeStruct((2 * kept, n_tensor * depth), mine.dtype),
        in_specs=whole_vmem(2),
        out_specs=pl.BlockSpec(memory_space=pltpu.VMEM),
        compiler_params=params(),
        name="by_source",
    )(mine, other)


def lay_out(blocks):
    kept = blocks[0][0].shape[0]
    half = sum(block.shape[1] for block in blocks[0])

    def kernel(*refs):
        out_ref = refs[-1]
        core = own_core()
        for flag in range(2):

            @pl.when(core == flag)
            def _():
                entry = 0
                for side in range(2):
                    begin = (flag ^ side) * half
                    for block in blocks[side]:
                        stop = begin + block.shape[1]
                        out_ref[:, begin:stop] = refs[entry][...]
                        begin, entry = stop, entry + 1

    flat = [block for side in blocks for block in side]
    return pl.pallas_call(
        kernel,
        out_shape=jax.ShapeDtypeStruct((kept, 2 * half), flat[0].dtype),
        in_specs=whole_vmem(len(flat)),
        out_specs=pl.BlockSpec(memory_space=pltpu.VMEM),
        compiler_params=params(),
        name="lay_out",
    )(*flat)


def body(
    train_states, qkv_cotangent, w_master, moment_one, moment_two, prompt_states, norm_gain, w_out
):
    n_dp = lax.axis_size("dp")
    n_tensor = lax.axis_size("tensor")
    line = n_dp // 2
    tensor_index = lax.axis_index("tensor")
    core, place = own_core(), own_place()
    siblings = [(i, i ^ 1) for i in range(n_dp)]
    rows, slice_width = w_master.shape
    tokens, width = train_states.shape
    length = prompt_states.shape[0]
    query_width = slice_width - 2 * HD

    kept_states, sent_states = norm_columns(prompt_states, norm_gain, rows, line)
    got_states = lax.ppermute(sent_states, "dp", siblings)

    packed = pack_columns(train_states, rows, line, tokens // n_tensor)
    pieces = [packed[0]] + [
        lax.ppermute(
            packed[distance], "dp", line_pairs([(i, i ^ distance) for i in range(line)])
        )
        for distance in range(1, line)
    ]
    pieces = tie(pieces, kept_states)

    cotangents = LineGather(tie((qkv_cotangent,), *pieces)[0], place, line)
    cotangents.hop()
    spread = PlaneGather(stack_pieces(pieces), n_tensor)
    for _ in range(2, line - 1):
        cotangents.hop()
    spread.second(*cotangents.arrived())
    cotangents.hop(*spread.passed()) if n_tensor == 4 else cotangents.hop()
    all_cotangents = place_cotangents((cotangents.low, cotangents.high), line, n_tensor)

    core_width = width // 2
    early_width = core_width // EARLY_SHARE
    begin = core * core_width
    w_early = lax.dynamic_slice(w_out, (0, begin), (w_out.shape[0], early_width))
    w_rest = lax.dynamic_slice(
        w_out, (0, begin + early_width), (w_out.shape[0], core_width - early_width)
    )
    early_weight = lax.all_gather(w_early, "tensor", axis=0, tiled=True)
    (w_rest,) = tie((w_rest,), spread.blocks, cotangents.low[-1], early_weight)
    rest_weight = lax.all_gather(w_rest, "tensor", axis=0, tiled=True)

    kept, sent = gradient_terms(spread.blocks, all_cotangents)
    got = lax.ppermute(sent, "dp", siblings)
    update_dir, weight = adam_rows(kept, got, w_master, moment_one, moment_two)

    weights = LineGather(weight, place, line)

    def add(totals, steps, last=False):
        slots = [weights.slot(step) for step in steps]
        return accumulate(totals, kept_states, got_states, slots, last)

    for _ in range(1, line - 1):
        weights.hop()
    totals = add(None, range(line - 2))
    cosine_table, sine_table = rope_tables(length, HD)
    cosine_table, sine_table, *totals = tie((cosine_table, sine_table, *totals))
    weights.hop(*totals, cosine_table, sine_table)
    totals = add(totals, [line - 2])
    totals = add(totals, [line - 1], True)
    attended = attention(
        totals[0], lax.ppermute(totals[1], "dp", siblings), cosine_table, sine_table
    )

    kept_rows = length // n_tensor
    heads = []
    for distance in range(n_tensor):
        target = tensor_index ^ distance
        block = lax.dynamic_slice(attended, (target * kept_rows, 0), (kept_rows, query_width))
        if distance:
            block = lax.ppermute(block, "tensor", [(j, j ^ distance) for j in range(n_tensor)])
        heads.append(block)
    (mine,) = stack_pieces([head[None] for head in heads])
    other = lax.ppermute(mine, "dp", siblings)
    both = by_source(mine, other, n_tensor)
    mine, sent = [], []
    for weight in (early_weight, rest_weight):
        made = jnp.dot(both, weight, preferred_element_type=jnp.float32).astype(jnp.bfloat16)
        mine.append(made[:kept_rows])
        sent.append(made[kept_rows:])
    summed = lay_out((mine, [lax.ppermute(rows, "dp", siblings) for rows in sent]))
    return (update_dir, summed)


def solution(mesh):
    placed = (
        P("dp", None),
        P("dp", "tensor"),
        P("dp", "tensor"),
        P("dp", "tensor"),
        P("dp", "tensor"),
        P("dp", None),
        P(),
        P("tensor", None),
    )
    return jax.shard_map(
        body,
        mesh=mesh,
        in_specs=placed,
        out_specs=(P("dp", "tensor"), P(("dp", "tensor"), None)),
        check_vma=False,
    )
```

```python
import functools

import jax
import jax.numpy as jnp
from jax import lax
from jax.experimental import pallas as pl
from jax.experimental.pallas import tpu as pltpu
from jax.sharding import PartitionSpec as P

HD = 128


beta_one = 0.9
beta_two = 0.95
bias_one = 1.0 - 0.9**8
bias_two = 1.0 - 0.95**8
learn_rate = 0.002
adam_eps = 1e-08
norm_eps = 1e-05
rope_base = 500000.0

MIB = 1024 * 1024
EARLY_SHARE = 8


def rope_tables(length, head_size):
    half_width = head_size // 2
    exponent = jnp.arange(half_width, dtype=jnp.float32) * (2.0 / head_size)
    inverse = jnp.power(jnp.float32(rope_base), -exponent)
    position = jnp.arange(length, dtype=jnp.float32)
    angles = position[:, None] * inverse[None, :]
    cosine_table = jnp.concatenate([jnp.cos(angles), jnp.cos(angles)], axis=1)
    sine_table = jnp.concatenate([-jnp.sin(angles), jnp.sin(angles)], axis=1)
    return (cosine_table, sine_table)


def params(mib=16):
    return pltpu.CompilerParams(vmem_limit_bytes=mib * MIB)


def whole_vmem(count):
    return [pl.BlockSpec(memory_space=pltpu.VMEM)] * count


def own_core():
    return lax.rem(lax.axis_index("dp"), 2)


def own_place():
    return lax.div(lax.axis_index("dp"), 2)


def pack_columns(train_states, rows, line, quarter):
    def kernel(index_ref, train_ref, *outs):
        place = own_place()
        for distance in range(line):
            for owner in range(2):
                column = pl.multiple_of(((place ^ distance) * 2 + owner) * rows, 128)
                outs[distance][owner] = train_ref[:, pl.ds(column, rows)]

    shapes = [jax.ShapeDtypeStruct((2, quarter, rows), train_states.dtype)] * line
    index = jnp.reshape(lax.axis_index("tensor"), (1,)).astype(jnp.int32)
    return pl.pallas_call(
        kernel,
        grid_spec=pltpu.PrefetchScalarGridSpec(
            num_scalar_prefetch=1,
            grid=(1,),
            in_specs=[
                pl.BlockSpec((quarter, train_states.shape[1]), lambda i, chosen: (chosen[0], 0))
            ],
            out_specs=[pl.BlockSpec(s.shape, lambda i, chosen: (0, 0, 0)) for s in shapes],
        ),
        out_shape=shapes,
        compiler_params=params(56),
        name="pack_columns",
    )(index, train_states)


def stack_pieces(pieces):
    outer, height, width = pieces[0].shape
    count = len(pieces)

    def kernel(*refs):
        for which in range(outer):
            for i in range(count):
                refs[count + which][i * height : (i + 1) * height] = refs[i][which]

    return pl.pallas_call(
        kernel,
        out_shape=[jax.ShapeDtypeStruct((count * height, width), pieces[0].dtype)] * outer,
        in_specs=whole_vmem(count),
        out_specs=whole_vmem(outer),
        compiler_params=params(),
        name="stack_pieces",
    )(*pieces)


def line_pairs(places):
    return [(2 * a + core, 2 * b + core) for a, b in places for core in range(2)]


def tie(arrays, *others):
    return lax.optimization_barrier((tuple(arrays), others))[0]


class LineGather:
    def __init__(self, block, place, count):
        self.place, self.count = place, count
        self.low, self.high = [block], [block]

    def hop(self, *behind):
        step, count = len(self.low), self.count
        up, down = self.low[-1], self.high[-1]
        if behind:
            up, down = tie((up, down), *behind)
        right = line_pairs([(i, i + 1) for i in range(step - 1, count - 1)])
        left = line_pairs([(i, i - 1) for i in range(1, count - step + 1)])
        self.low.append(lax.ppermute(up, "dp", right))
        self.high.append(lax.ppermute(down, "dp", left))

    def arrived(self):
        return self.low[-1], self.high[-1]

    def slot(self, step):
        if step == 0:
            return [(True, self.place, self.low[0])]
        sides = (self.low, self.high)
        return [
            (holds, owner, sides[side][entry])
            for holds, side, entry, owner in line_choice(step, self.place, self.count)
        ]


def line_choice(step, place, count):
    is_low, is_high = place >= step, place <= count - 1 - step
    spare = count - step
    return [
        (is_low, 0, step, place - step),
        (jnp.logical_and(jnp.logical_not(is_low), is_high), 1, step, place + step),
        (
            jnp.logical_and(jnp.logical_not(is_low), jnp.logical_not(is_high)),
            1,
            spare,
            place + spare,
        ),
    ][: 2 if 2 * step <= count else 3]


def place_cotangents(arrivals, line, n_tensor):
    tokens, width = arrivals[0][0].shape
    quarter = tokens // n_tensor
    low = [a.reshape(n_tensor, quarter, width) for a in arrivals[0]]
    high = [a.reshape(n_tensor, quarter, width) for a in arrivals[1][1:]]

    def kernel(*refs):
        low_refs = refs[: len(low)]
        high_refs = [low_refs[0]] + list(refs[len(low) : len(low) + len(high)])
        out_ref = refs[-1]
        place = own_place()

        def put(owner, source):
            begin = pl.multiple_of((owner ^ place) * quarter, quarter)
            out_ref[:, pl.ds(begin, quarter)] = source[...]

        put(place, low_refs[0])
        for step in range(1, line):
            for holds, side, entry, owner in line_choice(step, place, line):
                pl.when(holds)(functools.partial(put, owner, (low_refs, high_refs)[side][entry]))

    return pl.pallas_call(
        kernel,
        out_shape=jax.ShapeDtypeStruct((n_tensor, line * quarter, width), low[0].dtype),
        in_specs=whole_vmem(len(low) + len(high)),
        out_specs=pl.BlockSpec(memory_space=pltpu.VMEM),
        compiler_params=params(),
        name="place_cotangents",
    )(*low, *high)


def plane_permute(block, count, distance):
    return lax.ppermute(block, "tensor", [(j, j ^ distance) for j in range(count)])


class PlaneGather:
    def __init__(self, pair, count):
        self.count = count
        if count != 4:
            own = lax.axis_index("tensor")
            gathered = [lax.all_gather(block, "tensor", axis=0) for block in pair]
            self.blocks = [
                [lax.dynamic_index_in_dim(g, own ^ b, 0, keepdims=False) for g in gathered]
                for b in range(count)
            ]
            return
        one, two = [None, None], [None, None]
        for owner in range(2):
            one[owner] = plane_permute(pair[owner], count, 1)
            two[1 - owner] = plane_permute(pair[1 - owner], count, 2)
        self.blocks = [list(pair), one, two]

    def passed(self):
        return [self.blocks[1][0], self.blocks[2][1]]

    def second(self, *behind):
        if self.count == 4:
            up, down = tie(self.passed(), *behind)
            self.blocks.append(
                [plane_permute(up, self.count, 2), plane_permute(down, self.count, 1)]
            )


def gradient_term(blocks, cotangents, sibling):
    n_tensor, depth, width = cotangents.shape
    size = blocks[0][0].shape[1]
    flat = [block for pair in blocks for block in pair]

    def kernel(*refs):
        cotangent_ref, out_ref = refs[len(flat) :]
        index = lax.axis_index("tensor")
        owner = 1 - own_core() if sibling else own_core()
        total = None
        for distance in range(n_tensor):
            lower, upper = refs[2 * distance : 2 * distance + 2]
            product = lax.dot_general(
                jnp.where(owner == 0, lower[...], upper[...]),
                cotangent_ref[index ^ distance],
                (((0,), (0,)), ((), ())),
                preferred_element_type=jnp.float32,
            )
            total = product if total is None else total + product
        out_ref[...] = total.astype(out_ref.dtype)

    return pl.pallas_call(
        kernel,
        out_shape=jax.ShapeDtypeStruct((size, width), jnp.bfloat16 if sibling else jnp.float32),
        in_specs=whole_vmem(len(flat) + 1),
        out_specs=pl.BlockSpec(memory_space=pltpu.VMEM),
        compiler_params=params(28),
        cost_estimate=pl.CostEstimate(
            flops=2 * n_tensor * depth * size * width,
            bytes_accessed=n_tensor * depth * (4 * size + 2 * width) + 4 * size * width,
            transcendentals=0,
        ),
        name="gradient_term",
    )(*flat, cotangents)


def adam_rows(kept, got, w_master, moment_one, moment_two):
    rows, width = kept.shape
    tile = min(128, rows)

    def kernel(kept_ref, got_ref, master_ref, one_ref, two_ref, update_ref, weight_ref):
        gradient = kept_ref[...] + got_ref[...].astype(jnp.float32)
        moment_new = beta_one * one_ref[...] + (1.0 - beta_one) * gradient
        second_new = beta_two * two_ref[...] + (1.0 - beta_two) * gradient * gradient
        scaled = second_new * (1.0 / bias_two)
        update = moment_new * (1.0 / bias_one) / (scaled * lax.rsqrt(scaled) + adam_eps)
        update_ref[...] = update
        weight_ref[...] = (master_ref[...] - learn_rate * update).astype(weight_ref.dtype)

    here = pl.BlockSpec((tile, width), lambda i: (i, 0))
    return pl.pallas_call(
        kernel,
        grid=(rows // tile,),
        out_shape=[
            jax.ShapeDtypeStruct((rows, width), jnp.float32),
            jax.ShapeDtypeStruct((rows, width), jnp.bfloat16),
        ],
        in_specs=[here] * 5,
        out_specs=[here] * 2,
        compiler_params=params(),
        cost_estimate=pl.CostEstimate(
            flops=16 * rows * width, bytes_accessed=24 * rows * width, transcendentals=rows * width
        ),
        name="adam_rows",
    )(kept, got, w_master, moment_one, moment_two)


def norm_columns(states, gain, rows, line):
    length, width = states.shape
    tile = 64

    def kernel(states_ref, gain_ref, kept, sent):
        core = own_core()
        total = jnp.zeros((tile, 1), jnp.float32)
        for block in range(2 * line):
            piece = states_ref[:, block * rows : (block + 1) * rows].astype(jnp.float32)
            total = total + jnp.sum(piece * piece, axis=1, keepdims=True)
        scale = lax.rsqrt(total / width + norm_eps)
        for flag in range(2):

            @pl.when(core == flag)
            def _():
                for block in range(2 * line):
                    out = kept if block % 2 == flag else sent
                    columns = slice(block * rows, (block + 1) * rows)
                    piece = states_ref[:, columns].astype(jnp.float32)
                    out[block // 2] = (piece * scale * gain_ref[:, columns]).astype(out.dtype)

    return pl.pallas_call(
        kernel,
        grid=(length // tile,),
        out_shape=[jax.ShapeDtypeStruct((line, length, rows), jnp.bfloat16)] * 2,
        in_specs=[
            pl.BlockSpec((tile, width), lambda i: (i, 0)),
            pl.BlockSpec((1, width), lambda i: (0, 0)),
        ],
        out_specs=[pl.BlockSpec((line, tile, rows), lambda i: (0, i, 0))] * 2,
        compiler_params=params(),
        cost_estimate=pl.CostEstimate(
            flops=6 * length * width, bytes_accessed=4 * length * width, transcendentals=0
        ),
        name="norm_columns",
    )(states, gain.reshape(1, width))


def accumulate(total, states, slots, dtype=jnp.float32):
    _, length, depth = states.shape
    width = slots[0][0][2].shape[1]
    tile = min(256, length)
    count = len(slots)
    numbers, weights, entries = [], [], []
    for slot in slots:
        owner, which = jnp.int32(0), jnp.int32(0)
        for number, (holds, other, _) in enumerate(slot):
            owner = jnp.where(holds, other, owner)
            which = jnp.where(holds, number, which)
        numbers += [owner, which]
        here = []
        for _, _, weight in slot:
            known = [i for i, other in enumerate(weights) if other is weight]
            here.append(known[0] if known else len(weights))
            if not known:
                weights.append(weight)
        entries.append(here)
    numbers = jnp.stack([jnp.asarray(number, jnp.int32) for number in numbers])

    def kernel(numbers_ref, *refs):
        state_refs, weight_refs = refs[:count], refs[count : count + len(weights)]
        out_ref, sum_ref = refs[-2:]
        if total is None:
            sum_ref[...] = jnp.zeros_like(sum_ref)
        else:
            sum_ref[...] = refs[count + len(weights)][...]

        def add(state_ref, weight_ref):
            sum_ref[...] += jnp.dot(
                state_ref[0], weight_ref[...], preferred_element_type=jnp.float32
            )

        for slot in range(count):
            for number, entry in enumerate(entries[slot]):
                one = functools.partial(add, state_refs[slot], weight_refs[entry])
                if len(entries[slot]) == 1:
                    one()
                else:
                    pl.when(numbers_ref[2 * slot + 1] == number)(one)
        out_ref[...] = sum_ref[...].astype(out_ref.dtype)

    def state_spec(slot):
        return pl.BlockSpec((1, tile, depth), lambda i, chosen: (chosen[2 * slot], i, 0))

    before = [] if total is None else [total]
    row_spec = pl.BlockSpec((tile, width), lambda i, chosen: (i, 0))
    return pl.pallas_call(
        kernel,
        grid_spec=pltpu.PrefetchScalarGridSpec(
            num_scalar_prefetch=1,
            grid=(length // tile,),
            in_specs=[state_spec(slot) for slot in range(count)]
            + whole_vmem(len(weights))
            + [row_spec] * len(before),
            out_specs=row_spec,
            scratch_shapes=[pltpu.VMEM((tile, width), jnp.float32)],
        ),
        out_shape=jax.ShapeDtypeStruct((length, width), dtype),
        compiler_params=params(24),
        cost_estimate=pl.CostEstimate(
            flops=2 * count * length * depth * width,
            bytes_accessed=2 * count * depth * (length + width) + 8 * length * width,
            transcendentals=0,
        ),
        name="accumulate",
    )(numbers, *([states] * count), *weights, *before)


def attention(kept, got, cosine_table, sine_table):
    length, width = kept.shape
    heads = width // HD - 2
    tile = min(128, length)

    def rope(u, cosine, sine):
        return u * cosine + pltpu.roll(u, HD // 2, 1) * sine

    def kernel(kept_ref, got_ref, cos_ref, sin_ref, out_ref):
        def columns(index, here=slice(None)):
            there = slice(index * HD, (index + 1) * HD)
            return kept_ref[here, there] + got_ref[here, there].astype(jnp.float32)

        keys = rope(columns(heads), cos_ref[...], sin_ref[...]).astype(jnp.bfloat16)
        values = columns(heads + 1).astype(jnp.bfloat16)
        for begin in range(0, length, tile):
            here, upto = slice(begin, begin + tile), begin + tile
            row = lax.broadcasted_iota(jnp.int32, (tile, upto), 0) + begin
            seen = row >= lax.broadcasted_iota(jnp.int32, (tile, upto), 1)
            for head in range(heads):
                query = rope(columns(head, here), cos_ref[here], sin_ref[here])
                query = (query * HD**-0.5).astype(jnp.bfloat16)
                scores = lax.dot_general(
                    query,
                    keys[:upto],
                    (((1,), (1,)), ((), ())),
                    preferred_element_type=jnp.float32,
                )
                scores = jnp.where(seen, scores, -jnp.inf)
                raised = jnp.exp(scores - jnp.max(scores, axis=1, keepdims=True))
                weights = raised * (1.0 / jnp.sum(raised, axis=1, keepdims=True))
                out_ref[here, head * HD : (head + 1) * HD] = jnp.dot(
                    weights.astype(jnp.bfloat16), values[:upto], preferred_element_type=jnp.float32
                ).astype(jnp.bfloat16)

    return pl.pallas_call(
        kernel,
        out_shape=jax.ShapeDtypeStruct((length, heads * HD), jnp.bfloat16),
        in_specs=whole_vmem(4),
        out_specs=pl.BlockSpec(memory_space=pltpu.VMEM),
        compiler_params=params(),
        cost_estimate=pl.CostEstimate(
            flops=4 * heads * length * length * HD,
            bytes_accessed=9 * length * width,
            transcendentals=heads * length * length,
        ),
        name="attention",
    )(kept, got, cosine_table, sine_table)


def by_source(mine, other, n_tensor):
    kept, depth = mine.shape[0] // n_tensor, mine.shape[1]

    def kernel(mine_ref, other_ref, out_ref):
        index = lax.axis_index("tensor")
        for distance in range(n_tensor):
            columns = pl.ds(pl.multiple_of((index ^ distance) * depth, depth), depth)
            rows = slice(distance * kept, (distance + 1) * kept)
            out_ref[:kept, columns] = mine_ref[rows]
            out_ref[kept:, columns] = other_ref[rows]

    return pl.pallas_call(
        kernel,
        out_shape=jax.ShapeDtypeStruct((2 * kept, n_tensor * depth), mine.dtype),
        in_specs=whole_vmem(2),
        out_specs=pl.BlockSpec(memory_space=pltpu.VMEM),
        compiler_params=params(),
        name="by_source",
    )(mine, other)


def lay_out(blocks):
    kept = blocks[0][0].shape[0]
    half = sum(block.shape[1] for block in blocks[0])

    def kernel(*refs):
        out_ref = refs[-1]
        core = own_core()
        for flag in range(2):

            @pl.when(core == flag)
            def _():
                entry = 0
                for side in range(2):
                    begin = (flag ^ side) * half
                    for block in blocks[side]:
                        stop = begin + block.shape[1]
                        out_ref[:, begin:stop] = refs[entry][...]
                        begin, entry = stop, entry + 1

    flat = [block for side in blocks for block in side]
    return pl.pallas_call(
        kernel,
        out_shape=jax.ShapeDtypeStruct((kept, 2 * half), flat[0].dtype),
        in_specs=whole_vmem(len(flat)),
        out_specs=pl.BlockSpec(memory_space=pltpu.VMEM),
        compiler_params=params(),
        name="lay_out",
    )(*flat)


def body(
    train_states, qkv_cotangent, w_master, moment_one, moment_two, prompt_states, norm_gain, w_out
):
    n_dp = lax.axis_size("dp")
    n_tensor = lax.axis_size("tensor")
    line = n_dp // 2
    tensor_index = lax.axis_index("tensor")
    core, place = own_core(), own_place()
    siblings = [(i, i ^ 1) for i in range(n_dp)]
    rows, slice_width = w_master.shape
    tokens, width = train_states.shape
    length = prompt_states.shape[0]
    query_width = slice_width - 2 * HD

    kept_states, sent_states = norm_columns(prompt_states, norm_gain, rows, line)
    got_states = lax.ppermute(sent_states, "dp", siblings)

    packed = pack_columns(train_states, rows, line, tokens // n_tensor)
    pieces = [packed[0]] + [
        lax.ppermute(
            packed[distance], "dp", line_pairs([(i, i ^ distance) for i in range(line)])
        )
        for distance in range(1, line)
    ]
    pieces = tie(pieces, kept_states)

    cotangents = LineGather(tie((qkv_cotangent,), *pieces)[0], place, line)
    cotangents.hop()
    spread = PlaneGather(stack_pieces(pieces), n_tensor)
    for _ in range(2, line - 1):
        cotangents.hop()
    spread.second(*cotangents.arrived())
    cotangents.hop(*spread.passed()) if n_tensor == 4 else cotangents.hop()
    all_cotangents = place_cotangents((cotangents.low, cotangents.high), line, n_tensor)

    core_width = width // 2
    early_width = core_width // EARLY_SHARE
    begin = core * core_width
    (w_first,) = tie((w_out,), packed[0])
    w_early = lax.dynamic_slice(w_first, (0, begin), (w_out.shape[0], early_width))
    w_rest = lax.dynamic_slice(
        w_out, (0, begin + early_width), (w_out.shape[0], core_width - early_width)
    )
    early_weight = lax.all_gather(w_early, "tensor", axis=0, tiled=True)
    (w_rest,) = tie((w_rest,), spread.blocks, cotangents.arrived(), early_weight)
    rest_weight = lax.all_gather(w_rest, "tensor", axis=0, tiled=True)

    sent = gradient_term(spread.blocks, all_cotangents, True)
    got = lax.ppermute(sent, "dp", siblings)
    kept = gradient_term(spread.blocks, all_cotangents, False)
    update_dir, weight = adam_rows(kept, got, w_master, moment_one, moment_two)

    weights = LineGather(weight, place, line)

    def add(total, states, steps, dtype=jnp.float32):
        return accumulate(total, states, [weights.slot(step) for step in steps], dtype)

    for _ in range(1, line - 1):
        weights.hop()
    own_total = add(None, kept_states, range(line - 2))
    other_total = add(None, got_states, range(line - 2))
    cosine_table, sine_table = rope_tables(length, HD)
    cosine_table, sine_table, own_total, other_total = tie(
        (cosine_table, sine_table, own_total, other_total)
    )
    weights.hop(own_total, other_total, cosine_table, sine_table)
    other_total = add(other_total, got_states, [line - 2])
    own_total = add(own_total, kept_states, [line - 2])
    other_total = add(other_total, got_states, [line - 1], jnp.bfloat16)
    got_total = lax.ppermute(other_total, "dp", siblings)
    own_total = add(own_total, kept_states, [line - 1])
    attended = attention(own_total, got_total, cosine_table, sine_table)
    attended, rest_weight = tie((attended, rest_weight))

    kept_rows = length // n_tensor
    heads = []
    for distance in range(n_tensor):
        target = tensor_index ^ distance
        block = lax.dynamic_slice(attended, (target * kept_rows, 0), (kept_rows, query_width))
        if distance:
            block = lax.ppermute(block, "tensor", [(j, j ^ distance) for j in range(n_tensor)])
        heads.append(block)
    (mine,) = stack_pieces([head[None] for head in heads])
    other = lax.ppermute(mine, "dp", siblings)
    both = by_source(mine, other, n_tensor)
    mine, sent = [], []
    for weight in (early_weight, rest_weight):
        made = jnp.dot(both, weight, preferred_element_type=jnp.float32).astype(jnp.bfloat16)
        mine.append(made[:kept_rows])
        sent.append(made[kept_rows:])
    summed = lay_out((mine, [lax.ppermute(rows, "dp", siblings) for rows in sent]))
    return (update_dir, summed)


def solution(mesh):
    placed = (
        P("dp", None),
        P("dp", "tensor"),
        P("dp", "tensor"),
        P("dp", "tensor"),
        P("dp", "tensor"),
        P("dp", None),
        P(),
        P("tensor", None),
    )
    return jax.shard_map(
        body,
        mesh=mesh,
        in_specs=placed,
        out_specs=(P("dp", "tensor"), P(("dp", "tensor"), None)),
        check_vma=False,
    )
```

```python
import functools

import jax
import jax.numpy as jnp
from jax import lax
from jax.experimental import pallas as pl
from jax.experimental.pallas import tpu as pltpu
from jax.sharding import PartitionSpec as P

HD = 128


beta_one = 0.9
beta_two = 0.95
bias_one = 1.0 - 0.9**8
bias_two = 1.0 - 0.95**8
learn_rate = 0.002
adam_eps = 1e-08
norm_eps = 1e-05
rope_base = 500000.0

MIB = 1024 * 1024
EARLY_SHARE = 8


def rope_tables(length, head_size):
    half_width = head_size // 2
    exponent = jnp.arange(half_width, dtype=jnp.float32) * (2.0 / head_size)
    inverse = jnp.power(jnp.float32(rope_base), -exponent)
    position = jnp.arange(length, dtype=jnp.float32)
    angles = position[:, None] * inverse[None, :]
    cosine_table = jnp.concatenate([jnp.cos(angles), jnp.cos(angles)], axis=1)
    sine_table = jnp.concatenate([-jnp.sin(angles), jnp.sin(angles)], axis=1)
    return (cosine_table, sine_table)


def params(mib=16):
    return pltpu.CompilerParams(vmem_limit_bytes=mib * MIB)


def whole_vmem(count):
    return [pl.BlockSpec(memory_space=pltpu.VMEM)] * count


def own_core():
    return lax.rem(lax.axis_index("dp"), 2)


def own_place():
    return lax.div(lax.axis_index("dp"), 2)


def pack_columns(train_states, rows, line, quarter):
    def kernel(index_ref, train_ref, *outs):
        place = own_place()
        for distance in range(line):
            for owner in range(2):
                column = pl.multiple_of(((place ^ distance) * 2 + owner) * rows, 128)
                outs[distance][owner] = train_ref[:, pl.ds(column, rows)]

    shapes = [jax.ShapeDtypeStruct((2, quarter, rows), train_states.dtype)] * line
    index = jnp.reshape(lax.axis_index("tensor"), (1,)).astype(jnp.int32)
    return pl.pallas_call(
        kernel,
        grid_spec=pltpu.PrefetchScalarGridSpec(
            num_scalar_prefetch=1,
            grid=(1,),
            in_specs=[
                pl.BlockSpec((quarter, train_states.shape[1]), lambda i, chosen: (chosen[0], 0))
            ],
            out_specs=[pl.BlockSpec(s.shape, lambda i, chosen: (0, 0, 0)) for s in shapes],
        ),
        out_shape=shapes,
        compiler_params=params(56),
        name="pack_columns",
    )(index, train_states)


def stack_pieces(pieces):
    outer, height, width = pieces[0].shape
    count = len(pieces)

    def kernel(*refs):
        for which in range(outer):
            for i in range(count):
                refs[count + which][i * height : (i + 1) * height] = refs[i][which]

    return pl.pallas_call(
        kernel,
        out_shape=[jax.ShapeDtypeStruct((count * height, width), pieces[0].dtype)] * outer,
        in_specs=whole_vmem(count),
        out_specs=whole_vmem(outer),
        compiler_params=params(),
        name="stack_pieces",
    )(*pieces)


def line_pairs(places):
    return [(2 * a + core, 2 * b + core) for a, b in places for core in range(2)]


def tie(arrays, *others):
    return lax.optimization_barrier((tuple(arrays), others))[0]


class LineGather:
    def __init__(self, block, place, count, merge_last=False):
        self.place, self.count, self.merge_last = place, count, merge_last
        self.low, self.high = [block], [block]

    def hop(self, *behind):
        step, count = len(self.low), self.count
        up, down = self.low[-1], self.high[-1]
        if behind:
            up, down = tie((up, down), *behind)
        right = line_pairs([(i, i + 1) for i in range(step - 1, count - 1)])
        left = line_pairs([(i, i - 1) for i in range(1, count - step + 1)])
        if self.merge_last and step == count - 1:
            both = lax.ppermute(jnp.where(self.place == count - 2, up, down), "dp", right + left)
            self.low.append(both)
            self.high.append(both)
            return
        self.low.append(lax.ppermute(up, "dp", right))
        self.high.append(lax.ppermute(down, "dp", left))

    def arrived(self):
        return self.low[-1], self.high[-1]

    def slot(self, step):
        if step == 0:
            return self.place, self.low[0]
        sides = (self.low, self.high)
        choices = line_choice(step, self.place, self.count)
        _, side, entry, owner = choices[-1]
        block = sides[side][entry]
        for holds, side, entry, other in reversed(choices[:-1]):
            block = jnp.where(holds, sides[side][entry], block)
            owner = jnp.where(holds, other, owner)
        return owner, block


def line_choice(step, place, count):
    is_low, is_high = place >= step, place <= count - 1 - step
    spare = count - step
    return [
        (is_low, 0, step, place - step),
        (jnp.logical_and(jnp.logical_not(is_low), is_high), 1, step, place + step),
        (
            jnp.logical_and(jnp.logical_not(is_low), jnp.logical_not(is_high)),
            1,
            spare,
            place + spare,
        ),
    ][: 2 if 2 * step <= count else 3]


def place_cotangents(arrivals, line, n_tensor):
    tokens, width = arrivals[0][0].shape
    quarter = tokens // n_tensor
    low = [a.reshape(n_tensor, quarter, width) for a in arrivals[0]]
    high = [a.reshape(n_tensor, quarter, width) for a in arrivals[1][1:]]

    def kernel(*refs):
        low_refs = refs[: len(low)]
        high_refs = [low_refs[0]] + list(refs[len(low) : len(low) + len(high)])
        out_ref = refs[-1]
        place = own_place()

        def put(owner, source):
            begin = pl.multiple_of((owner ^ place) * quarter, quarter)
            out_ref[:, pl.ds(begin, quarter)] = source[...]

        put(place, low_refs[0])
        for step in range(1, line):
            for holds, side, entry, owner in line_choice(step, place, line):
                pl.when(holds)(functools.partial(put, owner, (low_refs, high_refs)[side][entry]))

    return pl.pallas_call(
        kernel,
        out_shape=jax.ShapeDtypeStruct((n_tensor, line * quarter, width), low[0].dtype),
        in_specs=whole_vmem(len(low) + len(high)),
        out_specs=pl.BlockSpec(memory_space=pltpu.VMEM),
        compiler_params=params(),
        name="place_cotangents",
    )(*low, *high)


def plane_permute(block, count, distance):
    return lax.ppermute(block, "tensor", [(j, j ^ distance) for j in range(count)])


class PlaneGather:
    def __init__(self, pair, count):
        self.count = count
        if count != 4:
            own = lax.axis_index("tensor")
            gathered = [lax.all_gather(block, "tensor", axis=0) for block in pair]
            self.blocks = [
                [lax.dynamic_index_in_dim(g, own ^ b, 0, keepdims=False) for g in gathered]
                for b in range(count)
            ]
            return
        one, two = [None, None], [None, None]
        for owner in range(2):
            one[owner] = plane_permute(pair[owner], count, 1)
            two[1 - owner] = plane_permute(pair[1 - owner], count, 2)
        self.blocks = [list(pair), one, two]

    def passed(self):
        return [self.blocks[1][0], self.blocks[2][1]]

    def second(self, *behind):
        if self.count == 4:
            up, down = tie(self.passed(), *behind)
            self.blocks.append(
                [plane_permute(up, self.count, 2), plane_permute(down, self.count, 1)]
            )


def gradient_term(blocks, cotangents, sibling):
    n_tensor, depth, width = cotangents.shape
    size = blocks[0][0].shape[1]
    flat = [block for pair in blocks for block in pair]

    def kernel(*refs):
        cotangent_ref, out_ref = refs[len(flat) :]
        index = lax.axis_index("tensor")
        owner = 1 - own_core() if sibling else own_core()
        total = None
        for distance in range(n_tensor):
            lower, upper = refs[2 * distance : 2 * distance + 2]
            product = lax.dot_general(
                jnp.where(owner == 0, lower[...], upper[...]),
                cotangent_ref[index ^ distance],
                (((0,), (0,)), ((), ())),
                preferred_element_type=jnp.float32,
            )
            total = product if total is None else total + product
        out_ref[...] = total.astype(out_ref.dtype)

    return pl.pallas_call(
        kernel,
        out_shape=jax.ShapeDtypeStruct((size, width), jnp.bfloat16 if sibling else jnp.float32),
        in_specs=whole_vmem(len(flat) + 1),
        out_specs=pl.BlockSpec(memory_space=pltpu.VMEM),
        compiler_params=params(28),
        cost_estimate=pl.CostEstimate(
            flops=2 * n_tensor * depth * size * width,
            bytes_accessed=n_tensor * depth * (4 * size + 2 * width) + 4 * size * width,
            transcendentals=0,
        ),
        name="gradient_term",
    )(*flat, cotangents)


def adam_rows(kept, got, w_master, moment_one, moment_two):
    rows, width = kept.shape
    tile = min(128, rows)

    def kernel(kept_ref, got_ref, master_ref, one_ref, two_ref, update_ref, weight_ref):
        gradient = kept_ref[...] + got_ref[...].astype(jnp.float32)
        moment_new = beta_one * one_ref[...] + (1.0 - beta_one) * gradient
        second_new = beta_two * two_ref[...] + (1.0 - beta_two) * gradient * gradient
        scaled = second_new * (1.0 / bias_two)
        update = moment_new * (1.0 / bias_one) / (scaled * lax.rsqrt(scaled) + adam_eps)
        update_ref[...] = update
        weight_ref[...] = (master_ref[...] - learn_rate * update).astype(weight_ref.dtype)

    here = pl.BlockSpec((tile, width), lambda i: (i, 0))
    return pl.pallas_call(
        kernel,
        grid=(rows // tile,),
        out_shape=[
            jax.ShapeDtypeStruct((rows, width), jnp.float32),
            jax.ShapeDtypeStruct((rows, width), jnp.bfloat16),
        ],
        in_specs=[here] * 5,
        out_specs=[here] * 2,
        compiler_params=params(),
        cost_estimate=pl.CostEstimate(
            flops=16 * rows * width, bytes_accessed=24 * rows * width, transcendentals=rows * width
        ),
        name="adam_rows",
    )(kept, got, w_master, moment_one, moment_two)


def norm_columns(states, gain, rows, line):
    length, width = states.shape
    tile = 64

    def kernel(states_ref, gain_ref, kept, sent):
        core = own_core()
        total = jnp.zeros((tile, 1), jnp.float32)
        for block in range(2 * line):
            piece = states_ref[:, block * rows : (block + 1) * rows].astype(jnp.float32)
            total = total + jnp.sum(piece * piece, axis=1, keepdims=True)
        scale = lax.rsqrt(total / width + norm_eps)
        for flag in range(2):

            @pl.when(core == flag)
            def _():
                for block in range(2 * line):
                    out = kept if block % 2 == flag else sent
                    columns = slice(block * rows, (block + 1) * rows)
                    piece = states_ref[:, columns].astype(jnp.float32)
                    out[block // 2] = (piece * scale * gain_ref[:, columns]).astype(out.dtype)

    return pl.pallas_call(
        kernel,
        grid=(length // tile,),
        out_shape=[jax.ShapeDtypeStruct((line, length, rows), jnp.bfloat16)] * 2,
        in_specs=[
            pl.BlockSpec((tile, width), lambda i: (i, 0)),
            pl.BlockSpec((1, width), lambda i: (0, 0)),
        ],
        out_specs=[pl.BlockSpec((line, tile, rows), lambda i: (0, i, 0))] * 2,
        compiler_params=params(),
        cost_estimate=pl.CostEstimate(
            flops=6 * length * width, bytes_accessed=4 * length * width, transcendentals=0
        ),
        name="norm_columns",
    )(states, gain.reshape(1, width))


def accumulate(totals, kept, got, slots, last=False):
    _, length, depth = kept.shape
    width = slots[0][1].shape[1]
    count = len(slots)
    tile = min(256, length)
    owners = jnp.stack([jnp.asarray(owner, jnp.int32) for owner, _ in slots])
    weights = [weight for _, weight in slots]

    def kernel(owners_ref, *refs):
        weight_refs = refs[2 * count : 3 * count]
        for side, out_ref in zip((1, 0), reversed(refs[-2:])):
            result = None if totals is None else refs[3 * count + side][...]
            for slot in range(count):
                product = jnp.dot(
                    refs[side * count + slot][0],
                    weight_refs[slot][...],
                    preferred_element_type=jnp.float32,
                )
                result = product if result is None else result + product
            out_ref[...] = result.astype(out_ref.dtype)

    def state_spec(slot):
        return pl.BlockSpec((1, tile, depth), lambda i, chosen: (chosen[slot], i, 0))

    before = list(totals or [])
    row_spec = pl.BlockSpec((tile, width), lambda i, chosen: (i, 0))
    return pl.pallas_call(
        kernel,
        grid_spec=pltpu.PrefetchScalarGridSpec(
            num_scalar_prefetch=1,
            grid=(length // tile,),
            in_specs=[state_spec(slot) for slot in range(count)] * 2
            + [pl.BlockSpec((depth, width), lambda i, chosen: (0, 0))] * count
            + [row_spec] * len(before),
            out_specs=[row_spec] * 2,
        ),
        out_shape=[
            jax.ShapeDtypeStruct((length, width), jnp.float32),
            jax.ShapeDtypeStruct((length, width), jnp.bfloat16 if last else jnp.float32),
        ],
        compiler_params=params(28),
        cost_estimate=pl.CostEstimate(
            flops=4 * count * length * depth * width,
            bytes_accessed=2 * count * depth * (2 * length + width) + 16 * length * width,
            transcendentals=0,
        ),
        name="accumulate",
    )(owners, *([kept] * count), *([got] * count), *weights, *before)


def attention(kept, got, cosine_table, sine_table):
    length, width = kept.shape
    heads = width // HD - 2
    tile = min(128, length)

    def rope(u, cosine, sine):
        return u * cosine + pltpu.roll(u, HD // 2, 1) * sine

    def kernel(kept_ref, got_ref, cos_ref, sin_ref, out_ref):
        def columns(index, here=slice(None)):
            there = slice(index * HD, (index + 1) * HD)
            return kept_ref[here, there] + got_ref[here, there].astype(jnp.float32)

        keys = rope(columns(heads), cos_ref[...], sin_ref[...]).astype(jnp.bfloat16)
        values = columns(heads + 1).astype(jnp.bfloat16)
        for begin in range(0, length, tile):
            here, upto = slice(begin, begin + tile), begin + tile
            row = lax.broadcasted_iota(jnp.int32, (tile, upto), 0) + begin
            seen = row >= lax.broadcasted_iota(jnp.int32, (tile, upto), 1)
            for head in range(heads):
                query = rope(columns(head, here), cos_ref[here], sin_ref[here])
                query = (query * HD**-0.5).astype(jnp.bfloat16)
                scores = lax.dot_general(
                    query,
                    keys[:upto],
                    (((1,), (1,)), ((), ())),
                    preferred_element_type=jnp.float32,
                )
                scores = jnp.where(seen, scores, -jnp.inf)
                raised = jnp.exp(scores - jnp.max(scores, axis=1, keepdims=True))
                weights = raised * (1.0 / jnp.sum(raised, axis=1, keepdims=True))
                out_ref[here, head * HD : (head + 1) * HD] = jnp.dot(
                    weights.astype(jnp.bfloat16), values[:upto], preferred_element_type=jnp.float32
                ).astype(jnp.bfloat16)

    return pl.pallas_call(
        kernel,
        out_shape=jax.ShapeDtypeStruct((length, heads * HD), jnp.bfloat16),
        in_specs=whole_vmem(4),
        out_specs=pl.BlockSpec(memory_space=pltpu.VMEM),
        compiler_params=params(),
        cost_estimate=pl.CostEstimate(
            flops=4 * heads * length * length * HD,
            bytes_accessed=9 * length * width,
            transcendentals=heads * length * length,
        ),
        name="attention",
    )(kept, got, cosine_table, sine_table)


def by_source(mine, other, n_tensor):
    kept, depth = mine.shape[0] // n_tensor, mine.shape[1]

    def kernel(mine_ref, other_ref, out_ref):
        index = lax.axis_index("tensor")
        for distance in range(n_tensor):
            columns = pl.ds(pl.multiple_of((index ^ distance) * depth, depth), depth)
            rows = slice(distance * kept, (distance + 1) * kept)
            out_ref[:kept, columns] = mine_ref[rows]
            out_ref[kept:, columns] = other_ref[rows]

    return pl.pallas_call(
        kernel,
        out_shape=jax.ShapeDtypeStruct((2 * kept, n_tensor * depth), mine.dtype),
        in_specs=whole_vmem(2),
        out_specs=pl.BlockSpec(memory_space=pltpu.VMEM),
        compiler_params=params(),
        name="by_source",
    )(mine, other)


def fetch(*arrays):
    parts = 4
    if sum(a.size * a.dtype.itemsize for a in arrays) > 20 * MIB:
        return arrays

    def kernel(*refs):
        sems = refs[-1]
        copies = []
        for which in range(len(arrays)):
            rows = arrays[which].shape[0] // parts
            for part in range(parts):
                here = pl.ds(part * rows, rows)
                copies.append(
                    pltpu.make_async_copy(
                        refs[which].at[here],
                        refs[len(arrays) + which].at[here],
                        sems.at[which * parts + part],
                    )
                )
        for copy in copies:
            copy.start()
        for copy in copies:
            copy.wait()

    return pl.pallas_call(
        kernel,
        out_shape=[jax.ShapeDtypeStruct(a.shape, a.dtype) for a in arrays],
        in_specs=[pl.BlockSpec(memory_space=pl.ANY)] * len(arrays),
        out_specs=whole_vmem(len(arrays)),
        scratch_shapes=[pltpu.SemaphoreType.DMA((parts * len(arrays),))],
        compiler_params=params(24),
        cost_estimate=pl.CostEstimate(
            flops=0, bytes_accessed=2 * sum(a.size * 2 for a in arrays), transcendentals=0
        ),
        name="fetch",
    )(*arrays)


def lay_out(blocks):
    kept = blocks[0][0].shape[0]
    half = sum(block.shape[1] for block in blocks[0])

    def kernel(*refs):
        out_ref = refs[-1]
        core = own_core()
        for flag in range(2):

            @pl.when(core == flag)
            def _():
                entry = 0
                for side in range(2):
                    begin = (flag ^ side) * half
                    for block in blocks[side]:
                        stop = begin + block.shape[1]
                        out_ref[:, begin:stop] = refs[entry][...]
                        begin, entry = stop, entry + 1

    flat = [block for side in blocks for block in side]
    return pl.pallas_call(
        kernel,
        out_shape=jax.ShapeDtypeStruct((kept, 2 * half), flat[0].dtype),
        in_specs=whole_vmem(len(flat)),
        out_specs=pl.BlockSpec(memory_space=pltpu.VMEM),
        compiler_params=params(),
        name="lay_out",
    )(*flat)


def body(
    train_states, qkv_cotangent, w_master, moment_one, moment_two, prompt_states, norm_gain, w_out
):
    n_dp = lax.axis_size("dp")
    n_tensor = lax.axis_size("tensor")
    line = n_dp // 2
    tensor_index = lax.axis_index("tensor")
    core, place = own_core(), own_place()
    siblings = [(i, i ^ 1) for i in range(n_dp)]
    rows, slice_width = w_master.shape
    tokens, width = train_states.shape
    length = prompt_states.shape[0]
    query_width = slice_width - 2 * HD

    kept_states, sent_states = norm_columns(prompt_states, norm_gain, rows, line)
    got_states = lax.ppermute(sent_states, "dp", siblings)

    packed = pack_columns(train_states, rows, line, tokens // n_tensor)
    pieces = [packed[0]] + [
        lax.ppermute(
            packed[distance], "dp", line_pairs([(i, i ^ distance) for i in range(line)])
        )
        for distance in range(1, line)
    ]
    pieces = tie(pieces, kept_states)

    stacked = stack_pieces(pieces)
    cotangents = LineGather(tie((qkv_cotangent,), *stacked)[0], place, line, True)
    cotangents.hop()
    spread = PlaneGather(stacked, n_tensor)
    for _ in range(2, line - 1):
        cotangents.hop()
    spread.second(*cotangents.arrived())
    cotangents.hop(*spread.passed()) if n_tensor == 4 else cotangents.hop()
    all_cotangents = place_cotangents((cotangents.low, cotangents.high), line, n_tensor)

    core_width = width // 2
    early_width = core_width // EARLY_SHARE
    begin = core * core_width
    (w_first,) = tie((w_out,), packed[0])
    w_early = lax.dynamic_slice(w_first, (0, begin), (w_out.shape[0], early_width))
    w_rest = lax.dynamic_slice(
        w_out, (0, begin + early_width), (w_out.shape[0], core_width - early_width)
    )
    early_weight = lax.all_gather(w_early, "tensor", axis=0, tiled=True)
    (w_rest,) = tie((w_rest,), spread.blocks, cotangents.arrived(), early_weight)
    rest_weight = lax.all_gather(w_rest, "tensor", axis=0, tiled=True)

    sent = gradient_term(spread.blocks, all_cotangents, True)
    got = lax.ppermute(sent, "dp", siblings)
    kept = gradient_term(spread.blocks, all_cotangents, False)
    update_dir, weight = adam_rows(kept, got, w_master, moment_one, moment_two)

    weights = LineGather(weight, place, line)

    def add(totals, steps, last=False):
        slots = [weights.slot(step) for step in steps]
        return accumulate(totals, kept_states, got_states, slots, last)

    for _ in range(1, line - 1):
        weights.hop()
    totals = add(None, range(line - 2))
    cosine_table, sine_table = rope_tables(length, HD)
    cosine_table, sine_table, *totals = tie((cosine_table, sine_table, *totals))
    weights.hop(*totals, cosine_table, sine_table)
    totals = add(totals, [line - 2])
    totals = add(totals, [line - 1], True)
    attended = attention(
        totals[0], lax.ppermute(totals[1], "dp", siblings), cosine_table, sine_table
    )

    kept_rows = length // n_tensor
    heads = []
    for distance in range(n_tensor):
        target = tensor_index ^ distance
        block = lax.dynamic_slice(attended, (target * kept_rows, 0), (kept_rows, query_width))
        if distance:
            block = lax.ppermute(block, "tensor", [(j, j ^ distance) for j in range(n_tensor)])
        heads.append(block)
    (mine,) = stack_pieces([head[None] for head in heads])
    fetched = fetch(early_weight, rest_weight)
    (mine,) = tie((mine,), *fetched)
    other = lax.ppermute(mine, "dp", siblings)
    both = by_source(mine, other, n_tensor)
    mine, sent = [], []
    for weight in fetched:
        made = jnp.dot(both, weight, preferred_element_type=jnp.float32).astype(jnp.bfloat16)
        mine.append(made[:kept_rows])
        sent.append(made[kept_rows:])
    summed = lay_out((mine, [lax.ppermute(rows, "dp", siblings) for rows in sent]))
    return (update_dir, summed)


def solution(mesh):
    placed = (
        P("dp", None),
        P("dp", "tensor"),
        P("dp", "tensor"),
        P("dp", "tensor"),
        P("dp", "tensor"),
        P("dp", None),
        P(),
        P("tensor", None),
    )
    return jax.shard_map(
        body,
        mesh=mesh,
        in_specs=placed,
        out_specs=(P("dp", "tensor"), P(("dp", "tensor"), None)),
        check_vma=False,
    )
```

```python
import functools

import jax
import jax.numpy as jnp
from jax import lax
from jax.experimental import pallas as pl
from jax.experimental.pallas import tpu as pltpu
from jax.sharding import PartitionSpec as P

HD = 128


beta_one = 0.9
beta_two = 0.95
bias_one = 1.0 - 0.9**8
bias_two = 1.0 - 0.95**8
learn_rate = 0.002
adam_eps = 1e-08
norm_eps = 1e-05
rope_base = 500000.0

MIB = 1024 * 1024
EARLY_SHARE = 8


def rope_tables(length, head_size):
    half_width = head_size // 2
    exponent = jnp.arange(half_width, dtype=jnp.float32) * (2.0 / head_size)
    inverse = jnp.power(jnp.float32(rope_base), -exponent)
    position = jnp.arange(length, dtype=jnp.float32)
    angles = position[:, None] * inverse[None, :]
    cosine_table = jnp.concatenate([jnp.cos(angles), jnp.cos(angles)], axis=1)
    sine_table = jnp.concatenate([-jnp.sin(angles), jnp.sin(angles)], axis=1)
    return (cosine_table, sine_table)


def params(mib=16):
    return pltpu.CompilerParams(vmem_limit_bytes=mib * MIB)


def whole_vmem(count):
    return [pl.BlockSpec(memory_space=pltpu.VMEM)] * count


def own_core():
    return lax.rem(lax.axis_index("dp"), 2)


def own_place():
    return lax.div(lax.axis_index("dp"), 2)


def pack_columns(train_states, w_out, rows, line, quarter, early_width):
    width = train_states.shape[1]
    early_blocks = width // 2 // early_width

    def kernel(chosen_ref, train_ref, w_out_ref, *outs):
        place = own_place()
        for distance in range(line):
            for owner in range(2):
                column = pl.multiple_of(((place ^ distance) * 2 + owner) * rows, 128)
                outs[distance][owner] = train_ref[:, pl.ds(column, rows)]
        outs[line][...] = w_out_ref[...]

    shapes = [jax.ShapeDtypeStruct((2, quarter, rows), train_states.dtype)] * line
    early = jax.ShapeDtypeStruct((w_out.shape[0], early_width), w_out.dtype)
    chosen = jnp.stack([lax.axis_index("tensor"), own_core() * early_blocks]).astype(jnp.int32)
    outs = pl.pallas_call(
        kernel,
        grid_spec=pltpu.PrefetchScalarGridSpec(
            num_scalar_prefetch=1,
            grid=(1,),
            in_specs=[
                pl.BlockSpec((quarter, width), lambda i, chosen: (chosen[0], 0)),
                pl.BlockSpec(early.shape, lambda i, chosen: (0, chosen[1])),
            ],
            out_specs=[pl.BlockSpec(s.shape, lambda i, chosen: (0, 0, 0)) for s in shapes]
            + [pl.BlockSpec(early.shape, lambda i, chosen: (0, 0))],
        ),
        out_shape=shapes + [early],
        compiler_params=params(56),
        name="pack_columns",
    )(chosen, train_states, w_out)
    return outs[:line], outs[line]


def stack_pieces(pieces):
    outer, height, width = pieces[0].shape
    count = len(pieces)

    def kernel(*refs):
        for which in range(outer):
            for i in range(count):
                refs[count + which][i * height : (i + 1) * height] = refs[i][which]

    return pl.pallas_call(
        kernel,
        out_shape=[jax.ShapeDtypeStruct((count * height, width), pieces[0].dtype)] * outer,
        in_specs=whole_vmem(count),
        out_specs=whole_vmem(outer),
        compiler_params=params(),
        name="stack_pieces",
    )(*pieces)


def line_pairs(places):
    return [(2 * a + core, 2 * b + core) for a, b in places for core in range(2)]


def tie(arrays, *others):
    return lax.optimization_barrier((tuple(arrays), others))[0]


class LineGather:
    def __init__(self, block, place, count, merge_last=False):
        self.place, self.count, self.merge_last = place, count, merge_last
        self.low, self.high = [block], [block]

    def hop(self, *behind):
        step, count = len(self.low), self.count
        up, down = self.low[-1], self.high[-1]
        if behind:
            up, down = tie((up, down), *behind)
        right = line_pairs([(i, i + 1) for i in range(step - 1, count - 1)])
        left = line_pairs([(i, i - 1) for i in range(1, count - step + 1)])
        if self.merge_last and step == count - 1:
            both = lax.ppermute(jnp.where(self.place == count - 2, up, down), "dp", right + left)
            self.low.append(both)
            self.high.append(both)
            return
        self.low.append(lax.ppermute(up, "dp", right))
        self.high.append(lax.ppermute(down, "dp", left))

    def arrived(self):
        return self.low[-1], self.high[-1]

    def slot(self, step):
        if step == 0:
            return self.place, self.low[0]
        sides = (self.low, self.high)
        choices = line_choice(step, self.place, self.count)
        _, side, entry, owner = choices[-1]
        block = sides[side][entry]
        for holds, side, entry, other in reversed(choices[:-1]):
            block = jnp.where(holds, sides[side][entry], block)
            owner = jnp.where(holds, other, owner)
        return owner, block


def line_choice(step, place, count):
    is_low, is_high = place >= step, place <= count - 1 - step
    spare = count - step
    return [
        (is_low, 0, step, place - step),
        (jnp.logical_and(jnp.logical_not(is_low), is_high), 1, step, place + step),
        (
            jnp.logical_and(jnp.logical_not(is_low), jnp.logical_not(is_high)),
            1,
            spare,
            place + spare,
        ),
    ][: 2 if 2 * step <= count else 3]


def place_cotangents(arrivals, line, n_tensor):
    tokens, width = arrivals[0][0].shape
    quarter = tokens // n_tensor
    low = [a.reshape(n_tensor, quarter, width) for a in arrivals[0]]
    high = [a.reshape(n_tensor, quarter, width) for a in arrivals[1][1:]]

    def kernel(*refs):
        low_refs = refs[: len(low)]
        high_refs = [low_refs[0]] + list(refs[len(low) : len(low) + len(high)])
        out_ref = refs[-1]
        place = own_place()

        def put(owner, source):
            begin = pl.multiple_of((owner ^ place) * quarter, quarter)
            out_ref[:, pl.ds(begin, quarter)] = source[...]

        put(place, low_refs[0])
        for step in range(1, line):
            for holds, side, entry, owner in line_choice(step, place, line):
                pl.when(holds)(functools.partial(put, owner, (low_refs, high_refs)[side][entry]))

    return pl.pallas_call(
        kernel,
        out_shape=jax.ShapeDtypeStruct((n_tensor, line * quarter, width), low[0].dtype),
        in_specs=whole_vmem(len(low) + len(high)),
        out_specs=pl.BlockSpec(memory_space=pltpu.VMEM),
        compiler_params=params(),
        name="place_cotangents",
    )(*low, *high)


def plane_permute(block, count, distance):
    return lax.ppermute(block, "tensor", [(j, j ^ distance) for j in range(count)])


class PlaneGather:
    def __init__(self, pair, count):
        self.count = count
        if count != 4:
            own = lax.axis_index("tensor")
            gathered = [lax.all_gather(block, "tensor", axis=0) for block in pair]
            self.blocks = [
                [lax.dynamic_index_in_dim(g, own ^ b, 0, keepdims=False) for g in gathered]
                for b in range(count)
            ]
            return
        one, two = [None, None], [None, None]
        for owner in range(2):
            one[owner] = plane_permute(pair[owner], count, 1)
            two[1 - owner] = plane_permute(pair[1 - owner], count, 2)
        self.blocks = [list(pair), one, two]

    def passed(self):
        return [self.blocks[1][0], self.blocks[2][1]]

    def second(self, *behind):
        if self.count == 4:
            up, down = tie(self.passed(), *behind)
            self.blocks.append(
                [plane_permute(up, self.count, 2), plane_permute(down, self.count, 1)]
            )


def gradient_term(blocks, cotangents, sibling):
    n_tensor, depth, width = cotangents.shape
    size = blocks[0][0].shape[1]
    flat = [block for pair in blocks for block in pair]

    def kernel(*refs):
        cotangent_ref, out_ref = refs[len(flat) :]
        index = lax.axis_index("tensor")
        owner = 1 - own_core() if sibling else own_core()
        total = None
        for distance in range(n_tensor):
            lower, upper = refs[2 * distance : 2 * distance + 2]
            product = lax.dot_general(
                jnp.where(owner == 0, lower[...], upper[...]),
                cotangent_ref[index ^ distance],
                (((0,), (0,)), ((), ())),
                preferred_element_type=jnp.float32,
            )
            total = product if total is None else total + product
        out_ref[...] = total.astype(out_ref.dtype)

    return pl.pallas_call(
        kernel,
        out_shape=jax.ShapeDtypeStruct((size, width), jnp.bfloat16 if sibling else jnp.float32),
        in_specs=whole_vmem(len(flat) + 1),
        out_specs=pl.BlockSpec(memory_space=pltpu.VMEM),
        compiler_params=params(28),
        cost_estimate=pl.CostEstimate(
            flops=2 * n_tensor * depth * size * width,
            bytes_accessed=n_tensor * depth * (4 * size + 2 * width) + 4 * size * width,
            transcendentals=0,
        ),
        name="gradient_term",
    )(*flat, cotangents)


def adam_rows(kept, got, w_master, moment_one, moment_two):
    rows, width = kept.shape
    tile = min(128, rows)

    def kernel(kept_ref, got_ref, master_ref, one_ref, two_ref, update_ref, weight_ref):
        gradient = kept_ref[...] + got_ref[...].astype(jnp.float32)
        moment_new = beta_one * one_ref[...] + (1.0 - beta_one) * gradient
        second_new = beta_two * two_ref[...] + (1.0 - beta_two) * gradient * gradient
        scaled = second_new * (1.0 / bias_two)
        update = moment_new * (1.0 / bias_one) / (scaled * lax.rsqrt(scaled) + adam_eps)
        update_ref[...] = update
        weight_ref[...] = (master_ref[...] - learn_rate * update).astype(weight_ref.dtype)

    here = pl.BlockSpec((tile, width), lambda i: (i, 0))
    return pl.pallas_call(
        kernel,
        grid=(rows // tile,),
        out_shape=[
            jax.ShapeDtypeStruct((rows, width), jnp.float32),
            jax.ShapeDtypeStruct((rows, width), jnp.bfloat16),
        ],
        in_specs=[here] * 5,
        out_specs=[here] * 2,
        compiler_params=params(),
        cost_estimate=pl.CostEstimate(
            flops=16 * rows * width, bytes_accessed=24 * rows * width, transcendentals=rows * width
        ),
        name="adam_rows",
    )(kept, got, w_master, moment_one, moment_two)


def norm_columns(states, gain, rows, line):
    length, width = states.shape
    tile = 64

    def kernel(states_ref, gain_ref, kept, sent):
        core = own_core()
        total = jnp.zeros((tile, 1), jnp.float32)
        for block in range(2 * line):
            piece = states_ref[:, block * rows : (block + 1) * rows].astype(jnp.float32)
            total = total + jnp.sum(piece * piece, axis=1, keepdims=True)
        scale = lax.rsqrt(total / width + norm_eps)
        for flag in range(2):

            @pl.when(core == flag)
            def _():
                for block in range(2 * line):
                    out = kept if block % 2 == flag else sent
                    columns = slice(block * rows, (block + 1) * rows)
                    piece = states_ref[:, columns].astype(jnp.float32)
                    out[block // 2] = (piece * scale * gain_ref[:, columns]).astype(out.dtype)

    return pl.pallas_call(
        kernel,
        grid=(length // tile,),
        out_shape=[jax.ShapeDtypeStruct((line, length, rows), jnp.bfloat16)] * 2,
        in_specs=[
            pl.BlockSpec((tile, width), lambda i: (i, 0)),
            pl.BlockSpec((1, width), lambda i: (0, 0)),
        ],
        out_specs=[pl.BlockSpec((line, tile, rows), lambda i: (0, i, 0))] * 2,
        compiler_params=params(),
        cost_estimate=pl.CostEstimate(
            flops=6 * length * width, bytes_accessed=4 * length * width, transcendentals=0
        ),
        name="norm_columns",
    )(states, gain.reshape(1, width))


def accumulate(totals, kept, got, slots, last=False):
    _, length, depth = kept.shape
    width = slots[0][1].shape[1]
    count = len(slots)
    tile = min(256, length)
    owners = jnp.stack([jnp.asarray(owner, jnp.int32) for owner, _ in slots])
    weights = [weight for _, weight in slots]

    def kernel(owners_ref, *refs):
        weight_refs = refs[2 * count : 3 * count]
        for side, out_ref in zip((1, 0), reversed(refs[-2:])):
            result = None if totals is None else refs[3 * count + side][...]
            for slot in range(count):
                product = jnp.dot(
                    refs[side * count + slot][0],
                    weight_refs[slot][...],
                    preferred_element_type=jnp.float32,
                )
                result = product if result is None else result + product
            out_ref[...] = result.astype(out_ref.dtype)

    def state_spec(slot):
        return pl.BlockSpec((1, tile, depth), lambda i, chosen: (chosen[slot], i, 0))

    before = list(totals or [])
    row_spec = pl.BlockSpec((tile, width), lambda i, chosen: (i, 0))
    return pl.pallas_call(
        kernel,
        grid_spec=pltpu.PrefetchScalarGridSpec(
            num_scalar_prefetch=1,
            grid=(length // tile,),
            in_specs=[state_spec(slot) for slot in range(count)] * 2
            + [pl.BlockSpec((depth, width), lambda i, chosen: (0, 0))] * count
            + [row_spec] * len(before),
            out_specs=[row_spec] * 2,
        ),
        out_shape=[
            jax.ShapeDtypeStruct((length, width), jnp.float32),
            jax.ShapeDtypeStruct((length, width), jnp.bfloat16 if last else jnp.float32),
        ],
        compiler_params=params(28),
        cost_estimate=pl.CostEstimate(
            flops=4 * count * length * depth * width,
            bytes_accessed=2 * count * depth * (2 * length + width) + 16 * length * width,
            transcendentals=0,
        ),
        name="accumulate",
    )(owners, *([kept] * count), *([got] * count), *weights, *before)


def attention(kept, got, cosine_table, sine_table):
    length, width = kept.shape
    heads = width // HD - 2
    tile = min(128, length)

    def rope(u, cosine, sine):
        return u * cosine + pltpu.roll(u, HD // 2, 1) * sine

    def kernel(kept_ref, got_ref, cos_ref, sin_ref, out_ref):
        def columns(index, here=slice(None)):
            there = slice(index * HD, (index + 1) * HD)
            return kept_ref[here, there] + got_ref[here, there].astype(jnp.float32)

        keys = rope(columns(heads), cos_ref[...], sin_ref[...]).astype(jnp.bfloat16)
        values = columns(heads + 1).astype(jnp.bfloat16)
        for begin in range(0, length, tile):
            here, upto = slice(begin, begin + tile), begin + tile
            row = lax.broadcasted_iota(jnp.int32, (tile, upto), 0) + begin
            seen = row >= lax.broadcasted_iota(jnp.int32, (tile, upto), 1)
            for head in range(heads):
                query = rope(columns(head, here), cos_ref[here], sin_ref[here])
                query = (query * HD**-0.5).astype(jnp.bfloat16)
                scores = lax.dot_general(
                    query,
                    keys[:upto],
                    (((1,), (1,)), ((), ())),
                    preferred_element_type=jnp.float32,
                )
                scores = jnp.where(seen, scores, -jnp.inf)
                raised = jnp.exp(scores - jnp.max(scores, axis=1, keepdims=True))
                weights = raised * (1.0 / jnp.sum(raised, axis=1, keepdims=True))
                out_ref[here, head * HD : (head + 1) * HD] = jnp.dot(
                    weights.astype(jnp.bfloat16), values[:upto], preferred_element_type=jnp.float32
                ).astype(jnp.bfloat16)

    return pl.pallas_call(
        kernel,
        out_shape=jax.ShapeDtypeStruct((length, heads * HD), jnp.bfloat16),
        in_specs=whole_vmem(4),
        out_specs=pl.BlockSpec(memory_space=pltpu.VMEM),
        compiler_params=params(),
        cost_estimate=pl.CostEstimate(
            flops=4 * heads * length * length * HD,
            bytes_accessed=9 * length * width,
            transcendentals=heads * length * length,
        ),
        name="attention",
    )(kept, got, cosine_table, sine_table)


def by_source(mine, other, n_tensor):
    kept, depth = mine.shape[0] // n_tensor, mine.shape[1]

    def kernel(mine_ref, other_ref, out_ref):
        index = lax.axis_index("tensor")
        for distance in range(n_tensor):
            columns = pl.ds(pl.multiple_of((index ^ distance) * depth, depth), depth)
            rows = slice(distance * kept, (distance + 1) * kept)
            out_ref[:kept, columns] = mine_ref[rows]
            out_ref[kept:, columns] = other_ref[rows]

    return pl.pallas_call(
        kernel,
        out_shape=jax.ShapeDtypeStruct((2 * kept, n_tensor * depth), mine.dtype),
        in_specs=whole_vmem(2),
        out_specs=pl.BlockSpec(memory_space=pltpu.VMEM),
        compiler_params=params(),
        name="by_source",
    )(mine, other)


def fetch(*arrays):
    parts = 4
    if sum(a.size * a.dtype.itemsize for a in arrays) > 20 * MIB:
        return arrays

    def kernel(*refs):
        sems = refs[-1]
        copies = []
        for which in range(len(arrays)):
            rows = arrays[which].shape[0] // parts
            for part in range(parts):
                here = pl.ds(part * rows, rows)
                copies.append(
                    pltpu.make_async_copy(
                        refs[which].at[here],
                        refs[len(arrays) + which].at[here],
                        sems.at[which * parts + part],
                    )
                )
        for copy in copies:
            copy.start()
        for copy in copies:
            copy.wait()

    return pl.pallas_call(
        kernel,
        out_shape=[jax.ShapeDtypeStruct(a.shape, a.dtype) for a in arrays],
        in_specs=[pl.BlockSpec(memory_space=pl.ANY)] * len(arrays),
        out_specs=whole_vmem(len(arrays)),
        scratch_shapes=[pltpu.SemaphoreType.DMA((parts * len(arrays),))],
        compiler_params=params(24),
        cost_estimate=pl.CostEstimate(
            flops=0, bytes_accessed=2 * sum(a.size * 2 for a in arrays), transcendentals=0
        ),
        name="fetch",
    )(*arrays)


def lay_out(blocks):
    kept = blocks[0][0].shape[0]
    half = sum(block.shape[1] for block in blocks[0])

    def kernel(*refs):
        out_ref = refs[-1]
        core = own_core()
        for flag in range(2):

            @pl.when(core == flag)
            def _():
                entry = 0
                for side in range(2):
                    begin = (flag ^ side) * half
                    for block in blocks[side]:
                        stop = begin + block.shape[1]
                        out_ref[:, begin:stop] = refs[entry][...]
                        begin, entry = stop, entry + 1

    flat = [block for side in blocks for block in side]
    return pl.pallas_call(
        kernel,
        out_shape=jax.ShapeDtypeStruct((kept, 2 * half), flat[0].dtype),
        in_specs=whole_vmem(len(flat)),
        out_specs=pl.BlockSpec(memory_space=pltpu.VMEM),
        compiler_params=params(),
        name="lay_out",
    )(*flat)


def body(
    train_states, qkv_cotangent, w_master, moment_one, moment_two, prompt_states, norm_gain, w_out
):
    n_dp = lax.axis_size("dp")
    n_tensor = lax.axis_size("tensor")
    line = n_dp // 2
    tensor_index = lax.axis_index("tensor")
    core, place = own_core(), own_place()
    siblings = [(i, i ^ 1) for i in range(n_dp)]
    rows, slice_width = w_master.shape
    tokens, width = train_states.shape
    length = prompt_states.shape[0]
    query_width = slice_width - 2 * HD

    kept_states, sent_states = norm_columns(prompt_states, norm_gain, rows, line)
    got_states = lax.ppermute(sent_states, "dp", siblings)

    core_width = width // 2
    early_width = core_width // EARLY_SHARE
    packed, w_early = pack_columns(
        train_states, w_out, rows, line, tokens // n_tensor, early_width
    )
    pieces = [packed[0]] + [
        lax.ppermute(
            packed[distance], "dp", line_pairs([(i, i ^ distance) for i in range(line)])
        )
        for distance in range(1, line)
    ]
    pieces = tie(pieces, kept_states)

    stacked = stack_pieces(pieces)
    cotangents = LineGather(tie((qkv_cotangent,), *stacked)[0], place, line, True)
    cotangents.hop()
    spread = PlaneGather(stacked, n_tensor)
    for _ in range(2, line - 1):
        cotangents.hop()
    spread.second(*cotangents.arrived())
    cotangents.hop(*spread.blocks[1], *spread.blocks[2])
    all_cotangents = place_cotangents((cotangents.low, cotangents.high), line, n_tensor)

    w_rest = lax.dynamic_slice(
        w_out,
        (0, core * core_width + early_width),
        (w_out.shape[0], core_width - early_width),
    )
    early_weight = lax.all_gather(w_early, "tensor", axis=0, tiled=True)
    (w_rest,) = tie((w_rest,), spread.blocks, cotangents.arrived(), early_weight)
    rest_weight = lax.all_gather(w_rest, "tensor", axis=0, tiled=True)

    sent = gradient_term(spread.blocks, all_cotangents, True)
    got = lax.ppermute(sent, "dp", siblings)
    kept = gradient_term(spread.blocks, all_cotangents, False)
    update_dir, weight = adam_rows(kept, got, w_master, moment_one, moment_two)

    weights = LineGather(weight, place, line)

    def add(totals, steps, last=False):
        slots = [weights.slot(step) for step in steps]
        return accumulate(totals, kept_states, got_states, slots, last)

    for _ in range(1, line - 1):
        weights.hop()
    totals = add(None, range(line - 2))
    cosine_table, sine_table = rope_tables(length, HD)
    cosine_table, sine_table, *totals = tie((cosine_table, sine_table, *totals))
    weights.hop(*totals, cosine_table, sine_table)
    totals = add(totals, [line - 2])
    totals = add(totals, [line - 1], True)
    attended = attention(
        totals[0], lax.ppermute(totals[1], "dp", siblings), cosine_table, sine_table
    )

    kept_rows = length // n_tensor
    heads = []
    for distance in range(n_tensor):
        target = tensor_index ^ distance
        block = lax.dynamic_slice(attended, (target * kept_rows, 0), (kept_rows, query_width))
        if distance:
            block = lax.ppermute(block, "tensor", [(j, j ^ distance) for j in range(n_tensor)])
        heads.append(block)
    fetched = fetch(early_weight, rest_weight)
    heads = tie(heads, *fetched)
    (mine,) = stack_pieces([head[None] for head in heads])
    other = lax.ppermute(mine, "dp", siblings)
    both = by_source(mine, other, n_tensor)
    mine, sent = [], []
    for weight in fetched:
        made = jnp.dot(both, weight, preferred_element_type=jnp.float32).astype(jnp.bfloat16)
        mine.append(made[:kept_rows])
        sent.append(made[kept_rows:])
    summed = lay_out((mine, [lax.ppermute(rows, "dp", siblings) for rows in sent]))
    return (update_dir, summed)


def solution(mesh):
    placed = (
        P("dp", None),
        P("dp", "tensor"),
        P("dp", "tensor"),
        P("dp", "tensor"),
        P("dp", "tensor"),
        P("dp", None),
        P(),
        P("tensor", None),
    )
    return jax.shard_map(
        body,
        mesh=mesh,
        in_specs=placed,
        out_specs=(P("dp", "tensor"), P(("dp", "tensor"), None)),
        check_vma=False,
    )
```

```python
import functools

import jax
import jax.numpy as jnp
from jax import lax
from jax.experimental import pallas as pl
from jax.experimental.pallas import tpu as pltpu
from jax.sharding import PartitionSpec as P

HD = 128


beta_one = 0.9
beta_two = 0.95
bias_one = 1.0 - 0.9**8
bias_two = 1.0 - 0.95**8
learn_rate = 0.002
adam_eps = 1e-08
norm_eps = 1e-05
rope_base = 500000.0

MIB = 1024 * 1024
EARLY_SHARE = 8


def rope_tables(length, head_size):
    half_width = head_size // 2
    exponent = jnp.arange(half_width, dtype=jnp.float32) * (2.0 / head_size)
    inverse = jnp.power(jnp.float32(rope_base), -exponent)
    position = jnp.arange(length, dtype=jnp.float32)
    angles = position[:, None] * inverse[None, :]
    cosine_table = jnp.concatenate([jnp.cos(angles), jnp.cos(angles)], axis=1)
    sine_table = jnp.concatenate([-jnp.sin(angles), jnp.sin(angles)], axis=1)
    return (cosine_table, sine_table)


def params(mib=16):
    return pltpu.CompilerParams(vmem_limit_bytes=mib * MIB)


def whole_vmem(count):
    return [pl.BlockSpec(memory_space=pltpu.VMEM)] * count


def own_core():
    return lax.rem(lax.axis_index("dp"), 2)


def own_place():
    return lax.div(lax.axis_index("dp"), 2)


def pack_columns(train_states, w_out, rows, line, quarter, early_width):
    width = train_states.shape[1]
    early_blocks = width // 2 // early_width

    def kernel(chosen_ref, train_ref, w_out_ref, *outs):
        place = own_place()
        for distance in range(line):
            for owner in range(2):
                column = pl.multiple_of(((place ^ distance) * 2 + owner) * rows, 128)
                outs[distance][owner] = train_ref[:, pl.ds(column, rows)]
        outs[line][...] = w_out_ref[...]

    shapes = [jax.ShapeDtypeStruct((2, quarter, rows), train_states.dtype)] * line
    early = jax.ShapeDtypeStruct((w_out.shape[0], early_width), w_out.dtype)
    chosen = jnp.stack([lax.axis_index("tensor"), own_core() * early_blocks]).astype(jnp.int32)
    outs = pl.pallas_call(
        kernel,
        grid_spec=pltpu.PrefetchScalarGridSpec(
            num_scalar_prefetch=1,
            grid=(1,),
            in_specs=[
                pl.BlockSpec((quarter, width), lambda i, chosen: (chosen[0], 0)),
                pl.BlockSpec(early.shape, lambda i, chosen: (0, chosen[1])),
            ],
            out_specs=[pl.BlockSpec(s.shape, lambda i, chosen: (0, 0, 0)) for s in shapes]
            + [pl.BlockSpec(early.shape, lambda i, chosen: (0, 0))],
        ),
        out_shape=shapes + [early],
        compiler_params=params(56),
        name="pack_columns",
    )(chosen, train_states, w_out)
    return outs[:line], outs[line]


def stack_pieces(pieces):
    outer, height, width = pieces[0].shape
    count = len(pieces)

    def kernel(*refs):
        for which in range(outer):
            for i in range(count):
                refs[count + which][i * height : (i + 1) * height] = refs[i][which]

    return pl.pallas_call(
        kernel,
        out_shape=[jax.ShapeDtypeStruct((count * height, width), pieces[0].dtype)] * outer,
        in_specs=whole_vmem(count),
        out_specs=whole_vmem(outer),
        compiler_params=params(),
        name="stack_pieces",
    )(*pieces)


def line_pairs(places):
    return [(2 * a + core, 2 * b + core) for a, b in places for core in range(2)]


def tie(arrays, *others):
    return lax.optimization_barrier((tuple(arrays), others))[0]


class LineGather:
    def __init__(self, block, place, count):
        self.place, self.count = place, count
        self.low, self.high = [block], [block]

    def hop(self, *behind):
        step, count = len(self.low), self.count
        up, down = self.low[-1], self.high[-1]
        if behind:
            up, down = tie((up, down), *behind)
        right = line_pairs([(i, i + 1) for i in range(step - 1, count - 1)])
        left = line_pairs([(i, i - 1) for i in range(1, count - step + 1)])
        self.low.append(lax.ppermute(up, "dp", right))
        self.high.append(lax.ppermute(down, "dp", left))

    def arrived(self):
        return self.low[-1], self.high[-1]

    def slot(self, step):
        if step == 0:
            return self.place, self.low[0]
        sides = (self.low, self.high)
        choices = line_choice(step, self.place, self.count)
        _, side, entry, owner = choices[-1]
        block = sides[side][entry]
        for holds, side, entry, other in reversed(choices[:-1]):
            block = jnp.where(holds, sides[side][entry], block)
            owner = jnp.where(holds, other, owner)
        return owner, block


def line_choice(step, place, count):
    is_low, is_high = place >= step, place <= count - 1 - step
    spare = count - step
    return [
        (is_low, 0, step, place - step),
        (jnp.logical_and(jnp.logical_not(is_low), is_high), 1, step, place + step),
        (
            jnp.logical_and(jnp.logical_not(is_low), jnp.logical_not(is_high)),
            1,
            spare,
            place + spare,
        ),
    ][: 2 if 2 * step <= count else 3]


def place_cotangents(blocks, n_tensor):
    tokens, width = blocks[0].shape
    quarter = tokens // n_tensor
    count = len(blocks)

    def kernel(*refs):
        for distance in range(count):
            refs[count][:, distance * quarter : (distance + 1) * quarter] = refs[distance][...]

    return pl.pallas_call(
        kernel,
        out_shape=jax.ShapeDtypeStruct((n_tensor, count * quarter, width), blocks[0].dtype),
        in_specs=whole_vmem(count),
        out_specs=pl.BlockSpec(memory_space=pltpu.VMEM),
        compiler_params=params(),
        name="place_cotangents",
    )(*[block.reshape(n_tensor, quarter, width) for block in blocks])


def plane_permute(block, count, distance):
    return lax.ppermute(block, "tensor", [(j, j ^ distance) for j in range(count)])


class PlaneGather:
    def __init__(self, pair, count):
        self.count = count
        if count != 4:
            own = lax.axis_index("tensor")
            gathered = [lax.all_gather(block, "tensor", axis=0) for block in pair]
            self.blocks = [
                [lax.dynamic_index_in_dim(g, own ^ b, 0, keepdims=False) for g in gathered]
                for b in range(count)
            ]
            return
        one, two = [None, None], [None, None]
        for owner in range(2):
            one[owner] = plane_permute(pair[owner], count, 1)
            two[1 - owner] = plane_permute(pair[1 - owner], count, 2)
        self.blocks = [list(pair), one, two]

    def passed(self):
        return [self.blocks[1][0], self.blocks[2][1]]

    def second(self, *behind):
        if self.count == 4:
            up, down = tie(self.passed(), *behind)
            self.blocks.append(
                [plane_permute(up, self.count, 2), plane_permute(down, self.count, 1)]
            )


def gradient_term(blocks, cotangents, sibling):
    n_tensor, depth, width = cotangents.shape
    size = blocks[0][0].shape[1]
    flat = [block for pair in blocks for block in pair]

    def kernel(*refs):
        cotangent_ref, out_ref = refs[len(flat) :]
        index = lax.axis_index("tensor")
        owner = 1 - own_core() if sibling else own_core()
        total = None
        for distance in range(n_tensor):
            lower, upper = refs[2 * distance : 2 * distance + 2]
            product = lax.dot_general(
                jnp.where(owner == 0, lower[...], upper[...]),
                cotangent_ref[index ^ distance],
                (((0,), (0,)), ((), ())),
                preferred_element_type=jnp.float32,
            )
            total = product if total is None else total + product
        out_ref[...] = total.astype(out_ref.dtype)

    return pl.pallas_call(
        kernel,
        out_shape=jax.ShapeDtypeStruct((size, width), jnp.bfloat16 if sibling else jnp.float32),
        in_specs=whole_vmem(len(flat) + 1),
        out_specs=pl.BlockSpec(memory_space=pltpu.VMEM),
        compiler_params=params(28),
        cost_estimate=pl.CostEstimate(
            flops=2 * n_tensor * depth * size * width,
            bytes_accessed=n_tensor * depth * (4 * size + 2 * width) + 4 * size * width,
            transcendentals=0,
        ),
        name="gradient_term",
    )(*flat, cotangents)


def adam_rows(kept, got, w_master, moment_one, moment_two):
    rows, width = kept.shape
    tile = min(128, rows)

    def kernel(kept_ref, got_ref, master_ref, one_ref, two_ref, update_ref, weight_ref):
        gradient = kept_ref[...] + got_ref[...].astype(jnp.float32)
        moment_new = beta_one * one_ref[...] + (1.0 - beta_one) * gradient
        second_new = beta_two * two_ref[...] + (1.0 - beta_two) * gradient * gradient
        scaled = second_new * (1.0 / bias_two)
        update = moment_new * (1.0 / bias_one) / (scaled * lax.rsqrt(scaled) + adam_eps)
        update_ref[...] = update
        weight_ref[...] = (master_ref[...] - learn_rate * update).astype(weight_ref.dtype)

    here = pl.BlockSpec((tile, width), lambda i: (i, 0))
    return pl.pallas_call(
        kernel,
        grid=(rows // tile,),
        out_shape=[
            jax.ShapeDtypeStruct((rows, width), jnp.float32),
            jax.ShapeDtypeStruct((rows, width), jnp.bfloat16),
        ],
        in_specs=[here] * 5,
        out_specs=[here] * 2,
        compiler_params=params(),
        cost_estimate=pl.CostEstimate(
            flops=16 * rows * width, bytes_accessed=24 * rows * width, transcendentals=rows * width
        ),
        name="adam_rows",
    )(kept, got, w_master, moment_one, moment_two)


def norm_columns(states, gain, rows, line):
    length, width = states.shape
    tile = 64

    def kernel(states_ref, gain_ref, kept, sent):
        core = own_core()
        total = jnp.zeros((tile, 1), jnp.float32)
        for block in range(2 * line):
            piece = states_ref[:, block * rows : (block + 1) * rows].astype(jnp.float32)
            total = total + jnp.sum(piece * piece, axis=1, keepdims=True)
        scale = lax.rsqrt(total / width + norm_eps)
        for flag in range(2):

            @pl.when(core == flag)
            def _():
                for block in range(2 * line):
                    out = kept if block % 2 == flag else sent
                    columns = slice(block * rows, (block + 1) * rows)
                    piece = states_ref[:, columns].astype(jnp.float32)
                    out[block // 2] = (piece * scale * gain_ref[:, columns]).astype(out.dtype)

    return pl.pallas_call(
        kernel,
        grid=(length // tile,),
        out_shape=[jax.ShapeDtypeStruct((line, length, rows), jnp.bfloat16)] * 2,
        in_specs=[
            pl.BlockSpec((tile, width), lambda i: (i, 0)),
            pl.BlockSpec((1, width), lambda i: (0, 0)),
        ],
        out_specs=[pl.BlockSpec((line, tile, rows), lambda i: (0, i, 0))] * 2,
        compiler_params=params(),
        cost_estimate=pl.CostEstimate(
            flops=6 * length * width, bytes_accessed=4 * length * width, transcendentals=0
        ),
        name="norm_columns",
    )(states, gain.reshape(1, width))


def accumulate(totals, kept, got, slots, last=False):
    _, length, depth = kept.shape
    width = slots[0][1].shape[1]
    count = len(slots)
    tile = min(256, length)
    owners = jnp.stack([jnp.asarray(owner, jnp.int32) for owner, _ in slots])
    weights = [weight for _, weight in slots]

    def kernel(owners_ref, *refs):
        weight_refs = refs[2 * count : 3 * count]
        for side, out_ref in zip((1, 0), reversed(refs[-2:])):
            result = None if totals is None else refs[3 * count + side][...]
            for slot in range(count):
                product = jnp.dot(
                    refs[side * count + slot][0],
                    weight_refs[slot][...],
                    preferred_element_type=jnp.float32,
                )
                result = product if result is None else result + product
            out_ref[...] = result.astype(out_ref.dtype)

    def state_spec(slot):
        return pl.BlockSpec((1, tile, depth), lambda i, chosen: (chosen[slot], i, 0))

    before = list(totals or [])
    row_spec = pl.BlockSpec((tile, width), lambda i, chosen: (i, 0))
    return pl.pallas_call(
        kernel,
        grid_spec=pltpu.PrefetchScalarGridSpec(
            num_scalar_prefetch=1,
            grid=(length // tile,),
            in_specs=[state_spec(slot) for slot in range(count)] * 2
            + [pl.BlockSpec((depth, width), lambda i, chosen: (0, 0))] * count
            + [row_spec] * len(before),
            out_specs=[row_spec] * 2,
        ),
        out_shape=[
            jax.ShapeDtypeStruct((length, width), jnp.float32),
            jax.ShapeDtypeStruct((length, width), jnp.bfloat16 if last else jnp.float32),
        ],
        compiler_params=params(20),
        cost_estimate=pl.CostEstimate(
            flops=4 * count * length * depth * width,
            bytes_accessed=2 * count * depth * (2 * length + width) + 16 * length * width,
            transcendentals=0,
        ),
        name="accumulate",
    )(owners, *([kept] * count), *([got] * count), *weights, *before)


def attention(kept, got, cosine_table, sine_table):
    length, width = kept.shape
    heads = width // HD - 2
    tile = min(128, length)

    def rope(u, cosine, sine):
        return u * cosine + pltpu.roll(u, HD // 2, 1) * sine

    def kernel(kept_ref, got_ref, cos_ref, sin_ref, out_ref):
        def columns(index, here=slice(None)):
            there = slice(index * HD, (index + 1) * HD)
            return kept_ref[here, there] + got_ref[here, there].astype(jnp.float32)

        keys = rope(columns(heads), cos_ref[...], sin_ref[...]).astype(jnp.bfloat16)
        values = columns(heads + 1).astype(jnp.bfloat16)
        for begin in range(0, length, tile):
            here, upto = slice(begin, begin + tile), begin + tile
            row = lax.broadcasted_iota(jnp.int32, (tile, upto), 0) + begin
            seen = row >= lax.broadcasted_iota(jnp.int32, (tile, upto), 1)
            for head in range(heads):
                query = rope(columns(head, here), cos_ref[here], sin_ref[here])
                query = (query * HD**-0.5).astype(jnp.bfloat16)
                scores = lax.dot_general(
                    query,
                    keys[:upto],
                    (((1,), (1,)), ((), ())),
                    preferred_element_type=jnp.float32,
                )
                scores = jnp.where(seen, scores, -jnp.inf)
                raised = jnp.exp(scores - jnp.max(scores, axis=1, keepdims=True))
                weights = raised * (1.0 / jnp.sum(raised, axis=1, keepdims=True))
                out_ref[here, head * HD : (head + 1) * HD] = jnp.dot(
                    weights.astype(jnp.bfloat16), values[:upto], preferred_element_type=jnp.float32
                ).astype(jnp.bfloat16)

    return pl.pallas_call(
        kernel,
        out_shape=jax.ShapeDtypeStruct((length, heads * HD), jnp.bfloat16),
        in_specs=whole_vmem(4),
        out_specs=pl.BlockSpec(memory_space=pltpu.VMEM),
        compiler_params=params(10),
        cost_estimate=pl.CostEstimate(
            flops=4 * heads * length * length * HD,
            bytes_accessed=9 * length * width,
            transcendentals=heads * length * length,
        ),
        name="attention",
    )(kept, got, cosine_table, sine_table)


def by_source(mine, other, n_tensor):
    kept, depth = mine.shape[0] // n_tensor, mine.shape[1]

    def kernel(mine_ref, other_ref, out_ref):
        index = lax.axis_index("tensor")
        for distance in range(n_tensor):
            columns = pl.ds(pl.multiple_of((index ^ distance) * depth, depth), depth)
            rows = slice(distance * kept, (distance + 1) * kept)
            out_ref[:kept, columns] = mine_ref[rows]
            out_ref[kept:, columns] = other_ref[rows]

    return pl.pallas_call(
        kernel,
        out_shape=jax.ShapeDtypeStruct((2 * kept, n_tensor * depth), mine.dtype),
        in_specs=whole_vmem(2),
        out_specs=pl.BlockSpec(memory_space=pltpu.VMEM),
        compiler_params=params(),
        name="by_source",
    )(mine, other)


def fetch(*arrays):
    parts = 4
    if sum(a.size * a.dtype.itemsize for a in arrays) > 20 * MIB:
        return arrays

    def kernel(*refs):
        sems = refs[-1]
        copies = []
        for which in range(len(arrays)):
            rows = arrays[which].shape[0] // parts
            for part in range(parts):
                here = pl.ds(part * rows, rows)
                copies.append(
                    pltpu.make_async_copy(
                        refs[which].at[here],
                        refs[len(arrays) + which].at[here],
                        sems.at[which * parts + part],
                    )
                )
        for copy in copies:
            copy.start()
        for copy in copies:
            copy.wait()

    return pl.pallas_call(
        kernel,
        out_shape=[jax.ShapeDtypeStruct(a.shape, a.dtype) for a in arrays],
        in_specs=[pl.BlockSpec(memory_space=pl.ANY)] * len(arrays),
        out_specs=whole_vmem(len(arrays)),
        scratch_shapes=[pltpu.SemaphoreType.DMA((parts * len(arrays),))],
        compiler_params=params(24),
        cost_estimate=pl.CostEstimate(
            flops=0, bytes_accessed=2 * sum(a.size * 2 for a in arrays), transcendentals=0
        ),
        name="fetch",
    )(*arrays)


def lay_out(blocks):
    kept = blocks[0][0].shape[0]
    half = sum(block.shape[1] for block in blocks[0])

    def kernel(*refs):
        out_ref = refs[-1]
        core = own_core()
        for flag in range(2):

            @pl.when(core == flag)
            def _():
                entry = 0
                for side in range(2):
                    begin = (flag ^ side) * half
                    for block in blocks[side]:
                        stop = begin + block.shape[1]
                        out_ref[:, begin:stop] = refs[entry][...]
                        begin, entry = stop, entry + 1

    flat = [block for side in blocks for block in side]
    return pl.pallas_call(
        kernel,
        out_shape=jax.ShapeDtypeStruct((kept, 2 * half), flat[0].dtype),
        in_specs=whole_vmem(len(flat)),
        out_specs=pl.BlockSpec(memory_space=pltpu.VMEM),
        compiler_params=params(),
        name="lay_out",
    )(*flat)


def body(
    train_states, qkv_cotangent, w_master, moment_one, moment_two, prompt_states, norm_gain, w_out
):
    n_dp = lax.axis_size("dp")
    n_tensor = lax.axis_size("tensor")
    line = n_dp // 2
    tensor_index = lax.axis_index("tensor")
    core, place = own_core(), own_place()
    siblings = [(i, i ^ 1) for i in range(n_dp)]
    rows, slice_width = w_master.shape
    tokens, width = train_states.shape
    length = prompt_states.shape[0]
    query_width = slice_width - 2 * HD

    kept_states, sent_states = norm_columns(prompt_states, norm_gain, rows, line)
    got_states = lax.ppermute(sent_states, "dp", siblings)

    core_width = width // 2
    early_width = core_width // EARLY_SHARE
    packed, w_early = pack_columns(
        train_states, w_out, rows, line, tokens // n_tensor, early_width
    )
    def across(block, distance):
        return lax.ppermute(block, "dp", line_pairs([(i, i ^ distance) for i in range(line)]))

    pieces = [packed[0]] + [across(packed[distance], distance) for distance in range(1, line)]
    pieces = tie(pieces, kept_states)

    cotangents = [qkv_cotangent, across(qkv_cotangent, 1)]
    spread = PlaneGather(stack_pieces(pieces), n_tensor)
    behind = pieces
    for distance in range(2, line):
        cotangents.append(across(tie((qkv_cotangent,), *behind)[0], distance))
        behind = cotangents[-1:]
    spread.second(cotangents[2], spread.blocks[1:])
    all_cotangents = place_cotangents(cotangents, n_tensor)

    w_rest = lax.dynamic_slice(
        w_out,
        (0, core * core_width + early_width),
        (w_out.shape[0], core_width - early_width),
    )
    early_weight = lax.all_gather(w_early, "tensor", axis=0, tiled=True)
    (w_rest,) = tie((w_rest,), spread.blocks, cotangents, early_weight)
    rest_weight = lax.all_gather(w_rest, "tensor", axis=0, tiled=True)

    sent = gradient_term(spread.blocks, all_cotangents, True)
    got = lax.ppermute(sent, "dp", siblings)
    kept = gradient_term(spread.blocks, all_cotangents, False)
    update_dir, weight = adam_rows(kept, got, w_master, moment_one, moment_two)

    weights = LineGather(weight, place, line)

    def add(totals, steps, last=False):
        slots = [weights.slot(step) for step in steps]
        return accumulate(totals, kept_states, got_states, slots, last)

    for _ in range(1, line - 1):
        weights.hop()
    totals = add(None, range(line - 2))
    cosine_table, sine_table = rope_tables(length, HD)
    cosine_table, sine_table, *totals = tie((cosine_table, sine_table, *totals))
    weights.hop(*totals, cosine_table, sine_table)
    totals = add(totals, [line - 2])
    totals = add(totals, [line - 1], True)
    attended = attention(
        totals[0], lax.ppermute(totals[1], "dp", siblings), cosine_table, sine_table
    )

    kept_rows = length // n_tensor
    heads = []
    for distance in range(n_tensor):
        target = tensor_index ^ distance
        block = lax.dynamic_slice(attended, (target * kept_rows, 0), (kept_rows, query_width))
        if distance:
            block = lax.ppermute(block, "tensor", [(j, j ^ distance) for j in range(n_tensor)])
        heads.append(block)
    fetched = fetch(early_weight, rest_weight)
    heads = tie(heads, *fetched)
    (mine,) = stack_pieces([head[None] for head in heads])
    other = lax.ppermute(mine, "dp", siblings)
    both = by_source(mine, other, n_tensor)
    mine, sent = [], []
    for weight in fetched:
        made = jnp.dot(both, weight, preferred_element_type=jnp.float32).astype(jnp.bfloat16)
        mine.append(made[:kept_rows])
        sent.append(made[kept_rows:])
    summed = lay_out((mine, [lax.ppermute(rows, "dp", siblings) for rows in sent]))
    return (update_dir, summed)


def solution(mesh):
    placed = (
        P("dp", None),
        P("dp", "tensor"),
        P("dp", "tensor"),
        P("dp", "tensor"),
        P("dp", "tensor"),
        P("dp", None),
        P(),
        P("tensor", None),
    )
    return jax.shard_map(
        body,
        mesh=mesh,
        in_specs=placed,
        out_specs=(P("dp", "tensor"), P(("dp", "tensor"), None)),
        check_vma=False,
    )
```

```python
import functools

import jax
import jax.numpy as jnp
from jax import lax
from jax.experimental import pallas as pl
from jax.experimental.pallas import tpu as pltpu
from jax.sharding import PartitionSpec as P

HD = 128


beta_one = 0.9
beta_two = 0.95
bias_one = 1.0 - 0.9**8
bias_two = 1.0 - 0.95**8
learn_rate = 0.002
adam_eps = 1e-08
norm_eps = 1e-05
rope_base = 500000.0

MIB = 1024 * 1024
EARLY_SHARE = 16


def rope_tables(length, head_size):
    half_width = head_size // 2
    exponent = jnp.arange(half_width, dtype=jnp.float32) * (2.0 / head_size)
    inverse = jnp.power(jnp.float32(rope_base), -exponent)
    position = jnp.arange(length, dtype=jnp.float32)
    angles = position[:, None] * inverse[None, :]
    cosine_table = jnp.concatenate([jnp.cos(angles), jnp.cos(angles)], axis=1)
    sine_table = jnp.concatenate([-jnp.sin(angles), jnp.sin(angles)], axis=1)
    return (cosine_table, sine_table)


def params(mib=16):
    return pltpu.CompilerParams(vmem_limit_bytes=mib * MIB)


def whole_vmem(count):
    return [pl.BlockSpec(memory_space=pltpu.VMEM)] * count


def own_core():
    return lax.rem(lax.axis_index("dp"), 2)


def own_place():
    return lax.div(lax.axis_index("dp"), 2)


def pack_columns(train_states, w_out, rows, line, quarter, early_width):
    width = train_states.shape[1]
    early_blocks = width // 2 // early_width

    def kernel(chosen_ref, train_ref, w_out_ref, *outs):
        place = own_place()
        for distance in range(line):
            for owner in range(2):
                column = pl.multiple_of(((place ^ distance) * 2 + owner) * rows, 128)
                outs[distance][owner] = train_ref[:, pl.ds(column, rows)]
        outs[line][...] = w_out_ref[...]

    shapes = [jax.ShapeDtypeStruct((2, quarter, rows), train_states.dtype)] * line
    early = jax.ShapeDtypeStruct((w_out.shape[0], early_width), w_out.dtype)
    chosen = jnp.stack([lax.axis_index("tensor"), own_core() * early_blocks]).astype(jnp.int32)
    outs = pl.pallas_call(
        kernel,
        grid_spec=pltpu.PrefetchScalarGridSpec(
            num_scalar_prefetch=1,
            grid=(1,),
            in_specs=[
                pl.BlockSpec((quarter, width), lambda i, chosen: (chosen[0], 0)),
                pl.BlockSpec(early.shape, lambda i, chosen: (0, chosen[1])),
            ],
            out_specs=[pl.BlockSpec(s.shape, lambda i, chosen: (0, 0, 0)) for s in shapes]
            + [pl.BlockSpec(early.shape, lambda i, chosen: (0, 0))],
        ),
        out_shape=shapes + [early],
        compiler_params=params(56),
        name="pack_columns",
    )(chosen, train_states, w_out)
    return outs[:line], outs[line]


def stack_pieces(pieces):
    outer, height, width = pieces[0].shape
    count = len(pieces)

    def kernel(*refs):
        for which in range(outer):
            for i in range(count):
                refs[count + which][i * height : (i + 1) * height] = refs[i][which]

    return pl.pallas_call(
        kernel,
        out_shape=[jax.ShapeDtypeStruct((count * height, width), pieces[0].dtype)] * outer,
        in_specs=whole_vmem(count),
        out_specs=whole_vmem(outer),
        compiler_params=params(),
        name="stack_pieces",
    )(*pieces)


def line_pairs(places):
    return [(2 * a + core, 2 * b + core) for a, b in places for core in range(2)]


def tie(arrays, *others):
    return lax.optimization_barrier((tuple(arrays), others))[0]


class LineGather:
    def __init__(self, block, place, count):
        self.place, self.count = place, count
        self.low, self.high = [block], [block]

    def hop(self, *behind):
        step, count = len(self.low), self.count
        up, down = self.low[-1], self.high[-1]
        if behind:
            up, down = tie((up, down), *behind)
        right = line_pairs([(i, i + 1) for i in range(step - 1, count - 1)])
        left = line_pairs([(i, i - 1) for i in range(1, count - step + 1)])
        self.low.append(lax.ppermute(up, "dp", right))
        self.high.append(lax.ppermute(down, "dp", left))

    def arrived(self):
        return self.low[-1], self.high[-1]

    def slot(self, step):
        if step == 0:
            return self.place, self.low[0]
        sides = (self.low, self.high)
        choices = line_choice(step, self.place, self.count)
        _, side, entry, owner = choices[-1]
        block = sides[side][entry]
        for holds, side, entry, other in reversed(choices[:-1]):
            block = jnp.where(holds, sides[side][entry], block)
            owner = jnp.where(holds, other, owner)
        return owner, block


def line_choice(step, place, count):
    is_low, is_high = place >= step, place <= count - 1 - step
    spare = count - step
    return [
        (is_low, 0, step, place - step),
        (jnp.logical_and(jnp.logical_not(is_low), is_high), 1, step, place + step),
        (
            jnp.logical_and(jnp.logical_not(is_low), jnp.logical_not(is_high)),
            1,
            spare,
            place + spare,
        ),
    ][: 2 if 2 * step <= count else 3]


def place_cotangents(blocks, n_tensor):
    tokens, width = blocks[0].shape
    quarter = tokens // n_tensor
    count = len(blocks)

    def kernel(*refs):
        for distance in range(count):
            refs[count][:, distance * quarter : (distance + 1) * quarter] = refs[distance][...]

    return pl.pallas_call(
        kernel,
        out_shape=jax.ShapeDtypeStruct((n_tensor, count * quarter, width), blocks[0].dtype),
        in_specs=whole_vmem(count),
        out_specs=pl.BlockSpec(memory_space=pltpu.VMEM),
        compiler_params=params(),
        name="place_cotangents",
    )(*[block.reshape(n_tensor, quarter, width) for block in blocks])


def plane_permute(block, count, distance):
    return lax.ppermute(block, "tensor", [(j, j ^ distance) for j in range(count)])


class PlaneGather:
    def __init__(self, pair, count):
        self.count = count
        if count != 4:
            own = lax.axis_index("tensor")
            gathered = [lax.all_gather(block, "tensor", axis=0) for block in pair]
            self.blocks = [
                [lax.dynamic_index_in_dim(g, own ^ b, 0, keepdims=False) for g in gathered]
                for b in range(count)
            ]
            return
        one, two = [None, None], [None, None]
        for owner in range(2):
            one[owner] = plane_permute(pair[owner], count, 1)
            two[1 - owner] = plane_permute(pair[1 - owner], count, 2)
        self.blocks = [list(pair), one, two]

    def passed(self):
        return [self.blocks[1][0], self.blocks[2][1]]

    def second(self, *behind):
        if self.count == 4:
            up, down = tie(self.passed(), *behind)
            self.blocks.append(
                [plane_permute(up, self.count, 2), plane_permute(down, self.count, 1)]
            )


def gradient_term(blocks, cotangents, sibling):
    n_tensor, depth, width = cotangents.shape
    size = blocks[0][0].shape[1]
    flat = [block for pair in blocks for block in pair]

    def kernel(*refs):
        cotangent_ref, out_ref = refs[len(flat) :]
        index = lax.axis_index("tensor")
        owner = 1 - own_core() if sibling else own_core()
        total = None
        for distance in range(n_tensor):
            lower, upper = refs[2 * distance : 2 * distance + 2]
            product = lax.dot_general(
                jnp.where(owner == 0, lower[...], upper[...]),
                cotangent_ref[index ^ distance],
                (((0,), (0,)), ((), ())),
                preferred_element_type=jnp.float32,
            )
            total = product if total is None else total + product
        out_ref[...] = total.astype(out_ref.dtype)

    return pl.pallas_call(
        kernel,
        out_shape=jax.ShapeDtypeStruct((size, width), jnp.bfloat16 if sibling else jnp.float32),
        in_specs=whole_vmem(len(flat) + 1),
        out_specs=pl.BlockSpec(memory_space=pltpu.VMEM),
        compiler_params=params(28),
        cost_estimate=pl.CostEstimate(
            flops=2 * n_tensor * depth * size * width,
            bytes_accessed=n_tensor * depth * (4 * size + 2 * width) + 4 * size * width,
            transcendentals=0,
        ),
        name="gradient_term",
    )(*flat, cotangents)


def adam_rows(kept, got, w_master, moment_one, moment_two):
    rows, width = kept.shape
    tile = min(128, rows)

    def kernel(kept_ref, got_ref, master_ref, one_ref, two_ref, update_ref, weight_ref):
        gradient = kept_ref[...] + got_ref[...].astype(jnp.float32)
        moment_new = beta_one * one_ref[...] + (1.0 - beta_one) * gradient
        second_new = beta_two * two_ref[...] + (1.0 - beta_two) * gradient * gradient
        scaled = second_new * (1.0 / bias_two)
        update = moment_new * (1.0 / bias_one) / (scaled * lax.rsqrt(scaled) + adam_eps)
        update_ref[...] = update
        weight_ref[...] = (master_ref[...] - learn_rate * update).astype(weight_ref.dtype)

    here = pl.BlockSpec((tile, width), lambda i: (i, 0))
    return pl.pallas_call(
        kernel,
        grid=(rows // tile,),
        out_shape=[
            jax.ShapeDtypeStruct((rows, width), jnp.float32),
            jax.ShapeDtypeStruct((rows, width), jnp.bfloat16),
        ],
        in_specs=[here] * 5,
        out_specs=[here] * 2,
        compiler_params=params(),
        cost_estimate=pl.CostEstimate(
            flops=16 * rows * width, bytes_accessed=24 * rows * width, transcendentals=rows * width
        ),
        name="adam_rows",
    )(kept, got, w_master, moment_one, moment_two)


def norm_columns(states, gain, rows, line):
    length, width = states.shape
    tile = 64

    def kernel(states_ref, gain_ref, kept, sent):
        core = own_core()
        total = jnp.zeros((tile, 1), jnp.float32)
        for block in range(2 * line):
            piece = states_ref[:, block * rows : (block + 1) * rows].astype(jnp.float32)
            total = total + jnp.sum(piece * piece, axis=1, keepdims=True)
        scale = lax.rsqrt(total / width + norm_eps)
        for flag in range(2):

            @pl.when(core == flag)
            def _():
                for block in range(2 * line):
                    out = kept if block % 2 == flag else sent
                    columns = slice(block * rows, (block + 1) * rows)
                    piece = states_ref[:, columns].astype(jnp.float32)
                    out[block // 2] = (piece * scale * gain_ref[:, columns]).astype(out.dtype)

    return pl.pallas_call(
        kernel,
        grid=(length // tile,),
        out_shape=[jax.ShapeDtypeStruct((line, length, rows), jnp.bfloat16)] * 2,
        in_specs=[
            pl.BlockSpec((tile, width), lambda i: (i, 0)),
            pl.BlockSpec((1, width), lambda i: (0, 0)),
        ],
        out_specs=[pl.BlockSpec((line, tile, rows), lambda i: (0, i, 0))] * 2,
        compiler_params=params(),
        cost_estimate=pl.CostEstimate(
            flops=6 * length * width, bytes_accessed=4 * length * width, transcendentals=0
        ),
        name="norm_columns",
    )(states, gain.reshape(1, width))


def accumulate(totals, kept, got, slots, last=False):
    _, length, depth = kept.shape
    width = slots[0][1].shape[1]
    count = len(slots)
    tile = min(256, length)
    owners = jnp.stack([jnp.asarray(owner, jnp.int32) for owner, _ in slots])
    weights = [weight for _, weight in slots]

    def kernel(owners_ref, *refs):
        weight_refs = refs[2 * count : 3 * count]
        for side, out_ref in zip((1, 0), reversed(refs[-2:])):
            result = None if totals is None else refs[3 * count + side][...]
            for slot in range(count):
                product = jnp.dot(
                    refs[side * count + slot][0],
                    weight_refs[slot][...],
                    preferred_element_type=jnp.float32,
                )
                result = product if result is None else result + product
            out_ref[...] = result.astype(out_ref.dtype)

    def state_spec(slot):
        return pl.BlockSpec((1, tile, depth), lambda i, chosen: (chosen[slot], i, 0))

    before = list(totals or [])
    row_spec = pl.BlockSpec((tile, width), lambda i, chosen: (i, 0))
    return pl.pallas_call(
        kernel,
        grid_spec=pltpu.PrefetchScalarGridSpec(
            num_scalar_prefetch=1,
            grid=(length // tile,),
            in_specs=[state_spec(slot) for slot in range(count)] * 2
            + [pl.BlockSpec((depth, width), lambda i, chosen: (0, 0))] * count
            + [row_spec] * len(before),
            out_specs=[row_spec] * 2,
        ),
        out_shape=[
            jax.ShapeDtypeStruct((length, width), jnp.float32),
            jax.ShapeDtypeStruct((length, width), jnp.bfloat16 if last else jnp.float32),
        ],
        compiler_params=params(20),
        cost_estimate=pl.CostEstimate(
            flops=4 * count * length * depth * width,
            bytes_accessed=2 * count * depth * (2 * length + width) + 16 * length * width,
            transcendentals=0,
        ),
        name="accumulate",
    )(owners, *([kept] * count), *([got] * count), *weights, *before)


def attention(kept, got, cosine_table, sine_table):
    length, width = kept.shape
    heads = width // HD - 2
    tile = min(128, length)

    def rope(u, cosine, sine):
        return u * cosine + pltpu.roll(u, HD // 2, 1) * sine

    def kernel(kept_ref, got_ref, cos_ref, sin_ref, out_ref):
        def columns(index, here=slice(None)):
            there = slice(index * HD, (index + 1) * HD)
            return kept_ref[here, there] + got_ref[here, there].astype(jnp.float32)

        keys = rope(columns(heads), cos_ref[...], sin_ref[...]).astype(jnp.bfloat16)
        values = columns(heads + 1).astype(jnp.bfloat16)
        for begin in range(0, length, tile):
            here, upto = slice(begin, begin + tile), begin + tile
            row = lax.broadcasted_iota(jnp.int32, (tile, upto), 0) + begin
            seen = row >= lax.broadcasted_iota(jnp.int32, (tile, upto), 1)
            for head in range(heads):
                query = rope(columns(head, here), cos_ref[here], sin_ref[here])
                query = (query * HD**-0.5).astype(jnp.bfloat16)
                scores = lax.dot_general(
                    query,
                    keys[:upto],
                    (((1,), (1,)), ((), ())),
                    preferred_element_type=jnp.float32,
                )
                scores = jnp.where(seen, scores, -jnp.inf)
                raised = jnp.exp(scores - jnp.max(scores, axis=1, keepdims=True))
                weights = raised * (1.0 / jnp.sum(raised, axis=1, keepdims=True))
                out_ref[here, head * HD : (head + 1) * HD] = jnp.dot(
                    weights.astype(jnp.bfloat16), values[:upto], preferred_element_type=jnp.float32
                ).astype(jnp.bfloat16)

    return pl.pallas_call(
        kernel,
        out_shape=jax.ShapeDtypeStruct((length, heads * HD), jnp.bfloat16),
        in_specs=whole_vmem(4),
        out_specs=pl.BlockSpec(memory_space=pltpu.VMEM),
        compiler_params=params(10),
        cost_estimate=pl.CostEstimate(
            flops=4 * heads * length * length * HD,
            bytes_accessed=9 * length * width,
            transcendentals=heads * length * length,
        ),
        name="attention",
    )(kept, got, cosine_table, sine_table)


def by_source(mine, other, n_tensor):
    kept, depth = mine.shape[0] // n_tensor, mine.shape[1]

    def kernel(mine_ref, other_ref, out_ref):
        index = lax.axis_index("tensor")
        for distance in range(n_tensor):
            columns = pl.ds(pl.multiple_of((index ^ distance) * depth, depth), depth)
            rows = slice(distance * kept, (distance + 1) * kept)
            out_ref[:kept, columns] = mine_ref[rows]
            out_ref[kept:, columns] = other_ref[rows]

    return pl.pallas_call(
        kernel,
        out_shape=jax.ShapeDtypeStruct((2 * kept, n_tensor * depth), mine.dtype),
        in_specs=whole_vmem(2),
        out_specs=pl.BlockSpec(memory_space=pltpu.VMEM),
        compiler_params=params(),
        name="by_source",
    )(mine, other)


def fetch(*arrays):
    parts = 4
    if sum(a.size * a.dtype.itemsize for a in arrays) > 20 * MIB:
        return arrays

    def kernel(*refs):
        sems = refs[-1]
        copies = []
        for which in range(len(arrays)):
            rows = arrays[which].shape[0] // parts
            for part in range(parts):
                here = pl.ds(part * rows, rows)
                copies.append(
                    pltpu.make_async_copy(
                        refs[which].at[here],
                        refs[len(arrays) + which].at[here],
                        sems.at[which * parts + part],
                    )
                )
        for copy in copies:
            copy.start()
        for copy in copies:
            copy.wait()

    return pl.pallas_call(
        kernel,
        out_shape=[jax.ShapeDtypeStruct(a.shape, a.dtype) for a in arrays],
        in_specs=[pl.BlockSpec(memory_space=pl.ANY)] * len(arrays),
        out_specs=whole_vmem(len(arrays)),
        scratch_shapes=[pltpu.SemaphoreType.DMA((parts * len(arrays),))],
        compiler_params=params(24),
        cost_estimate=pl.CostEstimate(
            flops=0, bytes_accessed=2 * sum(a.size * 2 for a in arrays), transcendentals=0
        ),
        name="fetch",
    )(*arrays)


def lay_out(blocks):
    kept = blocks[0][0].shape[0]
    half = sum(block.shape[1] for block in blocks[0])

    def kernel(*refs):
        out_ref = refs[-1]
        core = own_core()
        for flag in range(2):

            @pl.when(core == flag)
            def _():
                entry = 0
                for side in range(2):
                    begin = (flag ^ side) * half
                    for block in blocks[side]:
                        stop = begin + block.shape[1]
                        out_ref[:, begin:stop] = refs[entry][...]
                        begin, entry = stop, entry + 1

    flat = [block for side in blocks for block in side]
    return pl.pallas_call(
        kernel,
        out_shape=jax.ShapeDtypeStruct((kept, 2 * half), flat[0].dtype),
        in_specs=whole_vmem(len(flat)),
        out_specs=pl.BlockSpec(memory_space=pltpu.VMEM),
        compiler_params=params(),
        name="lay_out",
    )(*flat)


def body(
    train_states, qkv_cotangent, w_master, moment_one, moment_two, prompt_states, norm_gain, w_out
):
    n_dp = lax.axis_size("dp")
    n_tensor = lax.axis_size("tensor")
    line = n_dp // 2
    tensor_index = lax.axis_index("tensor")
    core, place = own_core(), own_place()
    siblings = [(i, i ^ 1) for i in range(n_dp)]
    rows, slice_width = w_master.shape
    tokens, width = train_states.shape
    length = prompt_states.shape[0]
    query_width = slice_width - 2 * HD

    kept_states, sent_states = norm_columns(prompt_states, norm_gain, rows, line)
    got_states = lax.ppermute(sent_states, "dp", siblings)

    core_width = width // 2
    early_width = core_width // EARLY_SHARE
    packed, w_early = pack_columns(
        train_states, w_out, rows, line, tokens // n_tensor, early_width
    )
    def across(block, distance):
        return lax.ppermute(block, "dp", line_pairs([(i, i ^ distance) for i in range(line)]))

    pieces = [packed[0]] + [across(packed[distance], distance) for distance in range(1, line)]
    pieces = tie(pieces, kept_states)

    cotangents = [qkv_cotangent, across(qkv_cotangent, 1)]
    spread = PlaneGather(stack_pieces(pieces), n_tensor)
    behind = pieces
    for distance in range(2, line):
        cotangents.append(across(tie((qkv_cotangent,), *behind)[0], distance))
        behind = cotangents[-1:]
    spread.second(cotangents[2], spread.blocks[1:])
    all_cotangents = place_cotangents(cotangents, n_tensor)

    w_rest = lax.dynamic_slice(
        w_out,
        (0, core * core_width + early_width),
        (w_out.shape[0], core_width - early_width),
    )
    early_weight = lax.all_gather(w_early, "tensor", axis=0, tiled=True)
    (w_rest,) = tie((w_rest,), spread.blocks, cotangents, early_weight)
    rest_weight = lax.all_gather(w_rest, "tensor", axis=0, tiled=True)

    sent = gradient_term(spread.blocks, all_cotangents, True)
    got = lax.ppermute(sent, "dp", siblings)
    kept = gradient_term(spread.blocks, all_cotangents, False)
    update_dir, weight = adam_rows(kept, got, w_master, moment_one, moment_two)

    weights = LineGather(weight, place, line)

    def add(totals, steps, last=False):
        slots = [weights.slot(step) for step in steps]
        return accumulate(totals, kept_states, got_states, slots, last)

    for _ in range(1, line - 1):
        weights.hop()
    totals = add(None, range(line - 2))
    cosine_table, sine_table = rope_tables(length, HD)
    cosine_table, sine_table, *totals = tie((cosine_table, sine_table, *totals))
    weights.hop(*totals, cosine_table, sine_table)
    totals = add(totals, [line - 2])
    totals = add(totals, [line - 1], True)
    attended = attention(
        totals[0], lax.ppermute(totals[1], "dp", siblings), cosine_table, sine_table
    )

    kept_rows = length // n_tensor
    heads = []
    for distance in range(n_tensor):
        target = tensor_index ^ distance
        block = lax.dynamic_slice(attended, (target * kept_rows, 0), (kept_rows, query_width))
        if distance:
            block = lax.ppermute(block, "tensor", [(j, j ^ distance) for j in range(n_tensor)])
        heads.append(block)
    fetched = fetch(early_weight, rest_weight)
    heads = tie(heads, *fetched)
    (mine,) = stack_pieces([head[None] for head in heads])
    other = lax.ppermute(mine, "dp", siblings)
    both = by_source(mine, other, n_tensor)
    mine, sent = [], []
    for weight in fetched:
        made = jnp.dot(both, weight, preferred_element_type=jnp.float32).astype(jnp.bfloat16)
        mine.append(made[:kept_rows])
        sent.append(made[kept_rows:])
    summed = lay_out((mine, [lax.ppermute(rows, "dp", siblings) for rows in sent]))
    return (update_dir, summed)


def solution(mesh):
    placed = (
        P("dp", None),
        P("dp", "tensor"),
        P("dp", "tensor"),
        P("dp", "tensor"),
        P("dp", "tensor"),
        P("dp", None),
        P(),
        P("tensor", None),
    )
    return jax.shard_map(
        body,
        mesh=mesh,
        in_specs=placed,
        out_specs=(P("dp", "tensor"), P(("dp", "tensor"), None)),
        check_vma=False,
    )
```

```python
import functools

import jax
import jax.numpy as jnp
from jax import lax
from jax.experimental import pallas as pl
from jax.experimental.pallas import tpu as pltpu
from jax.sharding import PartitionSpec as P

HD = 128


beta_one = 0.9
beta_two = 0.95
bias_one = 1.0 - 0.9**8
bias_two = 1.0 - 0.95**8
learn_rate = 0.002
adam_eps = 1e-08
norm_eps = 1e-05
rope_base = 500000.0

MIB = 1024 * 1024
EARLY_SHARE = 16


def rope_tables(length, head_size):
    half_width = head_size // 2
    exponent = jnp.arange(half_width, dtype=jnp.float32) * (2.0 / head_size)
    inverse = jnp.power(jnp.float32(rope_base), -exponent)
    position = jnp.arange(length, dtype=jnp.float32)
    angles = position[:, None] * inverse[None, :]
    cosine_table = jnp.concatenate([jnp.cos(angles), jnp.cos(angles)], axis=1)
    sine_table = jnp.concatenate([-jnp.sin(angles), jnp.sin(angles)], axis=1)
    return (cosine_table, sine_table)


def params(mib=16):
    return pltpu.CompilerParams(vmem_limit_bytes=mib * MIB)


def whole_vmem(count):
    return [pl.BlockSpec(memory_space=pltpu.VMEM)] * count


def own_core():
    return lax.rem(lax.axis_index("dp"), 2)


def own_place():
    return lax.div(lax.axis_index("dp"), 2)


def pack_columns(train_states, w_out, rows, line, quarter, early_width):
    width = train_states.shape[1]
    early_blocks = width // 2 // early_width

    def kernel(chosen_ref, train_ref, w_out_ref, *outs):
        place = own_place()
        for distance in range(line):
            for owner in range(2):
                column = pl.multiple_of(((place ^ distance) * 2 + owner) * rows, 128)
                outs[distance][owner] = train_ref[:, pl.ds(column, rows)]
        outs[line][...] = w_out_ref[...]

    shapes = [jax.ShapeDtypeStruct((2, quarter, rows), train_states.dtype)] * line
    early = jax.ShapeDtypeStruct((w_out.shape[0], early_width), w_out.dtype)
    chosen = jnp.stack([lax.axis_index("tensor"), own_core() * early_blocks]).astype(jnp.int32)
    outs = pl.pallas_call(
        kernel,
        grid_spec=pltpu.PrefetchScalarGridSpec(
            num_scalar_prefetch=1,
            grid=(1,),
            in_specs=[
                pl.BlockSpec((quarter, width), lambda i, chosen: (chosen[0], 0)),
                pl.BlockSpec(early.shape, lambda i, chosen: (0, chosen[1])),
            ],
            out_specs=[pl.BlockSpec(s.shape, lambda i, chosen: (0, 0, 0)) for s in shapes]
            + [pl.BlockSpec(early.shape, lambda i, chosen: (0, 0))],
        ),
        out_shape=shapes + [early],
        compiler_params=params(56),
        name="pack_columns",
    )(chosen, train_states, w_out)
    return outs[:line], outs[line]


def stack_pieces(pieces):
    outer, height, width = pieces[0].shape
    count = len(pieces)

    def kernel(*refs):
        for which in range(outer):
            for i in range(count):
                refs[count + which][i * height : (i + 1) * height] = refs[i][which]

    return pl.pallas_call(
        kernel,
        out_shape=[jax.ShapeDtypeStruct((count * height, width), pieces[0].dtype)] * outer,
        in_specs=whole_vmem(count),
        out_specs=whole_vmem(outer),
        compiler_params=params(),
        name="stack_pieces",
    )(*pieces)


def line_pairs(places):
    return [(2 * a + core, 2 * b + core) for a, b in places for core in range(2)]


def tie(arrays, *others):
    return lax.optimization_barrier((tuple(arrays), others))[0]


class LineGather:
    def __init__(self, block, place, count):
        self.place, self.count = place, count
        self.low, self.high = [block], [block]

    def hop(self, *behind):
        step, count = len(self.low), self.count
        up, down = self.low[-1], self.high[-1]
        if behind:
            up, down = tie((up, down), *behind)
        right = line_pairs([(i, i + 1) for i in range(step - 1, count - 1)])
        left = line_pairs([(i, i - 1) for i in range(1, count - step + 1)])
        self.low.append(lax.ppermute(up, "dp", right))
        self.high.append(lax.ppermute(down, "dp", left))

    def arrived(self):
        return self.low[-1], self.high[-1]

    def slot(self, step):
        if step == 0:
            return self.place, self.low[0]
        sides = (self.low, self.high)
        choices = line_choice(step, self.place, self.count)
        _, side, entry, owner = choices[-1]
        block = sides[side][entry]
        for holds, side, entry, other in reversed(choices[:-1]):
            block = jnp.where(holds, sides[side][entry], block)
            owner = jnp.where(holds, other, owner)
        return owner, block


def line_choice(step, place, count):
    is_low, is_high = place >= step, place <= count - 1 - step
    spare = count - step
    return [
        (is_low, 0, step, place - step),
        (jnp.logical_and(jnp.logical_not(is_low), is_high), 1, step, place + step),
        (
            jnp.logical_and(jnp.logical_not(is_low), jnp.logical_not(is_high)),
            1,
            spare,
            place + spare,
        ),
    ][: 2 if 2 * step <= count else 3]


def place_cotangents(blocks, n_tensor):
    tokens, width = blocks[0].shape
    quarter = tokens // n_tensor
    count = len(blocks)

    def kernel(*refs):
        for distance in range(count):
            refs[count][:, distance * quarter : (distance + 1) * quarter] = refs[distance][...]

    return pl.pallas_call(
        kernel,
        out_shape=jax.ShapeDtypeStruct((n_tensor, count * quarter, width), blocks[0].dtype),
        in_specs=whole_vmem(count),
        out_specs=pl.BlockSpec(memory_space=pltpu.VMEM),
        compiler_params=params(),
        name="place_cotangents",
    )(*[block.reshape(n_tensor, quarter, width) for block in blocks])


def plane_permute(block, count, distance):
    return lax.ppermute(block, "tensor", [(j, j ^ distance) for j in range(count)])


class PlaneGather:
    def __init__(self, pair, count):
        self.count = count
        if count != 4:
            own = lax.axis_index("tensor")
            gathered = [lax.all_gather(block, "tensor", axis=0) for block in pair]
            self.blocks = [
                [lax.dynamic_index_in_dim(g, own ^ b, 0, keepdims=False) for g in gathered]
                for b in range(count)
            ]
            return
        one, two = [None, None], [None, None]
        for owner in range(2):
            one[owner] = plane_permute(pair[owner], count, 1)
            two[1 - owner] = plane_permute(pair[1 - owner], count, 2)
        self.blocks = [list(pair), one, two]

    def passed(self):
        return [self.blocks[1][0], self.blocks[2][1]]

    def second(self, *behind):
        if self.count == 4:
            up, down = tie(self.passed(), *behind)
            self.blocks.append(
                [plane_permute(up, self.count, 2), plane_permute(down, self.count, 1)]
            )


def gradient_term(blocks, cotangents, sibling):
    n_tensor, depth, width = cotangents.shape
    size = blocks[0][0].shape[1]
    flat = [block for pair in blocks for block in pair]

    def kernel(*refs):
        cotangent_ref, out_ref = refs[len(flat) :]
        index = lax.axis_index("tensor")
        owner = 1 - own_core() if sibling else own_core()
        total = None
        for distance in range(n_tensor):
            lower, upper = refs[2 * distance : 2 * distance + 2]
            product = lax.dot_general(
                jnp.where(owner == 0, lower[...], upper[...]),
                cotangent_ref[index ^ distance],
                (((0,), (0,)), ((), ())),
                preferred_element_type=jnp.float32,
            )
            total = product if total is None else total + product
        out_ref[...] = total.astype(out_ref.dtype)

    return pl.pallas_call(
        kernel,
        out_shape=jax.ShapeDtypeStruct((size, width), jnp.bfloat16 if sibling else jnp.float32),
        in_specs=whole_vmem(len(flat) + 1),
        out_specs=pl.BlockSpec(memory_space=pltpu.VMEM),
        compiler_params=params(28),
        cost_estimate=pl.CostEstimate(
            flops=2 * n_tensor * depth * size * width,
            bytes_accessed=n_tensor * depth * (4 * size + 2 * width) + 4 * size * width,
            transcendentals=0,
        ),
        name="gradient_term",
    )(*flat, cotangents)


def adam_rows(kept, got, w_master, moment_one, moment_two):
    rows, width = kept.shape
    tile = min(128, rows)

    def kernel(kept_ref, got_ref, master_ref, one_ref, two_ref, update_ref, weight_ref):
        gradient = kept_ref[...] + got_ref[...].astype(jnp.float32)
        moment_new = beta_one * one_ref[...] + (1.0 - beta_one) * gradient
        second_new = beta_two * two_ref[...] + (1.0 - beta_two) * gradient * gradient
        scaled = second_new * (1.0 / bias_two)
        update = moment_new * (1.0 / bias_one) / (scaled * lax.rsqrt(scaled) + adam_eps)
        update_ref[...] = update
        weight_ref[...] = (master_ref[...] - learn_rate * update).astype(weight_ref.dtype)

    here = pl.BlockSpec((tile, width), lambda i: (i, 0))
    return pl.pallas_call(
        kernel,
        grid=(rows // tile,),
        out_shape=[
            jax.ShapeDtypeStruct((rows, width), jnp.float32),
            jax.ShapeDtypeStruct((rows, width), jnp.bfloat16),
        ],
        in_specs=[here] * 5,
        out_specs=[here] * 2,
        compiler_params=params(),
        cost_estimate=pl.CostEstimate(
            flops=16 * rows * width, bytes_accessed=24 * rows * width, transcendentals=rows * width
        ),
        name="adam_rows",
    )(kept, got, w_master, moment_one, moment_two)


def norm_columns(states, gain, rows, line):
    length, width = states.shape
    tile = 64

    def kernel(states_ref, gain_ref, kept, sent):
        core = own_core()
        total = jnp.zeros((tile, 1), jnp.float32)
        for block in range(2 * line):
            piece = states_ref[:, block * rows : (block + 1) * rows].astype(jnp.float32)
            total = total + jnp.sum(piece * piece, axis=1, keepdims=True)
        scale = lax.rsqrt(total / width + norm_eps)
        for flag in range(2):

            @pl.when(core == flag)
            def _():
                for block in range(2 * line):
                    out = kept if block % 2 == flag else sent
                    columns = slice(block * rows, (block + 1) * rows)
                    piece = states_ref[:, columns].astype(jnp.float32)
                    out[block // 2] = (piece * scale * gain_ref[:, columns]).astype(out.dtype)

    return pl.pallas_call(
        kernel,
        grid=(length // tile,),
        out_shape=[jax.ShapeDtypeStruct((line, length, rows), jnp.bfloat16)] * 2,
        in_specs=[
            pl.BlockSpec((tile, width), lambda i: (i, 0)),
            pl.BlockSpec((1, width), lambda i: (0, 0)),
        ],
        out_specs=[pl.BlockSpec((line, tile, rows), lambda i: (0, i, 0))] * 2,
        compiler_params=params(),
        cost_estimate=pl.CostEstimate(
            flops=6 * length * width, bytes_accessed=4 * length * width, transcendentals=0
        ),
        name="norm_columns",
    )(states, gain.reshape(1, width))


def accumulate(totals, kept, got, slots, last=False):
    _, length, depth = kept.shape
    width = slots[0][1].shape[1]
    count = len(slots)
    tile = min(256, length)
    owners = jnp.stack([jnp.asarray(owner, jnp.int32) for owner, _ in slots])
    weights = [weight for _, weight in slots]

    def kernel(owners_ref, *refs):
        weight_refs = refs[2 * count : 3 * count]
        for side, out_ref in zip((1, 0), reversed(refs[-2:])):
            result = None if totals is None else refs[3 * count + side][...]
            for slot in range(count):
                product = jnp.dot(
                    refs[side * count + slot][0],
                    weight_refs[slot][...],
                    preferred_element_type=jnp.float32,
                )
                result = product if result is None else result + product
            out_ref[...] = result.astype(out_ref.dtype)

    def state_spec(slot):
        return pl.BlockSpec((1, tile, depth), lambda i, chosen: (chosen[slot], i, 0))

    before = list(totals or [])
    row_spec = pl.BlockSpec((tile, width), lambda i, chosen: (i, 0))
    return pl.pallas_call(
        kernel,
        grid_spec=pltpu.PrefetchScalarGridSpec(
            num_scalar_prefetch=1,
            grid=(length // tile,),
            in_specs=[state_spec(slot) for slot in range(count)] * 2
            + [pl.BlockSpec((depth, width), lambda i, chosen: (0, 0))] * count
            + [row_spec] * len(before),
            out_specs=[row_spec] * 2,
        ),
        out_shape=[
            jax.ShapeDtypeStruct((length, width), jnp.float32),
            jax.ShapeDtypeStruct((length, width), jnp.bfloat16 if last else jnp.float32),
        ],
        compiler_params=params(20),
        cost_estimate=pl.CostEstimate(
            flops=4 * count * length * depth * width,
            bytes_accessed=2 * count * depth * (2 * length + width) + 16 * length * width,
            transcendentals=0,
        ),
        name="accumulate",
    )(owners, *([kept] * count), *([got] * count), *weights, *before)


def attention(kept, got, cosine_table, sine_table):
    length, width = kept.shape
    heads = width // HD - 2
    tile = min(128, length)

    def rope(u, cosine, sine):
        return u * cosine + pltpu.roll(u, HD // 2, 1) * sine

    def kernel(kept_ref, got_ref, cos_ref, sin_ref, out_ref):
        def columns(index, here=slice(None)):
            there = slice(index * HD, (index + 1) * HD)
            return kept_ref[here, there] + got_ref[here, there].astype(jnp.float32)

        keys = rope(columns(heads), cos_ref[...], sin_ref[...]).astype(jnp.bfloat16)
        values = columns(heads + 1).astype(jnp.bfloat16)
        for begin in range(0, length, tile):
            here, upto = slice(begin, begin + tile), begin + tile
            row = lax.broadcasted_iota(jnp.int32, (tile, upto), 0) + begin
            seen = row >= lax.broadcasted_iota(jnp.int32, (tile, upto), 1)
            for head in range(heads):
                query = rope(columns(head, here), cos_ref[here], sin_ref[here])
                query = (query * HD**-0.5).astype(jnp.bfloat16)
                scores = lax.dot_general(
                    query,
                    keys[:upto],
                    (((1,), (1,)), ((), ())),
                    preferred_element_type=jnp.float32,
                )
                scores = jnp.where(seen, scores, -jnp.inf)
                raised = jnp.exp(scores - jnp.max(scores, axis=1, keepdims=True))
                weights = raised * (1.0 / jnp.sum(raised, axis=1, keepdims=True))
                out_ref[here, head * HD : (head + 1) * HD] = jnp.dot(
                    weights.astype(jnp.bfloat16), values[:upto], preferred_element_type=jnp.float32
                ).astype(jnp.bfloat16)

    return pl.pallas_call(
        kernel,
        out_shape=jax.ShapeDtypeStruct((length, heads * HD), jnp.bfloat16),
        in_specs=whole_vmem(4),
        out_specs=pl.BlockSpec(memory_space=pltpu.VMEM),
        compiler_params=params(10),
        cost_estimate=pl.CostEstimate(
            flops=4 * heads * length * length * HD,
            bytes_accessed=9 * length * width,
            transcendentals=heads * length * length,
        ),
        name="attention",
    )(kept, got, cosine_table, sine_table)


def by_source(mine, other, n_tensor):
    kept, depth = mine.shape[0] // n_tensor, mine.shape[1]

    def kernel(mine_ref, other_ref, out_ref):
        index = lax.axis_index("tensor")
        for distance in range(n_tensor):
            columns = pl.ds(pl.multiple_of((index ^ distance) * depth, depth), depth)
            rows = slice(distance * kept, (distance + 1) * kept)
            out_ref[:kept, columns] = mine_ref[rows]
            out_ref[kept:, columns] = other_ref[rows]

    return pl.pallas_call(
        kernel,
        out_shape=jax.ShapeDtypeStruct((2 * kept, n_tensor * depth), mine.dtype),
        in_specs=whole_vmem(2),
        out_specs=pl.BlockSpec(memory_space=pltpu.VMEM),
        compiler_params=params(),
        name="by_source",
    )(mine, other)


def fetch(*pieces):
    parts = 4
    if sum(a.shape[0] * (stop - start) * a.dtype.itemsize for a, start, stop in pieces) > 12 * MIB:
        return [a[:, start:stop] for a, start, stop in pieces]
    count = len(pieces)

    def kernel(*refs):
        copies = []
        for which, (array, start, stop) in enumerate(pieces):
            rows = array.shape[0] // parts
            for part in range(parts):
                here = pl.ds(part * rows, rows)
                copies.append(
                    pltpu.make_async_copy(
                        refs[which].at[here, pl.ds(start, stop - start)],
                        refs[count + which].at[here],
                        refs[-1].at[which * parts + part],
                    )
                )
        for copy in copies:
            copy.start()
        for copy in copies:
            copy.wait()

    return pl.pallas_call(
        kernel,
        out_shape=[
            jax.ShapeDtypeStruct((a.shape[0], stop - start), a.dtype) for a, start, stop in pieces
        ],
        in_specs=[pl.BlockSpec(memory_space=pl.ANY)] * count,
        out_specs=whole_vmem(count),
        scratch_shapes=[pltpu.SemaphoreType.DMA((parts * count,))],
        compiler_params=params(44),
        cost_estimate=pl.CostEstimate(
            flops=0,
            bytes_accessed=4 * sum(a.shape[0] * (stop - start) for a, start, stop in pieces),
            transcendentals=0,
        ),
        name="fetch",
    )(*[a for a, _, _ in pieces])


def lay_out(blocks):
    kept = blocks[0][0].shape[0]
    half = sum(block.shape[1] for block in blocks[0])

    def kernel(*refs):
        out_ref = refs[-1]
        core = own_core()
        for flag in range(2):

            @pl.when(core == flag)
            def _():
                entry = 0
                for side in range(2):
                    begin = (flag ^ side) * half
                    for block in blocks[side]:
                        stop = begin + block.shape[1]
                        out_ref[:, begin:stop] = refs[entry][...]
                        begin, entry = stop, entry + 1

    flat = [block for side in blocks for block in side]
    return pl.pallas_call(
        kernel,
        out_shape=jax.ShapeDtypeStruct((kept, 2 * half), flat[0].dtype),
        in_specs=whole_vmem(len(flat)),
        out_specs=pl.BlockSpec(memory_space=pltpu.VMEM),
        compiler_params=params(),
        name="lay_out",
    )(*flat)


def body(
    train_states, qkv_cotangent, w_master, moment_one, moment_two, prompt_states, norm_gain, w_out
):
    n_dp = lax.axis_size("dp")
    n_tensor = lax.axis_size("tensor")
    line = n_dp // 2
    tensor_index = lax.axis_index("tensor")
    core, place = own_core(), own_place()
    siblings = [(i, i ^ 1) for i in range(n_dp)]
    rows, slice_width = w_master.shape
    tokens, width = train_states.shape
    length = prompt_states.shape[0]
    query_width = slice_width - 2 * HD

    kept_states, sent_states = norm_columns(prompt_states, norm_gain, rows, line)
    got_states = lax.ppermute(sent_states, "dp", siblings)

    core_width = width // 2
    early_width = core_width // EARLY_SHARE
    packed, w_early = pack_columns(
        train_states, w_out, rows, line, tokens // n_tensor, early_width
    )
    def across(block, distance):
        return lax.ppermute(block, "dp", line_pairs([(i, i ^ distance) for i in range(line)]))

    pieces = [packed[0]] + [across(packed[distance], distance) for distance in range(1, line)]
    w_rest = lax.dynamic_slice(
        w_out,
        (0, core * core_width + early_width),
        (w_out.shape[0], core_width - early_width),
    )
    pieces = tie(pieces, kept_states)

    cotangents = [qkv_cotangent, across(qkv_cotangent, 1)]
    spread = PlaneGather(stack_pieces(pieces), n_tensor)
    behind = pieces
    for distance in range(2, line):
        cotangents.append(across(tie((qkv_cotangent,), *behind)[0], distance))
        behind = cotangents[-1:]
    spread.second(cotangents[2], spread.blocks[1:])
    all_cotangents = place_cotangents(cotangents, n_tensor)

    early_weight = lax.all_gather(w_early, "tensor", axis=0, tiled=True)
    (w_rest,) = tie((w_rest,), spread.blocks, cotangents, early_weight)
    rest_weight = lax.all_gather(w_rest, "tensor", axis=0, tiled=True)

    sent = gradient_term(spread.blocks, all_cotangents, True)
    got = lax.ppermute(sent, "dp", siblings)
    kept = gradient_term(spread.blocks, all_cotangents, False)
    update_dir, weight = adam_rows(kept, got, w_master, moment_one, moment_two)

    weights = LineGather(weight, place, line)

    def add(totals, steps, last=False):
        slots = [weights.slot(step) for step in steps]
        return accumulate(totals, kept_states, got_states, slots, last)

    for _ in range(1, line - 1):
        weights.hop()
    totals = add(None, range(line - 2))
    cosine_table, sine_table = rope_tables(length, HD)
    cosine_table, sine_table, *totals = tie((cosine_table, sine_table, *totals))
    weights.hop(*totals, cosine_table, sine_table)
    totals = add(totals, [line - 2])
    totals = add(totals, [line - 1], True)
    attended = attention(
        totals[0], lax.ppermute(totals[1], "dp", siblings), cosine_table, sine_table
    )

    kept_rows = length // n_tensor
    heads = []
    for distance in range(n_tensor):
        target = tensor_index ^ distance
        block = lax.dynamic_slice(attended, (target * kept_rows, 0), (kept_rows, query_width))
        if distance:
            block = lax.ppermute(block, "tensor", [(j, j ^ distance) for j in range(n_tensor)])
        heads.append(block)
    rest_width = core_width - early_width
    half_width = rest_width // 2
    fetched = list(fetch((rest_weight, 0, half_width)))
    heads = tie(heads, *fetched)
    (mine,) = stack_pieces([head[None] for head in heads])
    other = lax.ppermute(mine, "dp", siblings)
    fetched += fetch((rest_weight, half_width, rest_width), (early_weight, 0, early_width))
    (other, *fetched) = tie((other, *fetched))
    both = by_source(mine, other, n_tensor)
    mine, sent = [], []
    for weight in fetched:
        made = jnp.dot(both, weight, preferred_element_type=jnp.float32).astype(jnp.bfloat16)
        mine.append(made[:kept_rows])
        sent.append(made[kept_rows:])
    swapped = [lax.ppermute(rows, "dp", siblings) for rows in sent]
    summed = lay_out([side[2:] + side[:2] for side in (mine, swapped)])
    return (update_dir, summed)


def solution(mesh):
    placed = (
        P("dp", None),
        P("dp", "tensor"),
        P("dp", "tensor"),
        P("dp", "tensor"),
        P("dp", "tensor"),
        P("dp", None),
        P(),
        P("tensor", None),
    )
    return jax.shard_map(
        body,
        mesh=mesh,
        in_specs=placed,
        out_specs=(P("dp", "tensor"), P(("dp", "tensor"), None)),
        check_vma=False,
    )
```

```python
import functools

import jax
import jax.numpy as jnp
from jax import lax
from jax.experimental import pallas as pl
from jax.experimental.pallas import tpu as pltpu
from jax.sharding import PartitionSpec as P

HD = 128


beta_one = 0.9
beta_two = 0.95
bias_one = 1.0 - 0.9**8
bias_two = 1.0 - 0.95**8
learn_rate = 0.002
adam_eps = 1e-08
norm_eps = 1e-05
rope_base = 500000.0

MIB = 1024 * 1024
EARLY_BLOCKS = 3


def rope_tables(length, head_size):
    half_width = head_size // 2
    exponent = jnp.arange(half_width, dtype=jnp.float32) * (2.0 / head_size)
    inverse = jnp.power(jnp.float32(rope_base), -exponent)
    position = jnp.arange(length, dtype=jnp.float32)
    angles = position[:, None] * inverse[None, :]
    cosine_table = jnp.concatenate([jnp.cos(angles), jnp.cos(angles)], axis=1)
    sine_table = jnp.concatenate([-jnp.sin(angles), jnp.sin(angles)], axis=1)
    return (cosine_table, sine_table)


def params(mib=16):
    return pltpu.CompilerParams(vmem_limit_bytes=mib * MIB)


def whole_vmem(count):
    return [pl.BlockSpec(memory_space=pltpu.VMEM)] * count


def own_core():
    return lax.rem(lax.axis_index("dp"), 2)


def own_place():
    return lax.div(lax.axis_index("dp"), 2)


def pack_columns(train_states, w_out, rows, line, quarter, early_width):
    width = train_states.shape[1]
    block = early_width // EARLY_BLOCKS

    def kernel(chosen_ref, train_ref, *refs):
        w_out_refs, outs = refs[:EARLY_BLOCKS], refs[EARLY_BLOCKS:]
        place = own_place()
        for distance in range(line):
            for owner in range(2):
                column = pl.multiple_of(((place ^ distance) * 2 + owner) * rows, 128)
                outs[distance][owner] = train_ref[:, pl.ds(column, rows)]
        for entry, w_out_ref in enumerate(w_out_refs):
            outs[line][:, entry * block : (entry + 1) * block] = w_out_ref[...]

    shapes = [jax.ShapeDtypeStruct((2, quarter, rows), train_states.dtype)] * line
    early = jax.ShapeDtypeStruct((w_out.shape[0], early_width), w_out.dtype)
    chosen = jnp.stack([lax.axis_index("tensor"), own_core() * (width // 2 // block)]).astype(jnp.int32)
    outs = pl.pallas_call(
        kernel,
        grid_spec=pltpu.PrefetchScalarGridSpec(
            num_scalar_prefetch=1,
            grid=(1,),
            in_specs=[
                pl.BlockSpec((quarter, width), lambda i, chosen: (chosen[0], 0)),
            ]
            + [
                pl.BlockSpec(
                    (w_out.shape[0], block), lambda i, chosen, entry=entry: (0, chosen[1] + entry)
                )
                for entry in range(EARLY_BLOCKS)
            ],
            out_specs=[pl.BlockSpec(s.shape, lambda i, chosen: (0, 0, 0)) for s in shapes]
            + [pl.BlockSpec(early.shape, lambda i, chosen: (0, 0))],
        ),
        out_shape=shapes + [early],
        compiler_params=params(56),
        name="pack_columns",
    )(chosen, train_states, *([w_out] * EARLY_BLOCKS))
    return outs[:line], outs[line]


def stack_pieces(pieces):
    outer, height, width = pieces[0].shape
    count = len(pieces)

    def kernel(*refs):
        for which in range(outer):
            for i in range(count):
                refs[count + which][i * height : (i + 1) * height] = refs[i][which]

    return pl.pallas_call(
        kernel,
        out_shape=[jax.ShapeDtypeStruct((count * height, width), pieces[0].dtype)] * outer,
        in_specs=whole_vmem(count),
        out_specs=whole_vmem(outer),
        compiler_params=params(),
        name="stack_pieces",
    )(*pieces)


def line_pairs(places):
    return [(2 * a + core, 2 * b + core) for a, b in places for core in range(2)]


def tie(arrays, *others):
    return lax.optimization_barrier((tuple(arrays), others))[0]


class LineGather:
    def __init__(self, block, place, count):
        self.place, self.count = place, count
        self.low, self.high = [block], [block]

    def hop(self, *behind):
        step, count = len(self.low), self.count
        up, down = self.low[-1], self.high[-1]
        if behind:
            up, down = tie((up, down), *behind)
        right = line_pairs([(i, i + 1) for i in range(step - 1, count - 1)])
        left = line_pairs([(i, i - 1) for i in range(1, count - step + 1)])
        self.low.append(lax.ppermute(up, "dp", right))
        self.high.append(lax.ppermute(down, "dp", left))

    def arrived(self):
        return self.low[-1], self.high[-1]

    def slot(self, step):
        if step == 0:
            return self.place, self.low[0]
        sides = (self.low, self.high)
        choices = line_choice(step, self.place, self.count)
        _, side, entry, owner = choices[-1]
        block = sides[side][entry]
        for holds, side, entry, other in reversed(choices[:-1]):
            block = jnp.where(holds, sides[side][entry], block)
            owner = jnp.where(holds, other, owner)
        return owner, block


def line_choice(step, place, count):
    is_low, is_high = place >= step, place <= count - 1 - step
    spare = count - step
    return [
        (is_low, 0, step, place - step),
        (jnp.logical_and(jnp.logical_not(is_low), is_high), 1, step, place + step),
        (
            jnp.logical_and(jnp.logical_not(is_low), jnp.logical_not(is_high)),
            1,
            spare,
            place + spare,
        ),
    ][: 2 if 2 * step <= count else 3]


def place_cotangents(blocks, n_tensor):
    tokens, width = blocks[0].shape
    quarter = tokens // n_tensor
    count = len(blocks)

    def kernel(*refs):
        for distance in range(count):
            refs[count][:, distance * quarter : (distance + 1) * quarter] = refs[distance][...]

    return pl.pallas_call(
        kernel,
        out_shape=jax.ShapeDtypeStruct((n_tensor, count * quarter, width), blocks[0].dtype),
        in_specs=whole_vmem(count),
        out_specs=pl.BlockSpec(memory_space=pltpu.VMEM),
        compiler_params=params(),
        name="place_cotangents",
    )(*[block.reshape(n_tensor, quarter, width) for block in blocks])


def plane_permute(block, count, distance):
    return lax.ppermute(block, "tensor", [(j, j ^ distance) for j in range(count)])


class PlaneGather:
    def __init__(self, pair, count):
        self.count = count
        if count != 4:
            own = lax.axis_index("tensor")
            gathered = [lax.all_gather(block, "tensor", axis=0) for block in pair]
            self.blocks = [
                [lax.dynamic_index_in_dim(g, own ^ b, 0, keepdims=False) for g in gathered]
                for b in range(count)
            ]
            return
        one, two = [None, None], [None, None]
        for owner in range(2):
            one[owner] = plane_permute(pair[owner], count, 1)
            two[1 - owner] = plane_permute(pair[1 - owner], count, 2)
        self.blocks = [list(pair), one, two]

    def passed(self):
        return [self.blocks[1][0], self.blocks[2][1]]

    def second(self, *behind):
        if self.count == 4:
            up, down = tie(self.passed(), *behind)
            self.blocks.append(
                [plane_permute(up, self.count, 2), plane_permute(down, self.count, 1)]
            )


def gradient_term(blocks, cotangents, sibling):
    n_tensor, depth, width = cotangents.shape
    size = blocks[0][0].shape[1]
    flat = [block for pair in blocks for block in pair]

    def kernel(*refs):
        cotangent_ref, out_ref = refs[len(flat) :]
        index = lax.axis_index("tensor")
        owner = 1 - own_core() if sibling else own_core()
        total = None
        for distance in range(n_tensor):
            lower, upper = refs[2 * distance : 2 * distance + 2]
            product = lax.dot_general(
                jnp.where(owner == 0, lower[...], upper[...]),
                cotangent_ref[index ^ distance],
                (((0,), (0,)), ((), ())),
                preferred_element_type=jnp.float32,
            )
            total = product if total is None else total + product
        out_ref[...] = total.astype(out_ref.dtype)

    return pl.pallas_call(
        kernel,
        out_shape=jax.ShapeDtypeStruct((size, width), jnp.bfloat16 if sibling else jnp.float32),
        in_specs=whole_vmem(len(flat) + 1),
        out_specs=pl.BlockSpec(memory_space=pltpu.VMEM),
        compiler_params=params(28),
        cost_estimate=pl.CostEstimate(
            flops=2 * n_tensor * depth * size * width,
            bytes_accessed=n_tensor * depth * (4 * size + 2 * width) + 4 * size * width,
            transcendentals=0,
        ),
        name="gradient_term",
    )(*flat, cotangents)


def adam_rows(kept, got, w_master, moment_one, moment_two):
    rows, width = kept.shape
    tile = min(128, rows)

    def kernel(kept_ref, got_ref, master_ref, one_ref, two_ref, update_ref, weight_ref):
        gradient = kept_ref[...] + got_ref[...].astype(jnp.float32)
        moment_new = beta_one * one_ref[...] + (1.0 - beta_one) * gradient
        second_new = beta_two * two_ref[...] + (1.0 - beta_two) * gradient * gradient
        scaled = second_new * (1.0 / bias_two)
        update = moment_new * (1.0 / bias_one) / (scaled * lax.rsqrt(scaled) + adam_eps)
        update_ref[...] = update
        weight_ref[...] = (master_ref[...] - learn_rate * update).astype(weight_ref.dtype)

    here = pl.BlockSpec((tile, width), lambda i: (i, 0))
    return pl.pallas_call(
        kernel,
        grid=(rows // tile,),
        out_shape=[
            jax.ShapeDtypeStruct((rows, width), jnp.float32),
            jax.ShapeDtypeStruct((rows, width), jnp.bfloat16),
        ],
        in_specs=[here] * 5,
        out_specs=[here] * 2,
        compiler_params=params(),
        cost_estimate=pl.CostEstimate(
            flops=16 * rows * width, bytes_accessed=24 * rows * width, transcendentals=rows * width
        ),
        name="adam_rows",
    )(kept, got, w_master, moment_one, moment_two)


def norm_columns(states, gain, rows, line):
    length, width = states.shape
    tile = 64

    def kernel(states_ref, gain_ref, kept, sent):
        core = own_core()
        total = jnp.zeros((tile, 1), jnp.float32)
        for block in range(2 * line):
            piece = states_ref[:, block * rows : (block + 1) * rows].astype(jnp.float32)
            total = total + jnp.sum(piece * piece, axis=1, keepdims=True)
        scale = lax.rsqrt(total / width + norm_eps)
        for flag in range(2):

            @pl.when(core == flag)
            def _():
                for block in range(2 * line):
                    out = kept if block % 2 == flag else sent
                    columns = slice(block * rows, (block + 1) * rows)
                    piece = states_ref[:, columns].astype(jnp.float32)
                    out[block // 2] = (piece * scale * gain_ref[:, columns]).astype(out.dtype)

    return pl.pallas_call(
        kernel,
        grid=(length // tile,),
        out_shape=[jax.ShapeDtypeStruct((line, length, rows), jnp.bfloat16)] * 2,
        in_specs=[
            pl.BlockSpec((tile, width), lambda i: (i, 0)),
            pl.BlockSpec((1, width), lambda i: (0, 0)),
        ],
        out_specs=[pl.BlockSpec((line, tile, rows), lambda i: (0, i, 0))] * 2,
        compiler_params=params(),
        cost_estimate=pl.CostEstimate(
            flops=6 * length * width, bytes_accessed=4 * length * width, transcendentals=0
        ),
        name="norm_columns",
    )(states, gain.reshape(1, width))


def accumulate(totals, kept, got, slots, last=False):
    _, length, depth = kept.shape
    width = slots[0][1].shape[1]
    count = len(slots)
    tile = min(256, length)
    owners = jnp.stack([jnp.asarray(owner, jnp.int32) for owner, _ in slots])
    weights = [weight for _, weight in slots]

    def kernel(owners_ref, *refs):
        weight_refs = refs[2 * count : 3 * count]
        for side, out_ref in zip((1, 0), reversed(refs[-2:])):
            result = None if totals is None else refs[3 * count + side][...]
            for slot in range(count):
                product = jnp.dot(
                    refs[side * count + slot][0],
                    weight_refs[slot][...],
                    preferred_element_type=jnp.float32,
                )
                result = product if result is None else result + product
            out_ref[...] = result.astype(out_ref.dtype)

    def state_spec(slot):
        return pl.BlockSpec((1, tile, depth), lambda i, chosen: (chosen[slot], i, 0))

    before = list(totals or [])
    row_spec = pl.BlockSpec((tile, width), lambda i, chosen: (i, 0))
    return pl.pallas_call(
        kernel,
        grid_spec=pltpu.PrefetchScalarGridSpec(
            num_scalar_prefetch=1,
            grid=(length // tile,),
            in_specs=[state_spec(slot) for slot in range(count)] * 2
            + [pl.BlockSpec((depth, width), lambda i, chosen: (0, 0))] * count
            + [row_spec] * len(before),
            out_specs=[row_spec] * 2,
        ),
        out_shape=[
            jax.ShapeDtypeStruct((length, width), jnp.float32),
            jax.ShapeDtypeStruct((length, width), jnp.bfloat16 if last else jnp.float32),
        ],
        compiler_params=params(20),
        cost_estimate=pl.CostEstimate(
            flops=4 * count * length * depth * width,
            bytes_accessed=2 * count * depth * (2 * length + width) + 16 * length * width,
            transcendentals=0,
        ),
        name="accumulate",
    )(owners, *([kept] * count), *([got] * count), *weights, *before)


def attention(kept, got, cosine_table, sine_table):
    length, width = kept.shape
    heads = width // HD - 2
    tile = min(128, length)

    def rope(u, cosine, sine):
        return u * cosine + pltpu.roll(u, HD // 2, 1) * sine

    def kernel(kept_ref, got_ref, cos_ref, sin_ref, out_ref):
        def columns(index, here=slice(None)):
            there = slice(index * HD, (index + 1) * HD)
            return kept_ref[here, there] + got_ref[here, there].astype(jnp.float32)

        keys = rope(columns(heads), cos_ref[...], sin_ref[...]).astype(jnp.bfloat16)
        values = columns(heads + 1).astype(jnp.bfloat16)
        for begin in range(0, length, tile):
            here, upto = slice(begin, begin + tile), begin + tile
            row = lax.broadcasted_iota(jnp.int32, (tile, upto), 0) + begin
            seen = row >= lax.broadcasted_iota(jnp.int32, (tile, upto), 1)
            for head in range(heads):
                query = rope(columns(head, here), cos_ref[here], sin_ref[here])
                query = (query * HD**-0.5).astype(jnp.bfloat16)
                scores = lax.dot_general(
                    query,
                    keys[:upto],
                    (((1,), (1,)), ((), ())),
                    preferred_element_type=jnp.float32,
                )
                scores = jnp.where(seen, scores, -jnp.inf)
                raised = jnp.exp(scores - jnp.max(scores, axis=1, keepdims=True))
                weights = raised * (1.0 / jnp.sum(raised, axis=1, keepdims=True))
                out_ref[here, head * HD : (head + 1) * HD] = jnp.dot(
                    weights.astype(jnp.bfloat16), values[:upto], preferred_element_type=jnp.float32
                ).astype(jnp.bfloat16)

    return pl.pallas_call(
        kernel,
        out_shape=jax.ShapeDtypeStruct((length, heads * HD), jnp.bfloat16),
        in_specs=whole_vmem(4),
        out_specs=pl.BlockSpec(memory_space=pltpu.VMEM),
        compiler_params=params(10),
        cost_estimate=pl.CostEstimate(
            flops=4 * heads * length * length * HD,
            bytes_accessed=9 * length * width,
            transcendentals=heads * length * length,
        ),
        name="attention",
    )(kept, got, cosine_table, sine_table)


def by_source(mine, other, n_tensor):
    kept, depth = mine.shape[0] // n_tensor, mine.shape[1]

    def kernel(mine_ref, other_ref, out_ref):
        index = lax.axis_index("tensor")
        for distance in range(n_tensor):
            columns = pl.ds(pl.multiple_of((index ^ distance) * depth, depth), depth)
            rows = slice(distance * kept, (distance + 1) * kept)
            out_ref[:kept, columns] = mine_ref[rows]
            out_ref[kept:, columns] = other_ref[rows]

    return pl.pallas_call(
        kernel,
        out_shape=jax.ShapeDtypeStruct((2 * kept, n_tensor * depth), mine.dtype),
        in_specs=whole_vmem(2),
        out_specs=pl.BlockSpec(memory_space=pltpu.VMEM),
        compiler_params=params(),
        name="by_source",
    )(mine, other)


def fetch(*arrays):
    parts = 4
    if sum(a.size * a.dtype.itemsize for a in arrays) > 20 * MIB:
        return arrays

    def kernel(*refs):
        sems = refs[-1]
        copies = []
        for which in range(len(arrays)):
            rows = arrays[which].shape[0] // parts
            for part in range(parts):
                here = pl.ds(part * rows, rows)
                copies.append(
                    pltpu.make_async_copy(
                        refs[which].at[here],
                        refs[len(arrays) + which].at[here],
                        sems.at[which * parts + part],
                    )
                )
        for copy in copies:
            copy.start()
        for copy in copies:
            copy.wait()

    return pl.pallas_call(
        kernel,
        out_shape=[jax.ShapeDtypeStruct(a.shape, a.dtype) for a in arrays],
        in_specs=[pl.BlockSpec(memory_space=pl.ANY)] * len(arrays),
        out_specs=whole_vmem(len(arrays)),
        scratch_shapes=[pltpu.SemaphoreType.DMA((parts * len(arrays),))],
        compiler_params=params(24),
        cost_estimate=pl.CostEstimate(
            flops=0, bytes_accessed=2 * sum(a.size * 2 for a in arrays), transcendentals=0
        ),
        name="fetch",
    )(*arrays)


def lay_out(blocks):
    kept = blocks[0][0].shape[0]
    half = sum(block.shape[1] for block in blocks[0])

    def kernel(*refs):
        out_ref = refs[-1]
        core = own_core()
        for flag in range(2):

            @pl.when(core == flag)
            def _():
                entry = 0
                for side in range(2):
                    begin = (flag ^ side) * half
                    for block in blocks[side]:
                        stop = begin + block.shape[1]
                        out_ref[:, begin:stop] = refs[entry][...]
                        begin, entry = stop, entry + 1

    flat = [block for side in blocks for block in side]
    return pl.pallas_call(
        kernel,
        out_shape=jax.ShapeDtypeStruct((kept, 2 * half), flat[0].dtype),
        in_specs=whole_vmem(len(flat)),
        out_specs=pl.BlockSpec(memory_space=pltpu.VMEM),
        compiler_params=params(),
        name="lay_out",
    )(*flat)


def body(
    train_states, qkv_cotangent, w_master, moment_one, moment_two, prompt_states, norm_gain, w_out
):
    n_dp = lax.axis_size("dp")
    n_tensor = lax.axis_size("tensor")
    line = n_dp // 2
    tensor_index = lax.axis_index("tensor")
    core, place = own_core(), own_place()
    siblings = [(i, i ^ 1) for i in range(n_dp)]
    rows, slice_width = w_master.shape
    tokens, width = train_states.shape
    length = prompt_states.shape[0]
    query_width = slice_width - 2 * HD

    kept_states, sent_states = norm_columns(prompt_states, norm_gain, rows, line)
    got_states = lax.ppermute(sent_states, "dp", siblings)

    core_width = width // 2
    early_width = EARLY_BLOCKS * core_width // 32
    packed, w_early = pack_columns(
        train_states, w_out, rows, line, tokens // n_tensor, early_width
    )
    def across(block, distance):
        return lax.ppermute(block, "dp", line_pairs([(i, i ^ distance) for i in range(line)]))

    pieces = [packed[0]] + [across(packed[distance], distance) for distance in range(1, line)]
    pieces = tie(pieces, kept_states)

    cotangents = [qkv_cotangent, across(qkv_cotangent, 1)]
    spread = PlaneGather(stack_pieces(pieces), n_tensor)
    behind = pieces
    for distance in range(2, line):
        cotangents.append(across(tie((qkv_cotangent,), *behind)[0], distance))
        behind = cotangents[-1:]
    spread.second(cotangents[2], spread.blocks[1:])
    all_cotangents = place_cotangents(cotangents, n_tensor)

    w_rest = lax.dynamic_slice(
        w_out,
        (0, core * core_width + early_width),
        (w_out.shape[0], core_width - early_width),
    )
    early_weight = lax.all_gather(w_early, "tensor", axis=0, tiled=True)
    (w_rest,) = tie((w_rest,), spread.blocks, cotangents, early_weight)
    rest_weight = lax.all_gather(w_rest, "tensor", axis=0, tiled=True)

    sent = gradient_term(spread.blocks, all_cotangents, True)
    got = lax.ppermute(sent, "dp", siblings)
    kept = gradient_term(spread.blocks, all_cotangents, False)
    update_dir, weight = adam_rows(kept, got, w_master, moment_one, moment_two)

    weights = LineGather(weight, place, line)

    def add(totals, steps, last=False):
        slots = [weights.slot(step) for step in steps]
        return accumulate(totals, kept_states, got_states, slots, last)

    for _ in range(1, line - 1):
        weights.hop()
    totals = add(None, range(line - 2))
    cosine_table, sine_table = rope_tables(length, HD)
    cosine_table, sine_table, *totals = tie((cosine_table, sine_table, *totals))
    weights.hop(*totals, cosine_table, sine_table)
    totals = add(totals, [line - 2])
    totals = add(totals, [line - 1], True)
    attended = attention(
        totals[0], lax.ppermute(totals[1], "dp", siblings), cosine_table, sine_table
    )

    kept_rows = length // n_tensor
    heads = []
    for distance in range(n_tensor):
        target = tensor_index ^ distance
        block = lax.dynamic_slice(attended, (target * kept_rows, 0), (kept_rows, query_width))
        if distance:
            block = lax.ppermute(block, "tensor", [(j, j ^ distance) for j in range(n_tensor)])
        heads.append(block)
    fetched = fetch(early_weight, rest_weight)
    heads = tie(heads, *fetched)
    (mine,) = stack_pieces([head[None] for head in heads])
    other = lax.ppermute(mine, "dp", siblings)
    both = by_source(mine, other, n_tensor)
    mine, sent = [], []
    for weight in fetched:
        made = jnp.dot(both, weight, preferred_element_type=jnp.float32).astype(jnp.bfloat16)
        mine.append(made[:kept_rows])
        sent.append(made[kept_rows:])
    summed = lay_out((mine, [lax.ppermute(rows, "dp", siblings) for rows in sent]))
    return (update_dir, summed)


def solution(mesh):
    placed = (
        P("dp", None),
        P("dp", "tensor"),
        P("dp", "tensor"),
        P("dp", "tensor"),
        P("dp", "tensor"),
        P("dp", None),
        P(),
        P("tensor", None),
    )
    return jax.shard_map(
        body,
        mesh=mesh,
        in_specs=placed,
        out_specs=(P("dp", "tensor"), P(("dp", "tensor"), None)),
        check_vma=False,
    )
```

```python
import functools

import jax
import jax.numpy as jnp
from jax import lax
from jax.experimental import pallas as pl
from jax.experimental.pallas import tpu as pltpu
from jax.sharding import PartitionSpec as P

HD = 128


beta_one = 0.9
beta_two = 0.95
bias_one = 1.0 - 0.9**8
bias_two = 1.0 - 0.95**8
learn_rate = 0.002
adam_eps = 1e-08
norm_eps = 1e-05
rope_base = 500000.0

MIB = 1024 * 1024
EARLY_BLOCKS = 3


def rope_tables(length, head_size):
    half_width = head_size // 2
    exponent = jnp.arange(half_width, dtype=jnp.float32) * (2.0 / head_size)
    inverse = jnp.power(jnp.float32(rope_base), -exponent)
    position = jnp.arange(length, dtype=jnp.float32)
    angles = position[:, None] * inverse[None, :]
    cosine_table = jnp.concatenate([jnp.cos(angles), jnp.cos(angles)], axis=1)
    sine_table = jnp.concatenate([-jnp.sin(angles), jnp.sin(angles)], axis=1)
    return (cosine_table, sine_table)


def params(mib=16):
    return pltpu.CompilerParams(vmem_limit_bytes=mib * MIB)


def whole_vmem(count):
    return [pl.BlockSpec(memory_space=pltpu.VMEM)] * count


def own_core():
    return lax.rem(lax.axis_index("dp"), 2)


def own_place():
    return lax.div(lax.axis_index("dp"), 2)


def pack_columns(train_states, w_out, rows, line, quarter, early_width):
    width = train_states.shape[1]
    block = early_width // EARLY_BLOCKS

    def kernel(chosen_ref, train_ref, *refs):
        w_out_refs, outs = refs[:EARLY_BLOCKS], refs[EARLY_BLOCKS:]
        place = own_place()
        for distance in range(line):
            for owner in range(2):
                column = pl.multiple_of(((place ^ distance) * 2 + owner) * rows, 128)
                outs[distance][owner] = train_ref[:, pl.ds(column, rows)]
        for entry, w_out_ref in enumerate(w_out_refs):
            outs[line][:, entry * block : (entry + 1) * block] = w_out_ref[...]

    shapes = [jax.ShapeDtypeStruct((2, quarter, rows), train_states.dtype)] * line
    early = jax.ShapeDtypeStruct((w_out.shape[0], early_width), w_out.dtype)
    chosen = jnp.stack([lax.axis_index("tensor"), own_core() * (width // 2 // block)]).astype(jnp.int32)
    outs = pl.pallas_call(
        kernel,
        grid_spec=pltpu.PrefetchScalarGridSpec(
            num_scalar_prefetch=1,
            grid=(1,),
            in_specs=[
                pl.BlockSpec((quarter, width), lambda i, chosen: (chosen[0], 0)),
            ]
            + [
                pl.BlockSpec(
                    (w_out.shape[0], block), lambda i, chosen, entry=entry: (0, chosen[1] + entry)
                )
                for entry in range(EARLY_BLOCKS)
            ],
            out_specs=[pl.BlockSpec(s.shape, lambda i, chosen: (0, 0, 0)) for s in shapes]
            + [pl.BlockSpec(early.shape, lambda i, chosen: (0, 0))],
        ),
        out_shape=shapes + [early],
        compiler_params=params(56),
        name="pack_columns",
    )(chosen, train_states, *([w_out] * EARLY_BLOCKS))
    return outs[:line], outs[line]


def stack_pieces(pieces):
    outer, height, width = pieces[0].shape
    count = len(pieces)

    def kernel(*refs):
        for which in range(outer):
            for i in range(count):
                refs[count + which][i * height : (i + 1) * height] = refs[i][which]

    return pl.pallas_call(
        kernel,
        out_shape=[jax.ShapeDtypeStruct((count * height, width), pieces[0].dtype)] * outer,
        in_specs=whole_vmem(count),
        out_specs=whole_vmem(outer),
        compiler_params=params(),
        name="stack_pieces",
    )(*pieces)


def line_pairs(places):
    return [(2 * a + core, 2 * b + core) for a, b in places for core in range(2)]


def tie(arrays, *others):
    return lax.optimization_barrier((tuple(arrays), others))[0]


class LineGather:
    def __init__(self, block, place, count):
        self.place, self.count = place, count
        self.low, self.high = [block], [block]

    def hop(self, *behind):
        step, count = len(self.low), self.count
        up, down = self.low[-1], self.high[-1]
        if behind:
            up, down = tie((up, down), *behind)
        right = line_pairs([(i, i + 1) for i in range(step - 1, count - 1)])
        left = line_pairs([(i, i - 1) for i in range(1, count - step + 1)])
        if step == count - 1:
            self.high.append(lax.ppermute(down, "dp", left))
            self.low.append(lax.ppermute(up, "dp", right))
            return
        self.low.append(lax.ppermute(up, "dp", right))
        self.high.append(lax.ppermute(down, "dp", left))

    def arrived(self):
        return self.low[-1], self.high[-1]

    def slot(self, step):
        if step == 0:
            return self.place, self.low[0]
        sides = (self.low, self.high)
        choices = line_choice(step, self.place, self.count)
        _, side, entry, owner = choices[-1]
        block = sides[side][entry]
        for holds, side, entry, other in reversed(choices[:-1]):
            block = jnp.where(holds, sides[side][entry], block)
            owner = jnp.where(holds, other, owner)
        return owner, block


def line_choice(step, place, count):
    is_low, is_high = place >= step, place <= count - 1 - step
    spare = count - step
    return [
        (is_low, 0, step, place - step),
        (jnp.logical_and(jnp.logical_not(is_low), is_high), 1, step, place + step),
        (
            jnp.logical_and(jnp.logical_not(is_low), jnp.logical_not(is_high)),
            1,
            spare,
            place + spare,
        ),
    ][: 2 if 2 * step <= count else 3]


def place_cotangents(blocks, n_tensor):
    tokens, width = blocks[0].shape
    quarter = tokens // n_tensor
    count = len(blocks)

    def kernel(*refs):
        for distance in range(count):
            refs[count][:, distance * quarter : (distance + 1) * quarter] = refs[distance][...]

    return pl.pallas_call(
        kernel,
        out_shape=jax.ShapeDtypeStruct((n_tensor, count * quarter, width), blocks[0].dtype),
        in_specs=whole_vmem(count),
        out_specs=pl.BlockSpec(memory_space=pltpu.VMEM),
        compiler_params=params(),
        name="place_cotangents",
    )(*[block.reshape(n_tensor, quarter, width) for block in blocks])


def plane_permute(block, count, distance):
    return lax.ppermute(block, "tensor", [(j, j ^ distance) for j in range(count)])


class PlaneGather:
    def __init__(self, pair, count):
        self.count = count
        if count != 4:
            own = lax.axis_index("tensor")
            gathered = [lax.all_gather(block, "tensor", axis=0) for block in pair]
            self.blocks = [
                [lax.dynamic_index_in_dim(g, own ^ b, 0, keepdims=False) for g in gathered]
                for b in range(count)
            ]
            return
        one, two = [None, None], [None, None]
        for owner in range(2):
            one[owner] = plane_permute(pair[owner], count, 1)
            two[1 - owner] = plane_permute(pair[1 - owner], count, 2)
        self.blocks = [list(pair), one, two]

    def passed(self):
        return [self.blocks[1][0], self.blocks[2][1]]

    def second(self, *behind):
        if self.count == 4:
            up, down = tie(self.passed(), *behind)
            self.blocks.append(
                [plane_permute(up, self.count, 2), plane_permute(down, self.count, 1)]
            )


def gradient_term(blocks, cotangents, sibling):
    n_tensor, depth, width = cotangents.shape
    size = blocks[0][0].shape[1]
    flat = [block for pair in blocks for block in pair]

    def kernel(*refs):
        cotangent_ref, out_ref = refs[len(flat) :]
        index = lax.axis_index("tensor")
        owner = 1 - own_core() if sibling else own_core()
        total = None
        for distance in range(n_tensor):
            lower, upper = refs[2 * distance : 2 * distance + 2]
            product = lax.dot_general(
                jnp.where(owner == 0, lower[...], upper[...]),
                cotangent_ref[index ^ distance],
                (((0,), (0,)), ((), ())),
                preferred_element_type=jnp.float32,
            )
            total = product if total is None else total + product
        out_ref[...] = total.astype(out_ref.dtype)

    return pl.pallas_call(
        kernel,
        out_shape=jax.ShapeDtypeStruct((size, width), jnp.bfloat16 if sibling else jnp.float32),
        in_specs=whole_vmem(len(flat) + 1),
        out_specs=pl.BlockSpec(memory_space=pltpu.VMEM),
        compiler_params=params(28),
        cost_estimate=pl.CostEstimate(
            flops=2 * n_tensor * depth * size * width,
            bytes_accessed=n_tensor * depth * (4 * size + 2 * width) + 4 * size * width,
            transcendentals=0,
        ),
        name="gradient_term",
    )(*flat, cotangents)


def adam_rows(kept, got, w_master, moment_one, moment_two):
    rows, width = kept.shape
    tile = min(128, rows)

    def kernel(kept_ref, got_ref, master_ref, one_ref, two_ref, update_ref, weight_ref):
        gradient = kept_ref[...] + got_ref[...].astype(jnp.float32)
        moment_new = beta_one * one_ref[...] + (1.0 - beta_one) * gradient
        second_new = beta_two * two_ref[...] + (1.0 - beta_two) * gradient * gradient
        scaled = second_new * (1.0 / bias_two)
        update = moment_new * (1.0 / bias_one) / (scaled * lax.rsqrt(scaled) + adam_eps)
        update_ref[...] = update
        weight_ref[...] = (master_ref[...] - learn_rate * update).astype(weight_ref.dtype)

    here = pl.BlockSpec((tile, width), lambda i: (i, 0))
    return pl.pallas_call(
        kernel,
        grid=(rows // tile,),
        out_shape=[
            jax.ShapeDtypeStruct((rows, width), jnp.float32),
            jax.ShapeDtypeStruct((rows, width), jnp.bfloat16),
        ],
        in_specs=[here] * 5,
        out_specs=[here] * 2,
        compiler_params=params(),
        cost_estimate=pl.CostEstimate(
            flops=16 * rows * width, bytes_accessed=24 * rows * width, transcendentals=rows * width
        ),
        name="adam_rows",
    )(kept, got, w_master, moment_one, moment_two)


def norm_columns(states, gain, rows, line):
    length, width = states.shape
    tile = 64

    def kernel(states_ref, gain_ref, kept, sent):
        core = own_core()
        total = jnp.zeros((tile, 1), jnp.float32)
        for block in range(2 * line):
            piece = states_ref[:, block * rows : (block + 1) * rows].astype(jnp.float32)
            total = total + jnp.sum(piece * piece, axis=1, keepdims=True)
        scale = lax.rsqrt(total / width + norm_eps)
        for flag in range(2):

            @pl.when(core == flag)
            def _():
                for block in range(2 * line):
                    out = kept if block % 2 == flag else sent
                    columns = slice(block * rows, (block + 1) * rows)
                    piece = states_ref[:, columns].astype(jnp.float32)
                    out[block // 2] = (piece * scale * gain_ref[:, columns]).astype(out.dtype)

    return pl.pallas_call(
        kernel,
        grid=(length // tile,),
        out_shape=[jax.ShapeDtypeStruct((line, length, rows), jnp.bfloat16)] * 2,
        in_specs=[
            pl.BlockSpec((tile, width), lambda i: (i, 0)),
            pl.BlockSpec((1, width), lambda i: (0, 0)),
        ],
        out_specs=[pl.BlockSpec((line, tile, rows), lambda i: (0, i, 0))] * 2,
        compiler_params=params(),
        cost_estimate=pl.CostEstimate(
            flops=6 * length * width, bytes_accessed=4 * length * width, transcendentals=0
        ),
        name="norm_columns",
    )(states, gain.reshape(1, width))


def accumulate(totals, states, slots, dtypes):
    _, length, depth = states[0].shape
    sides = len(states)
    width = slots[0][1].shape[1]
    count = len(slots)
    tile = min(256, length)
    owners = jnp.stack([jnp.asarray(owner, jnp.int32) for owner, _ in slots])
    weights = [weight for _, weight in slots]

    def kernel(owners_ref, *refs):
        weight_refs = refs[sides * count : (sides + 1) * count]
        for side, out_ref in enumerate(refs[-sides:]):
            result = None if totals is None else refs[(sides + 1) * count + side][...]
            for slot in range(count):
                product = jnp.dot(
                    refs[side * count + slot][0],
                    weight_refs[slot][...],
                    preferred_element_type=jnp.float32,
                )
                result = product if result is None else result + product
            out_ref[...] = result.astype(out_ref.dtype)

    def state_spec(slot):
        return pl.BlockSpec((1, tile, depth), lambda i, chosen: (chosen[slot], i, 0))

    before = list(totals or [])
    row_spec = pl.BlockSpec((tile, width), lambda i, chosen: (i, 0))
    return pl.pallas_call(
        kernel,
        grid_spec=pltpu.PrefetchScalarGridSpec(
            num_scalar_prefetch=1,
            grid=(length // tile,),
            in_specs=[state_spec(slot) for slot in range(count)] * sides
            + [pl.BlockSpec((depth, width), lambda i, chosen: (0, 0))] * count
            + [row_spec] * len(before),
            out_specs=[row_spec] * sides,
        ),
        out_shape=[jax.ShapeDtypeStruct((length, width), dtype) for dtype in dtypes],
        compiler_params=params(20),
        cost_estimate=pl.CostEstimate(
            flops=2 * sides * count * length * depth * width,
            bytes_accessed=2 * count * depth * (2 * length + width) + 16 * length * width,
            transcendentals=0,
        ),
        name="accumulate",
    )(owners, *[array for array in states for _ in range(count)], *weights, *before)


def attention(kept, got, cosine_table, sine_table):
    length, width = kept.shape
    heads = width // HD - 2
    tile = min(128, length)

    def rope(u, cosine, sine):
        return u * cosine + pltpu.roll(u, HD // 2, 1) * sine

    def kernel(kept_ref, got_ref, cos_ref, sin_ref, out_ref):
        def columns(index, here=slice(None)):
            there = slice(index * HD, (index + 1) * HD)
            return kept_ref[here, there] + got_ref[here, there].astype(jnp.float32)

        keys = rope(columns(heads), cos_ref[...], sin_ref[...]).astype(jnp.bfloat16)
        values = columns(heads + 1).astype(jnp.bfloat16)
        for begin in range(0, length, tile):
            here, upto = slice(begin, begin + tile), begin + tile
            row = lax.broadcasted_iota(jnp.int32, (tile, upto), 0) + begin
            seen = row >= lax.broadcasted_iota(jnp.int32, (tile, upto), 1)
            for head in range(heads):
                query = rope(columns(head, here), cos_ref[here], sin_ref[here])
                query = (query * HD**-0.5).astype(jnp.bfloat16)
                scores = lax.dot_general(
                    query,
                    keys[:upto],
                    (((1,), (1,)), ((), ())),
                    preferred_element_type=jnp.float32,
                )
                scores = jnp.where(seen, scores, -jnp.inf)
                raised = jnp.exp(scores - jnp.max(scores, axis=1, keepdims=True))
                weights = raised * (1.0 / jnp.sum(raised, axis=1, keepdims=True))
                out_ref[here, head * HD : (head + 1) * HD] = jnp.dot(
                    weights.astype(jnp.bfloat16), values[:upto], preferred_element_type=jnp.float32
                ).astype(jnp.bfloat16)

    return pl.pallas_call(
        kernel,
        out_shape=jax.ShapeDtypeStruct((length, heads * HD), jnp.bfloat16),
        in_specs=whole_vmem(4),
        out_specs=pl.BlockSpec(memory_space=pltpu.VMEM),
        compiler_params=params(10),
        cost_estimate=pl.CostEstimate(
            flops=4 * heads * length * length * HD,
            bytes_accessed=9 * length * width,
            transcendentals=heads * length * length,
        ),
        name="attention",
    )(kept, got, cosine_table, sine_table)


def by_source(mine, other, n_tensor):
    kept, depth = mine.shape[0] // n_tensor, mine.shape[1]

    def kernel(mine_ref, other_ref, out_ref):
        index = lax.axis_index("tensor")
        for distance in range(n_tensor):
            columns = pl.ds(pl.multiple_of((index ^ distance) * depth, depth), depth)
            rows = slice(distance * kept, (distance + 1) * kept)
            out_ref[:kept, columns] = mine_ref[rows]
            out_ref[kept:, columns] = other_ref[rows]

    return pl.pallas_call(
        kernel,
        out_shape=jax.ShapeDtypeStruct((2 * kept, n_tensor * depth), mine.dtype),
        in_specs=whole_vmem(2),
        out_specs=pl.BlockSpec(memory_space=pltpu.VMEM),
        compiler_params=params(),
        name="by_source",
    )(mine, other)


def fetch(*arrays):
    parts = 4
    if sum(a.size * a.dtype.itemsize for a in arrays) > 20 * MIB:
        return arrays

    def kernel(*refs):
        sems = refs[-1]
        copies = []
        for which in range(len(arrays)):
            rows = arrays[which].shape[0] // parts
            for part in range(parts):
                here = pl.ds(part * rows, rows)
                copies.append(
                    pltpu.make_async_copy(
                        refs[which].at[here],
                        refs[len(arrays) + which].at[here],
                        sems.at[which * parts + part],
                    )
                )
        for copy in copies:
            copy.start()
        for copy in copies:
            copy.wait()

    return pl.pallas_call(
        kernel,
        out_shape=[jax.ShapeDtypeStruct(a.shape, a.dtype) for a in arrays],
        in_specs=[pl.BlockSpec(memory_space=pl.ANY)] * len(arrays),
        out_specs=whole_vmem(len(arrays)),
        scratch_shapes=[pltpu.SemaphoreType.DMA((parts * len(arrays),))],
        compiler_params=params(24),
        cost_estimate=pl.CostEstimate(
            flops=0, bytes_accessed=2 * sum(a.size * 2 for a in arrays), transcendentals=0
        ),
        name="fetch",
    )(*arrays)


def lay_out(blocks):
    kept = blocks[0][0].shape[0]
    half = sum(block.shape[1] for block in blocks[0])

    def kernel(*refs):
        out_ref = refs[-1]
        core = own_core()
        for flag in range(2):

            @pl.when(core == flag)
            def _():
                entry = 0
                for side in range(2):
                    begin = (flag ^ side) * half
                    for block in blocks[side]:
                        stop = begin + block.shape[1]
                        out_ref[:, begin:stop] = refs[entry][...]
                        begin, entry = stop, entry + 1

    flat = [block for side in blocks for block in side]
    return pl.pallas_call(
        kernel,
        out_shape=jax.ShapeDtypeStruct((kept, 2 * half), flat[0].dtype),
        in_specs=whole_vmem(len(flat)),
        out_specs=pl.BlockSpec(memory_space=pltpu.VMEM),
        compiler_params=params(),
        name="lay_out",
    )(*flat)


def body(
    train_states, qkv_cotangent, w_master, moment_one, moment_two, prompt_states, norm_gain, w_out
):
    n_dp = lax.axis_size("dp")
    n_tensor = lax.axis_size("tensor")
    line = n_dp // 2
    tensor_index = lax.axis_index("tensor")
    core, place = own_core(), own_place()
    siblings = [(i, i ^ 1) for i in range(n_dp)]
    rows, slice_width = w_master.shape
    tokens, width = train_states.shape
    length = prompt_states.shape[0]
    query_width = slice_width - 2 * HD

    kept_states, sent_states = norm_columns(prompt_states, norm_gain, rows, line)
    got_states = lax.ppermute(sent_states, "dp", siblings)

    core_width = width // 2
    early_width = EARLY_BLOCKS * core_width // 32
    packed, w_early = pack_columns(
        train_states, w_out, rows, line, tokens // n_tensor, early_width
    )
    def across(block, distance):
        return lax.ppermute(block, "dp", line_pairs([(i, i ^ distance) for i in range(line)]))

    pieces = [packed[0]] + [across(packed[distance], distance) for distance in range(1, line)]
    pieces = tie(pieces, kept_states)

    cotangents = [qkv_cotangent, across(qkv_cotangent, 1)]
    spread = PlaneGather(stack_pieces(pieces), n_tensor)
    behind = pieces
    for distance in range(2, line):
        cotangents.append(across(tie((qkv_cotangent,), *behind)[0], distance))
        behind = cotangents[-1:]
    spread.second(cotangents[2], spread.blocks[1:])
    all_cotangents = place_cotangents(cotangents, n_tensor)

    w_rest = lax.dynamic_slice(
        w_out,
        (0, core * core_width + early_width),
        (w_out.shape[0], core_width - early_width),
    )
    early_weight = lax.all_gather(w_early, "tensor", axis=0, tiled=True)
    (w_rest,) = tie((w_rest,), spread.blocks, cotangents, early_weight)
    rest_weight = lax.all_gather(w_rest, "tensor", axis=0, tiled=True)

    sent = gradient_term(spread.blocks, all_cotangents, True)
    got = lax.ppermute(sent, "dp", siblings)
    kept = gradient_term(spread.blocks, all_cotangents, False)
    update_dir, weight = adam_rows(kept, got, w_master, moment_one, moment_two)

    weights = LineGather(weight, place, line)

    def add(totals, states, steps, dtype=jnp.float32):
        slots = [weights.slot(step) for step in steps]
        return accumulate(totals, states, slots, [dtype] * len(states))

    both_states = (kept_states, got_states)
    for _ in range(1, line - 1):
        weights.hop()
    totals = add(None, both_states, range(line - 2))
    cosine_table, sine_table = rope_tables(length, HD)
    cosine_table, sine_table, *totals = tie((cosine_table, sine_table, *totals))
    weights.hop(*totals, cosine_table, sine_table)
    own_total, other_total = add(totals, both_states, [line - 2])
    (other_total,) = add([other_total], [got_states], [line - 1], jnp.bfloat16)
    got_total = lax.ppermute(other_total, "dp", siblings)
    (own_total,) = add([own_total], [kept_states], [line - 1])
    attended = attention(own_total, got_total, cosine_table, sine_table)

    kept_rows = length // n_tensor
    heads = []
    for distance in range(n_tensor):
        target = tensor_index ^ distance
        block = lax.dynamic_slice(attended, (target * kept_rows, 0), (kept_rows, query_width))
        if distance:
            block = lax.ppermute(block, "tensor", [(j, j ^ distance) for j in range(n_tensor)])
        heads.append(block)
    fetched = fetch(early_weight, rest_weight)
    heads = tie(heads, *fetched)
    (mine,) = stack_pieces([head[None] for head in heads])
    other = lax.ppermute(mine, "dp", siblings)
    both = by_source(mine, other, n_tensor)
    mine, sent = [], []
    for weight in fetched:
        made = jnp.dot(both, weight, preferred_element_type=jnp.float32).astype(jnp.bfloat16)
        mine.append(made[:kept_rows])
        sent.append(made[kept_rows:])
    summed = lay_out((mine, [lax.ppermute(rows, "dp", siblings) for rows in sent]))
    return (update_dir, summed)


def solution(mesh):
    placed = (
        P("dp", None),
        P("dp", "tensor"),
        P("dp", "tensor"),
        P("dp", "tensor"),
        P("dp", "tensor"),
        P("dp", None),
        P(),
        P("tensor", None),
    )
    return jax.shard_map(
        body,
        mesh=mesh,
        in_specs=placed,
        out_specs=(P("dp", "tensor"), P(("dp", "tensor"), None)),
        check_vma=False,
    )
```

```python
import functools

import jax
import jax.numpy as jnp
from jax import lax
from jax.experimental import pallas as pl
from jax.experimental.pallas import tpu as pltpu
from jax.sharding import PartitionSpec as P

HD = 128


beta_one = 0.9
beta_two = 0.95
bias_one = 1.0 - 0.9**8
bias_two = 1.0 - 0.95**8
learn_rate = 0.002
adam_eps = 1e-08
norm_eps = 1e-05
rope_base = 500000.0

MIB = 1024 * 1024
EARLY_BLOCKS = 3


def rope_tables(length, head_size):
    half_width = head_size // 2
    exponent = jnp.arange(half_width, dtype=jnp.float32) * (2.0 / head_size)
    inverse = jnp.power(jnp.float32(rope_base), -exponent)
    position = jnp.arange(length, dtype=jnp.float32)
    angles = position[:, None] * inverse[None, :]
    cosine_table = jnp.concatenate([jnp.cos(angles), jnp.cos(angles)], axis=1)
    sine_table = jnp.concatenate([-jnp.sin(angles), jnp.sin(angles)], axis=1)
    return (cosine_table, sine_table)


def params(mib=16):
    return pltpu.CompilerParams(vmem_limit_bytes=mib * MIB)


def whole_vmem(count):
    return [pl.BlockSpec(memory_space=pltpu.VMEM)] * count


def own_core():
    return lax.rem(lax.axis_index("dp"), 2)


def own_place():
    return lax.div(lax.axis_index("dp"), 2)


def pack_columns(train_states, w_out, rows, line, quarter, early_width):
    width = train_states.shape[1]
    block = early_width // EARLY_BLOCKS

    def kernel(chosen_ref, train_ref, *refs):
        w_out_refs, outs = refs[:EARLY_BLOCKS], refs[EARLY_BLOCKS:]
        place = own_place()
        for distance in range(line):
            for owner in range(2):
                column = pl.multiple_of(((place ^ distance) * 2 + owner) * rows, 128)
                outs[distance][owner] = train_ref[:, pl.ds(column, rows)]
        for entry, w_out_ref in enumerate(w_out_refs):
            outs[line][:, entry * block : (entry + 1) * block] = w_out_ref[...]

    shapes = [jax.ShapeDtypeStruct((2, quarter, rows), train_states.dtype)] * line
    early = jax.ShapeDtypeStruct((w_out.shape[0], early_width), w_out.dtype)
    chosen = jnp.stack([lax.axis_index("tensor"), own_core() * (width // 2 // block)]).astype(jnp.int32)
    outs = pl.pallas_call(
        kernel,
        grid_spec=pltpu.PrefetchScalarGridSpec(
            num_scalar_prefetch=1,
            grid=(1,),
            in_specs=[
                pl.BlockSpec((quarter, width), lambda i, chosen: (chosen[0], 0)),
            ]
            + [
                pl.BlockSpec(
                    (w_out.shape[0], block), lambda i, chosen, entry=entry: (0, chosen[1] + entry)
                )
                for entry in range(EARLY_BLOCKS)
            ],
            out_specs=[pl.BlockSpec(s.shape, lambda i, chosen: (0, 0, 0)) for s in shapes]
            + [pl.BlockSpec(early.shape, lambda i, chosen: (0, 0))],
        ),
        out_shape=shapes + [early],
        compiler_params=params(56),
        name="pack_columns",
    )(chosen, train_states, *([w_out] * EARLY_BLOCKS))
    return outs[:line], outs[line]


def stack_pieces(pieces):
    outer, height, width = pieces[0].shape
    count = len(pieces)

    def kernel(*refs):
        for which in range(outer):
            for i in range(count):
                refs[count + which][i * height : (i + 1) * height] = refs[i][which]

    return pl.pallas_call(
        kernel,
        out_shape=[jax.ShapeDtypeStruct((count * height, width), pieces[0].dtype)] * outer,
        in_specs=whole_vmem(count),
        out_specs=whole_vmem(outer),
        compiler_params=params(),
        name="stack_pieces",
    )(*pieces)


def line_pairs(places):
    return [(2 * a + core, 2 * b + core) for a, b in places for core in range(2)]


def tie(arrays, *others):
    return lax.optimization_barrier((tuple(arrays), others))[0]


class LineGather:
    def __init__(self, block, place, count):
        self.place, self.count = place, count
        self.low, self.high = [block], [block]

    def hop(self, *behind):
        step, count = len(self.low), self.count
        up, down = self.low[-1], self.high[-1]
        if behind:
            up, down = tie((up, down), *behind)
        right = line_pairs([(i, i + 1) for i in range(step - 1, count - 1)])
        left = line_pairs([(i, i - 1) for i in range(1, count - step + 1)])
        if step == count - 1:
            self.high.append(lax.ppermute(down, "dp", left))
            self.low.append(lax.ppermute(up, "dp", right))
            return
        self.low.append(lax.ppermute(up, "dp", right))
        self.high.append(lax.ppermute(down, "dp", left))

    def arrived(self):
        return self.low[-1], self.high[-1]

    def slot(self, step):
        if step == 0:
            return self.place, self.low[0]
        sides = (self.low, self.high)
        choices = line_choice(step, self.place, self.count)
        _, side, entry, owner = choices[-1]
        block = sides[side][entry]
        for holds, side, entry, other in reversed(choices[:-1]):
            block = jnp.where(holds, sides[side][entry], block)
            owner = jnp.where(holds, other, owner)
        return owner, block


def line_choice(step, place, count):
    is_low, is_high = place >= step, place <= count - 1 - step
    spare = count - step
    return [
        (is_low, 0, step, place - step),
        (jnp.logical_and(jnp.logical_not(is_low), is_high), 1, step, place + step),
        (
            jnp.logical_and(jnp.logical_not(is_low), jnp.logical_not(is_high)),
            1,
            spare,
            place + spare,
        ),
    ][: 2 if 2 * step <= count else 3]


def place_cotangents(blocks, n_tensor):
    tokens, width = blocks[0].shape
    quarter = tokens // n_tensor
    count = len(blocks)

    def kernel(*refs):
        for distance in range(count):
            refs[count][:, distance * quarter : (distance + 1) * quarter] = refs[distance][...]

    return pl.pallas_call(
        kernel,
        out_shape=jax.ShapeDtypeStruct((n_tensor, count * quarter, width), blocks[0].dtype),
        in_specs=whole_vmem(count),
        out_specs=pl.BlockSpec(memory_space=pltpu.VMEM),
        compiler_params=params(),
        name="place_cotangents",
    )(*[block.reshape(n_tensor, quarter, width) for block in blocks])


def plane_permute(block, count, distance):
    return lax.ppermute(block, "tensor", [(j, j ^ distance) for j in range(count)])


class PlaneGather:
    def __init__(self, pair, count):
        self.count = count
        if count != 4:
            own = lax.axis_index("tensor")
            gathered = [lax.all_gather(block, "tensor", axis=0) for block in pair]
            self.blocks = [
                [lax.dynamic_index_in_dim(g, own ^ b, 0, keepdims=False) for g in gathered]
                for b in range(count)
            ]
            return
        one, two = [None, None], [None, None]
        for owner in range(2):
            one[owner] = plane_permute(pair[owner], count, 1)
            two[1 - owner] = plane_permute(pair[1 - owner], count, 2)
        self.blocks = [list(pair), one, two]

    def passed(self):
        return [self.blocks[1][0], self.blocks[2][1]]

    def second(self, *behind):
        if self.count == 4:
            up, down = tie(self.passed(), *behind)
            self.blocks.append(
                [plane_permute(up, self.count, 2), plane_permute(down, self.count, 1)]
            )


def gradient_term(blocks, cotangents, sibling):
    n_tensor, depth, width = cotangents.shape
    size = blocks[0][0].shape[1]
    flat = [block for pair in blocks for block in pair]

    def kernel(*refs):
        cotangent_ref, out_ref = refs[len(flat) :]
        index = lax.axis_index("tensor")
        owner = 1 - own_core() if sibling else own_core()
        total = None
        for distance in range(n_tensor):
            lower, upper = refs[2 * distance : 2 * distance + 2]
            product = lax.dot_general(
                jnp.where(owner == 0, lower[...], upper[...]),
                cotangent_ref[index ^ distance],
                (((0,), (0,)), ((), ())),
                preferred_element_type=jnp.float32,
            )
            total = product if total is None else total + product
        out_ref[...] = total.astype(out_ref.dtype)

    return pl.pallas_call(
        kernel,
        out_shape=jax.ShapeDtypeStruct((size, width), jnp.bfloat16 if sibling else jnp.float32),
        in_specs=whole_vmem(len(flat) + 1),
        out_specs=pl.BlockSpec(memory_space=pltpu.VMEM),
        compiler_params=params(28),
        cost_estimate=pl.CostEstimate(
            flops=2 * n_tensor * depth * size * width,
            bytes_accessed=n_tensor * depth * (4 * size + 2 * width) + 4 * size * width,
            transcendentals=0,
        ),
        name="gradient_term",
    )(*flat, cotangents)


def adam_rows(kept, got, w_master, moment_one, moment_two):
    rows, width = kept.shape
    tile = min(128, rows)

    def kernel(kept_ref, got_ref, master_ref, one_ref, two_ref, update_ref, weight_ref):
        gradient = kept_ref[...] + got_ref[...].astype(jnp.float32)
        moment_new = beta_one * one_ref[...] + (1.0 - beta_one) * gradient
        second_new = beta_two * two_ref[...] + (1.0 - beta_two) * gradient * gradient
        scaled = second_new * (1.0 / bias_two)
        update = moment_new * (1.0 / bias_one) / (scaled * lax.rsqrt(scaled) + adam_eps)
        update_ref[...] = update
        weight_ref[...] = (master_ref[...] - learn_rate * update).astype(weight_ref.dtype)

    here = pl.BlockSpec((tile, width), lambda i: (i, 0))
    return pl.pallas_call(
        kernel,
        grid=(rows // tile,),
        out_shape=[
            jax.ShapeDtypeStruct((rows, width), jnp.float32),
            jax.ShapeDtypeStruct((rows, width), jnp.bfloat16),
        ],
        in_specs=[here] * 5,
        out_specs=[here] * 2,
        compiler_params=params(),
        cost_estimate=pl.CostEstimate(
            flops=16 * rows * width, bytes_accessed=24 * rows * width, transcendentals=rows * width
        ),
        name="adam_rows",
    )(kept, got, w_master, moment_one, moment_two)


def norm_columns(states, gain, rows, line):
    length, width = states.shape
    tile = 64

    def kernel(states_ref, gain_ref, kept, sent):
        core = own_core()
        total = jnp.zeros((tile, 1), jnp.float32)
        for block in range(2 * line):
            piece = states_ref[:, block * rows : (block + 1) * rows].astype(jnp.float32)
            total = total + jnp.sum(piece * piece, axis=1, keepdims=True)
        scale = lax.rsqrt(total / width + norm_eps)
        for flag in range(2):

            @pl.when(core == flag)
            def _():
                for block in range(2 * line):
                    out = kept if block % 2 == flag else sent
                    columns = slice(block * rows, (block + 1) * rows)
                    piece = states_ref[:, columns].astype(jnp.float32)
                    out[block // 2] = (piece * scale * gain_ref[:, columns]).astype(out.dtype)

    return pl.pallas_call(
        kernel,
        grid=(length // tile,),
        out_shape=[jax.ShapeDtypeStruct((line, length, rows), jnp.bfloat16)] * 2,
        in_specs=[
            pl.BlockSpec((tile, width), lambda i: (i, 0)),
            pl.BlockSpec((1, width), lambda i: (0, 0)),
        ],
        out_specs=[pl.BlockSpec((line, tile, rows), lambda i: (0, i, 0))] * 2,
        compiler_params=params(),
        cost_estimate=pl.CostEstimate(
            flops=6 * length * width, bytes_accessed=4 * length * width, transcendentals=0
        ),
        name="norm_columns",
    )(states, gain.reshape(1, width))


def accumulate(totals, states, slots, dtypes):
    _, length, depth = states[0].shape
    sides = len(states)
    width = slots[0][1].shape[1]
    count = len(slots)
    tile = min(256, length)
    owners = jnp.stack([jnp.asarray(owner, jnp.int32) for owner, _ in slots])
    weights = [weight for _, weight in slots]

    def kernel(owners_ref, *refs):
        weight_refs = refs[sides * count : (sides + 1) * count]
        for side, out_ref in enumerate(refs[-sides:]):
            result = None if totals is None else refs[(sides + 1) * count + side][...]
            for slot in range(count):
                product = jnp.dot(
                    refs[side * count + slot][0],
                    weight_refs[slot][...],
                    preferred_element_type=jnp.float32,
                )
                result = product if result is None else result + product
            out_ref[...] = result.astype(out_ref.dtype)

    def state_spec(slot):
        return pl.BlockSpec((1, tile, depth), lambda i, chosen: (chosen[slot], i, 0))

    before = list(totals or [])
    row_spec = pl.BlockSpec((tile, width), lambda i, chosen: (i, 0))
    return pl.pallas_call(
        kernel,
        grid_spec=pltpu.PrefetchScalarGridSpec(
            num_scalar_prefetch=1,
            grid=(length // tile,),
            in_specs=[state_spec(slot) for slot in range(count)] * sides
            + [pl.BlockSpec((depth, width), lambda i, chosen: (0, 0))] * count
            + [row_spec] * len(before),
            out_specs=[row_spec] * sides,
        ),
        out_shape=[jax.ShapeDtypeStruct((length, width), dtype) for dtype in dtypes],
        compiler_params=params(20 if count > 1 else 8 + 4 * sides),
        cost_estimate=pl.CostEstimate(
            flops=2 * sides * count * length * depth * width,
            bytes_accessed=2 * count * depth * (2 * length + width) + 16 * length * width,
            transcendentals=0,
        ),
        name="accumulate",
    )(owners, *[array for array in states for _ in range(count)], *weights, *before)


def attention(kept, got, cosine_table, sine_table):
    length, width = kept.shape
    heads = width // HD - 2
    tile = min(128, length)

    def rope(u, cosine, sine):
        return u * cosine + pltpu.roll(u, HD // 2, 1) * sine

    def kernel(kept_ref, got_ref, cos_ref, sin_ref, out_ref):
        def columns(index, here=slice(None)):
            there = slice(index * HD, (index + 1) * HD)
            return kept_ref[here, there] + got_ref[here, there].astype(jnp.float32)

        keys = rope(columns(heads), cos_ref[...], sin_ref[...]).astype(jnp.bfloat16)
        values = columns(heads + 1).astype(jnp.bfloat16)
        for begin in range(0, length, tile):
            here, upto = slice(begin, begin + tile), begin + tile
            row = lax.broadcasted_iota(jnp.int32, (tile, upto), 0) + begin
            seen = row >= lax.broadcasted_iota(jnp.int32, (tile, upto), 1)
            for head in range(heads):
                query = rope(columns(head, here), cos_ref[here], sin_ref[here])
                query = (query * HD**-0.5).astype(jnp.bfloat16)
                scores = lax.dot_general(
                    query,
                    keys[:upto],
                    (((1,), (1,)), ((), ())),
                    preferred_element_type=jnp.float32,
                )
                scores = jnp.where(seen, scores, -jnp.inf)
                raised = jnp.exp(scores - jnp.max(scores, axis=1, keepdims=True))
                weights = raised * (1.0 / jnp.sum(raised, axis=1, keepdims=True))
                out_ref[here, head * HD : (head + 1) * HD] = jnp.dot(
                    weights.astype(jnp.bfloat16), values[:upto], preferred_element_type=jnp.float32
                ).astype(jnp.bfloat16)

    return pl.pallas_call(
        kernel,
        out_shape=jax.ShapeDtypeStruct((length, heads * HD), jnp.bfloat16),
        in_specs=whole_vmem(4),
        out_specs=pl.BlockSpec(memory_space=pltpu.VMEM),
        compiler_params=params(10),
        cost_estimate=pl.CostEstimate(
            flops=4 * heads * length * length * HD,
            bytes_accessed=9 * length * width,
            transcendentals=heads * length * length,
        ),
        name="attention",
    )(kept, got, cosine_table, sine_table)


def by_source(mine, other, n_tensor):
    kept, depth = mine.shape[0] // n_tensor, mine.shape[1]

    def kernel(mine_ref, other_ref, out_ref):
        index = lax.axis_index("tensor")
        for distance in range(n_tensor):
            columns = pl.ds(pl.multiple_of((index ^ distance) * depth, depth), depth)
            rows = slice(distance * kept, (distance + 1) * kept)
            out_ref[:kept, columns] = mine_ref[rows]
            out_ref[kept:, columns] = other_ref[rows]

    return pl.pallas_call(
        kernel,
        out_shape=jax.ShapeDtypeStruct((2 * kept, n_tensor * depth), mine.dtype),
        in_specs=whole_vmem(2),
        out_specs=pl.BlockSpec(memory_space=pltpu.VMEM),
        compiler_params=params(),
        name="by_source",
    )(mine, other)


def fetch(*arrays):
    parts = 4
    if sum(a.size * a.dtype.itemsize for a in arrays) > 20 * MIB:
        return arrays

    def kernel(*refs):
        sems = refs[-1]
        copies = []
        for which in range(len(arrays)):
            rows = arrays[which].shape[0] // parts
            for part in range(parts):
                here = pl.ds(part * rows, rows)
                copies.append(
                    pltpu.make_async_copy(
                        refs[which].at[here],
                        refs[len(arrays) + which].at[here],
                        sems.at[which * parts + part],
                    )
                )
        for copy in copies:
            copy.start()
        for copy in copies:
            copy.wait()

    return pl.pallas_call(
        kernel,
        out_shape=[jax.ShapeDtypeStruct(a.shape, a.dtype) for a in arrays],
        in_specs=[pl.BlockSpec(memory_space=pl.ANY)] * len(arrays),
        out_specs=whole_vmem(len(arrays)),
        scratch_shapes=[pltpu.SemaphoreType.DMA((parts * len(arrays),))],
        compiler_params=params(24),
        cost_estimate=pl.CostEstimate(
            flops=0, bytes_accessed=2 * sum(a.size * 2 for a in arrays), transcendentals=0
        ),
        name="fetch",
    )(*arrays)


def lay_out(blocks):
    kept = blocks[0][0].shape[0]
    half = sum(block.shape[1] for block in blocks[0])

    def kernel(*refs):
        out_ref = refs[-1]
        core = own_core()
        for flag in range(2):

            @pl.when(core == flag)
            def _():
                entry = 0
                for side in range(2):
                    begin = (flag ^ side) * half
                    for block in blocks[side]:
                        stop = begin + block.shape[1]
                        out_ref[:, begin:stop] = refs[entry][...]
                        begin, entry = stop, entry + 1

    flat = [block for side in blocks for block in side]
    return pl.pallas_call(
        kernel,
        out_shape=jax.ShapeDtypeStruct((kept, 2 * half), flat[0].dtype),
        in_specs=whole_vmem(len(flat)),
        out_specs=pl.BlockSpec(memory_space=pltpu.VMEM),
        compiler_params=params(),
        name="lay_out",
    )(*flat)


def body(
    train_states, qkv_cotangent, w_master, moment_one, moment_two, prompt_states, norm_gain, w_out
):
    n_dp = lax.axis_size("dp")
    n_tensor = lax.axis_size("tensor")
    line = n_dp // 2
    tensor_index = lax.axis_index("tensor")
    core, place = own_core(), own_place()
    siblings = [(i, i ^ 1) for i in range(n_dp)]
    rows, slice_width = w_master.shape
    tokens, width = train_states.shape
    length = prompt_states.shape[0]
    query_width = slice_width - 2 * HD

    kept_states, sent_states = norm_columns(prompt_states, norm_gain, rows, line)
    got_states = lax.ppermute(sent_states, "dp", siblings)

    core_width = width // 2
    early_width = EARLY_BLOCKS * core_width // 32
    packed, w_early = pack_columns(
        train_states, w_out, rows, line, tokens // n_tensor, early_width
    )
    def across(block, distance):
        return lax.ppermute(block, "dp", line_pairs([(i, i ^ distance) for i in range(line)]))

    pieces = [packed[0]] + [across(packed[distance], distance) for distance in range(1, line)]
    pieces = tie(pieces, kept_states)

    cotangents = [qkv_cotangent, across(qkv_cotangent, 1)]
    spread = PlaneGather(stack_pieces(pieces), n_tensor)
    behind = pieces
    for distance in range(2, line):
        cotangents.append(across(tie((qkv_cotangent,), *behind)[0], distance))
        behind = cotangents[-1:]
    spread.second(cotangents[2], spread.blocks[1:])
    all_cotangents = place_cotangents(cotangents, n_tensor)

    w_rest = lax.dynamic_slice(
        w_out,
        (0, core * core_width + early_width),
        (w_out.shape[0], core_width - early_width),
    )
    early_weight = lax.all_gather(w_early, "tensor", axis=0, tiled=True)
    (w_rest,) = tie((w_rest,), spread.blocks, cotangents, early_weight)
    rest_weight = lax.all_gather(w_rest, "tensor", axis=0, tiled=True)

    sent = gradient_term(spread.blocks, all_cotangents, True)
    got = lax.ppermute(sent, "dp", siblings)
    kept = gradient_term(spread.blocks, all_cotangents, False)
    update_dir, weight = adam_rows(kept, got, w_master, moment_one, moment_two)

    weights = LineGather(weight, place, line)

    def add(totals, states, steps, dtype=jnp.float32):
        slots = [weights.slot(step) for step in steps]
        return accumulate(totals, states, slots, [dtype] * len(states))

    both_states = (kept_states, got_states)
    for _ in range(1, line - 1):
        weights.hop()
    totals = add(None, both_states, range(line - 2))
    cosine_table, sine_table = rope_tables(length, HD)
    cosine_table, sine_table, *totals = tie((cosine_table, sine_table, *totals))
    weights.hop(*totals, cosine_table, sine_table)
    own_total, other_total = add(totals, both_states, [line - 2])
    (other_total,) = add([other_total], [got_states], [line - 1], jnp.bfloat16)
    got_total = lax.ppermute(other_total, "dp", siblings)
    (own_total,) = add([own_total], [kept_states], [line - 1])
    attended = attention(own_total, got_total, cosine_table, sine_table)

    kept_rows = length // n_tensor
    heads = []
    for distance in range(n_tensor):
        target = tensor_index ^ distance
        block = lax.dynamic_slice(attended, (target * kept_rows, 0), (kept_rows, query_width))
        if distance:
            block = lax.ppermute(block, "tensor", [(j, j ^ distance) for j in range(n_tensor)])
        heads.append(block)
    fetched = fetch(early_weight, rest_weight)
    heads = tie(heads, *fetched)
    (mine,) = stack_pieces([head[None] for head in heads])
    other = lax.ppermute(mine, "dp", siblings)
    both = by_source(mine, other, n_tensor)
    mine, sent = [], []
    for weight in fetched:
        made = jnp.dot(both, weight, preferred_element_type=jnp.float32).astype(jnp.bfloat16)
        mine.append(made[:kept_rows])
        sent.append(made[kept_rows:])
    summed = lay_out((mine, [lax.ppermute(rows, "dp", siblings) for rows in sent]))
    return (update_dir, summed)


def solution(mesh):
    placed = (
        P("dp", None),
        P("dp", "tensor"),
        P("dp", "tensor"),
        P("dp", "tensor"),
        P("dp", "tensor"),
        P("dp", None),
        P(),
        P("tensor", None),
    )
    return jax.shard_map(
        body,
        mesh=mesh,
        in_specs=placed,
        out_specs=(P("dp", "tensor"), P(("dp", "tensor"), None)),
        check_vma=False,
    )
```
